32 devices in a mesh: dp: 4 (over z), seq: 8 (over y, x, core).
Axes of the slice: x: 2, y: 2, z: 4, core: 2. Of those that a mesh axis runs over, the one named last changes fastest.
Arguments:
- hidden_in: bfloat16 [4, 2048, 2048], P('dp', 'seq'), may hold values from -6 to 6
- positions: int32 [4, 2048], P('dp', 'seq'), may hold values from 0 to 2047, as said below
- expert_ids: int32 [4, 2048, 6], P('dp', 'seq'), may hold values from 0 to 15, all different within a row; in each aligned block of 256 rows (0 to 255, 256 to 511, ..., all dimensions but the last counted through in order) at most 160 rows name the same one
- gate_weights: float32 [4, 2048, 6], P('dp', 'seq'), may hold values from 0.05 to 0.5
- attention_gain: bfloat16 [2048], P('dp'), may hold values from 0.25 to 1.75
- w_query: bfloat16 [2048, 3072], P('dp'), may hold values from -0.125 to 0.125
- w_compress: bfloat16 [2048, 576], P('dp'), may hold values from -0.125 to 0.125
- latent_gain: bfloat16 [512], P('dp'), may hold values from 0.25 to 1.75
- w_expand: bfloat16 [512, 4096], P('dp'), may hold values from -0.25 to 0.25
- w_output: bfloat16 [2048, 2048], P('dp'), may hold values from -1.5 to 1.5
- feedforward_gain: bfloat16 [2048], P('dp'), may hold values from 0.25 to 1.75
- w_shared_in: bfloat16 [2048, 5632], P('dp'), may hold values from -0.125 to 0.125
- w_shared_out: bfloat16 [2816, 2048], P('dp'), may hold values from -0.109375 to 0.109375
- w_expert_in: bfloat16 [32, 2048, 1408], P(('dp', 'seq')), may hold values from -0.125 to 0.125
- w_expert_out: bfloat16 [32, 704, 2048], P(('dp', 'seq')), may hold values from -0.15625 to 0.15625
- cotangent: bfloat16 [4, 2048, 2048], P('dp', 'seq'), may hold values from -6 to 6
Outputs:
- block_out: bfloat16 [4, 2048, 2048], P('dp', 'seq')
- hidden_gradient: bfloat16 [4, 2048, 2048], P('dp', 'seq')
- gate_gradient: float32 [4, 2048, 6], P('dp', 'seq')
- attention_gain_gradient: float32 [2048], P('dp')
- w_query_gradient: float32 [2048, 3072], P('dp')
- w_compress_gradient: float32 [2048, 576], P('dp')
- latent_gain_gradient: float32 [512], P('dp')
- w_expand_gradient: float32 [512, 4096], P('dp')
- w_output_gradient: float32 [2048, 2048], P('dp')
- feedforward_gain_gradient: float32 [2048], P('dp')
- w_shared_in_gradient: float32 [2048, 5632], P('dp')
- w_shared_out_gradient: float32 [2816, 2048], P('dp')
- w_expert_in_gradient: float32 [32, 2048, 1408], P(('dp', 'seq'))
- w_expert_out_gradient: float32 [32, 704, 2048], P(('dp', 'seq'))
The draws below stay inside these ranges and needn't reach their ends.
Inputs may be any that keep to these rules, and one draw needn't show every extreme that they name: `expert_ids`: each token names 6 different experts. Within the tokens of one sequence that one device holds (aligned blocks of 256 tokens) no expert is named by more than 160 tokens, a bound that some block reaches. `positions`: each sequence is a pack of documents; a token's position counts from the start of its document, and the first sequence is one document.
All inputs are finite; a program needn't handle non-finite values.
Results may differ from the reference program's by a relative error of at most 0.017.
Values may be sent and summed in bfloat16 or wider, within the bound.
A program may use at most 512 MiB of HBM per device.

```python
import math
import jax
import jax.numpy as jnp
import numpy as np
from jax import lax

D = 2048
HEADS = 16
NOPE = 128
ROPE = 64
VDIM = 128
LATENT = 512
FFE = 1408
TOP = 6
LEN = 2048
QK = 192
SH_FF = 2816
HALF = 704
LEN_DEV = 256
SEQS = 4
EXPERTS = 16
CAP_BLK = 160
N_SEQ = 8


def draw_positions(key, part):
    boundary = jax.random.randint(key, (SEQS, LEN), 0, LEN) < 8
    column_index = jnp.broadcast_to(jnp.arange(LEN, dtype=jnp.int32)[None, :], (SEQS, LEN))
    boundary = boundary.at[:, 0].set(True)
    boundary = boundary.at[0, :].set(column_index[0] == 0)
    segment_start = jnp.where(boundary, column_index, 0)
    return column_index - lax.cummax(segment_start, axis=1)


def block_scale(rng, dims, pieces, smallest, top_value):
    gain = 1.0
    for position, parts in pieces:
        heights = jax.random.uniform(jax.random.fold_in(jax.random.fold_in(rng, 6), position), (parts,), jnp.float32, smallest / len(pieces), top_value / len(pieces))
        gain = gain * jnp.repeat(jnp.exp(heights), dims[position] // parts).reshape((-1,) + (1,) * (len(dims) - 1 - position))
    return gain


def deal_out(stream_key, own, number, rows, number_of, top, most, skew):
    ranking = jax.random.permutation(stream_key, number_of)
    heavy_load, usual = shares(number_of, rows * top, most, skew, True), shares(number_of, rows * top, most, skew, False)
    places = jnp.arange(number_of)

    def named(lengths, turn):
        used = int((lengths > 0).sum())
        fixed = max(1, used // 4)
        shifted = fixed + (places - fixed + turn * (used - fixed)) % max(1, number_of - fixed)
        return jnp.zeros((number_of,), jnp.int32).at[ranking[jnp.where(places < fixed, places, shifted)]].set(jnp.asarray(lengths, jnp.int32))

    lengths = jnp.where(number % 4 == 0, named(heavy_load, number // 4), named(usual, number - number // 4 - 1))
    mixed = jax.random.permutation(jax.random.fold_in(own, 3), number_of)
    donor, receiver = mixed[0:number_of // 2 * 2:2], mixed[1:number_of // 2 * 2:2]
    room = jnp.minimum(lengths[donor] - 1, most - lengths[receiver]) // 2
    room = jnp.where((donor == ranking[0]) | (receiver == ranking[0]) | (lengths[receiver] == 0), 0, jnp.maximum(room, 0))
    shifted = jax.random.randint(jax.random.fold_in(own, 4), (number_of // 2,), 0, 1 << 20) % (room + 1)
    lengths = lengths.at[donor].add(-shifted).at[receiver].add(shifted)
    items = jnp.searchsorted(jnp.cumsum(lengths), jnp.arange(rows * top), side="right").astype(jnp.int32)
    table = items.reshape(top, rows).T
    table = table[jax.random.permutation(jax.random.fold_in(own, 1), rows)]
    turn = jax.random.randint(jax.random.fold_in(own, 2), (rows, 1), 0, top)
    return jnp.take_along_axis(table, (jnp.arange(top)[None, :] + turn) % top, axis=1)


def shares(count, total, reach, lean, full):
    portions = [(1 << 20) // math.isqrt(rank ** lean) + 1 for rank in range(1, count + 1)]
    largest = reach if full else min(reach, max(-(-total // count), total * portions[0] // sum(portions)))
    least = 1 if total - largest >= count - 1 else 0
    holding, rest = [largest] + [least] * (count - 1), total - largest - least * (count - 1)
    while rest > 0:
        free = [i for i in range(1, count) if holding[i] < largest] or [i for i in range(1, count) if holding[i] < reach]
        mass, left = sum([portions[i] for i in free]), rest
        for i in free:
            more = min(reach - holding[i], max(1, left * portions[i] // mass), rest)
            holding[i] = holding[i] + more
            rest = rest - more
    return np.array(holding)


def gaussian(own_key, extent, scale, most, cuts=(), kind=jnp.bfloat16):
    loudness = block_scale(own_key, extent, cuts, -0.22, 0.18) if cuts else 1.0
    drawn = jax.random.normal(own_key, extent, jnp.float32) * scale * loudness
    return jnp.minimum(jnp.maximum(drawn, -most), most).astype(kind)


def setup_inputs(seed: int = 0) -> dict:
    arg_keys = jax.random.split(jax.random.key(seed), 17)
    hidden_in = gaussian(arg_keys[0], (SEQS, LEN, D), 1.0, 6.0, ((0, 4), (1, 8)))
    positions = draw_positions(jax.random.fold_in(arg_keys[16], 71), 0)
    expert_ids_keys = jax.random.split(jax.random.fold_in(arg_keys[2], 1), SEQS * LEN // LEN_DEV)
    expert_ids_turns = jax.random.permutation(jax.random.fold_in(arg_keys[2], 3), SEQS * LEN // LEN_DEV)
    expert_ids = jax.vmap(lambda own, number: deal_out(jax.random.fold_in(arg_keys[2], 2), own, number, LEN_DEV, EXPERTS, TOP, CAP_BLK, 1))(expert_ids_keys, expert_ids_turns).reshape((SEQS, LEN, TOP))
    gate_weights = jnp.clip(jnp.exp(math.log(0.5) - 2.3025851 * jax.random.uniform(arg_keys[3], (SEQS, LEN, TOP), jnp.float32) ** block_scale(arg_keys[3], (SEQS, LEN, TOP), ((0, 4), (1, 8)), -0.2, 0.2)), 0.05, 0.5)
    attention_gain = jnp.clip(1.0 + 0.15 * jax.random.normal(arg_keys[4], (D,), jnp.float32), 0.25, 1.75).astype(jnp.bfloat16)
    w_query = gaussian(arg_keys[5], (D, HEADS * QK), D ** -0.5, 0.125, ((0, 4),))
    w_compress = gaussian(arg_keys[6], (D, LATENT + ROPE), D ** -0.5, 0.125, ((0, 4),))
    latent_gain = jnp.clip(1.0 + 0.15 * jax.random.normal(arg_keys[7], (LATENT,), jnp.float32), 0.25, 1.75).astype(jnp.bfloat16)
    w_expand = gaussian(arg_keys[8], (LATENT, HEADS * (NOPE + VDIM)), LATENT ** -0.5, 0.25, ((0, 4),))
    w_output = gaussian(arg_keys[9], (HEADS * VDIM, D), (max(1, HEADS * VDIM * 16 // LEN)) ** -0.5, 1.5, ((0, 4),))
    feedforward_gain = jnp.clip(1.0 + 0.15 * jax.random.normal(arg_keys[10], (D,), jnp.float32), 0.25, 1.75).astype(jnp.bfloat16)
    w_shared_in = gaussian(arg_keys[11], (D, 2 * SH_FF), D ** -0.5, 0.125, ((0, 4),))
    w_shared_out = gaussian(arg_keys[12], (SH_FF, D), SH_FF ** -0.5, 0.109375, ((0, 4),))
    w_expert_in = gaussian(arg_keys[13], (2 * EXPERTS, D, 2 * HALF), D ** -0.5, 0.125, ((0, 32),))
    w_expert_out = gaussian(arg_keys[14], (2 * EXPERTS, HALF, D), FFE ** -0.5, 0.15625, ((0, 32),))
    cotangent = gaussian(arg_keys[15], (SEQS, LEN, D), 1.0, 6.0, ((0, 4), (1, 8)))
    return {"hidden_in": hidden_in, "positions": positions, "expert_ids": expert_ids, "gate_weights": gate_weights, "attention_gain": attention_gain, "w_query": w_query, "w_compress": w_compress, "latent_gain": latent_gain, "w_expand": w_expand, "w_output": w_output, "feedforward_gain": feedforward_gain, "w_shared_in": w_shared_in, "w_shared_out": w_shared_out, "w_expert_in": w_expert_in, "w_expert_out": w_expert_out, "cotangent": cotangent}


EPSILON = 1e-06
HIGHEST_PRECISION = lax.Precision.HIGHEST

@jax.custom_vjp
def low(v):
    return lax.optimization_barrier(v.astype(jnp.bfloat16)).astype(jnp.float32)

@jax.custom_vjp
def low_back(v):
    return v

def low_keep(v):
    return (low(v), None)

def low_pass(kept, grad):
    return (grad,)

def back_keep(v):
    return (v, None)

def back_low(kept, grad):
    return (low(grad),)
low.defvjp(low_keep, low_pass)
low_back.defvjp(back_keep, back_low)

def matmul(left, right):
    return jnp.dot(left, right, precision=HIGHEST_PRECISION)

def sigmoid_linear(entries):
    return entries / (1.0 + jnp.exp(-entries))

def rms_scale(entries):
    return lax.rsqrt(lax.optimization_barrier(jnp.mean(entries * entries, axis=-1, keepdims=True)) + EPSILON)

def rotary_angles(position_row):
    steps_index = jnp.arange(ROPE // 2, dtype=jnp.float32)
    frequency = 10000.0 ** (-2.0 * steps_index / ROPE)
    return position_row.astype(jnp.float32)[..., None] * frequency

def rotate(values, angle):
    half_width = values.shape[-1] // 2
    front_half = values[..., :half_width]
    back_half = values[..., half_width:]
    cosine_values = jnp.cos(angle)
    sine_values = jnp.sin(angle)
    return jnp.concatenate([front_half * cosine_values - back_half * sine_values, front_half * sine_values + back_half * cosine_values], axis=-1)

def attend(queries, keys_all, values_all):
    block_rows = min(512, LEN)
    scale_factor = 1.0 / math.sqrt(QK)
    key_index = jnp.arange(LEN, dtype=jnp.int32)

    def one_block(block_start):
        query_rows = lax.dynamic_slice_in_dim(queries, block_start, block_rows, 0)
        scores = low_back(jnp.einsum('qhd,khd->hqk', query_rows, keys_all, precision=HIGHEST_PRECISION) * scale_factor)
        query_index = block_start + jnp.arange(block_rows, dtype=jnp.int32)
        allowed = key_index[None, :] <= query_index[:, None]
        scores = jnp.where(allowed[None], scores, -1e+30)
        largest = lax.optimization_barrier(jnp.max(scores, axis=-1, keepdims=True))
        weights = jnp.exp(scores - largest)
        weights = low(weights / lax.optimization_barrier(jnp.sum(weights, axis=-1, keepdims=True)))
        return jnp.einsum('hqk,khd->qhd', weights, values_all, precision=HIGHEST_PRECISION)
    starts = jnp.arange(LEN // block_rows, dtype=jnp.int32) * block_rows
    return lax.map(jax.checkpoint(one_block), starts).reshape(LEN, HEADS, VDIM)

def routed_experts(moe_rows, sequence_ids, sequence_gates, w_expert_in, w_expert_out):
    capacity = N_SEQ * CAP_BLK
    flat_ids = sequence_ids.reshape(LEN * TOP)
    one_hot = (flat_ids[:, None] == jnp.arange(EXPERTS, dtype=jnp.int32)[None, :]).astype(jnp.int32)
    within = lax.optimization_barrier(jnp.sum((jnp.cumsum(one_hot, axis=0) - 1) * one_hot, axis=1))
    target = flat_ids * capacity + within
    owners = jnp.zeros((EXPERTS * capacity,), jnp.int32).at[target].set(jnp.arange(LEN * TOP, dtype=jnp.int32) // TOP)
    filled = jnp.zeros((EXPERTS * capacity,), jnp.float32).at[target].set(1.0)

    def one_expert(operands):
        weight_in, weight_out, owner_rows, filled_rows = operands
        gathered = moe_rows[owner_rows] * filled_rows[:, None]
        total = jnp.zeros((capacity, D), jnp.float32)
        for half_index in range(2):
            taken_rows = low_back(gathered)
            gate_up = low_back(matmul(taken_rows, weight_in[half_index]))
            hidden = low(sigmoid_linear(gate_up[:, :HALF]) * gate_up[:, HALF:])
            total = total + low_back(low(matmul(hidden, weight_out[half_index])))
        return total
    produced = lax.map(jax.checkpoint(one_expert), (w_expert_in.reshape(EXPERTS, 2, D, 2 * HALF), w_expert_out.reshape(EXPERTS, 2, HALF, D), owners.reshape(EXPERTS, capacity), filled.reshape(EXPERTS, capacity)))
    picked = produced.reshape(EXPERTS * capacity, D)[target].reshape(LEN, TOP, D)
    return lax.optimization_barrier(jnp.sum(sequence_gates[:, :, None] * picked, axis=1))

def one_sequence(params, hidden_rows, position_row, id_rows, gate_rows):
    attention_gain, w_query, w_compress, latent_gain, w_expand, w_output, feedforward_gain, w_shared_in, w_shared_out, w_expert_in, w_expert_out = params
    normed = low(hidden_rows * rms_scale(hidden_rows) * attention_gain)
    angle_table = rotary_angles(position_row)
    query_raw = low_back(matmul(normed, w_query)).reshape(LEN, HEADS, QK)
    queries = jnp.concatenate([query_raw[..., :NOPE], rotate(query_raw[..., NOPE:], angle_table[:, None, :])], axis=-1)
    queries = low_back(low(queries))
    compressed = low_back(matmul(normed, w_compress))
    latent = compressed[:, :LATENT]
    key_rotary = rotate(compressed[:, LATENT:], angle_table)
    latent_normed = low(latent * rms_scale(latent) * latent_gain)
    expanded = matmul(latent_normed, w_expand).reshape(LEN, HEADS, NOPE + VDIM)
    keys_all = jnp.concatenate([expanded[..., :NOPE], jnp.broadcast_to(key_rotary[:, None, :], (LEN, HEADS, ROPE))], axis=-1)
    keys_all = low_back(low(keys_all))
    values_all = low_back(low(expanded[..., NOPE:]))
    attended = low_back(low(attend(queries, keys_all, values_all))).reshape(LEN, HEADS * VDIM)
    middle = hidden_rows + low_back(matmul(attended, w_output))
    moe_rows = low(middle * rms_scale(middle) * feedforward_gain)
    shared_gate_up = low_back(matmul(moe_rows, w_shared_in))
    shared_hidden = low(sigmoid_linear(shared_gate_up[:, :SH_FF]) * shared_gate_up[:, SH_FF:])
    shared_result = matmul(shared_hidden, w_shared_out)
    return middle + shared_result + routed_experts(moe_rows, id_rows, gate_rows, w_expert_in, w_expert_out)

def reference(hidden_in, positions, expert_ids, gate_weights, attention_gain, w_query, w_compress, latent_gain, w_expand, w_output, feedforward_gain, w_shared_in, w_shared_out, w_expert_in, w_expert_out, cotangent):
    param_floats = tuple((array.astype(jnp.float32) for array in (attention_gain, w_query, w_compress, latent_gain, w_expand, w_output, feedforward_gain, w_shared_in, w_shared_out, w_expert_in, w_expert_out)))

    def forward(hidden_float, gates_float, *params):

        def step(nothing, items):
            hidden_rows, position_row, id_rows, gate_rows = items
            return (nothing, one_sequence(params, hidden_rows, position_row, id_rows, gate_rows))
        nothing, results = lax.scan(jax.checkpoint(step), jnp.zeros((), jnp.float32), (hidden_float, positions, expert_ids, gates_float))
        return results
    output, pullback = jax.vjp(forward, hidden_in.astype(jnp.float32), gate_weights.astype(jnp.float32), *param_floats)
    gradients = pullback(cotangent.astype(jnp.float32))
    return (output.astype(jnp.bfloat16), gradients[0].astype(jnp.bfloat16), gradients[1], gradients[2], gradients[3], gradients[4], gradients[5], gradients[6], gradients[7], gradients[8], gradients[9], gradients[10], gradients[11], gradients[12])
```

```python
import math

import jax
import jax.numpy as jnp
from jax import lax
from jax.sharding import PartitionSpec as P

HEADS = 16
NOPE = 128
ROPE = 64
VDIM = 128
LATENT = 512
TOP = 6
QK = 192
SH_FF = 2816
HALF = 704
EPSILON = 1e-06
BF = jnp.bfloat16
F32 = jnp.float32


def rms_scale(entries):
    return lax.rsqrt(jnp.mean(entries * entries, axis=-1, keepdims=True) + EPSILON)


def rotary_angles(position_rows):
    steps_index = jnp.arange(ROPE // 2, dtype=F32)
    frequency = 10000.0 ** (-2.0 * steps_index / ROPE)
    return position_rows.astype(F32)[..., None] * frequency


def rotate(values, cosine_values, sine_values):
    half_width = values.shape[-1] // 2
    front_half = values[..., :half_width]
    back_half = values[..., half_width:]
    return jnp.concatenate(
        [
            front_half * cosine_values - back_half * sine_values,
            front_half * sine_values + back_half * cosine_values,
        ],
        axis=-1,
    )


def norm_backward(upstream, entries, inverse_scale, gain_row):
    scaled = upstream * gain_row
    return inverse_scale * scaled - entries * inverse_scale**3 * jnp.mean(
        scaled * entries, axis=-1, keepdims=True
    )


def dot(a, b):
    return jnp.dot(a, b, preferred_element_type=F32)


def dot_nt(a, b):
    return jnp.einsum("ik,jk->ij", a, b, preferred_element_type=F32)


def dot_tn(a, b):
    return jnp.einsum("ki,kj->ij", a, b, preferred_element_type=F32)


def attention_forward(queries, keys_all, values_all):
    length, head_count, head_width = queries.shape
    block_rows = min(512, length)
    scale_factor = 1.0 / math.sqrt(head_width)
    outs = []
    logs = []
    for start in range(0, length, block_rows):
        end = start + block_rows
        scores = (
            jnp.einsum(
                "qhd,khd->hqk", queries[start:end], keys_all[:end], preferred_element_type=F32
            )
            * scale_factor
        )
        allowed = jnp.arange(end)[None, :] <= (start + jnp.arange(block_rows))[:, None]
        scores = jnp.where(allowed[None], scores, -1e30)
        largest = jnp.max(scores, axis=-1, keepdims=True)
        weights = jnp.exp(scores - largest)
        totals = jnp.sum(weights, axis=-1, keepdims=True)
        shares = (weights / totals).astype(BF)
        attended = jnp.einsum("hqk,khd->qhd", shares, values_all[:end], preferred_element_type=F32)
        outs.append(attended.astype(BF))
        logs.append((largest + jnp.log(totals))[..., 0])
    return jnp.concatenate(outs, axis=0), logs


def attention_backward(queries, keys_all, values_all, logs, upstream_heads):
    length, head_count, head_width = queries.shape
    block_rows = min(512, length)
    scale_factor = 1.0 / math.sqrt(head_width)
    key_sums = jnp.zeros((length, head_count, head_width), F32)
    value_sums = jnp.zeros((length, head_count, VDIM), F32)
    query_grads = []
    for index, start in enumerate(range(0, length, block_rows)):
        end = start + block_rows
        query_rows = queries[start:end]
        upstream = upstream_heads[start:end]
        scores = (
            jnp.einsum("qhd,khd->hqk", query_rows, keys_all[:end], preferred_element_type=F32)
            * scale_factor
        )
        allowed = jnp.arange(end)[None, :] <= (start + jnp.arange(block_rows))[:, None]
        scores = jnp.where(allowed[None], scores, -1e30)
        shares = jnp.exp(scores - logs[index][..., None])
        share_grad = jnp.einsum(
            "qhd,khd->hqk", upstream, values_all[:end], preferred_element_type=F32
        )
        centre = jnp.sum(shares * share_grad, axis=-1, keepdims=True)
        score_grad = (shares * (share_grad - centre)).astype(BF)
        query_grads.append(
            jnp.einsum("hqk,khd->qhd", score_grad, keys_all[:end], preferred_element_type=F32)
            * scale_factor
        )
        key_sums = key_sums.at[:end].add(
            jnp.einsum("hqk,qhd->khd", score_grad, query_rows, preferred_element_type=F32)
            * scale_factor
        )
        value_sums = value_sums.at[:end].add(
            jnp.einsum("hqk,qhd->khd", shares.astype(BF), upstream, preferred_element_type=F32)
        )
    return (
        jnp.concatenate(query_grads, axis=0).astype(BF),
        key_sums.astype(BF),
        value_sums.astype(BF),
    )


def on_device(
    hidden_in,
    positions,
    expert_ids,
    gate_weights,
    attention_gain,
    w_query,
    w_compress,
    latent_gain,
    w_expand,
    w_output,
    feedforward_gain,
    w_shared_in,
    w_shared_out,
    w_expert_in,
    w_expert_out,
    cotangent,
):
    n_dp = lax.axis_size("dp")
    n_seq = lax.axis_size("seq")
    n_all = n_dp * n_seq
    both = ("dp", "seq")
    dp_index = lax.axis_index("dp")
    seq_index = lax.axis_index("seq")
    sequence_count, rows, features = hidden_in.shape
    rows = sequence_count * rows
    length = rows * n_seq
    heads = HEADS // n_seq
    shard = features // n_dp
    expert_count = n_all // 2
    capacity = max(2, rows * TOP * 5 // (expert_count * 3))
    units = SH_FF // n_all

    hidden = hidden_in.reshape(rows, features)
    upstream_rows = cotangent.reshape(rows, features)
    upstream_float = upstream_rows.astype(F32)
    id_rows = expert_ids.reshape(rows, TOP)
    gate_table = gate_weights.reshape(rows, TOP)

    hidden_all = lax.all_gather(hidden, "seq", axis=0, tiled=True)
    gains = lax.all_gather(
        jnp.concatenate([attention_gain, feedforward_gain, latent_gain]), "dp", axis=0
    ).astype(F32)
    first_gain = gains[:, :shard].reshape(features)
    second_gain = gains[:, shard : 2 * shard].reshape(features)
    latent_gain_row = gains[:, 2 * shard :].reshape(LATENT)
    positions_all = lax.all_gather(positions.reshape(rows), "seq", axis=0, tiled=True)
    query_part = lax.dynamic_slice_in_dim(w_query, seq_index * heads * QK, heads * QK, 1)
    expand_part = lax.dynamic_slice_in_dim(
        w_expand, seq_index * heads * (NOPE + VDIM), heads * (NOPE + VDIM), 1
    )
    query_weight = lax.all_gather(query_part, "dp", axis=0, tiled=True)
    compress_weight = lax.all_gather(w_compress, "dp", axis=0, tiled=True)
    expand_weight = lax.all_gather(expand_part, "dp", axis=0, tiled=True)
    output_weight = lax.all_gather(w_output, "dp", axis=0, tiled=True)
    shared_part = lax.dynamic_index_in_dim(
        w_shared_in.reshape(shard, 2, n_dp, n_seq, units), seq_index, 3, keepdims=False
    )
    shared_in = (
        lax.all_to_all(
            shared_part.transpose(2, 0, 1, 3), "dp", split_axis=0, concat_axis=0, tiled=True
        )
        .reshape(features, 2 * units)
    )
    shared_out = lax.dynamic_slice_in_dim(w_shared_out, seq_index * units, units, 0)
    upstream_all = lax.all_gather(upstream_rows, both, axis=0, tiled=True)
    ids_all = lax.all_gather(id_rows.T, both, axis=0)
    gates_all = lax.all_gather(gate_table.T, both, axis=0)

    hidden_all_float = hidden_all.astype(F32)
    normed_all = (hidden_all_float * rms_scale(hidden_all_float) * first_gain).astype(BF)
    angles = rotary_angles(positions_all)
    cosine_all, sine_all = jnp.cos(angles), jnp.sin(angles)
    query_raw = dot(normed_all, query_weight).reshape(length, heads, QK)
    queries = jnp.concatenate(
        [
            query_raw[..., :NOPE],
            rotate(query_raw[..., NOPE:], cosine_all[:, None], sine_all[:, None]),
        ],
        axis=-1,
    ).astype(BF)
    compressed = dot(normed_all, compress_weight)
    latent = compressed[:, :LATENT]
    key_rotary = rotate(compressed[:, LATENT:], cosine_all, sine_all)
    latent_scale = rms_scale(latent)
    latent_normed = (latent * latent_scale * latent_gain_row).astype(BF)
    expanded = dot(latent_normed, expand_weight).reshape(length, heads, NOPE + VDIM)
    keys_all = jnp.concatenate(
        [expanded[..., :NOPE], jnp.broadcast_to(key_rotary[:, None, :], (length, heads, ROPE))],
        axis=-1,
    ).astype(BF)
    values_all = expanded[..., NOPE:].astype(BF)
    attended_heads, logs = attention_forward(queries, keys_all, values_all)
    attended = lax.all_to_all(
        attended_heads.reshape(length, heads * VDIM), "seq", split_axis=0, concat_axis=1, tiled=True
    )
    hidden_float = hidden.astype(F32)
    middle = hidden_float + dot(attended, output_weight)
    second_scale = rms_scale(middle)
    moe_rows = (middle * second_scale * second_gain).astype(BF)

    rows_all = lax.all_gather(moe_rows, both, axis=0, tiled=True)
    attended_all = lax.all_gather(attended, "seq", axis=0, tiled=True)
    expert = (dp_index * n_seq + seq_index) // 2
    named = ids_all == expert
    chosen = jnp.any(named, axis=1)
    gate_rows = jnp.sum(jnp.where(named, gates_all, 0.0), axis=1)
    before = (jnp.arange(rows)[:, None] < jnp.arange(rows)[None, :]).astype(BF)
    place = dot(chosen.astype(BF), before).astype(jnp.int32)
    picked = chosen[:, None, :] & (
        place[:, None, :] == jnp.arange(capacity, dtype=jnp.int32)[None, :, None]
    )
    pick = picked.astype(BF)
    gate_slots = jnp.sum(jnp.where(picked, gate_rows[:, None, :], 0.0), axis=2)[..., None]
    rows_blocks = rows_all.reshape(n_all, rows, features)
    upstream_blocks = upstream_all.reshape(n_all, rows, features)
    slot_rows = jnp.einsum("bst,btd->bsd", pick, rows_blocks, preferred_element_type=F32)
    slot_rows = slot_rows.astype(BF).reshape(n_all * capacity, features)
    slot_cot = jnp.einsum("bst,btd->bsd", pick, upstream_blocks, preferred_element_type=F32)
    slot_upstream = (slot_cot * gate_slots).astype(BF).reshape(n_all * capacity, features)
    weight_in, weight_out = w_expert_in[0], w_expert_out[0]

    def gated(rows_in, upstream, w_in, w_out, width):
        gate_up = dot(rows_in, w_in)
        gate, up = gate_up[:, :width], gate_up[:, width:]
        sigmoid = 1.0 / (1.0 + jnp.exp(-gate))
        active = gate * sigmoid
        hidden_units = (active * up).astype(BF)
        hidden_back = dot_nt(upstream, w_out)
        gate_back = hidden_back * up * sigmoid * (1.0 + gate * (1.0 - sigmoid))
        both_back = jnp.concatenate([gate_back, hidden_back * active], axis=-1).astype(BF)
        return hidden_units, both_back, dot_tn(rows_in, both_back), dot_tn(hidden_units, upstream)

    hidden_units, both_back, expert_in_grad, expert_out_grad = gated(
        slot_rows, slot_upstream, weight_in, weight_out, HALF
    )
    slot_result = dot(hidden_units, weight_out).astype(BF)
    slot_back = dot_nt(both_back, weight_in).astype(BF)
    shared_units, shared_both_back, shared_in_grad, shared_out_grad = gated(
        rows_all, upstream_all, shared_in, shared_out, units
    )
    slot_back = slot_back.reshape(n_all, capacity, features)
    back_part = jnp.einsum("bst,bsd->btd", pick, slot_back, preferred_element_type=F32)
    back_part = back_part.reshape(n_all * rows, features) + dot_nt(shared_both_back, shared_in)
    back_sum = lax.psum_scatter(back_part.astype(BF), both, scatter_dimension=0, tiled=True)

    slot_float = slot_result.astype(F32).reshape(n_all, capacity, features)
    slot_gate_grad = jnp.sum(slot_float * slot_cot, axis=-1)
    weighted = (slot_float * gate_slots).astype(BF)
    out_part = jnp.einsum("bst,bsd->btd", pick, weighted, preferred_element_type=F32)
    out_part = out_part.reshape(n_all * rows, features) + dot(shared_units, shared_out)
    out_sum = lax.psum_scatter(out_part.astype(BF), both, scatter_dimension=0, tiled=True)
    token_gate_grad = jnp.sum(jnp.where(picked, slot_gate_grad[..., None], 0.0), axis=1)
    gate_grads = lax.all_to_all(token_gate_grad, both, split_axis=0, concat_axis=0, tiled=True)
    gate_grads = jnp.sum(gate_grads.reshape(expert_count, 2, rows), axis=1)
    gate_gradient = jnp.sum(
        jnp.where(
            id_rows[:, :, None] == jnp.arange(expert_count, dtype=jnp.int32),
            gate_grads.T[:, None, :],
            0.0,
        ),
        axis=-1,
    )
    block_out = (middle + out_sum.astype(F32)).astype(BF)

    moe_back = back_sum.astype(F32)
    second_gain_grad = jnp.sum(moe_back * middle * second_scale, axis=0)
    middle_back = upstream_float + norm_backward(moe_back, middle, second_scale, second_gain)
    middle_low = middle_back.astype(BF)
    middle_columns = lax.all_to_all(middle_low, "seq", split_axis=1, concat_axis=0, tiled=True)
    output_grad = dot_tn(attended_all, middle_columns)
    attended_back = dot_nt(middle_low, output_weight).astype(BF)
    upstream_heads = lax.all_to_all(
        attended_back, "seq", split_axis=1, concat_axis=0, tiled=True
    ).reshape(length, heads, VDIM)
    query_back, key_back, value_back = attention_backward(
        queries, keys_all, values_all, logs, upstream_heads
    )
    query_raw_back = (
        jnp.concatenate(
            [
                query_back[..., :NOPE].astype(F32),
                rotate(query_back[..., NOPE:].astype(F32), cosine_all[:, None], -sine_all[:, None]),
            ],
            axis=-1,
        )
        .astype(BF)
        .reshape(length, heads * QK)
    )
    expanded_back = jnp.concatenate([key_back[..., :NOPE], value_back], axis=-1).reshape(
        length, heads * (NOPE + VDIM)
    )
    query_grad = dot_tn(normed_all, query_raw_back)
    expand_grad = dot_tn(latent_normed, expanded_back)
    partial_back = jnp.concatenate(
        [
            dot_nt(query_raw_back, query_weight),
            dot_nt(expanded_back, expand_weight),
            jnp.sum(key_back[..., NOPE:].astype(F32), axis=1),
        ],
        axis=-1,
    ).astype(BF)
    summed_back = lax.psum_scatter(partial_back, "seq", scatter_dimension=0, tiled=True).astype(F32)
    latent_normed_back = summed_back[:, features : features + LATENT]
    own = seq_index * rows

    def mine(array):
        return lax.dynamic_slice_in_dim(array, own, rows, 0)

    latent_own, latent_scale_own = mine(latent), mine(latent_scale)
    latent_gain_grad = jnp.sum(latent_normed_back * latent_own * latent_scale_own, axis=0)
    latent_back = norm_backward(latent_normed_back, latent_own, latent_scale_own, latent_gain_row)
    rotary_back = rotate(summed_back[:, features + LATENT :], mine(cosine_all), -mine(sine_all))
    compressed_back = jnp.concatenate([latent_back, rotary_back], axis=-1).astype(BF)
    compressed_back_all = lax.all_gather(compressed_back, "seq", axis=0, tiled=True)
    width = (LATENT + ROPE) // n_seq
    compress_grad = dot_tn(
        normed_all, lax.dynamic_slice_in_dim(compressed_back_all, seq_index * width, width, 1)
    )
    normed_back = summed_back[:, :features] + dot_nt(compressed_back, compress_weight)
    first_scale = rms_scale(hidden_float)
    first_gain_grad = jnp.sum(normed_back * hidden_float * first_scale, axis=0)
    hidden_gradient = (
        middle_back + norm_backward(normed_back, hidden_float, first_scale, first_gain)
    ).astype(BF)

    gain_grads = lax.psum(
        jnp.concatenate([first_gain_grad, second_gain_grad, latent_gain_grad]), both
    )
    latent_shard = LATENT // n_dp

    def gain_part(start, size):
        return lax.dynamic_slice_in_dim(gain_grads, start + dp_index * size, size, 0)

    def over_dp(grad):
        return lax.psum_scatter(grad, "dp", scatter_dimension=0, tiled=True).astype(BF)

    def columns(part):
        return lax.all_gather(part, "seq", axis=1, tiled=True).astype(F32)

    shared_in_out = lax.all_to_all(
        shared_in_grad.astype(BF).reshape(n_dp, shard, 2, units),
        "dp",
        split_axis=0,
        concat_axis=0,
        tiled=True,
    )
    shared_in_out = lax.all_gather(shared_in_out, "seq", axis=0)
    shared_in_out = shared_in_out.transpose(2, 3, 1, 0, 4).reshape(shard, 2 * SH_FF).astype(F32)
    shared_out_out = lax.all_gather(
        shared_out_grad.astype(BF), "seq", axis=0, tiled=True
    ).astype(F32)
    return (
        block_out.reshape(hidden_in.shape),
        hidden_gradient.reshape(hidden_in.shape),
        gate_gradient.reshape(gate_weights.shape),
        gain_part(0, shard),
        columns(over_dp(query_grad)),
        columns(over_dp(compress_grad)),
        gain_part(2 * features, latent_shard),
        columns(over_dp(expand_grad)),
        columns(over_dp(output_grad)),
        gain_part(features, shard),
        shared_in_out,
        shared_out_out,
        expert_in_grad[None],
        expert_out_grad[None],
    )


def solution(mesh):
    token = P("dp", "seq", None)
    row = P("dp", None)
    half = P(("dp", "seq"), None, None)
    return jax.shard_map(
        on_device,
        mesh=mesh,
        in_specs=(
            token, P("dp", "seq"), token, token, P("dp"), row, row, P("dp"), row, row,
            P("dp"), row, row, half, half, token,
        ),
        out_specs=(
            token, token, token, P("dp"), row, row, P("dp"), row, row, P("dp"), row, row,
            half, half,
        ),
        check_vma=False,
    )
```

```python
import functools
import math

import jax
import jax.numpy as jnp
from jax import lax
from jax.experimental import pallas as pl
from jax.experimental.pallas import tpu as pltpu
from jax.sharding import PartitionSpec as P

HEADS = 16
NOPE = 128
ROPE = 64
VDIM = 128
LATENT = 512
TOP = 6
QK = 192
SH_FF = 2816
HALF = 704
EPSILON = 1e-06
BF = jnp.bfloat16
F32 = jnp.float32


def rms_scale(entries):
    return lax.rsqrt(jnp.mean(entries * entries, axis=-1, keepdims=True) + EPSILON)


def rotary_angles(position_rows):
    steps_index = jnp.arange(ROPE // 2, dtype=F32)
    frequency = 10000.0 ** (-2.0 * steps_index / ROPE)
    return position_rows.astype(F32)[..., None] * frequency


def rotate(values, cosine_values, sine_values):
    half_width = values.shape[-1] // 2
    front_half = values[..., :half_width]
    back_half = values[..., half_width:]
    return jnp.concatenate(
        [
            front_half * cosine_values - back_half * sine_values,
            front_half * sine_values + back_half * cosine_values,
        ],
        axis=-1,
    )


def norm_backward(upstream, entries, inverse_scale, gain_row):
    scaled = upstream * gain_row
    return inverse_scale * scaled - entries * inverse_scale**3 * jnp.mean(
        scaled * entries, axis=-1, keepdims=True
    )


def dot(a, b):
    return jnp.dot(a, b, preferred_element_type=F32)


def dot_nt(a, b):
    return jnp.einsum("ik,jk->ij", a, b, preferred_element_type=F32)


def dot_tn(a, b):
    return jnp.einsum("ki,kj->ij", a, b, preferred_element_type=F32)


def attention_forward(queries, keys_all, values_all):
    length, head_count, head_width = queries.shape
    block_rows = min(512, length)
    scale_factor = 1.0 / math.sqrt(head_width)
    outs = []
    logs = []
    for start in range(0, length, block_rows):
        end = start + block_rows
        scores = (
            jnp.einsum(
                "qhd,khd->hqk", queries[start:end], keys_all[:end], preferred_element_type=F32
            )
            * scale_factor
        )
        allowed = jnp.arange(end)[None, :] <= (start + jnp.arange(block_rows))[:, None]
        scores = jnp.where(allowed[None], scores, -1e30)
        largest = jnp.max(scores, axis=-1, keepdims=True)
        weights = jnp.exp(scores - largest)
        totals = jnp.sum(weights, axis=-1, keepdims=True)
        shares = (weights / totals).astype(BF)
        attended = jnp.einsum("hqk,khd->qhd", shares, values_all[:end], preferred_element_type=F32)
        outs.append(attended.astype(BF))
        logs.append((largest + jnp.log(totals))[..., 0])
    return jnp.concatenate(outs, axis=0), logs


def attention_backward(queries, keys_all, values_all, logs, upstream_heads):
    length, head_count, head_width = queries.shape
    block_rows = min(512, length)
    scale_factor = 1.0 / math.sqrt(head_width)
    key_sums = jnp.zeros((length, head_count, head_width), F32)
    value_sums = jnp.zeros((length, head_count, VDIM), F32)
    query_grads = []
    for index, start in enumerate(range(0, length, block_rows)):
        end = start + block_rows
        query_rows = queries[start:end]
        upstream = upstream_heads[start:end]
        scores = (
            jnp.einsum("qhd,khd->hqk", query_rows, keys_all[:end], preferred_element_type=F32)
            * scale_factor
        )
        allowed = jnp.arange(end)[None, :] <= (start + jnp.arange(block_rows))[:, None]
        scores = jnp.where(allowed[None], scores, -1e30)
        shares = jnp.exp(scores - logs[index][..., None])
        share_grad = jnp.einsum(
            "qhd,khd->hqk", upstream, values_all[:end], preferred_element_type=F32
        )
        centre = jnp.sum(shares * share_grad, axis=-1, keepdims=True)
        score_grad = (shares * (share_grad - centre)).astype(BF)
        query_grads.append(
            jnp.einsum("hqk,khd->qhd", score_grad, keys_all[:end], preferred_element_type=F32)
            * scale_factor
        )
        key_sums = key_sums.at[:end].add(
            jnp.einsum("hqk,qhd->khd", score_grad, query_rows, preferred_element_type=F32)
            * scale_factor
        )
        value_sums = value_sums.at[:end].add(
            jnp.einsum("hqk,qhd->khd", shares.astype(BF), upstream, preferred_element_type=F32)
        )
    return (
        jnp.concatenate(query_grads, axis=0).astype(BF),
        key_sums.astype(BF),
        value_sums.astype(BF),
    )


def copy_kernel(places_ref, in_ref, out_ref):
    out_ref[...] = in_ref[...]


def reorder(stack, places):
    count = stack.shape[0]
    if stack.size * stack.dtype.itemsize < 2**20 or stack.ndim != 3:
        return jnp.stack(
            [lax.dynamic_index_in_dim(stack, places[j], 0, keepdims=False) for j in range(count)]
        )
    block = (1, *stack.shape[1:])
    return pl.pallas_call(
        copy_kernel,
        grid_spec=pltpu.PrefetchScalarGridSpec(
            num_scalar_prefetch=1,
            grid=(count,),
            in_specs=[pl.BlockSpec(block, lambda j, order: (order[j], 0, 0))],
            out_specs=pl.BlockSpec(block, lambda j, order: (j, 0, 0)),
        ),
        out_shape=jax.ShapeDtypeStruct(stack.shape, stack.dtype),
        compiler_params=params(40),
        cost_estimate=pl.CostEstimate(
            flops=0, bytes_accessed=2 * stack.size * stack.dtype.itemsize, transcendentals=0
        ),
    )(places.astype(jnp.int32), stack)


def small_take(table, index):
    table = jnp.array(table, jnp.int32)
    hit = index[:, None] == jnp.arange(table.shape[0])[None, :]
    return jnp.sum(jnp.where(hit, table[None, :], 0), axis=1)


def params(limit=60):
    return pltpu.CompilerParams(
        vmem_limit_bytes=limit * 2**20, dimension_semantics=("arbitrary",)
    )


MESH_ID = pl.DeviceIdType.MESH


def neighbours():
    dp = lax.axis_index("dp")
    seq = lax.axis_index("seq")
    core = {"dp": dp, "seq": seq + 1 - 2 * (seq % 2)}
    across_x = {"dp": dp, "seq": seq + 2 - 4 * ((seq // 2) % 2)}
    across_y = {"dp": dp, "seq": seq + 4 - 8 * (seq // 4)}
    following = {"dp": (dp + 1) % 4, "seq": seq}
    previous = {"dp": (dp + 3) % 4, "seq": seq}
    return core, across_x, across_y, following, previous


def greet(devices):
    barrier = pltpu.get_barrier_semaphore()
    for device in devices:
        pl.semaphore_signal(barrier, inc=1, device_id=device, device_id_type=MESH_ID)
    pl.semaphore_wait(barrier, len(devices))


class Courier:
    def __init__(self, send_sems, recv_sems):
        self.send_sems, self.recv_sems = send_sems, recv_sems
        self.sent, self.open = [], []

    def send(self, source, target, device):
        index = len(self.sent)
        copy = pltpu.make_async_remote_copy(
            src_ref=source,
            dst_ref=target,
            send_sem=self.send_sems.at[index],
            recv_sem=self.recv_sems.at[index],
            device_id=device,
            device_id_type=MESH_ID,
        )
        copy.start()
        self.sent.append(copy)
        self.open.append(copy)
        return copy

    def take(self, copy):
        copy.wait_recv()
        self.open = [other for other in self.open if other is not copy]

    def finish(self):
        for copy in list(self.open):
            self.take(copy)
        for copy in self.sent:
            copy.wait_send()


def gather_all_kernel(in_ref, out_ref, send_sems, recv_sems, local_sem):
    core, across_x, across_y, following, previous = neighbours()
    greet((core, across_x, across_y, following, previous))
    half = in_ref.shape[0] // 2
    top, bottom = pl.ds(0, half), pl.ds(half, half)
    own = pltpu.make_async_copy(in_ref, out_ref.at[0], local_sem)
    own.start()
    post = Courier(send_sems, recv_sems)
    ring = late = None
    for i in range(4):
        base = 8 * i
        block = in_ref if i == 0 else out_ref.at[base]
        if ring is not None:
            post.take(ring)
        if i < 3:
            ring = post.send(block, out_ref.at[base + 8], following)
        by_x = post.send(block, out_ref.at[base + 1], across_x)
        by_y = post.send(block, out_ref.at[base + 2], across_y)
        post.send(block, out_ref.at[base + 4], core)
        post.take(by_x)
        far_top = post.send(out_ref.at[base + 1, top], out_ref.at[base + 3, top], across_y)
        post.send(out_ref.at[base + 1], out_ref.at[base + 5], core)
        post.take(by_y)
        far_bottom = post.send(
            out_ref.at[base + 2, bottom], out_ref.at[base + 3, bottom], across_x
        )
        post.send(out_ref.at[base + 2], out_ref.at[base + 6], core)
        if late is not None:
            post.take(late[0])
            post.take(late[1])
            post.send(out_ref.at[base - 5], out_ref.at[base - 1], core)
        late = (far_top, far_bottom)
    post.take(late[0])
    post.take(late[1])
    post.send(out_ref.at[27], out_ref.at[31], core)
    own.wait()
    post.finish()


def gather_all(block, collective_id):
    rows, columns = block.shape
    return pl.pallas_call(
        gather_all_kernel,
        out_shape=jax.ShapeDtypeStruct((32, rows, columns), block.dtype),
        in_specs=[pl.BlockSpec(memory_space=pl.ANY)],
        out_specs=pl.BlockSpec(memory_space=pl.ANY),
        scratch_shapes=[
            pltpu.SemaphoreType.DMA((39,)),
            pltpu.SemaphoreType.DMA((39,)),
            pltpu.SemaphoreType.DMA,
        ],
        compiler_params=pltpu.CompilerParams(
            collective_id=collective_id, has_side_effects=True, vmem_limit_bytes=16 * 2**20
        ),
        cost_estimate=pl.CostEstimate(
            flops=0, bytes_accessed=64 * rows * columns * 2, transcendentals=0
        ),
    )(block)


def accumulate(target, *sources):
    rows = target.shape[0]
    step = 16

    def body(k, carry):
        part = pl.ds(pl.multiple_of(k * step, step), step)
        total = target[part].astype(F32)
        for source in sources:
            total = total + source[part].astype(F32)
        target[part] = total.astype(target.dtype)
        return carry

    lax.fori_loop(0, rows // step, body, 0)


def scatter_all_kernel(
    in_ref, out_ref, held, far, near, ring, stage, send_sems, recv_sems, local_sems
):
    core, across_x, across_y, following, previous = neighbours()
    greet((core, across_x, across_y, following, previous))
    rows = out_ref.shape[0]
    half = rows // 2
    top, bottom = pl.ds(0, half), pl.ds(half, half)
    post = Courier(send_sems, recv_sems)
    order = (1, 2, 3, 0)
    by_core, by_far, by_near, loads = {}, {}, {}, {}
    by_ring = None

    def load(n):
        i = order[n]
        loads[i] = pltpu.make_async_copy(
            in_ref.at[pl.ds(8 * i, 4)], stage.at[n % 2], local_sems.at[n % 2]
        )
        loads[i].start()

    load(0)
    for i in order:
        by_core[i] = post.send(in_ref.at[pl.ds(8 * i + 4, 4)], held.at[i], core)

    def first(n):
        i = order[n]
        if n < 3:
            load(n + 1)
        loads[i].wait()
        post.take(by_core[i])
        accumulate(held.at[i, 3], stage.at[n % 2, 3])
        by_far[i] = (
            post.send(held.at[i, 3, top], far.at[i, 0], across_y),
            post.send(held.at[i, 3, bottom], far.at[i, 1], across_x),
        )
        for k in (1, 2, 0):
            accumulate(held.at[i, k], stage.at[n % 2, k])

    def second(n):
        i = order[n]
        post.take(by_far[i][0])
        accumulate(held.at[i, 1, top], far.at[i, 0])
        to_x = post.send(held.at[i, 1], near.at[i, 0], across_x)
        post.take(by_far[i][1])
        accumulate(held.at[i, 2, bottom], far.at[i, 1])
        to_y = post.send(held.at[i, 2], near.at[i, 1], across_y)
        by_near[i] = (to_x, to_y)

    def third(n, before):
        i = order[n]
        post.take(by_near[i][0])
        post.take(by_near[i][1])
        sources = [near.at[i, 0], near.at[i, 1]]
        if before is not None:
            post.take(before)
            sources.append(ring.at[n - 1])
        accumulate(held.at[i, 0], *sources)
        if n < 3:
            return post.send(held.at[i, 0], ring.at[n], following)
        return None

    first(0)
    first(1)
    second(0)
    first(2)
    second(1)
    by_ring = third(0, by_ring)
    first(3)
    second(2)
    by_ring = third(1, by_ring)
    second(3)
    by_ring = third(2, by_ring)
    third(3, by_ring)
    out_ref[...] = held[0, 0]
    post.finish()


def scatter_all(parts, collective_id):
    _, rows, columns = parts.shape
    dtype = parts.dtype
    return pl.pallas_call(
        scatter_all_kernel,
        out_shape=jax.ShapeDtypeStruct((rows, columns), dtype),
        in_specs=[pl.BlockSpec(memory_space=pl.ANY)],
        out_specs=pl.BlockSpec(memory_space=pltpu.VMEM),
        scratch_shapes=[
            pltpu.VMEM((4, 4, rows, columns), dtype),
            pltpu.VMEM((4, 2, rows // 2, columns), dtype),
            pltpu.VMEM((4, 2, rows, columns), dtype),
            pltpu.VMEM((3, rows, columns), dtype),
            pltpu.VMEM((2, 4, rows, columns), dtype),
            pltpu.SemaphoreType.DMA((23,)),
            pltpu.SemaphoreType.DMA((23,)),
            pltpu.SemaphoreType.DMA((2,)),
        ],
        compiler_params=pltpu.CompilerParams(
            collective_id=collective_id, has_side_effects=True, vmem_limit_bytes=56 * 2**20
        ),
        cost_estimate=pl.CostEstimate(
            flops=32 * rows * columns, bytes_accessed=64 * rows * columns * 2, transcendentals=0
        ),
    )(parts)


def gather_start_kernel(
    hidden, named, gains, query, expand, compress, hidden_all, named_all, gains_all, query_all,
    expand_all, compress_all, send_sems, recv_sems, local_sems
):
    dp = lax.axis_index("dp")
    seq = lax.axis_index("seq")
    core, across_x, across_y, following, previous = neighbours()
    greet((core, across_x, across_y, following, previous))
    post = Courier(send_sems, recv_sems)
    rows = hidden.shape[0]
    top, bottom = pl.ds(0, rows // 2), pl.ds(rows // 2, rows // 2)
    by_x = seq + 2 - 4 * ((seq // 2) % 2)
    by_y = seq + 4 - 8 * (seq // 4)
    by_both = by_x + 4 - 8 * (seq // 4)
    x_copy = post.send(hidden, hidden_all.at[seq], across_x)
    y_copy = post.send(hidden, hidden_all.at[seq], across_y)
    core_half = compress.shape[0] // 2
    mine = pl.ds(pl.multiple_of((seq % 2) * core_half, core_half), core_half)
    locals_ = [
        pltpu.make_async_copy(source, target, local_sems.at[n])
        for n, (source, target) in enumerate(
            (
                (hidden, hidden_all.at[seq]),
                (named, named_all.at[0, 0]),
                (gains, gains_all.at[dp]),
                (query, query_all.at[dp]),
                (expand, expand_all.at[dp]),
                (compress, compress_all.at[dp]),
            )
        )
    ]
    for copy in locals_:
        copy.start()

    def hop(i):
        at = (dp + 5 - i) % 4
        first = i == 1
        return [
            post.send(gains if first else gains_all.at[at], gains_all.at[at], following),
            post.send(named if first else named_all.at[0, i - 1], named_all.at[0, i], following),
            post.send(query if first else query_all.at[at], query_all.at[at], following),
            post.send(expand if first else expand_all.at[at], expand_all.at[at], following),
            post.send(
                compress.at[mine] if first else compress_all.at[at, mine],
                compress_all.at[at, mine],
                following,
            ),
        ]

    ring = hop(1)
    post.send(hidden, hidden_all.at[seq], core)
    post.take(x_copy)
    far_top = post.send(hidden_all.at[by_x, top], hidden_all.at[by_x, top], across_y)
    post.send(hidden_all.at[by_x], hidden_all.at[by_x], core)
    post.take(y_copy)
    far_bottom = post.send(hidden_all.at[by_y, bottom], hidden_all.at[by_y, bottom], across_x)
    post.send(hidden_all.at[by_y], hidden_all.at[by_y], core)
    for i in (2, 3, 4):
        for copy in ring:
            post.take(copy)
        at = (dp + 5 - i) % 4
        if i < 4:
            ring = hop(i)
        post.send(compress_all.at[at, mine], compress_all.at[at, mine], core)
        if i == 3:
            post.take(far_top)
            post.take(far_bottom)
            post.send(hidden_all.at[by_both], hidden_all.at[by_both], core)
    locals_[1].wait()
    post.take(post.send(named_all.at[0], named_all.at[1], across_x))
    post.take(post.send(named_all.at[pl.ds(0, 2)], named_all.at[pl.ds(2, 2)], across_y))
    post.send(named_all.at[pl.ds(0, 4)], named_all.at[pl.ds(4, 4)], core)
    for n, copy in enumerate(locals_):
        if n != 1:
            copy.wait()
    post.finish()


def gather_start(hidden, named, gains, query, expand, compress, collective_id):
    anywhere = pl.BlockSpec(memory_space=pl.ANY)
    total = 8 + 5 * 3 + 3 + 3
    return pl.pallas_call(
        gather_start_kernel,
        out_shape=[
            jax.ShapeDtypeStruct((8, *hidden.shape), hidden.dtype),
            jax.ShapeDtypeStruct((8, 4, *named.shape), named.dtype),
        ]
        + [jax.ShapeDtypeStruct((4, *x.shape), x.dtype) for x in (gains, query, expand, compress)],
        in_specs=[anywhere] * 6,
        out_specs=[anywhere] * 6,
        scratch_shapes=[
            pltpu.SemaphoreType.DMA((total,)),
            pltpu.SemaphoreType.DMA((total,)),
            pltpu.SemaphoreType.DMA((6,)),
        ],
        compiler_params=pltpu.CompilerParams(
            collective_id=collective_id, has_side_effects=True, vmem_limit_bytes=16 * 2**20
        ),
        cost_estimate=pl.CostEstimate(flops=0, bytes_accessed=2**26, transcendentals=0),
    )(hidden, named, gains, query, expand, compress)


PADDED_HALF = 768
TILE = 256


def flip(value, change):
    return value + change - 2 * value * change


def experts_kernel(
    remote, capacity, rows_in, place_ref, gate_ref, weight_in, weight_out, shared_in,
    shared_out, rows_all, slot_rows, slot_up, hidden_ref, back_ref, units_ref, part_ref,
    in_grad, out_grad, rows_buffer, cot_buffer, load_sems, *sems
):
    step = pl.program_id(0)
    steps = pl.num_programs(0)
    rows = place_ref.shape[2]
    features = slot_rows.shape[1]
    slot = step % 2
    gathered = rows_all if remote else rows_in

    def loads(at, into):
        found = []
        for b in range(2):
            block = 2 * at + b
            part = pl.ds(b * rows, rows)
            for kind, buffer in enumerate((rows_buffer, cot_buffer)):
                found.append(
                    pltpu.make_async_copy(
                        gathered.at[block, kind],
                        buffer.at[into, part],
                        load_sems.at[into, 2 * b + kind],
                    )
                )
        return found

    if remote:
        send_sems, recv_sems, own_sem = sems
        core, across_x, across_y, following, previous = neighbours()
        half = rows // 2
        top, bottom = pl.ds(0, half), pl.ds(half, half)

        def copy(index, source, target, device):
            return pltpu.make_async_remote_copy(
                src_ref=source,
                dst_ref=target,
                send_sem=send_sems.at[index],
                recv_sem=recv_sems.at[index],
                device_id=device,
                device_id_type=MESH_ID,
            )

        def block_of(i):
            return rows_in if i == 0 else rows_all.at[8 * i]

        def along(i):
            return copy(9 * i, block_of(i), rows_all.at[8 * i + 8], following)

        def by_x(i):
            return copy(9 * i + 1, block_of(i), rows_all.at[8 * i + 1], across_x)

        def by_y(i):
            return copy(9 * i + 2, block_of(i), rows_all.at[8 * i + 2], across_y)

        def far(i, which):
            if which == 0:
                return copy(
                    9 * i + 3, rows_all.at[8 * i + 1, :, top], rows_all.at[8 * i + 3, :, top], across_y
                )
            return copy(
                9 * i + 4, rows_all.at[8 * i + 2, :, bottom], rows_all.at[8 * i + 3, :, bottom], across_x
            )

        def to_core(i, k):
            source = block_of(i) if k == 0 else rows_all.at[8 * i + k]
            return copy(9 * i + 5 + k, source, rows_all.at[8 * i + 4 + k], core)

        def begin(i):
            if i < 3:
                along(i).start()
            by_x(i).start()
            by_y(i).start()
            to_core(i, 0).start()

        def ready(i, m):
            if m == 0:
                by_x(i).wait_recv()
                far(i, 0).start()
                to_core(i, 1).start()
                by_y(i).wait_recv()
                far(i, 1).start()
                to_core(i, 2).start()
                if i < 3:
                    along(i).wait_recv()
                    begin(i + 1)
            elif m == 1:
                far(i, 0).wait_recv()
                far(i, 1).wait_recv()
                to_core(i, 3).start()
            elif m == 2:
                to_core(i, 0).wait_recv()
                to_core(i, 1).wait_recv()
            else:
                to_core(i, 2).wait_recv()
                to_core(i, 3).wait_recv()

        @pl.when(step == 0)
        def _():
            greet((core, across_x, across_y, following, previous))
            own = pltpu.make_async_copy(rows_in, rows_all.at[0], own_sem)
            own.start()
            begin(0)
            own.wait()
            ready(0, 0)
            for load in loads(0, 0):
                load.start()
    else:

        @pl.when(step == 0)
        def _():
            for load in loads(0, 0):
                load.start()

    @pl.when(step == 0)
    def _():
        in_grad[...] = jnp.zeros_like(in_grad)
        out_grad[...] = jnp.zeros_like(out_grad)

    for load in loads(step, slot):
        load.wait()

    picks = []
    for b in range(2):
        chosen = one_hot(place_ref, 2 * step + b, capacity)
        pick = chosen.astype(F32)
        picks.append(pick.T.astype(BF))
        pick = pick.astype(BF)
        gates = jnp.sum(jnp.where(chosen, gate_ref[2 * step + b], 0.0), axis=1, keepdims=True)
        part = pl.ds(b * rows, rows)
        slots = pl.ds(b * capacity, capacity)
        slot_rows[slots] = dot(pick, rows_buffer[slot, part]).astype(BF)
        slot_up[slots] = (dot(pick, cot_buffer[slot, part]) * gates).astype(BF)

    def gated(gate, up, hidden_back):
        sigmoid = 1.0 / (1.0 + jnp.exp(-gate))
        active = gate * sigmoid
        gate_back = hidden_back * up * sigmoid * (1.0 + gate * (1.0 - sigmoid))
        return (active * up).astype(BF), gate_back.astype(BF), (hidden_back * active).astype(BF)

    def hidden_tile(t, carry):
        part = pl.ds(pl.multiple_of(t * TILE, TILE), TILE)
        second = pl.ds(pl.multiple_of(PADDED_HALF + t * TILE, TILE), TILE)
        gate = dot(slot_rows[...], weight_in[:, part])
        up = dot(slot_rows[...], weight_in[:, second])
        hidden_back = dot_nt(slot_up[...], weight_out[part])
        hidden_ref[:, part], back_ref[:, part], back_ref[:, second] = gated(gate, up, hidden_back)
        return carry

    lax.fori_loop(0, PADDED_HALF // TILE, hidden_tile, 0)

    width = shared_out.shape[0]
    rows_pair, cot_pair = rows_buffer[slot], cot_buffer[slot]
    gate_up = dot(rows_pair, shared_in[...])
    hidden_back = dot_nt(cot_pair, shared_out[...])
    units, gate_back, up_back = gated(gate_up[:, :width], gate_up[:, width:], hidden_back)
    units_ref[...] = units
    shared_back = jnp.concatenate([gate_back, up_back], axis=1)
    in_grad[...] += dot_tn(shared_back, rows_pair)
    out_grad[...] += dot_tn(units, cot_pair)

    if remote:
        for m in range(4):
            for i in range(4):
                if i == 0 and m == 0:
                    continue

                @pl.when(step + 1 == 4 * i + m)
                def _():
                    ready(i, m)

    @pl.when(step + 1 < steps)
    def _():
        for load in loads(step + 1, 1 - slot):
            load.start()

    def back_tile(t, carry):
        part = pl.ds(pl.multiple_of(t * 2 * TILE, 2 * TILE), 2 * TILE)
        slot_back = dot_nt(back_ref[...], weight_in[part]).astype(BF)
        shared_part = dot_nt(shared_back, shared_in[part])
        for b in range(2):
            tokens = slice(b * rows, (b + 1) * rows)
            total = dot(picks[b], slot_back[b * capacity : (b + 1) * capacity])
            part_ref[b, :, part] = (total + shared_part[tokens]).astype(BF)
        return carry

    lax.fori_loop(0, features // (2 * TILE), back_tile, 0)

    if remote:

        @pl.when(step + 1 == steps)
        def _():
            for i in range(4):
                if i < 3:
                    along(i).wait_send()
                by_x(i).wait_send()
                by_y(i).wait_send()
                far(i, 0).wait_send()
                far(i, 1).wait_send()
                for k in range(4):
                    to_core(i, k).wait_send()


def one_hot(place_ref, block, capacity):
    place = place_ref[block]
    rows = place.shape[1]
    return lax.broadcasted_iota(jnp.int32, (capacity, rows), 0) == place


def experts(
    remote, capacity, rows_in, places, gates, weight_in, weight_out, shared_in, shared_out
):
    blocks, _, rows = places.shape
    features = weight_in.shape[0]
    width = shared_out.shape[0]
    steps = blocks // 2

    def whole(array):
        return pl.BlockSpec(
            array.shape, lambda j: (0,) * array.ndim, pipeline_mode=pl.Buffered(1)
        )

    def tiled(height, columns):
        return pl.BlockSpec((height, columns), lambda j: (j, 0))

    anywhere = pl.BlockSpec(memory_space=pl.ANY)
    slots = 2 * capacity
    scratch = [
        pltpu.VMEM((2, 2 * rows, features), BF),
        pltpu.VMEM((2, 2 * rows, features), BF),
        pltpu.SemaphoreType.DMA((2, 4)),
    ]
    if remote:
        scratch += [
            pltpu.SemaphoreType.DMA((36,)),
            pltpu.SemaphoreType.DMA((36,)),
            pltpu.SemaphoreType.DMA,
        ]
    found = pl.pallas_call(
        functools.partial(experts_kernel, remote, capacity),
        grid=(steps,),
        in_specs=[anywhere]
        + [whole(x) for x in (places, gates, weight_in, weight_out, shared_in, shared_out)],
        out_specs=[
            anywhere,
            tiled(slots, features),
            tiled(slots, features),
            tiled(slots, PADDED_HALF),
            tiled(slots, 2 * PADDED_HALF),
            tiled(2 * rows, width),
            pl.BlockSpec((2, rows, features), lambda j: (j, 0, 0)),
            pl.BlockSpec((2 * width, features), lambda j: (0, 0)),
            pl.BlockSpec((width, features), lambda j: (0, 0)),
        ],
        out_shape=[
            jax.ShapeDtypeStruct((blocks if remote else 1, 2, rows, features), BF),
            jax.ShapeDtypeStruct((steps * slots, features), BF),
            jax.ShapeDtypeStruct((steps * slots, features), BF),
            jax.ShapeDtypeStruct((steps * slots, PADDED_HALF), BF),
            jax.ShapeDtypeStruct((steps * slots, 2 * PADDED_HALF), BF),
            jax.ShapeDtypeStruct((blocks * rows, width), BF),
            jax.ShapeDtypeStruct((blocks, rows, features), BF),
            jax.ShapeDtypeStruct((2 * width, features), F32),
            jax.ShapeDtypeStruct((width, features), F32),
        ],
        scratch_shapes=scratch,
        compiler_params=pltpu.CompilerParams(
            vmem_limit_bytes=60 * 2**20,
            dimension_semantics=("arbitrary",),
            **({"collective_id": 3, "has_side_effects": True} if remote else {}),
        ),
        cost_estimate=pl.CostEstimate(
            flops=steps * slots * features * 2 * 3 * 2 * PADDED_HALF,
            bytes_accessed=blocks * features * 8 * rows,
            transcendentals=0,
        ),
    )(rows_in, places, gates, weight_in, weight_out, shared_in, shared_out)
    return found[1:]


def plane_scatter_kernel(
    in_ref, out_ref, held, far, near, stage, send_sems, recv_sems, local_sems
):
    core, across_x, across_y, _, _ = neighbours()
    greet((core, across_x, across_y))
    seq = lax.axis_index("seq")
    rows = out_ref.shape[0]
    top, bottom = pl.ds(0, rows // 2), pl.ds(rows // 2, rows // 2)
    post = Courier(send_sems, recv_sems)
    x_seq = seq + 2 - 4 * ((seq // 2) % 2)
    y_seq = seq + 4 - 8 * (seq // 4)
    xy_seq = x_seq + 4 - 8 * (seq // 4)
    core_step = 1 - 2 * (seq % 2)
    loads, arriving = {}, {}
    for k, place in ((3, xy_seq), (1, x_seq), (2, y_seq), (0, seq)):
        arriving[k] = post.send(in_ref.at[place + core_step], held.at[k], core)
        loads[k] = pltpu.make_async_copy(in_ref.at[place], stage.at[k], local_sems.at[k])
        loads[k].start()

    def join(k):
        loads[k].wait()
        post.take(arriving[k])
        accumulate(held.at[k], stage.at[k])

    join(3)
    far_top = post.send(held.at[3, top], far.at[0], across_y)
    far_bottom = post.send(held.at[3, bottom], far.at[1], across_x)
    join(1)
    x_bottom = post.send(held.at[1, bottom], near.at[0, bottom], across_x)
    join(2)
    y_top = post.send(held.at[2, top], near.at[1, top], across_y)
    join(0)
    post.take(far_top)
    accumulate(held.at[1, top], far.at[0])
    x_top = post.send(held.at[1, top], near.at[0, top], across_x)
    post.take(far_bottom)
    accumulate(held.at[2, bottom], far.at[1])
    y_bottom = post.send(held.at[2, bottom], near.at[1, bottom], across_y)
    for copy in (x_bottom, y_top, x_top, y_bottom):
        post.take(copy)
    accumulate(held.at[0], near.at[0], near.at[1])
    out_ref[...] = held[0]
    post.finish()


def plane_scatter(parts, collective_id):
    _, rows, columns = parts.shape
    return pl.pallas_call(
        plane_scatter_kernel,
        out_shape=jax.ShapeDtypeStruct((rows, columns), parts.dtype),
        in_specs=[pl.BlockSpec(memory_space=pl.ANY)],
        out_specs=pl.BlockSpec(memory_space=pltpu.VMEM),
        scratch_shapes=[
            pltpu.VMEM((4, rows, columns), parts.dtype),
            pltpu.VMEM((2, rows // 2, columns), parts.dtype),
            pltpu.VMEM((2, rows, columns), parts.dtype),
            pltpu.VMEM((4, rows, columns), parts.dtype),
            pltpu.SemaphoreType.DMA((10,)),
            pltpu.SemaphoreType.DMA((10,)),
            pltpu.SemaphoreType.DMA((4,)),
        ],
        compiler_params=pltpu.CompilerParams(
            collective_id=collective_id, has_side_effects=True, vmem_limit_bytes=32 * 2**20
        ),
        cost_estimate=pl.CostEstimate(
            flops=8 * rows * columns, bytes_accessed=16 * rows * columns, transcendentals=0
        ),
    )(parts)


def spread(post, source, found, n, core, across_x, across_y):
    seq = lax.axis_index("seq")
    rows = source.shape[0]
    top, bottom = pl.ds(0, rows // 2), pl.ds(rows // 2, rows // 2)
    x_seq = seq + 2 - 4 * ((seq // 2) % 2)
    y_seq = seq + 4 - 8 * (seq // 4)
    xy_seq = x_seq + 4 - 8 * (seq // 4)
    x_copy = post.send(source, found.at[seq], across_x)
    y_copy = post.send(source, found.at[seq], across_y)
    post.send(source, found.at[seq], core)
    yield
    post.take(x_copy)
    far_top = post.send(found.at[x_seq, top], found.at[x_seq, top], across_y)
    post.send(found.at[x_seq], found.at[x_seq], core)
    post.take(y_copy)
    far_bottom = post.send(found.at[y_seq, bottom], found.at[y_seq, bottom], across_x)
    post.send(found.at[y_seq], found.at[y_seq], core)
    yield
    post.take(far_top)
    post.take(far_bottom)
    post.send(found.at[xy_seq], found.at[xy_seq], core)


def plane_gather_kernel(in_ref, out_ref, send_sems, recv_sems, local_sem):
    core, across_x, across_y, _, _ = neighbours()
    greet((core, across_x, across_y))
    own = pltpu.make_async_copy(in_ref, out_ref.at[lax.axis_index("seq")], local_sem)
    own.start()
    post = Courier(send_sems, recv_sems)
    for _ in spread(post, in_ref, out_ref, 0, core, across_x, across_y):
        pass
    own.wait()
    post.finish()


def plane_gather(block, collective_id):
    anywhere = pl.BlockSpec(memory_space=pl.ANY)
    return pl.pallas_call(
        plane_gather_kernel,
        out_shape=jax.ShapeDtypeStruct((8, *block.shape), block.dtype),
        in_specs=[anywhere],
        out_specs=anywhere,
        scratch_shapes=[
            pltpu.SemaphoreType.DMA((8,)),
            pltpu.SemaphoreType.DMA((8,)),
            pltpu.SemaphoreType.DMA,
        ],
        compiler_params=pltpu.CompilerParams(
            collective_id=collective_id, has_side_effects=True, vmem_limit_bytes=16 * 2**20
        ),
        cost_estimate=pl.CostEstimate(
            flops=0, bytes_accessed=32 * block.size, transcendentals=0
        ),
    )(block)


def grads_kernel(in_ref, out_ref, total, ring, send_sems, recv_sems, local_sems):
    dp = lax.axis_index("dp")
    core, across_x, across_y, following, previous = neighbours()
    greet((core, across_x, across_y, following, previous))
    post = Courier(send_sems, recv_sems)
    loads = []
    for n, i in enumerate((1, 2, 3, 0)):
        load = pltpu.make_async_copy(in_ref.at[(dp + 4 - i) % 4], total.at[n], local_sems.at[n])
        load.start()
        loads.append(load)
    loads[0].wait()
    before = post.send(total.at[0], ring.at[0], following)
    for n in (1, 2, 3):
        loads[n].wait()
        post.take(before)
        accumulate(total.at[n], ring.at[n - 1])
        if n < 3:
            before = post.send(total.at[n], ring.at[n], following)
    own = pltpu.make_async_copy(total.at[3], out_ref.at[lax.axis_index("seq")], local_sems.at[0])
    own.start()
    for _ in spread(post, total.at[3], out_ref, 0, core, across_x, across_y):
        pass
    own.wait()
    post.finish()


def sum_grads(parts, collective_id):
    _, rows, columns = parts.shape
    anywhere = pl.BlockSpec(memory_space=pl.ANY)
    return pl.pallas_call(
        grads_kernel,
        out_shape=jax.ShapeDtypeStruct((8, rows, columns), parts.dtype),
        in_specs=[anywhere],
        out_specs=anywhere,
        scratch_shapes=[
            pltpu.VMEM((4, rows, columns), parts.dtype),
            pltpu.VMEM((3, rows, columns), parts.dtype),
            pltpu.SemaphoreType.DMA((11,)),
            pltpu.SemaphoreType.DMA((11,)),
            pltpu.SemaphoreType.DMA((4,)),
        ],
        compiler_params=pltpu.CompilerParams(
            collective_id=collective_id, has_side_effects=True, vmem_limit_bytes=32 * 2**20
        ),
        cost_estimate=pl.CostEstimate(
            flops=0, bytes_accessed=32 * rows * columns, transcendentals=0
        ),
    )(parts)


def out_kernel(
    capacity, order_ref, place_ref, gate_ref, hidden_ref, up_ref, units_ref, weight_ref, shared_ref,
    gate_grad_ref, part_ref
):
    rows = place_ref.shape[2]
    features = part_ref.shape[2]
    chosen = one_hot(place_ref, 0, capacity)
    pick = chosen.astype(F32).T.astype(BF)
    gates = jnp.sum(jnp.where(chosen, gate_ref[0], 0.0), axis=1, keepdims=True)

    def tile(t, slot_grad):
        part = pl.ds(pl.multiple_of(t * 2 * TILE, 2 * TILE), 2 * TILE)
        result = dot(hidden_ref[...], weight_ref[:, part]).astype(BF).astype(F32)
        slot_grad += jnp.sum(result * up_ref[:, part].astype(F32), axis=1, keepdims=True)
        total = dot(pick, (result * gates).astype(BF)) + dot(units_ref[...], shared_ref[:, part])
        part_ref[0, :, part] = total.astype(BF)
        return slot_grad

    slot_grad = lax.fori_loop(
        0, features // (2 * TILE), tile, jnp.zeros((capacity, 1), F32)
    )
    slot_grad = slot_grad / jnp.where(gates > 0.0, gates, 1.0)
    gate_grad_ref[0] = jnp.sum(jnp.where(chosen, slot_grad, 0.0), axis=0, keepdims=True)


def out_side(capacity, order, places, gates, hidden, up, units, weight_out, shared_out):
    blocks, _, rows = places.shape
    features = up.shape[1]
    one = pl.BlockSpec((1, 1, rows), lambda j, order: (j, 0, 0))

    def tiled(height, columns):
        return pl.BlockSpec((height, columns), lambda j, order: (j, 0))

    def whole(array):
        return pl.BlockSpec(array.shape, lambda j, order: (0, 0))

    return pl.pallas_call(
        functools.partial(out_kernel, capacity),
        grid_spec=pltpu.PrefetchScalarGridSpec(
            num_scalar_prefetch=1,
            grid=(blocks,),
            in_specs=[
                one,
                one,
                tiled(capacity, PADDED_HALF),
                tiled(capacity, features),
                tiled(rows, units.shape[1]),
                whole(weight_out),
                whole(shared_out),
            ],
            out_specs=[
                pl.BlockSpec((1, 1, rows), lambda j, order: (order[j], 0, 0)),
                pl.BlockSpec((1, rows, features), lambda j, order: (order[j], 0, 0)),
            ],
        ),
        out_shape=[
            jax.ShapeDtypeStruct((blocks, 1, rows), F32),
            jax.ShapeDtypeStruct((blocks, rows, features), BF),
        ],
        compiler_params=params(48),
        cost_estimate=pl.CostEstimate(
            flops=blocks * 2 * features * (capacity * PADDED_HALF + rows * 2 * capacity),
            bytes_accessed=blocks * features * 2 * (rows + capacity),
            transcendentals=0,
        ),
    )(order, places, gates, hidden, up, units, weight_out, shared_out)


def on_device(
    hidden_in,
    positions,
    expert_ids,
    gate_weights,
    attention_gain,
    w_query,
    w_compress,
    latent_gain,
    w_expand,
    w_output,
    feedforward_gain,
    w_shared_in,
    w_shared_out,
    w_expert_in,
    w_expert_out,
    cotangent,
):
    n_dp = lax.axis_size("dp")
    n_seq = lax.axis_size("seq")
    n_all = n_dp * n_seq
    fast = (n_dp, n_seq) == (4, 8)
    both = ("dp", "seq")
    dp_index = lax.axis_index("dp")
    seq_index = lax.axis_index("seq")
    sequence_count, rows, features = hidden_in.shape
    rows = sequence_count * rows
    length = rows * n_seq
    heads = HEADS // n_seq
    shard = features // n_dp
    expert_count = n_all // 2
    capacity = max(2, rows * TOP * 5 // (expert_count * 3))
    capacity = (capacity + 15) // 16 * 16
    units = SH_FF // n_all
    padded_units = (units + 127) // 128 * 128
    expand_width = heads * (NOPE + VDIM)

    hidden = hidden_in.reshape(rows, features)
    upstream_rows = cotangent.reshape(rows, features)
    upstream_float = upstream_rows.astype(F32)
    id_rows = expert_ids.reshape(rows, TOP)
    gate_table = gate_weights.reshape(rows, TOP)

    gains_own = jnp.concatenate([attention_gain, feedforward_gain, latent_gain])
    named_own = jnp.concatenate(
        [id_rows.T.astype(F32), gate_table.T, positions.reshape(1, rows).astype(F32)]
    )
    query_part = lax.dynamic_slice_in_dim(w_query, seq_index * heads * QK, heads * QK, 1)
    expand_part = lax.dynamic_slice_in_dim(w_expand, seq_index * expand_width, expand_width, 1)
    if fast:
        named_own = jnp.pad(named_own, ((0, 16 - named_own.shape[0]), (0, 0)))
        gains_size = gains_own.shape[0]
        gains_own = jnp.pad(gains_own, (0, 2048 - gains_size)).reshape(16, 128)
        hidden_all, named_all, gains, query_weight, expand_weight, compress_weight = gather_start(
            hidden, named_own, gains_own, query_part, expand_part, w_compress, 1
        )
        gains = gains.reshape(n_dp, 2048)[:, :gains_size]
        plane_places = seq_index ^ jnp.array([0, 2, 4, 6, 1, 3, 5, 7], jnp.int32)
        dp_places = (dp_index - jnp.arange(n_dp)) % n_dp
        block_places = (dp_places[:, None] * n_seq + plane_places[None, :]).reshape(n_all)
        slot_of_seq = small_take([0, 4, 1, 5, 2, 6, 3, 7], seq_index ^ jnp.arange(n_seq))
        positions_all = reorder(named_all[:, 0, 2 * TOP], slot_of_seq)
        named_all = named_all.swapaxes(0, 1).reshape(n_all, 16, rows)
    else:
        hidden_all = lax.all_gather(hidden, "seq", axis=0)
        named_all = lax.all_gather(named_own, both, axis=0)
        positions_all = lax.dynamic_slice_in_dim(named_all, dp_index * n_seq, n_seq, 0)[:, 2 * TOP]
        gains = lax.all_gather(gains_own, "dp", axis=0)
        query_weight = lax.all_gather(query_part, "dp", axis=0)
        expand_weight = lax.all_gather(expand_part, "dp", axis=0)
        compress_weight = lax.all_gather(w_compress, "dp", axis=0)
        block_places = jnp.arange(n_all, dtype=jnp.int32)
    hidden_all = hidden_all.reshape(length, features)
    query_weight = query_weight.reshape(features, heads * QK)
    expand_weight = expand_weight.reshape(LATENT, expand_width)
    compress_weight = compress_weight.reshape(features, LATENT + ROPE)
    gains = gains.astype(F32)
    first_gain = gains[:, :shard].reshape(features)
    second_gain = gains[:, shard : 2 * shard].reshape(features)
    latent_gain_row = gains[:, 2 * shard :].reshape(LATENT)
    output_weight = lax.all_gather(w_output, "dp", axis=0, tiled=True)
    shared_part = lax.dynamic_index_in_dim(
        w_shared_in.reshape(shard, 2, n_dp, n_seq, units), seq_index, 3, keepdims=False
    )
    shared_in = lax.all_to_all(
        shared_part.transpose(2, 0, 1, 3), "dp", split_axis=0, concat_axis=0, tiled=True
    ).reshape(features, 2, units)
    pad = padded_units - units
    shared_in = jnp.pad(shared_in, ((0, 0), (0, 0), (0, pad))).reshape(features, 2 * padded_units)
    shared_out = lax.dynamic_slice_in_dim(w_shared_out, seq_index * units, units, 0)
    shared_out = jnp.pad(shared_out, ((0, pad), (0, 0)))
    pad = PADDED_HALF - HALF
    weight_in = jnp.pad(
        w_expert_in.reshape(features, 2, HALF), ((0, 0), (0, 0), (0, pad))
    ).reshape(features, 2 * PADDED_HALF)
    weight_out = jnp.pad(w_expert_out[0], ((0, pad), (0, 0)))
    expert = (dp_index * n_seq + seq_index) // 2
    named = named_all[:, :TOP] == expert.astype(F32)
    chosen = jnp.any(named, axis=1)
    gate_rows = jnp.sum(jnp.where(named, named_all[:, TOP : 2 * TOP], 0.0), axis=1)[:, None]
    before = (jnp.arange(rows)[:, None] < jnp.arange(rows)[None, :]).astype(BF)
    place = dot(chosen.astype(BF), before).astype(jnp.int32)
    place = jnp.where(chosen, place, -1)[:, None]

    hidden_all_float = hidden_all.astype(F32)
    normed_all = (hidden_all_float * rms_scale(hidden_all_float) * first_gain).astype(BF)
    angles = rotary_angles(positions_all.reshape(length))
    cosine_all, sine_all = jnp.cos(angles), jnp.sin(angles)
    query_raw = dot(normed_all, query_weight).reshape(length, heads, QK)
    queries = jnp.concatenate(
        [
            query_raw[..., :NOPE],
            rotate(query_raw[..., NOPE:], cosine_all[:, None], sine_all[:, None]),
        ],
        axis=-1,
    ).astype(BF)
    compressed = dot(normed_all, compress_weight)
    latent = compressed[:, :LATENT]
    key_rotary = rotate(compressed[:, LATENT:], cosine_all, sine_all)
    latent_scale = rms_scale(latent)
    latent_normed = (latent * latent_scale * latent_gain_row).astype(BF)
    expanded = dot(latent_normed, expand_weight).reshape(length, heads, NOPE + VDIM)
    keys_all = jnp.concatenate(
        [expanded[..., :NOPE], jnp.broadcast_to(key_rotary[:, None, :], (length, heads, ROPE))],
        axis=-1,
    ).astype(BF)
    values_all = expanded[..., NOPE:].astype(BF)
    attended_heads, logs = attention_forward(queries, keys_all, values_all)
    attended = lax.all_to_all(
        attended_heads.reshape(length, heads * VDIM), "seq", split_axis=0, concat_axis=1, tiled=True
    )
    hidden_float = hidden.astype(F32)
    middle = hidden_float + dot(attended, output_weight)
    second_scale = rms_scale(middle)
    moe_rows = (middle * second_scale * second_gain).astype(BF)

    sent = jnp.stack([moe_rows, upstream_rows])
    if not fast:
        sent = lax.all_gather(sent, both, axis=0)
    slot_rows, slot_up, hidden_units, both_back, shared_units, back_parts, shared_in_grad, shared_out_grad = experts(
        fast, capacity, sent, place, gate_rows, weight_in, weight_out, shared_in, shared_out
    )
    if fast:
        moe_back = scatter_all(back_parts, 4)
    else:
        moe_back = lax.psum_scatter(
            back_parts.reshape(n_all * rows, features), both, scatter_dimension=0, tiled=True
        )
    moe_back = moe_back.astype(F32)
    gate_grads, out_parts = out_side(
        capacity, block_places, place, gate_rows, hidden_units, slot_up, shared_units, weight_out,
        shared_out,
    )
    out_sum = lax.psum_scatter(
        out_parts.reshape(n_all * rows, features), both, scatter_dimension=0, tiled=True
    )
    block_out = (middle + out_sum.astype(F32)).astype(BF)
    gate_grads = lax.all_to_all(gate_grads, both, split_axis=0, concat_axis=0, tiled=True)
    gate_grads = jnp.sum(gate_grads.reshape(expert_count, 2, rows), axis=1)
    gate_gradient = jnp.sum(
        jnp.where(
            id_rows[:, :, None] == jnp.arange(expert_count, dtype=jnp.int32),
            gate_grads.T[:, None, :],
            0.0,
        ),
        axis=-1,
    )
    expert_in_grad = dot_tn(slot_rows, both_back)
    expert_in_grad = jnp.concatenate(
        [expert_in_grad[:, :HALF], expert_in_grad[:, PADDED_HALF : PADDED_HALF + HALF]], axis=1
    )
    expert_out_grad = dot_tn(hidden_units, slot_up)[:HALF]

    second_gain_grad = jnp.sum(moe_back * middle * second_scale, axis=0)
    middle_back = upstream_float + norm_backward(moe_back, middle, second_scale, second_gain)
    middle_low = middle_back.astype(BF)
    attended_back = dot_nt(middle_low, output_weight).astype(BF)
    upstream_heads = lax.all_to_all(
        attended_back, "seq", split_axis=1, concat_axis=0, tiled=True
    ).reshape(length, heads, VDIM)
    attended_all = lax.all_gather(attended, "seq", axis=0, tiled=True)
    middle_columns = lax.all_to_all(middle_low, "seq", split_axis=1, concat_axis=0, tiled=True)
    output_grad = dot_tn(attended_all, middle_columns)

    query_back, key_back, value_back = attention_backward(
        queries, keys_all, values_all, logs, upstream_heads
    )
    query_raw_back = (
        jnp.concatenate(
            [
                query_back[..., :NOPE].astype(F32),
                rotate(query_back[..., NOPE:].astype(F32), cosine_all[:, None], -sine_all[:, None]),
            ],
            axis=-1,
        )
        .astype(BF)
        .reshape(length, heads * QK)
    )
    expanded_back = jnp.concatenate([key_back[..., :NOPE], value_back], axis=-1).reshape(
        length, expand_width
    )
    partial_back = jnp.concatenate(
        [
            dot_nt(query_raw_back, query_weight),
            dot_nt(expanded_back, expand_weight),
            jnp.sum(key_back[..., NOPE:].astype(F32), axis=1),
        ],
        axis=-1,
    ).astype(BF)
    if fast:
        partial_back = jnp.pad(partial_back, ((0, 0), (0, 64)))
        summed_back = plane_scatter(partial_back.reshape(n_seq, rows, -1), 5)
    else:
        summed_back = lax.psum_scatter(partial_back, "seq", scatter_dimension=0, tiled=True)
    summed_back = summed_back[:, : features + LATENT + ROPE].astype(F32)
    query_grad = dot_tn(normed_all, query_raw_back)
    expand_grad = dot_tn(latent_normed, expanded_back)
    latent_normed_back = summed_back[:, features : features + LATENT]
    own = seq_index * rows

    def mine(array):
        return lax.dynamic_slice_in_dim(array, own, rows, 0)

    latent_own, latent_scale_own = mine(latent), mine(latent_scale)
    latent_gain_grad = jnp.sum(latent_normed_back * latent_own * latent_scale_own, axis=0)
    latent_back = norm_backward(latent_normed_back, latent_own, latent_scale_own, latent_gain_row)
    rotary_back = rotate(summed_back[:, features + LATENT :], mine(cosine_all), -mine(sine_all))
    compressed_back = jnp.concatenate([latent_back, rotary_back], axis=-1).astype(BF)
    width = (LATENT + ROPE) // n_seq
    if fast:
        compressed_back_all = plane_gather(jnp.pad(compressed_back, ((0, 0), (0, 64))), 6)
        compressed_back_all = compressed_back_all[:, :, : LATENT + ROPE]
    else:
        compressed_back_all = lax.all_gather(compressed_back, "seq", axis=0)
    compressed_back_all = compressed_back_all.reshape(length, LATENT + ROPE)
    compress_grad = dot_tn(
        normed_all, lax.dynamic_slice_in_dim(compressed_back_all, seq_index * width, width, 1)
    )
    normed_back = summed_back[:, :features] + dot_nt(compressed_back, compress_weight)
    first_scale = rms_scale(hidden_float)
    first_gain_grad = jnp.sum(normed_back * hidden_float * first_scale, axis=0)
    hidden_gradient = (
        middle_back + norm_backward(normed_back, hidden_float, first_scale, first_gain)
    ).astype(BF)

    gain_grads = jnp.concatenate([first_gain_grad, second_gain_grad, latent_gain_grad])
    bit = 1
    while bit < n_seq:
        gain_grads = gain_grads + lax.ppermute(
            gain_grads, "seq", [(i, i ^ bit) for i in range(n_seq)]
        )
        bit *= 2
    bit = 1
    while bit < n_dp:
        gain_grads = gain_grads + lax.ppermute(
            gain_grads, "dp", [(i, i ^ bit) for i in range(n_dp)]
        )
        bit *= 2
    latent_shard = LATENT // n_dp

    def gain_part(start, size):
        return lax.dynamic_slice_in_dim(gain_grads, start + dp_index * size, size, 0)

    widths = [heads * QK, expand_width * latent_shard // shard, features // n_seq, width]
    parts = jnp.concatenate(
        [
            query_grad.reshape(n_dp, shard, -1),
            expand_grad.reshape(n_dp, shard, -1),
            output_grad.reshape(n_dp, shard, -1),
            compress_grad.reshape(n_dp, shard, -1),
        ],
        axis=-1,
    )
    if fast:
        extra = -parts.shape[-1] % 128
        summed = sum_grads(jnp.pad(parts, ((0, 0), (0, 0), (0, extra))).astype(BF), 7)
    else:
        summed = lax.psum_scatter(parts, "dp", scatter_dimension=0)
        summed = lax.all_gather(summed.astype(BF), "seq", axis=0)

    def columns(start, size, height):
        found = summed[:, :, start : start + size].reshape(n_seq, height, -1)
        return found.transpose(1, 0, 2).reshape(height, -1).astype(F32)

    starts = [sum(widths[:n]) for n in range(4)]
    shared_in_grad = shared_in_grad.reshape(2, padded_units, n_dp, shard)[:, :units].astype(BF)
    shared_in_out = lax.all_to_all(
        shared_in_grad.transpose(2, 3, 0, 1), "dp", split_axis=0, concat_axis=0, tiled=True
    )
    shared_in_out = lax.all_gather(shared_in_out, "seq", axis=0)
    shared_in_out = shared_in_out.transpose(2, 3, 1, 0, 4).reshape(shard, 2 * SH_FF).astype(F32)
    shared_out_out = lax.all_gather(
        shared_out_grad[:units].astype(BF), "seq", axis=0, tiled=True
    ).astype(F32)
    return (
        block_out.reshape(hidden_in.shape),
        hidden_gradient.reshape(hidden_in.shape),
        gate_gradient.reshape(gate_weights.shape),
        gain_part(0, shard),
        columns(starts[0], widths[0], shard),
        columns(starts[3], widths[3], shard),
        gain_part(2 * features, latent_shard),
        columns(starts[1], widths[1], latent_shard),
        columns(starts[2], widths[2], shard),
        gain_part(features, shard),
        shared_in_out,
        shared_out_out,
        expert_in_grad[None],
        expert_out_grad[None],
    )


def solution(mesh):
    token = P("dp", "seq", None)
    row = P("dp", None)
    half = P(("dp", "seq"), None, None)
    return jax.shard_map(
        on_device,
        mesh=mesh,
        in_specs=(
            token, P("dp", "seq"), token, token, P("dp"), row, row, P("dp"), row, row,
            P("dp"), row, row, half, half, token,
        ),
        out_specs=(
            token, token, token, P("dp"), row, row, P("dp"), row, row, P("dp"), row, row,
            half, half,
        ),
        check_vma=False,
    )
```

```python
import functools
import math

import jax
import jax.numpy as jnp
from jax import lax
from jax.experimental import pallas as pl
from jax.experimental.pallas import tpu as pltpu
from jax.sharding import PartitionSpec as P

HEADS = 16
NOPE = 128
ROPE = 64
VDIM = 128
LATENT = 512
TOP = 6
QK = 192
SH_FF = 2816
HALF = 704
EPSILON = 1e-06
BF = jnp.bfloat16
F32 = jnp.float32


def rms_scale(entries):
    return lax.rsqrt(jnp.mean(entries * entries, axis=-1, keepdims=True) + EPSILON)


def rotary_angles(position_rows):
    steps_index = jnp.arange(ROPE // 2, dtype=F32)
    frequency = 10000.0 ** (-2.0 * steps_index / ROPE)
    return position_rows.astype(F32)[..., None] * frequency


def rotate(values, cosine_values, sine_values):
    half_width = values.shape[-1] // 2
    front_half = values[..., :half_width]
    back_half = values[..., half_width:]
    return jnp.concatenate(
        [
            front_half * cosine_values - back_half * sine_values,
            front_half * sine_values + back_half * cosine_values,
        ],
        axis=-1,
    )


def norm_backward(upstream, entries, inverse_scale, gain_row):
    scaled = upstream * gain_row
    return inverse_scale * scaled - entries * inverse_scale**3 * jnp.mean(
        scaled * entries, axis=-1, keepdims=True
    )


def dot(a, b):
    return jnp.dot(a, b, preferred_element_type=F32)


def dot_nt(a, b):
    return jnp.einsum("ik,jk->ij", a, b, preferred_element_type=F32)


def dot_tn(a, b):
    return jnp.einsum("ki,kj->ij", a, b, preferred_element_type=F32)


def copy_kernel(places_ref, in_ref, out_ref):
    out_ref[...] = in_ref[...]


def reorder(stack, places):
    count = stack.shape[0]
    if stack.size * stack.dtype.itemsize < 2**20 or stack.ndim != 3:
        return jnp.stack(
            [lax.dynamic_index_in_dim(stack, places[j], 0, keepdims=False) for j in range(count)]
        )
    block = (1, *stack.shape[1:])
    return pl.pallas_call(
        copy_kernel,
        grid_spec=pltpu.PrefetchScalarGridSpec(
            num_scalar_prefetch=1,
            grid=(count,),
            in_specs=[pl.BlockSpec(block, lambda j, order: (order[j], 0, 0))],
            out_specs=pl.BlockSpec(block, lambda j, order: (j, 0, 0)),
        ),
        out_shape=jax.ShapeDtypeStruct(stack.shape, stack.dtype),
        compiler_params=params(40),
        cost_estimate=pl.CostEstimate(
            flops=0, bytes_accessed=2 * stack.size * stack.dtype.itemsize, transcendentals=0
        ),
    )(places.astype(jnp.int32), stack)


def small_take(table, index):
    table = jnp.array(table, jnp.int32)
    hit = index[:, None] == jnp.arange(table.shape[0])[None, :]
    return jnp.sum(jnp.where(hit, table[None, :], 0), axis=1)


def params(limit=60):
    return pltpu.CompilerParams(
        vmem_limit_bytes=limit * 2**20, dimension_semantics=("arbitrary",)
    )


MESH_ID = pl.DeviceIdType.MESH
OWN_SLOTS = (0, 2, 3, 6)
CORE_SLOTS = (1, 4, 5, 7)


def neighbours():
    dp = lax.axis_index("dp")
    seq = lax.axis_index("seq")
    core = {"dp": dp, "seq": seq + 1 - 2 * (seq % 2)}
    across_x = {"dp": dp, "seq": seq + 2 - 4 * ((seq // 2) % 2)}
    across_y = {"dp": dp, "seq": seq + 4 - 8 * (seq // 4)}
    following = {"dp": (dp + 1) % 4, "seq": seq}
    previous = {"dp": (dp + 3) % 4, "seq": seq}
    return core, across_x, across_y, following, previous


def greet(devices):
    barrier = pltpu.get_barrier_semaphore()
    for device in devices:
        pl.semaphore_signal(barrier, inc=1, device_id=device, device_id_type=MESH_ID)
    pl.semaphore_wait(barrier, len(devices))


class Courier:
    def __init__(self, send_sems, recv_sems):
        self.send_sems, self.recv_sems = send_sems, recv_sems
        self.sent, self.open = [], []

    def send(self, source, target, device):
        index = len(self.sent)
        copy = pltpu.make_async_remote_copy(
            src_ref=source,
            dst_ref=target,
            send_sem=self.send_sems.at[index],
            recv_sem=self.recv_sems.at[index],
            device_id=device,
            device_id_type=MESH_ID,
        )
        copy.start()
        self.sent.append(copy)
        self.open.append(copy)
        return copy

    def take(self, copy):
        copy.wait_recv()
        self.open = [other for other in self.open if other is not copy]

    def finish(self):
        for copy in list(self.open):
            self.take(copy)
        for copy in self.sent:
            copy.wait_send()


def accumulate(target, *sources):
    rows = target.shape[0]
    step = 16

    def body(k, carry):
        part = pl.ds(pl.multiple_of(k * step, step), step)
        total = target[part].astype(F32)
        for source in sources:
            total = total + source[part].astype(F32)
        target[part] = total.astype(target.dtype)
        return carry

    lax.fori_loop(0, rows // step, body, 0)


SCATTER_ORDER = (1, 2, 3, 0)


class ScatterAll:
    @staticmethod
    def scratch(rows, columns, dtype):
        return [
            pltpu.VMEM((4, 4, rows, columns), dtype),
            pltpu.VMEM((4, 2, rows // 2, columns), dtype),
            pltpu.VMEM((4, 2, rows, columns), dtype),
            pltpu.VMEM((3, rows, columns), dtype),
            pltpu.VMEM((4, rows, columns), dtype),
            pltpu.SemaphoreType.DMA((35,)),
            pltpu.SemaphoreType.DMA((35,)),
            pltpu.SemaphoreType.DMA((4,)),
        ]

    def __init__(self, in_ref, held, far, near, ring, stage, send_sems, recv_sems, local_sems):
        self.in_ref, self.held, self.far, self.near = in_ref, held, far, near
        self.ring, self.stage = ring, stage
        self.send_sems, self.recv_sems, self.local_sems = send_sems, recv_sems, local_sems
        self.core, self.across_x, self.across_y, self.following, self.previous = neighbours()
        rows = held.shape[2]
        self.top, self.bottom = pl.ds(0, rows // 2), pl.ds(rows // 2, rows // 2)

    def copy(self, index, source, target, device):
        return pltpu.make_async_remote_copy(
            src_ref=source,
            dst_ref=target,
            send_sem=self.send_sems.at[index],
            recv_sem=self.recv_sems.at[index],
            device_id=device,
            device_id_type=MESH_ID,
        )

    def to_core(self, i, k):
        source = self.in_ref.at[8 * i + CORE_SLOTS[k]]
        return self.copy(19 + 4 * i + k, source, self.held.at[i, k], self.core)

    def far_copy(self, i, which):
        part = self.bottom if which else self.top
        device = self.across_x if which else self.across_y
        return self.copy(2 * i + which, self.held.at[i, 3, part], self.far.at[i, which], device)

    def near_copy(self, i, which):
        device = self.across_y if which else self.across_x
        return self.copy(8 + 2 * i + which, self.held.at[i, 1 + which], self.near.at[i, which], device)

    def ring_copy(self, n):
        return self.copy(
            16 + n, self.held.at[SCATTER_ORDER[n], 0], self.ring.at[n], self.following
        )

    def loads(self, n):
        i = SCATTER_ORDER[n]
        return [
            pltpu.make_async_copy(
                self.in_ref.at[8 * i + OWN_SLOTS[k]], self.stage.at[k], self.local_sems.at[k]
            )
            for k in range(4)
        ]

    def begin(self):
        greet((self.core, self.across_x, self.across_y, self.following, self.previous))
        for i in SCATTER_ORDER:
            for k in (3, 1, 2, 0):
                self.to_core(i, k).start()
        for load in self.loads(0):
            load.start()

    def first(self, n):
        i = SCATTER_ORDER[n]
        loads = self.loads(n)
        later = self.loads(n + 1) if n < 3 else None
        for k in (3, 1, 2, 0):
            loads[k].wait()
            self.to_core(i, k).wait_recv()
            accumulate(self.held.at[i, k], self.stage.at[k])
            if later:
                later[k].start()
            if k == 3:
                self.far_copy(i, 0).start()
                self.far_copy(i, 1).start()

    def second(self, n):
        i = SCATTER_ORDER[n]
        self.far_copy(i, 0).wait_recv()
        accumulate(self.held.at[i, 1, self.top], self.far.at[i, 0])
        self.near_copy(i, 0).start()
        self.far_copy(i, 1).wait_recv()
        accumulate(self.held.at[i, 2, self.bottom], self.far.at[i, 1])
        self.near_copy(i, 1).start()

    def third(self, n):
        i = SCATTER_ORDER[n]
        self.near_copy(i, 0).wait_recv()
        self.near_copy(i, 1).wait_recv()
        sources = [self.near.at[i, 0], self.near.at[i, 1]]
        if n > 0:
            self.ring_copy(n - 1).wait_recv()
            sources.append(self.ring.at[n - 1])
        accumulate(self.held.at[i, 0], *sources)
        if n < 3:
            self.ring_copy(n).start()

    def events(self):
        first, second, third = self.first, self.second, self.third
        plan = [
            (first, 0), (first, 1), (second, 0), (first, 2), (second, 1), (third, 0), (first, 3),
            (second, 2), (third, 1), (second, 3), (third, 2), (third, 3),
        ]
        return [functools.partial(f, n) for f, n in plan]

    def finish(self, out_ref):
        out_ref[...] = self.held[0, 0]
        for i in range(4):
            for k in range(4):
                self.to_core(i, k).wait_send()
            for which in range(2):
                self.far_copy(i, which).wait_send()
                self.near_copy(i, which).wait_send()
        for n in range(3):
            self.ring_copy(n).wait_send()


def scatter_all_kernel(in_ref, out_ref, *scratch):
    scatter = ScatterAll(in_ref, *scratch)
    scatter.begin()
    for event in scatter.events():
        event()
    scatter.finish(out_ref)


def scatter_all(parts, collective_id):
    _, rows, columns = parts.shape
    return pl.pallas_call(
        scatter_all_kernel,
        out_shape=jax.ShapeDtypeStruct((rows, columns), parts.dtype),
        in_specs=[pl.BlockSpec(memory_space=pl.ANY)],
        out_specs=pl.BlockSpec(memory_space=pltpu.VMEM),
        scratch_shapes=ScatterAll.scratch(rows, columns, parts.dtype),
        compiler_params=pltpu.CompilerParams(
            collective_id=collective_id, has_side_effects=True, vmem_limit_bytes=56 * 2**20
        ),
        cost_estimate=pl.CostEstimate(
            flops=32 * rows * columns, bytes_accessed=64 * rows * columns * 2, transcendentals=0
        ),
    )(parts)


def spread(post, source, place, core, across_x, across_y):
    seq = lax.axis_index("seq")
    x_seq = seq + 2 - 4 * ((seq // 2) % 2)
    y_seq = seq + 4 - 8 * (seq // 4)
    xy_seq = x_seq + 4 - 8 * (seq // 4)
    x_copy = post.send(source, place(seq), across_x)
    y_copy = post.send(source, place(seq), across_y)
    post.send(source, place(seq), core)
    yield
    post.take(x_copy)
    far_top = post.send(place(x_seq, 0), place(x_seq, 0), across_y)
    post.send(place(x_seq), place(x_seq), core)
    post.take(y_copy)
    far_bottom = post.send(place(y_seq, 1), place(y_seq, 1), across_x)
    post.send(place(y_seq), place(y_seq), core)
    yield
    post.take(far_top)
    post.take(far_bottom)
    post.send(place(xy_seq), place(xy_seq), core)


def blocks_of(found):
    half = found.shape[1] // 2

    def place(index, part=None):
        if part is None:
            return found.at[index]
        return found.at[index, pl.ds(part * half, half)]

    return place


def advance(*spreads):
    for one in spreads:
        for _ in one:
            break


def gather_start_kernel(
    hidden, named, gains, query, expand, compress, output, hidden_all, named_all, gains_all,
    query_all, expand_all, compress_all, output_all, send_sems, recv_sems, local_sems
):
    dp = lax.axis_index("dp")
    seq = lax.axis_index("seq")
    core, across_x, across_y, following, previous = neighbours()
    greet((core, across_x, across_y, following, previous))
    post = Courier(send_sems, recv_sems)
    strip = output.shape[0] // 8
    own_strip = pl.ds(pl.multiple_of(seq * strip, strip), strip)
    core_half = compress.shape[0] // 2
    mine = pl.ds(pl.multiple_of((seq % 2) * core_half, core_half), core_half)
    hidden_spread = spread(post, hidden, blocks_of(hidden_all), core, across_x, across_y)
    advance(hidden_spread)

    def hop(i):
        at = (dp + 5 - i) % 4
        first = i == 1
        return [
            post.send(query if first else query_all.at[at], query_all.at[at], following),
            post.send(
                compress.at[mine] if first else compress_all.at[at, mine],
                compress_all.at[at, mine],
                following,
            ),
            post.send(expand if first else expand_all.at[at], expand_all.at[at], following),
            post.send(gains if first else gains_all.at[at], gains_all.at[at], following),
            post.send(named if first else named_all.at[0, i - 1], named_all.at[0, i], following),
            post.send(
                output.at[own_strip] if first else output_all.at[at, own_strip],
                output_all.at[at, own_strip],
                following,
            ),
        ]

    def strip_spread(at):
        def place(index, part=None):
            if part is None:
                where = pl.ds(pl.multiple_of(index * strip, strip), strip)
            else:
                half = strip // 2
                where = pl.ds(pl.multiple_of(index * strip + part * half, half), half)
            return output_all.at[at, where]

        return spread(post, place(seq), place, core, across_x, across_y)

    ring = hop(1)
    locals_ = [
        pltpu.make_async_copy(source, target, local_sems.at[n])
        for n, (source, target) in enumerate(
            (
                (hidden, hidden_all.at[seq]),
                (named, named_all.at[0, 0]),
                (gains, gains_all.at[dp]),
                (query, query_all.at[dp]),
                (expand, expand_all.at[dp]),
                (compress, compress_all.at[dp]),
                (output, output_all.at[dp]),
            )
        )
    ]
    for copy in locals_:
        copy.start()
    spreads = []
    for i in (2, 3, 4):
        for copy in ring:
            post.take(copy)
        at = (dp + 5 - i) % 4
        if i < 4:
            ring = hop(i)
        post.send(compress_all.at[at, mine], compress_all.at[at, mine], core)
        advance(*spreads)
        if i < 4:
            advance(hidden_spread)
        spreads.append(strip_spread(at))
        advance(spreads[-1])
    locals_[1].wait()
    names_x = post.send(named_all.at[0], named_all.at[1], across_x)
    advance(*spreads)
    post.take(names_x)
    names_y = post.send(named_all.at[pl.ds(0, 2)], named_all.at[pl.ds(2, 2)], across_y)
    advance(*spreads)
    post.take(names_y)
    post.send(named_all.at[pl.ds(0, 4)], named_all.at[pl.ds(4, 4)], core)
    for n, copy in enumerate(locals_):
        if n != 1:
            copy.wait()
    post.finish()


def gather_start(hidden, named, gains, query, expand, compress, output, collective_id):
    anywhere = pl.BlockSpec(memory_space=pl.ANY)
    total = 8 + 6 * 3 + 3 + 3 + 8 * 3
    return pl.pallas_call(
        gather_start_kernel,
        out_shape=[
            jax.ShapeDtypeStruct((8, *hidden.shape), hidden.dtype),
            jax.ShapeDtypeStruct((8, 4, *named.shape), named.dtype),
        ]
        + [jax.ShapeDtypeStruct((4, *x.shape), x.dtype) for x in (gains, query, expand, compress, output)],
        in_specs=[anywhere] * 7,
        out_specs=[anywhere] * 7,
        scratch_shapes=[
            pltpu.SemaphoreType.DMA((total,)),
            pltpu.SemaphoreType.DMA((total,)),
            pltpu.SemaphoreType.DMA((7,)),
        ],
        compiler_params=pltpu.CompilerParams(
            collective_id=collective_id, has_side_effects=True, vmem_limit_bytes=16 * 2**20
        ),
        cost_estimate=pl.CostEstimate(flops=0, bytes_accessed=2**26, transcendentals=0),
    )(hidden, named, gains, query, expand, compress, output)


PADDED_HALF = 768
TILE = 256


def flip(value, change):
    return value + change - 2 * value * change


def pair_of(step, remote):
    if not remote:
        return step
    first = 1 - (step + 15) // 16
    last = (step + 3) // 16
    turn_of, place = (step + 3) // 4 - 1, (step + 3) % 4
    ahead = 1 - (place + 3) // 4
    return (1 - first) * (1 - last) * (4 * turn_of + place + 4 * ahead) + last * step


def experts_kernel(
    remote, capacity, rows_in, place_ref, gate_ref, weight_in_ref, weight_out_ref, shared_in,
    shared_out, rows_all, in_grad_ref, out_grad_ref, hidden_out, units_ref, part_ref,
    shared_in_grad, shared_out_grad, rows_buffer, cot_buffer, weight_in, weight_up, weight_out,
    slot_rows_pair, slot_up_pair, hidden_pair, back_pair, in_grad, out_grad, rows_out, load_sems,
    weight_sems, *sems
):
    step = pl.program_id(0)
    steps = pl.num_programs(0)
    rows = place_ref.shape[2]
    features = weight_in.shape[0]
    pair = pair_of(step, remote)
    slot = step % 2
    half_slots = 2 * capacity
    now = pl.ds(pl.multiple_of(slot * half_slots, half_slots), half_slots)
    slot_rows, slot_up = slot_rows_pair.at[now], slot_up_pair.at[now]
    hidden_ref, back_ref = hidden_pair.at[now], back_pair.at[now]
    gathered = rows_all if remote else rows_in

    def loads(at, into):
        found = []
        for b in range(2):
            block = 2 * pair_of(at, remote) + b
            part = pl.ds(b * rows, rows)
            for kind, buffer in enumerate((rows_buffer, cot_buffer)):
                found.append(
                    pltpu.make_async_copy(
                        gathered.at[block, kind],
                        buffer.at[into, part],
                        load_sems.at[into, 2 * b + kind],
                    )
                )
        return found

    if remote:
        send_sems, recv_sems, own_sem = sems
        core, across_x, across_y, following, previous = neighbours()
        half = rows // 2
        top, bottom = pl.ds(0, half), pl.ds(half, half)

        def copy(index, source, target, device):
            return pltpu.make_async_remote_copy(
                src_ref=source,
                dst_ref=target,
                send_sem=send_sems.at[index],
                recv_sem=recv_sems.at[index],
                device_id=device,
                device_id_type=MESH_ID,
            )

        def block_of(i):
            return rows_in if i == 0 else rows_all.at[8 * i]

        def along(i):
            return copy(9 * i, block_of(i), rows_all.at[8 * i + 8], following)

        def by_x(i):
            return copy(9 * i + 1, block_of(i), rows_all.at[8 * i + 2], across_x)

        def by_y(i):
            return copy(9 * i + 2, block_of(i), rows_all.at[8 * i + 3], across_y)

        def far(i, which):
            if which == 0:
                return copy(
                    9 * i + 3, rows_all.at[8 * i + 2, :, top], rows_all.at[8 * i + 6, :, top], across_y
                )
            return copy(
                9 * i + 4, rows_all.at[8 * i + 3, :, bottom], rows_all.at[8 * i + 6, :, bottom], across_x
            )

        def to_core(i, k):
            source = block_of(i) if k == 0 else rows_all.at[8 * i + OWN_SLOTS[k]]
            return copy(9 * i + 5 + k, source, rows_all.at[8 * i + CORE_SLOTS[k]], core)

        def begin_plane(i):
            by_x(i).start()
            by_y(i).start()

        def plane_arrived(i):
            by_x(i).wait_recv()
            far(i, 0).start()
            to_core(i, 1).start()
            by_y(i).wait_recv()
            far(i, 1).start()
            to_core(i, 2).start()

        def far_arrived(i):
            far(i, 0).wait_recv()
            far(i, 1).wait_recv()
            to_core(i, 3).start()

        def along_arrived(i):
            along(i).wait_recv()
            if i < 2:
                along(i + 1).start()
            to_core(i + 1, 0).start()

        def core_arrived(i, *which):
            for k in which:
                to_core(i, k).wait_recv()

        ready = {
            0: [(core_arrived, 0, 0)],
            1: [(along_arrived, 0), (plane_arrived, 0), (core_arrived, 1, 0)],
            2: [(begin_plane, 1)],
            3: [(core_arrived, 0, 1, 2), (far_arrived, 0)],
            4: [(core_arrived, 0, 3), (along_arrived, 1)],
            5: [(core_arrived, 2, 0), (plane_arrived, 1)],
            6: [(begin_plane, 2)],
            7: [(core_arrived, 1, 1, 2), (far_arrived, 1), (along_arrived, 2)],
            8: [(core_arrived, 1, 3)],
            9: [(core_arrived, 3, 0), (plane_arrived, 2)],
            10: [(begin_plane, 3)],
            11: [(core_arrived, 2, 1, 2), (far_arrived, 2)],
            12: [(core_arrived, 2, 3)],
            13: [(plane_arrived, 3)],
            14: [(core_arrived, 3, 1, 2)],
            15: [(far_arrived, 3), (core_arrived, 3, 3)],
        }

        def prepare(at):
            for event, *given in ready[at]:
                event(*given)

        @pl.when(step == 0)
        def _():
            greet((core, across_x, across_y, following, previous))
            own = pltpu.make_async_copy(rows_in, rows_all.at[0], own_sem)
            own.start()
            along(0).start()
            begin_plane(0)
            to_core(0, 0).start()
            own.wait()

    @pl.when(step == 0)
    def _():
        weights = (
            pltpu.make_async_copy(weight_in_ref, weight_in, weight_sems.at[0]),
            pltpu.make_async_copy(weight_out_ref, weight_out.at[pl.ds(0, HALF)], weight_sems.at[1]),
        )
        for copy_in in weights:
            copy_in.start()
        in_grad[...] = jnp.zeros_like(in_grad)
        out_grad[...] = jnp.zeros_like(out_grad)
        shared_in_grad[...] = jnp.zeros_like(shared_in_grad)
        shared_out_grad[...] = jnp.zeros_like(shared_out_grad)
        weight_out[pl.ds(HALF, PADDED_HALF - HALF)] = jnp.zeros(
            (PADDED_HALF - HALF, features), BF
        )
        for copy_in in weights:
            copy_in.wait()

        def split(k, carry):
            part = pl.ds(pl.multiple_of(k * 128, 128), 128)
            up = weight_in[part, HALF:].astype(F32)
            up = jnp.concatenate([up, jnp.zeros((128, PADDED_HALF - HALF), F32)], axis=1)
            weight_up[part] = up.astype(BF)
            return carry

        lax.fori_loop(0, features // 128, split, 0)
        if remote:
            prepare(0)
        for load in loads(0, 0):
            load.start()

    for load in loads(step, slot):
        load.wait()

    picks = []
    for b in range(2):
        chosen = one_hot(place_ref, 2 * pair + b, capacity)
        pick = chosen.astype(F32)
        picks.append(pick.T.astype(BF))
        pick = pick.astype(BF)
        gates = jnp.sum(jnp.where(chosen, gate_ref[2 * pair + b], 0.0), axis=1, keepdims=True)
        part = pl.ds(b * rows, rows)
        slots = pl.ds(b * capacity, capacity)
        slot_rows[slots] = dot(pick, rows_buffer[slot, part]).astype(BF)
        slot_up[slots] = (dot(pick, cot_buffer[slot, part]) * gates).astype(BF)

    def gated(gate, up, hidden_back):
        sigmoid = 1.0 / (1.0 + jnp.exp(-gate))
        active = gate * sigmoid
        gate_back = hidden_back * up * sigmoid * (1.0 + gate * (1.0 - sigmoid))
        return (active * up).astype(BF), gate_back.astype(BF), (hidden_back * active).astype(BF)

    def hidden_tile(t, carry):
        part = pl.ds(pl.multiple_of(t * TILE, TILE), TILE)
        second = pl.ds(pl.multiple_of(PADDED_HALF + t * TILE, TILE), TILE)
        gate = dot(slot_rows[...], weight_in[:, part])
        up = dot(slot_rows[...], weight_up[:, part])
        hidden_back = dot_nt(slot_up[...], weight_out[part])
        hidden_ref[:, part], back_ref[:, part], back_ref[:, second] = gated(gate, up, hidden_back)
        return carry

    lax.fori_loop(0, PADDED_HALF // TILE, hidden_tile, 0)
    hidden_out[...] = hidden_ref[...]

    width = shared_out.shape[0]
    rows_pair, cot_pair = rows_buffer[slot], cot_buffer[slot]
    gate_up = dot(rows_pair, shared_in[...])
    hidden_back = dot_nt(cot_pair, shared_out[...])
    units, gate_back, up_back = gated(gate_up[:, :width], gate_up[:, width:], hidden_back)
    units_ref[...] = units
    shared_back = jnp.concatenate([gate_back, up_back], axis=1)
    shared_in_grad[...] += dot_tn(shared_back, rows_pair)
    shared_out_grad[...] += dot_tn(units, cot_pair)

    if remote:
        for at in range(1, 16):

            @pl.when(step + 1 == at)
            def _():
                prepare(at)

    @pl.when(step + 1 < steps)
    def _():
        for load in loads(step + 1, 1 - slot):
            load.start()

    def back_tile(t, carry):
        part = pl.ds(pl.multiple_of(t * 2 * TILE, 2 * TILE), 2 * TILE)
        slot_back = dot_nt(back_ref[:, :PADDED_HALF], weight_in[part, :PADDED_HALF])
        slot_back = (slot_back + dot_nt(back_ref[:, PADDED_HALF:], weight_up[part])).astype(BF)
        shared_part = dot_nt(shared_back, shared_in[part])
        for b in range(2):
            tokens = slice(b * rows, (b + 1) * rows)
            total = dot(picks[b], slot_back[b * capacity : (b + 1) * capacity])
            part_ref[b, :, part] = (total + shared_part[tokens]).astype(BF)
        return carry

    lax.fori_loop(0, features // (2 * TILE), back_tile, 0)

    @pl.when(slot == 1)
    def _():
        def in_tile(t, carry):
            part = pl.ds(pl.multiple_of(t * TILE, TILE), TILE)
            in_grad[part] += dot_tn(slot_rows_pair[:, part], back_pair[...])
            return carry

        lax.fori_loop(0, features // TILE, in_tile, 0)

        def out_tile(t, carry):
            part = pl.ds(pl.multiple_of(t * TILE, TILE), TILE)
            out_grad[part] += dot_tn(hidden_pair[:, part], slot_up_pair[...])
            return carry

        lax.fori_loop(0, PADDED_HALF // TILE, out_tile, 0)

    @pl.when(step + 1 == steps)
    def _():
        whole_out = pltpu.make_async_copy(
            out_grad.at[pl.ds(0, HALF)], out_grad_ref, weight_sems.at[0]
        )
        whole_out.start()
        height = rows_out.shape[1]

        def out_copy(k):
            part = pl.ds(pl.multiple_of(k * height, height), height)
            return pltpu.make_async_copy(
                rows_out.at[k % 2], in_grad_ref.at[part], load_sems.at[k % 2, 0]
            )

        def write(k, carry):
            @pl.when(k >= 2)
            def _():
                out_copy(k - 2).wait()

            part = pl.ds(pl.multiple_of(k * height, height), height)
            rows_out[k % 2] = jnp.concatenate(
                [in_grad[part, :HALF], in_grad[part, PADDED_HALF : PADDED_HALF + HALF]], axis=1
            )
            out_copy(k).start()
            return carry

        count = features // height
        lax.fori_loop(0, count, write, 0)
        out_copy(count - 2).wait()
        out_copy(count - 1).wait()
        whole_out.wait()

    if remote:

        @pl.when(step + 1 == steps)
        def _():
            for i in range(4):
                if i < 3:
                    along(i).wait_send()
                by_x(i).wait_send()
                by_y(i).wait_send()
                far(i, 0).wait_send()
                far(i, 1).wait_send()
                for k in range(4):
                    to_core(i, k).wait_send()


def one_hot(place_ref, block, capacity):
    place = place_ref[block]
    rows = place.shape[1]
    return lax.broadcasted_iota(jnp.int32, (capacity, rows), 0) == place


def experts(
    remote, capacity, rows_in, places, gates, weight_in, weight_out, shared_in, shared_out
):
    blocks, _, rows = places.shape
    features = weight_in.shape[0]
    width = shared_out.shape[0]
    steps = blocks // 2

    def whole(array):
        return pl.BlockSpec(
            array.shape, lambda j: (0,) * array.ndim, pipeline_mode=pl.Buffered(1)
        )

    def tiled(height, columns):
        return pl.BlockSpec((height, columns), lambda j: (pair_of(j, remote), 0))

    anywhere = pl.BlockSpec(memory_space=pl.ANY)
    slots = 2 * capacity
    scratch = [
        pltpu.VMEM((2, 2 * rows, features), BF),
        pltpu.VMEM((2, 2 * rows, features), BF),
        pltpu.VMEM(weight_in.shape, BF),
        pltpu.VMEM((features, PADDED_HALF), BF),
        pltpu.VMEM((PADDED_HALF, features), BF),
        pltpu.VMEM((2 * slots, features), BF),
        pltpu.VMEM((2 * slots, features), BF),
        pltpu.VMEM((2 * slots, PADDED_HALF), BF),
        pltpu.VMEM((2 * slots, 2 * PADDED_HALF), BF),
        pltpu.VMEM((features, 2 * PADDED_HALF), F32),
        pltpu.VMEM((PADDED_HALF, features), F32),
        pltpu.VMEM((2, 64, 2 * HALF), F32),
        pltpu.SemaphoreType.DMA((2, 4)),
        pltpu.SemaphoreType.DMA((2,)),
    ]
    if remote:
        scratch += [
            pltpu.SemaphoreType.DMA((36,)),
            pltpu.SemaphoreType.DMA((36,)),
            pltpu.SemaphoreType.DMA,
        ]
    found = pl.pallas_call(
        functools.partial(experts_kernel, remote, capacity),
        grid=(steps,),
        in_specs=[anywhere, whole(places), whole(gates), anywhere, anywhere]
        + [whole(x) for x in (shared_in, shared_out)],
        out_specs=[
            anywhere,
            anywhere,
            anywhere,
            tiled(slots, PADDED_HALF),
            tiled(2 * rows, width),
            pl.BlockSpec((2, rows, features), lambda j: (pair_of(j, remote), 0, 0)),
            pl.BlockSpec(
                (2 * width, features), lambda j: (0, 0), pipeline_mode=pl.Buffered(1)
            ),
            pl.BlockSpec((width, features), lambda j: (0, 0), pipeline_mode=pl.Buffered(1)),
        ],
        out_shape=[
            jax.ShapeDtypeStruct((blocks if remote else 1, 2, rows, features), BF),
            jax.ShapeDtypeStruct(weight_in.shape, F32),
            jax.ShapeDtypeStruct(weight_out.shape, F32),
            jax.ShapeDtypeStruct((steps * slots, PADDED_HALF), BF),
            jax.ShapeDtypeStruct((blocks * rows, width), BF),
            jax.ShapeDtypeStruct((blocks, rows, features), BF),
            jax.ShapeDtypeStruct((2 * width, features), F32),
            jax.ShapeDtypeStruct((width, features), F32),
        ],
        scratch_shapes=scratch,
        compiler_params=pltpu.CompilerParams(
            vmem_limit_bytes=63 * 2**20,
            dimension_semantics=("arbitrary",),
            **({"collective_id": 3, "has_side_effects": True} if remote else {}),
        ),
        cost_estimate=pl.CostEstimate(
            flops=steps * slots * features * 2 * 3 * 2 * PADDED_HALF,
            bytes_accessed=blocks * features * 8 * rows,
            transcendentals=0,
        ),
    )(rows_in, places, gates, weight_in, weight_out, shared_in, shared_out)
    return found


def plane_scatter_kernel(
    in_ref, out_ref, held, far, near, stage, send_sems, recv_sems, local_sems
):
    core, across_x, across_y, _, _ = neighbours()
    greet((core, across_x, across_y))
    seq = lax.axis_index("seq")
    rows = out_ref.shape[0]
    top, bottom = pl.ds(0, rows // 2), pl.ds(rows // 2, rows // 2)
    post = Courier(send_sems, recv_sems)
    x_seq = seq + 2 - 4 * ((seq // 2) % 2)
    y_seq = seq + 4 - 8 * (seq // 4)
    xy_seq = x_seq + 4 - 8 * (seq // 4)
    core_step = 1 - 2 * (seq % 2)
    loads, arriving = {}, {}
    for k, place in ((3, xy_seq), (1, x_seq), (2, y_seq), (0, seq)):
        arriving[k] = post.send(in_ref.at[place + core_step], held.at[k], core)
        loads[k] = pltpu.make_async_copy(in_ref.at[place], stage.at[k], local_sems.at[k])
        loads[k].start()

    def join(k):
        loads[k].wait()
        post.take(arriving[k])
        accumulate(held.at[k], stage.at[k])

    join(3)
    far_top = post.send(held.at[3, top], far.at[0], across_y)
    far_bottom = post.send(held.at[3, bottom], far.at[1], across_x)
    join(1)
    x_bottom = post.send(held.at[1, bottom], near.at[0, bottom], across_x)
    join(2)
    y_top = post.send(held.at[2, top], near.at[1, top], across_y)
    join(0)
    post.take(far_top)
    accumulate(held.at[1, top], far.at[0])
    x_top = post.send(held.at[1, top], near.at[0, top], across_x)
    post.take(far_bottom)
    accumulate(held.at[2, bottom], far.at[1])
    y_bottom = post.send(held.at[2, bottom], near.at[1, bottom], across_y)
    for copy in (x_bottom, y_top, x_top, y_bottom):
        post.take(copy)
    accumulate(held.at[0], near.at[0], near.at[1])
    out_ref[...] = held[0]
    post.finish()


def plane_scatter(parts, collective_id):
    _, rows, columns = parts.shape
    return pl.pallas_call(
        plane_scatter_kernel,
        out_shape=jax.ShapeDtypeStruct((rows, columns), parts.dtype),
        in_specs=[pl.BlockSpec(memory_space=pl.ANY)],
        out_specs=pl.BlockSpec(memory_space=pltpu.VMEM),
        scratch_shapes=[
            pltpu.VMEM((4, rows, columns), parts.dtype),
            pltpu.VMEM((2, rows // 2, columns), parts.dtype),
            pltpu.VMEM((2, rows, columns), parts.dtype),
            pltpu.VMEM((4, rows, columns), parts.dtype),
            pltpu.SemaphoreType.DMA((10,)),
            pltpu.SemaphoreType.DMA((10,)),
            pltpu.SemaphoreType.DMA((4,)),
        ],
        compiler_params=pltpu.CompilerParams(
            collective_id=collective_id, has_side_effects=True, vmem_limit_bytes=32 * 2**20
        ),
        cost_estimate=pl.CostEstimate(
            flops=8 * rows * columns, bytes_accessed=16 * rows * columns, transcendentals=0
        ),
    )(parts)


def plane_gather_kernel(in_ref, out_ref, send_sems, recv_sems, local_sem):
    core, across_x, across_y, _, _ = neighbours()
    greet((core, across_x, across_y))
    own = pltpu.make_async_copy(in_ref, out_ref.at[lax.axis_index("seq")], local_sem)
    own.start()
    post = Courier(send_sems, recv_sems)
    for _ in spread(post, in_ref, blocks_of(out_ref), core, across_x, across_y):
        pass
    own.wait()
    post.finish()


def plane_gather(block, collective_id):
    anywhere = pl.BlockSpec(memory_space=pl.ANY)
    return pl.pallas_call(
        plane_gather_kernel,
        out_shape=jax.ShapeDtypeStruct((8, *block.shape), block.dtype),
        in_specs=[anywhere],
        out_specs=anywhere,
        scratch_shapes=[
            pltpu.SemaphoreType.DMA((8,)),
            pltpu.SemaphoreType.DMA((8,)),
            pltpu.SemaphoreType.DMA,
        ],
        compiler_params=pltpu.CompilerParams(
            collective_id=collective_id, has_side_effects=True, vmem_limit_bytes=16 * 2**20
        ),
        cost_estimate=pl.CostEstimate(
            flops=0, bytes_accessed=32 * block.size, transcendentals=0
        ),
    )(block)


def grads_kernel(in_ref, out_ref, total, ring, send_sems, recv_sems, local_sems):
    dp = lax.axis_index("dp")
    core, across_x, across_y, following, previous = neighbours()
    greet((core, across_x, across_y, following, previous))
    post = Courier(send_sems, recv_sems)
    loads = []
    for n, i in enumerate((1, 2, 3, 0)):
        load = pltpu.make_async_copy(in_ref.at[(dp + 4 - i) % 4], total.at[n], local_sems.at[n])
        load.start()
        loads.append(load)
    loads[0].wait()
    before = post.send(total.at[0], ring.at[0], following)
    for n in (1, 2, 3):
        loads[n].wait()
        post.take(before)
        accumulate(total.at[n], ring.at[n - 1])
        if n < 3:
            before = post.send(total.at[n], ring.at[n], following)
    own = pltpu.make_async_copy(total.at[3], out_ref.at[lax.axis_index("seq")], local_sems.at[0])
    own.start()
    for _ in spread(post, total.at[3], blocks_of(out_ref), core, across_x, across_y):
        pass
    own.wait()
    post.finish()


def sum_grads(parts, collective_id):
    _, rows, columns = parts.shape
    anywhere = pl.BlockSpec(memory_space=pl.ANY)
    return pl.pallas_call(
        grads_kernel,
        out_shape=jax.ShapeDtypeStruct((8, rows, columns), parts.dtype),
        in_specs=[anywhere],
        out_specs=anywhere,
        scratch_shapes=[
            pltpu.VMEM((4, rows, columns), parts.dtype),
            pltpu.VMEM((3, rows, columns), parts.dtype),
            pltpu.SemaphoreType.DMA((11,)),
            pltpu.SemaphoreType.DMA((11,)),
            pltpu.SemaphoreType.DMA((4,)),
        ],
        compiler_params=pltpu.CompilerParams(
            collective_id=collective_id, has_side_effects=True, vmem_limit_bytes=32 * 2**20
        ),
        cost_estimate=pl.CostEstimate(
            flops=0, bytes_accessed=32 * rows * columns, transcendentals=0
        ),
    )(parts)


OUT_EVENTS = (3, 5, 7, 9, 13, 17, 18, 23, 27, 30, 31, 31)


def out_terms(capacity, place_ref, gate_ref, hidden_ref, cot_ref, units_ref, weight_ref, shared_ref,
              gate_grad_ref, part_ref):
    features = part_ref.shape[2]
    chosen = one_hot(place_ref, 0, capacity)
    pick = chosen.astype(F32)
    pick, spread_pick = pick.astype(BF), pick.T.astype(BF)
    gates = jnp.sum(jnp.where(chosen, gate_ref[0], 0.0), axis=1, keepdims=True)

    def tile(t, slot_grad):
        part = pl.ds(pl.multiple_of(t * 2 * TILE, 2 * TILE), 2 * TILE)
        result = dot(hidden_ref[:, :HALF], weight_ref[:, part]).astype(BF).astype(F32)
        slot_grad += jnp.sum(result * dot(pick, cot_ref[0, 0, :, part]), axis=1, keepdims=True)
        total = dot(spread_pick, (result * gates).astype(BF)) + dot(units_ref[...], shared_ref[:, part])
        part_ref[0, :, part] = total.astype(BF)
        return slot_grad

    slot_grad = lax.fori_loop(0, features // (2 * TILE), tile, jnp.zeros((capacity, 1), F32))
    gate_grad_ref[0] = jnp.sum(jnp.where(chosen, slot_grad, 0.0), axis=0, keepdims=True)


def out_kernel(remote, capacity, back_ref, *refs):
    step = pl.program_id(0)
    terms, sum_ref, scratch = refs[:9], refs[9], refs[10:]
    if remote:
        scatter = ScatterAll(back_ref, *scratch)
        pl.when(step == 0)(scatter.begin)
    out_terms(capacity, *terms)
    if remote:
        events = scatter.events()
        for at in sorted(set(OUT_EVENTS)):

            @pl.when(step == at)
            def _():
                for event, when in zip(events, OUT_EVENTS):
                    if when == at:
                        event()
                if at == OUT_EVENTS[-1]:
                    scatter.finish(sum_ref)


def out_side(remote, capacity, back_parts, places, gates, hidden, sent, units, weight_out, shared_out):
    blocks, _, rows = places.shape
    features = sent.shape[-1]
    one = pl.BlockSpec((1, 1, rows), lambda j: (j, 0, 0))

    def tiled(height, columns):
        return pl.BlockSpec((height, columns), lambda j: (j, 0))

    def whole(array):
        return pl.BlockSpec(array.shape, lambda j: (0, 0), pipeline_mode=pl.Buffered(1))

    return pl.pallas_call(
        functools.partial(out_kernel, remote, capacity),
        grid=(blocks,),
        in_specs=[
            pl.BlockSpec(memory_space=pl.ANY),
            one,
            one,
            tiled(capacity, PADDED_HALF),
            pl.BlockSpec((1, 1, rows, features), lambda j: (j, 1, 0, 0)),
            tiled(rows, units.shape[1]),
            whole(weight_out),
            whole(shared_out),
        ],
        out_specs=[
            one,
            pl.BlockSpec((1, rows, features), lambda j: (j, 0, 0)),
            pl.BlockSpec((rows, features), lambda j: (0, 0)),
        ],
        out_shape=[
            jax.ShapeDtypeStruct((blocks, 1, rows), F32),
            jax.ShapeDtypeStruct((blocks, rows, features), BF),
            jax.ShapeDtypeStruct((rows, features), BF),
        ],
        scratch_shapes=ScatterAll.scratch(rows, features, BF) if remote else [],
        compiler_params=pltpu.CompilerParams(
            vmem_limit_bytes=60 * 2**20,
            dimension_semantics=("arbitrary",),
            **({"collective_id": 4, "has_side_effects": True} if remote else {}),
        ),
        cost_estimate=pl.CostEstimate(
            flops=blocks * 2 * features * (capacity * PADDED_HALF + rows * 2 * capacity),
            bytes_accessed=blocks * features * 2 * (rows + capacity),
            transcendentals=0,
        ),
    )(back_parts, places, gates, hidden, sent, units, weight_out, shared_out)


def swap_halves(values):
    column = lax.broadcasted_iota(jnp.int32, values.shape, 1)
    return jnp.where(column % 64 < 32, pltpu.roll(values, 96, 1), pltpu.roll(values, 32, 1))


def turn(values, cosine, sine, sign):
    column = lax.broadcasted_iota(jnp.int32, values.shape, 1)
    signed = jnp.where(column % 64 < 32, -sign * sine, sign * sine)
    return values * cosine + swap_halves(values) * signed


def project_kernel(
    hidden_ref, gain_ref, query_ref, compress_ref, latent_gain_ref, expand_ref, cosine_ref, sine_ref,
    normed_out, query_out, key_out, value_out, latent_out, latent_normed_out
):
    entries = hidden_ref[...].astype(F32)
    normed = (entries * rms_scale(entries) * gain_ref[...]).astype(BF)
    normed_out[...] = normed
    cosine, sine = cosine_ref[...], sine_ref[...]
    query = dot(normed, query_ref[...])
    nope = query.shape[1] - 128
    query_out[:, :nope] = query[:, :nope].astype(BF)
    query_out[:, nope:] = turn(query[:, nope:], cosine, sine, 1.0).astype(BF)
    compressed = dot(normed, compress_ref[...])
    latent = compressed[:, :LATENT]
    latent_out[...] = latent
    latent_normed = (latent * rms_scale(latent) * latent_gain_ref[...]).astype(BF)
    latent_normed_out[...] = latent_normed
    rotary = compressed[:, LATENT:]
    rotary = jnp.concatenate([rotary, rotary], axis=1)
    expanded = dot(latent_normed, expand_ref[...]).astype(BF)
    key_out[:, :nope] = expanded[:, :nope]
    key_out[:, nope:] = turn(rotary, cosine, sine, 1.0).astype(BF)
    value_out[...] = expanded[:, nope:]


def project(hidden_all, first_gain, query_weight, compress_weight, latent_gain, expand_weight, cosine, sine):
    length, features = hidden_all.shape
    block = 256
    query_width = query_weight.shape[1]
    values = query_width - 128

    def tiled(columns):
        return pl.BlockSpec((block, columns), lambda j: (j, 0))

    def whole(array):
        return pl.BlockSpec(array.shape, lambda j: (0, 0), pipeline_mode=pl.Buffered(1))

    return pl.pallas_call(
        project_kernel,
        grid=(length // block,),
        in_specs=[
            tiled(features),
            whole(first_gain),
            whole(query_weight),
            whole(compress_weight),
            whole(latent_gain),
            whole(expand_weight),
            tiled(128),
            tiled(128),
        ],
        out_specs=[
            tiled(features), tiled(query_width), tiled(query_width), tiled(values), tiled(LATENT),
            tiled(LATENT),
        ],
        out_shape=[
            jax.ShapeDtypeStruct((length, features), BF),
            jax.ShapeDtypeStruct((length, query_width), BF),
            jax.ShapeDtypeStruct((length, query_width), BF),
            jax.ShapeDtypeStruct((length, values), BF),
            jax.ShapeDtypeStruct((length, LATENT), F32),
            jax.ShapeDtypeStruct((length, LATENT), BF),
        ],
        compiler_params=params(48),
        cost_estimate=pl.CostEstimate(
            flops=2 * length * features * (query_width + 640), bytes_accessed=2**25, transcendentals=0
        ),
    )(hidden_all, first_gain, query_weight, compress_weight, latent_gain, expand_weight, cosine, sine)


BLOCK = 512
SCALE = 1.0 / math.sqrt(QK)


def head_keys(key_ref, rotary_ref, part, head):
    rotary = rotary_ref[part]
    column = lax.broadcasted_iota(jnp.int32, rotary.shape, 1)
    rotary = jnp.where(column // 64 == head, rotary.astype(F32), 0.0).astype(BF)
    return jnp.concatenate([key_ref[part], rotary], axis=1)


def masked_scores(query, keys, block, j):
    scores = dot_nt(query, keys) * SCALE
    row = block * BLOCK + lax.broadcasted_iota(jnp.int32, scores.shape, 0)
    column = j * BLOCK + lax.broadcasted_iota(jnp.int32, scores.shape, 1)
    return jnp.where(column <= row, scores, -1e30)


def tile_of(j):
    return pl.ds(pl.multiple_of(j * BLOCK, BLOCK), BLOCK)


def attend_kernel(query_ref, turned_ref, key_ref, rotary_ref, value_ref, out_ref, log_ref, scores_ref):
    head, block = pl.program_id(0), pl.program_id(1)
    query = jnp.concatenate([query_ref[...], turned_ref[...]], axis=1)

    def score(j, largest):
        scores = masked_scores(query, head_keys(key_ref, rotary_ref, tile_of(j), head), block, j)
        scores_ref[j] = scores
        return jnp.maximum(largest, jnp.max(scores, axis=1, keepdims=True))

    largest = lax.fori_loop(0, block + 1, score, jnp.full((BLOCK, 1), -1e30, F32))

    def weigh(j, carry):
        total, found = carry
        weights = jnp.exp(scores_ref[j] - largest)
        total += jnp.sum(weights, axis=1, keepdims=True)
        return total, found + dot(weights.astype(BF), value_ref[tile_of(j)])

    total, found = lax.fori_loop(
        0, block + 1, weigh, (jnp.zeros((BLOCK, 1), F32), jnp.zeros((BLOCK, VDIM), F32))
    )
    out_ref[...] = (found / total).astype(BF)
    log_ref[0] = jnp.broadcast_to(largest + jnp.log(total), (BLOCK, 128))


def attention_specs(length, heads):
    return [
        pl.BlockSpec((BLOCK, 128), lambda h, b: (b, h)),
        pl.BlockSpec((BLOCK, 128), lambda h, b: (b, heads)),
        pl.BlockSpec((length, 128), lambda h, b: (0, h)),
        pl.BlockSpec((length, 128), lambda h, b: (0, heads)),
        pl.BlockSpec((length, VDIM), lambda h, b: (0, h)),
    ]


def attend(queries, keys, values):
    length = queries.shape[0]
    heads = values.shape[1] // VDIM
    blocks = length // BLOCK
    return pl.pallas_call(
        attend_kernel,
        grid=(heads, blocks),
        in_specs=attention_specs(length, heads),
        out_specs=[
            pl.BlockSpec((BLOCK, VDIM), lambda h, b: (b, h)),
            pl.BlockSpec((1, BLOCK, 128), lambda h, b: (h, b, 0)),
        ],
        out_shape=[
            jax.ShapeDtypeStruct((length, heads * VDIM), BF),
            jax.ShapeDtypeStruct((heads, length, 128), F32),
        ],
        scratch_shapes=[pltpu.VMEM((blocks, BLOCK, BLOCK), F32)],
        compiler_params=pltpu.CompilerParams(
            vmem_limit_bytes=40 * 2**20, dimension_semantics=("arbitrary", "arbitrary")
        ),
        cost_estimate=pl.CostEstimate(
            flops=heads * length * length * 384, bytes_accessed=2**23, transcendentals=0
        ),
    )(queries, queries, keys, keys, values)


BACK_EVENTS = (0, 1, 1, 2, 3, 4, 4, 5, 6, 6, 7, 7)


def attend_back_kernel(
    remote, query_ref, turned_ref, key_ref, rotary_ref, value_ref, upstream_ref, log_ref, cosine_ref,
    sine_ref, parts_ref, query_back, turned_back, key_back, rotary_back, value_back, sum_ref,
    shares_ref, slopes_ref, key_sum, value_sum, *scratch
):
    head, block = pl.program_id(0), pl.program_id(1)
    heads, blocks = pl.num_programs(0), pl.num_programs(1)
    step = head * blocks + block
    if remote:
        scatter = ScatterAll(parts_ref, *scratch)
        pl.when(step == 0)(scatter.begin)
    query = jnp.concatenate([query_ref[...], turned_ref[...]], axis=1)
    upstream = upstream_ref[...]
    log_row = log_ref[0][:, :1]

    @pl.when(block == 0)
    def _():
        key_sum[...] = jnp.zeros_like(key_sum)
        value_sum[...] = jnp.zeros_like(value_sum)

    def score(j, centre):
        scores = masked_scores(query, head_keys(key_ref, rotary_ref, tile_of(j), head), block, j)
        shares = jnp.exp(scores - log_row)
        slopes = dot_nt(upstream, value_ref[tile_of(j)])
        shares_ref[j] = shares
        slopes_ref[j] = slopes
        return centre + jnp.sum(shares * slopes, axis=1, keepdims=True)

    centre = lax.fori_loop(0, block + 1, score, jnp.zeros((BLOCK, 1), F32))

    def back(j, found):
        part = tile_of(j)
        shares = shares_ref[j]
        score_back = (shares * (slopes_ref[j] - centre)).astype(BF)
        value_sum[part] += dot_tn(shares.astype(BF), upstream)
        key_sum[part] += dot_tn(score_back, query)
        return found + dot(score_back, head_keys(key_ref, rotary_ref, part, head))

    found = lax.fori_loop(0, block + 1, back, jnp.zeros((BLOCK, 256), F32)) * SCALE
    query_back[...] = found[:, :128].astype(BF)
    turned = found[:, 128:].astype(BF).astype(F32)
    turned_back[...] = turn(turned, cosine_ref[...], sine_ref[...], -1.0).astype(BF)

    @pl.when(block == blocks - 1)
    def _():
        key_back[...] = (key_sum[:, :128] * SCALE).astype(BF)
        value_back[...] = value_sum[...].astype(BF)
        column = lax.broadcasted_iota(jnp.int32, rotary_back.shape, 1)
        rotary = jnp.where(column // 64 == head, key_sum[:, 128:] * SCALE, 0.0).astype(BF)
        rotary_back[...] = jnp.where(head == 0, rotary.astype(F32), rotary_back[...] + rotary.astype(F32))

    if remote:
        events = scatter.events()
        for at in sorted(set(BACK_EVENTS)):

            @pl.when(step == at)
            def _():
                for event, when in zip(events, BACK_EVENTS):
                    if when == at:
                        event()
                if at == BACK_EVENTS[-1]:
                    scatter.finish(sum_ref)


def attend_back(remote, queries, keys, values, upstream, logs, cosine, sine, parts):
    length = queries.shape[0]
    heads = values.shape[1] // VDIM
    blocks = length // BLOCK
    _, rows, features = parts.shape
    row = pl.BlockSpec((BLOCK, 128), lambda h, b: (b, 0))
    return pl.pallas_call(
        functools.partial(attend_back_kernel, remote),
        grid=(heads, blocks),
        in_specs=attention_specs(length, heads)
        + [
            pl.BlockSpec((BLOCK, VDIM), lambda h, b: (b, h)),
            pl.BlockSpec((1, BLOCK, 128), lambda h, b: (h, b, 0)),
            row,
            row,
            pl.BlockSpec(memory_space=pl.ANY),
        ],
        out_specs=[
            pl.BlockSpec((BLOCK, 128), lambda h, b: (b, h)),
            pl.BlockSpec((BLOCK, 128), lambda h, b: (b, h)),
            pl.BlockSpec((length, 128), lambda h, b: (0, h)),
            pl.BlockSpec((length, 128), lambda h, b: (0, 0)),
            pl.BlockSpec((length, VDIM), lambda h, b: (0, h)),
            pl.BlockSpec((rows, features), lambda h, b: (0, 0)),
        ],
        out_shape=[
            jax.ShapeDtypeStruct((length, heads * 128), BF),
            jax.ShapeDtypeStruct((length, heads * 128), BF),
            jax.ShapeDtypeStruct((length, heads * 128), BF),
            jax.ShapeDtypeStruct((length, 128), F32),
            jax.ShapeDtypeStruct((length, heads * VDIM), BF),
            jax.ShapeDtypeStruct((rows, features), BF),
        ],
        scratch_shapes=[
            pltpu.VMEM((blocks, BLOCK, BLOCK), F32),
            pltpu.VMEM((blocks, BLOCK, BLOCK), F32),
            pltpu.VMEM((length, 256), F32),
            pltpu.VMEM((length, VDIM), F32),
        ]
        + (ScatterAll.scratch(rows, features, BF) if remote else []),
        compiler_params=pltpu.CompilerParams(
            vmem_limit_bytes=62 * 2**20,
            dimension_semantics=("arbitrary", "arbitrary"),
            **({"collective_id": 8, "has_side_effects": True} if remote else {}),
        ),
        cost_estimate=pl.CostEstimate(
            flops=heads * length * length * 1024, bytes_accessed=2**26, transcendentals=0
        ),
    )(queries, queries, keys, keys, values, upstream, logs, cosine, sine, parts)


def partial_kernel(
    query_ref, turned_ref, key_ref, value_ref, rotary_ref, query_weight, expand_weight, out_ref
):
    nope = query_ref.shape[1]
    features = query_weight.shape[0]
    out_ref[:, :features] = (
        dot_nt(query_ref[...], query_weight[:, :nope])
        + dot_nt(turned_ref[...], query_weight[:, nope:])
    ).astype(BF)
    out_ref[:, features : features + LATENT] = (
        dot_nt(key_ref[...], expand_weight[:, :nope])
        + dot_nt(value_ref[...], expand_weight[:, nope:])
    ).astype(BF)
    rotary = rotary_ref[...]
    out_ref[:, features + LATENT :] = (rotary + pltpu.roll(rotary, ROPE, 1)).astype(BF)


def partial_terms(rows, query_back, turned_back, key_back, value_back, rotary_sum, query_weight, expand_weight):
    length = query_back.shape[0]
    columns = query_weight.shape[0] + LATENT + 128

    def tiled(array):
        return pl.BlockSpec((rows, array.shape[1]), lambda j: (j, 0))

    def whole(array):
        return pl.BlockSpec(array.shape, lambda j: (0, 0))

    given = (query_back, turned_back, key_back, value_back, rotary_sum)
    return pl.pallas_call(
        partial_kernel,
        grid=(length // rows,),
        in_specs=[tiled(x) for x in given] + [whole(query_weight), whole(expand_weight)],
        out_specs=pl.BlockSpec((rows, columns), lambda j: (j, 0)),
        out_shape=jax.ShapeDtypeStruct((length, columns), BF),
        compiler_params=params(40),
        cost_estimate=pl.CostEstimate(
            flops=2 * length * columns * 384, bytes_accessed=2**24, transcendentals=0
        ),
    )(*given, query_weight, expand_weight)


def tie_kernel(in_ref, _, out_ref):
    out_ref[...] = in_ref[...]


def tie(array, other):
    return pl.pallas_call(
        tie_kernel,
        in_specs=[pl.BlockSpec(memory_space=pltpu.VMEM), pl.BlockSpec(memory_space=pl.ANY)],
        out_specs=pl.BlockSpec(memory_space=pltpu.VMEM),
        out_shape=jax.ShapeDtypeStruct(array.shape, array.dtype),
        compiler_params=pltpu.CompilerParams(vmem_limit_bytes=16 * 2**20),
        cost_estimate=pl.CostEstimate(flops=0, bytes_accessed=4 * array.size, transcendentals=0),
    )(array, other)


def on_device(
    hidden_in,
    positions,
    expert_ids,
    gate_weights,
    attention_gain,
    w_query,
    w_compress,
    latent_gain,
    w_expand,
    w_output,
    feedforward_gain,
    w_shared_in,
    w_shared_out,
    w_expert_in,
    w_expert_out,
    cotangent,
):
    n_dp = lax.axis_size("dp")
    n_seq = lax.axis_size("seq")
    n_all = n_dp * n_seq
    fast = (n_dp, n_seq) == (4, 8)
    both = ("dp", "seq")
    dp_index = lax.axis_index("dp")
    seq_index = lax.axis_index("seq")
    sequence_count, rows, features = hidden_in.shape
    rows = sequence_count * rows
    length = rows * n_seq
    heads = HEADS // n_seq
    shard = features // n_dp
    expert_count = n_all // 2
    capacity = max(2, rows * TOP * 5 // (expert_count * 3))
    capacity = (capacity + 15) // 16 * 16
    units = SH_FF // n_all
    padded_units = (units + 127) // 128 * 128
    expand_width = heads * (NOPE + VDIM)

    hidden = hidden_in.reshape(rows, features)
    upstream_rows = cotangent.reshape(rows, features)
    upstream_float = upstream_rows.astype(F32)
    id_rows = expert_ids.reshape(rows, TOP)
    gate_table = gate_weights.reshape(rows, TOP)

    gains_own = jnp.concatenate([attention_gain, feedforward_gain, latent_gain])
    named_own = jnp.concatenate(
        [id_rows.T.astype(F32), gate_table.T, positions.reshape(1, rows).astype(F32)]
    )
    query_width = heads * NOPE + 128
    query_part = lax.dynamic_slice_in_dim(w_query, seq_index * heads * QK, heads * QK, 1)
    query_part = query_part.reshape(shard, heads, QK)
    query_part = jnp.concatenate(
        [
            query_part[..., :NOPE].reshape(shard, -1),
            query_part[..., NOPE:].reshape(shard, -1),
            jnp.zeros((shard, 128 - heads * ROPE), BF),
        ],
        axis=1,
    )
    expand_part = lax.dynamic_slice_in_dim(w_expand, seq_index * expand_width, expand_width, 1)
    expand_part = expand_part.reshape(-1, heads, NOPE + VDIM)
    expand_part = jnp.concatenate(
        [part.reshape(-1, heads * NOPE) for part in jnp.split(expand_part, 2, axis=-1)], axis=1
    )
    if fast:
        named_own = jnp.pad(named_own, ((0, 16 - named_own.shape[0]), (0, 0)))
        gains_size = gains_own.shape[0]
        gains_own = jnp.pad(gains_own, (0, 2048 - gains_size)).reshape(16, 128)
        (
            hidden_all, named_all, gains, query_weight, expand_weight, compress_weight,
            output_weight,
        ) = gather_start(
            hidden, named_own, gains_own, query_part, expand_part, w_compress, w_output, 1
        )
        gains = gains.reshape(n_dp, 2048)[:, :gains_size]
        dp_places = (dp_index - jnp.arange(n_dp)) % n_dp
        slot_of_seq = small_take([0, 1, 2, 4, 3, 5, 6, 7], seq_index ^ jnp.arange(n_seq))
        named_all = jnp.stack([named_all[k] for k in (0, 4, 1, 2, 5, 6, 3, 7)])
        positions_all = reorder(named_all[:, 0, 2 * TOP], slot_of_seq)
        named_all = named_all.swapaxes(0, 1).reshape(n_all, 16, rows)
    else:
        hidden_all = lax.all_gather(hidden, "seq", axis=0)
        named_all = lax.all_gather(named_own, both, axis=0)
        positions_all = lax.dynamic_slice_in_dim(named_all, dp_index * n_seq, n_seq, 0)[:, 2 * TOP]
        gains = lax.all_gather(gains_own, "dp", axis=0)
        query_weight = lax.all_gather(query_part, "dp", axis=0)
        expand_weight = lax.all_gather(expand_part, "dp", axis=0)
        compress_weight = lax.all_gather(w_compress, "dp", axis=0)
        output_weight = lax.all_gather(w_output, "dp", axis=0)
    hidden_all = hidden_all.reshape(length, features)
    query_weight = query_weight.reshape(features, query_width)
    expand_weight = expand_weight.reshape(LATENT, expand_width)
    compress_weight = compress_weight.reshape(features, LATENT + ROPE)
    gains = gains.astype(F32)
    first_gain = gains[:, :shard].reshape(features)
    second_gain = gains[:, shard : 2 * shard].reshape(features)
    latent_gain_row = gains[:, 2 * shard :].reshape(LATENT)
    output_weight = output_weight.reshape(HEADS * VDIM, features)
    shared_part = jnp.stack(
        [
            jnp.stack(
                [
                    lax.dynamic_slice_in_dim(
                        w_shared_in, half * SH_FF + (z * n_seq + seq_index) * units, units, 1
                    )
                    for half in range(2)
                ],
                axis=1,
            )
            for z in range(n_dp)
        ]
    )
    shared_in = lax.all_to_all(
        shared_part, "dp", split_axis=0, concat_axis=0, tiled=True
    ).reshape(features, 2, units)
    pad = padded_units - units
    shared_in = jnp.pad(shared_in, ((0, 0), (0, 0), (0, pad))).reshape(features, 2 * padded_units)
    shared_out = lax.dynamic_slice_in_dim(w_shared_out, seq_index * units, units, 0)
    shared_out = jnp.pad(shared_out, ((0, pad), (0, 0)))
    weight_in, weight_out = w_expert_in[0], w_expert_out[0]
    expert = (dp_index * n_seq + seq_index) // 2
    named = named_all[:, :TOP] == expert.astype(F32)
    chosen = jnp.any(named, axis=1)
    gate_rows = jnp.sum(jnp.where(named, named_all[:, TOP : 2 * TOP], 0.0), axis=1)[:, None]
    before = (jnp.arange(rows)[:, None] < jnp.arange(rows)[None, :]).astype(BF)
    place = dot(chosen.astype(BF), before).astype(jnp.int32)
    place = jnp.where(chosen, place, -1)[:, None]

    angles = rotary_angles(positions_all.reshape(length))
    angles = jnp.concatenate([angles] * 4, axis=1)
    cosine_all, sine_all = jnp.cos(angles), jnp.sin(angles)
    normed_all, queries, keys_all, values_all, latent, latent_normed = project(
        hidden_all, first_gain[None], query_weight, compress_weight, latent_gain_row[None],
        expand_weight, cosine_all, sine_all,
    )
    attended_heads, logs = attend(queries, keys_all, values_all)
    attended = lax.all_to_all(
        attended_heads, "seq", split_axis=0, concat_axis=1, tiled=True
    )
    hidden_float = hidden.astype(F32)
    middle = hidden_float + dot(attended, output_weight)
    second_scale = rms_scale(middle)
    moe_rows = (middle * second_scale * second_gain).astype(BF)

    sent = jnp.stack([moe_rows, upstream_rows])
    if not fast:
        sent = lax.all_gather(sent, both, axis=0)
    (
        sent_all, expert_in_grad, expert_out_grad, hidden_units, shared_units, back_parts,
        shared_in_grad, shared_out_grad,
    ) = experts(
        fast, capacity, sent, place, gate_rows, weight_in, weight_out, shared_in, shared_out
    )
    gate_grads, out_parts, moe_back = out_side(
        fast, capacity, back_parts, place, gate_rows, hidden_units, sent_all if fast else sent, shared_units,
        weight_out, shared_out,
    )
    if fast:
        gate_grads = reorder(gate_grads.reshape(n_dp, n_seq, rows), dp_places)
        gate_grads = reorder(gate_grads.swapaxes(0, 1), slot_of_seq).swapaxes(0, 1)
        gate_grads = gate_grads.reshape(n_all, 1, rows)
    else:
        moe_back = lax.psum_scatter(
            back_parts.reshape(n_all * rows, features), both, scatter_dimension=0, tiled=True
        )
    moe_back = moe_back.astype(F32)
    gate_grads = lax.all_to_all(gate_grads, both, split_axis=0, concat_axis=0, tiled=True)
    gate_grads = jnp.sum(gate_grads.reshape(expert_count, 2, rows), axis=1)
    gate_gradient = jnp.sum(
        jnp.where(
            id_rows[:, :, None] == jnp.arange(expert_count, dtype=jnp.int32),
            gate_grads.T[:, None, :],
            0.0,
        ),
        axis=-1,
    )
    second_gain_grad = jnp.sum(moe_back * middle * second_scale, axis=0)
    middle_back = upstream_float + norm_backward(moe_back, middle, second_scale, second_gain)
    middle_low = middle_back.astype(BF)
    attended_back = dot_nt(middle_low, output_weight).astype(BF)
    upstream_heads = lax.all_to_all(
        attended_back, "seq", split_axis=1, concat_axis=0, tiled=True
    )
    attended_all = lax.all_gather(tie(attended, middle_low), "seq", axis=0, tiled=True)
    middle_columns = lax.all_to_all(middle_low, "seq", split_axis=1, concat_axis=0, tiled=True)
    output_grad = dot_tn(attended_all, middle_columns)

    query_back, turned_back, key_back, rotary_sum, value_back, out_sum = attend_back(
        fast, queries, keys_all, values_all, upstream_heads, logs, cosine_all, sine_all, out_parts
    )
    if not fast:
        out_sum = lax.psum_scatter(
            out_parts.reshape(n_all * rows, features), both, scatter_dimension=0, tiled=True
        )
    block_out = (middle + out_sum.astype(F32)).astype(BF)
    turned_back = sum(turned_back[:, 128 * h : 128 * h + 128] for h in range(heads))
    query_raw_back = jnp.concatenate([query_back, turned_back], axis=1)
    expanded_back = jnp.concatenate([key_back, value_back], axis=1)
    partial_back = partial_terms(
        rows, query_back, turned_back, key_back, value_back, rotary_sum, query_weight, expand_weight
    )
    if fast:
        summed_back = plane_scatter(partial_back.reshape(n_seq, rows, -1), 5)
    else:
        summed_back = lax.psum_scatter(partial_back, "seq", scatter_dimension=0, tiled=True)
    summed_back = summed_back[:, : features + LATENT + ROPE].astype(F32)
    query_grad = dot_tn(normed_all, query_raw_back)
    expand_grad = dot_tn(latent_normed, expanded_back)
    latent_normed_back = summed_back[:, features : features + LATENT]
    own = seq_index * rows

    def mine(array):
        return lax.dynamic_slice_in_dim(array, own, rows, 0)

    latent_own = mine(latent)
    latent_scale_own = rms_scale(latent_own)
    latent_gain_grad = jnp.sum(latent_normed_back * latent_own * latent_scale_own, axis=0)
    latent_back = norm_backward(latent_normed_back, latent_own, latent_scale_own, latent_gain_row)
    half_turn = ROPE // 2
    rotary_back = rotate(
        summed_back[:, features + LATENT :],
        mine(cosine_all)[:, :half_turn],
        -mine(sine_all)[:, :half_turn],
    )
    compressed_back = jnp.concatenate([latent_back, rotary_back], axis=-1).astype(BF)
    width = (LATENT + ROPE) // n_seq
    if fast:
        compressed_back_all = plane_gather(jnp.pad(compressed_back, ((0, 0), (0, 64))), 6)
        compressed_back_all = compressed_back_all[:, :, : LATENT + ROPE]
    else:
        compressed_back_all = lax.all_gather(compressed_back, "seq", axis=0)
    compressed_back_all = compressed_back_all.reshape(length, LATENT + ROPE)
    compress_grad = dot_tn(
        normed_all, lax.dynamic_slice_in_dim(compressed_back_all, seq_index * width, width, 1)
    )
    normed_back = summed_back[:, :features] + dot_nt(compressed_back, compress_weight)
    first_scale = rms_scale(hidden_float)
    first_gain_grad = jnp.sum(normed_back * hidden_float * first_scale, axis=0)
    hidden_gradient = (
        middle_back + norm_backward(normed_back, hidden_float, first_scale, first_gain)
    ).astype(BF)

    gain_grads = jnp.concatenate([first_gain_grad, second_gain_grad, latent_gain_grad])
    bit = 1
    while bit < n_seq:
        gain_grads = gain_grads + lax.ppermute(
            gain_grads, "seq", [(i, i ^ bit) for i in range(n_seq)]
        )
        bit *= 2
    bit = 1
    while bit < n_dp:
        gain_grads = gain_grads + lax.ppermute(
            gain_grads, "dp", [(i, i ^ bit) for i in range(n_dp)]
        )
        bit *= 2
    latent_shard = LATENT // n_dp

    def gain_part(start, size):
        return lax.dynamic_slice_in_dim(gain_grads, start + dp_index * size, size, 0)

    widths = [query_width, expand_width * latent_shard // shard, features // n_seq, width]
    parts = jnp.concatenate(
        [
            query_grad.reshape(n_dp, shard, -1),
            expand_grad.reshape(n_dp, shard, -1),
            output_grad.reshape(n_dp, shard, -1),
            compress_grad.reshape(n_dp, shard, -1),
        ],
        axis=-1,
    )
    if fast:
        extra = -parts.shape[-1] % 128
        summed = sum_grads(jnp.pad(parts, ((0, 0), (0, 0), (0, extra))).astype(BF), 7)
    else:
        summed = lax.psum_scatter(parts, "dp", scatter_dimension=0)
        summed = lax.all_gather(summed.astype(BF), "seq", axis=0)

    def columns(start, size, height):
        found = summed[:, :, start : start + size].reshape(n_seq, height, -1)
        return found.transpose(1, 0, 2).reshape(height, -1).astype(F32)

    def in_heads(start, size, height, first, second):
        found = summed[:, :, start : start + size].reshape(n_seq, height, -1)
        cut = heads * first
        found = jnp.concatenate(
            [
                found[:, :, :cut].reshape(n_seq, height, heads, first),
                found[:, :, cut : cut + heads * second].reshape(n_seq, height, heads, second),
            ],
            axis=-1,
        )
        return found.transpose(1, 0, 2, 3).reshape(height, -1).astype(F32)

    starts = [sum(widths[:n]) for n in range(4)]
    shared_in_grad = shared_in_grad.reshape(2, padded_units, n_dp, shard)[:, :units].astype(BF)
    shared_in_out = lax.all_to_all(
        shared_in_grad.transpose(2, 3, 0, 1), "dp", split_axis=0, concat_axis=0, tiled=True
    )
    shared_in_out = lax.all_gather(shared_in_out, "seq", axis=0)
    shared_in_out = shared_in_out.transpose(2, 3, 1, 0, 4).reshape(shard, 2 * SH_FF).astype(F32)
    shared_out_out = lax.all_gather(
        shared_out_grad[:units].astype(BF), "seq", axis=0, tiled=True
    ).astype(F32)
    return (
        block_out.reshape(hidden_in.shape),
        hidden_gradient.reshape(hidden_in.shape),
        gate_gradient.reshape(gate_weights.shape),
        gain_part(0, shard),
        in_heads(starts[0], widths[0], shard, NOPE, ROPE),
        columns(starts[3], widths[3], shard),
        gain_part(2 * features, latent_shard),
        in_heads(starts[1], widths[1], latent_shard, NOPE, VDIM),
        columns(starts[2], widths[2], shard),
        gain_part(features, shard),
        shared_in_out,
        shared_out_out,
        expert_in_grad[None],
        expert_out_grad[None],
    )


def solution(mesh):
    token = P("dp", "seq", None)
    row = P("dp", None)
    half = P(("dp", "seq"), None, None)
    return jax.shard_map(
        on_device,
        mesh=mesh,
        in_specs=(
            token, P("dp", "seq"), token, token, P("dp"), row, row, P("dp"), row, row,
            P("dp"), row, row, half, half, token,
        ),
        out_specs=(
            token, token, token, P("dp"), row, row, P("dp"), row, row, P("dp"), row, row,
            half, half,
        ),
        check_vma=False,
    )
```

```python
import functools
import math

import jax
import jax.numpy as jnp
from jax import lax
from jax.experimental import pallas as pl
from jax.experimental.pallas import tpu as pltpu
from jax.sharding import PartitionSpec as P

HEADS = 16
NOPE = 128
ROPE = 64
VDIM = 128
LATENT = 512
TOP = 6
QK = 192
SH_FF = 2816
HALF = 704
EPSILON = 1e-06
BF = jnp.bfloat16
F32 = jnp.float32


def rms_scale(entries):
    return lax.rsqrt(jnp.mean(entries * entries, axis=-1, keepdims=True) + EPSILON)


def rotary_angles(position_rows):
    steps_index = jnp.arange(ROPE // 2, dtype=F32)
    frequency = 10000.0 ** (-2.0 * steps_index / ROPE)
    return position_rows.astype(F32)[..., None] * frequency


def rotate(values, cosine_values, sine_values):
    half_width = values.shape[-1] // 2
    front_half = values[..., :half_width]
    back_half = values[..., half_width:]
    return jnp.concatenate(
        [
            front_half * cosine_values - back_half * sine_values,
            front_half * sine_values + back_half * cosine_values,
        ],
        axis=-1,
    )


def norm_backward(upstream, entries, inverse_scale, gain_row):
    scaled = upstream * gain_row
    return inverse_scale * scaled - entries * inverse_scale**3 * jnp.mean(
        scaled * entries, axis=-1, keepdims=True
    )


def dot(a, b):
    return jnp.dot(a, b, preferred_element_type=F32)


def dot_nt(a, b):
    return jnp.einsum("ik,jk->ij", a, b, preferred_element_type=F32)


def dot_tn(a, b):
    return jnp.einsum("ki,kj->ij", a, b, preferred_element_type=F32)


def copy_kernel(places_ref, in_ref, out_ref):
    out_ref[...] = in_ref[...]


def reorder(stack, places):
    count = stack.shape[0]
    if stack.size * stack.dtype.itemsize < 2**20 or stack.ndim != 3:
        return jnp.stack(
            [lax.dynamic_index_in_dim(stack, places[j], 0, keepdims=False) for j in range(count)]
        )
    block = (1, *stack.shape[1:])
    return pl.pallas_call(
        copy_kernel,
        grid_spec=pltpu.PrefetchScalarGridSpec(
            num_scalar_prefetch=1,
            grid=(count,),
            in_specs=[pl.BlockSpec(block, lambda j, order: (order[j], 0, 0))],
            out_specs=pl.BlockSpec(block, lambda j, order: (j, 0, 0)),
        ),
        out_shape=jax.ShapeDtypeStruct(stack.shape, stack.dtype),
        compiler_params=params(40),
        cost_estimate=pl.CostEstimate(
            flops=0, bytes_accessed=2 * stack.size * stack.dtype.itemsize, transcendentals=0
        ),
    )(places.astype(jnp.int32), stack)


def small_take(table, index):
    table = jnp.array(table, jnp.int32)
    hit = index[:, None] == jnp.arange(table.shape[0])[None, :]
    return jnp.sum(jnp.where(hit, table[None, :], 0), axis=1)


def params(limit=60):
    return pltpu.CompilerParams(
        vmem_limit_bytes=limit * 2**20, dimension_semantics=("arbitrary",)
    )


MESH_ID = pl.DeviceIdType.MESH
OWN_SLOTS = (0, 2, 3, 6)
CORE_SLOTS = (1, 4, 5, 7)


def neighbours():
    dp = lax.axis_index("dp")
    seq = lax.axis_index("seq")
    core = {"dp": dp, "seq": seq + 1 - 2 * (seq % 2)}
    across_x = {"dp": dp, "seq": seq + 2 - 4 * ((seq // 2) % 2)}
    across_y = {"dp": dp, "seq": seq + 4 - 8 * (seq // 4)}
    following = {"dp": (dp + 1) % 4, "seq": seq}
    previous = {"dp": (dp + 3) % 4, "seq": seq}
    return core, across_x, across_y, following, previous


def greet(devices):
    barrier = pltpu.get_barrier_semaphore()
    for device in devices:
        pl.semaphore_signal(barrier, inc=1, device_id=device, device_id_type=MESH_ID)
    pl.semaphore_wait(barrier, len(devices))


class Courier:
    def __init__(self, send_sems, recv_sems):
        self.send_sems, self.recv_sems = send_sems, recv_sems
        self.sent, self.open = [], []

    def send(self, source, target, device):
        index = len(self.sent)
        copy = pltpu.make_async_remote_copy(
            src_ref=source,
            dst_ref=target,
            send_sem=self.send_sems.at[index],
            recv_sem=self.recv_sems.at[index],
            device_id=device,
            device_id_type=MESH_ID,
        )
        copy.start()
        self.sent.append(copy)
        self.open.append(copy)
        return copy

    def take(self, copy):
        copy.wait_recv()
        self.open = [other for other in self.open if other is not copy]

    def finish(self):
        for copy in list(self.open):
            self.take(copy)
        for copy in self.sent:
            copy.wait_send()


def accumulate(target, *sources):
    rows = target.shape[0]
    step = 16

    def body(k, carry):
        part = pl.ds(pl.multiple_of(k * step, step), step)
        total = target[part].astype(F32)
        for source in sources:
            total = total + source[part].astype(F32)
        target[part] = total.astype(target.dtype)
        return carry

    lax.fori_loop(0, rows // step, body, 0)


SCATTER_ORDER = (1, 2, 3, 0)


class ScatterAll:
    @staticmethod
    def scratch(rows, columns, dtype):
        return [
            pltpu.VMEM((4, 4, rows, columns), dtype),
            pltpu.VMEM((4, 2, rows // 2, columns), dtype),
            pltpu.VMEM((4, 2, rows, columns), dtype),
            pltpu.VMEM((3, rows, columns), dtype),
            pltpu.VMEM((4, rows, columns), dtype),
            pltpu.SemaphoreType.DMA((35,)),
            pltpu.SemaphoreType.DMA((35,)),
            pltpu.SemaphoreType.DMA((4,)),
        ]

    def __init__(self, in_ref, held, far, near, ring, stage, send_sems, recv_sems, local_sems):
        self.in_ref, self.held, self.far, self.near = in_ref, held, far, near
        self.ring, self.stage = ring, stage
        self.send_sems, self.recv_sems, self.local_sems = send_sems, recv_sems, local_sems
        self.core, self.across_x, self.across_y, self.following, self.previous = neighbours()
        rows = held.shape[2]
        self.top, self.bottom = pl.ds(0, rows // 2), pl.ds(rows // 2, rows // 2)

    def copy(self, index, source, target, device):
        return pltpu.make_async_remote_copy(
            src_ref=source,
            dst_ref=target,
            send_sem=self.send_sems.at[index],
            recv_sem=self.recv_sems.at[index],
            device_id=device,
            device_id_type=MESH_ID,
        )

    def to_core(self, i, k):
        source = self.in_ref.at[8 * i + CORE_SLOTS[k]]
        return self.copy(19 + 4 * i + k, source, self.held.at[i, k], self.core)

    def far_copy(self, i, which):
        part = self.bottom if which else self.top
        device = self.across_x if which else self.across_y
        return self.copy(2 * i + which, self.held.at[i, 3, part], self.far.at[i, which], device)

    def near_copy(self, i, which):
        device = self.across_y if which else self.across_x
        return self.copy(8 + 2 * i + which, self.held.at[i, 1 + which], self.near.at[i, which], device)

    def ring_copy(self, n):
        return self.copy(
            16 + n, self.held.at[SCATTER_ORDER[n], 0], self.ring.at[n], self.following
        )

    def loads(self, n):
        i = SCATTER_ORDER[n]
        return [
            pltpu.make_async_copy(
                self.in_ref.at[8 * i + OWN_SLOTS[k]], self.stage.at[k], self.local_sems.at[k]
            )
            for k in range(4)
        ]

    def begin(self, *others):
        greet((self.core, self.across_x, self.across_y, self.following, self.previous, *others))
        for i in SCATTER_ORDER:
            for k in (3, 1, 2, 0):
                self.to_core(i, k).start()
        for load in self.loads(0):
            load.start()

    def first(self, n):
        i = SCATTER_ORDER[n]
        loads = self.loads(n)
        later = self.loads(n + 1) if n < 3 else None
        for k in (3, 1, 2, 0):
            loads[k].wait()
            self.to_core(i, k).wait_recv()
            accumulate(self.held.at[i, k], self.stage.at[k])
            if later:
                later[k].start()
            if k == 3:
                self.far_copy(i, 0).start()
                self.far_copy(i, 1).start()

    def second(self, n):
        i = SCATTER_ORDER[n]
        self.far_copy(i, 0).wait_recv()
        accumulate(self.held.at[i, 1, self.top], self.far.at[i, 0])
        self.near_copy(i, 0).start()
        self.far_copy(i, 1).wait_recv()
        accumulate(self.held.at[i, 2, self.bottom], self.far.at[i, 1])
        self.near_copy(i, 1).start()

    def third(self, n):
        i = SCATTER_ORDER[n]
        self.near_copy(i, 0).wait_recv()
        self.near_copy(i, 1).wait_recv()
        sources = [self.near.at[i, 0], self.near.at[i, 1]]
        if n > 0:
            self.ring_copy(n - 1).wait_recv()
            sources.append(self.ring.at[n - 1])
        accumulate(self.held.at[i, 0], *sources)
        if n < 3:
            self.ring_copy(n).start()

    def events(self):
        first, second, third = self.first, self.second, self.third
        plan = [
            (first, 0), (first, 1), (second, 0), (first, 2), (second, 1), (third, 0), (first, 3),
            (second, 2), (third, 1), (second, 3), (third, 2), (third, 3),
        ]
        return [functools.partial(f, n) for f, n in plan]

    def finish(self, out_ref):
        out_ref[...] = self.held[0, 0]
        for i in range(4):
            for k in range(4):
                self.to_core(i, k).wait_send()
            for which in range(2):
                self.far_copy(i, which).wait_send()
                self.near_copy(i, which).wait_send()
        for n in range(3):
            self.ring_copy(n).wait_send()


def scatter_all_kernel(in_ref, out_ref, *scratch):
    scatter = ScatterAll(in_ref, *scratch)
    scatter.begin()
    for event in scatter.events():
        event()
    scatter.finish(out_ref)


def scatter_all(parts, collective_id):
    _, rows, columns = parts.shape
    return pl.pallas_call(
        scatter_all_kernel,
        out_shape=jax.ShapeDtypeStruct((rows, columns), parts.dtype),
        in_specs=[pl.BlockSpec(memory_space=pl.ANY)],
        out_specs=pl.BlockSpec(memory_space=pltpu.VMEM),
        scratch_shapes=ScatterAll.scratch(rows, columns, parts.dtype),
        compiler_params=pltpu.CompilerParams(
            collective_id=collective_id, has_side_effects=True, vmem_limit_bytes=56 * 2**20
        ),
        cost_estimate=pl.CostEstimate(
            flops=32 * rows * columns, bytes_accessed=64 * rows * columns * 2, transcendentals=0
        ),
    )(parts)


def spread(post, source, place, core, across_x, across_y):
    seq = lax.axis_index("seq")
    x_seq = seq + 2 - 4 * ((seq // 2) % 2)
    y_seq = seq + 4 - 8 * (seq // 4)
    xy_seq = x_seq + 4 - 8 * (seq // 4)
    x_copy = post.send(source, place(seq), across_x)
    y_copy = post.send(source, place(seq), across_y)
    post.send(source, place(seq), core)
    yield
    post.take(x_copy)
    far_top = post.send(place(x_seq, 0), place(x_seq, 0), across_y)
    post.send(place(x_seq), place(x_seq), core)
    post.take(y_copy)
    far_bottom = post.send(place(y_seq, 1), place(y_seq, 1), across_x)
    post.send(place(y_seq), place(y_seq), core)
    yield
    post.take(far_top)
    post.take(far_bottom)
    post.send(place(xy_seq), place(xy_seq), core)


def blocks_of(found):
    half = found.shape[1] // 2

    def place(index, part=None):
        if part is None:
            return found.at[index]
        return found.at[index, pl.ds(part * half, half)]

    return place


def advance(*spreads):
    for one in spreads:
        for _ in one:
            break


def gather_start_kernel(
    hidden, named, gains, query, expand, compress, output, hidden_all, named_all, gains_all,
    query_all, expand_all, compress_all, output_all, send_sems, recv_sems, local_sems
):
    dp = lax.axis_index("dp")
    seq = lax.axis_index("seq")
    core, across_x, across_y, following, previous = neighbours()
    greet((core, across_x, across_y, following, previous))
    post = Courier(send_sems, recv_sems)
    strip = output.shape[0] // 8
    own_strip = pl.ds(pl.multiple_of(seq * strip, strip), strip)
    core_half = compress.shape[0] // 2
    mine = pl.ds(pl.multiple_of((seq % 2) * core_half, core_half), core_half)
    hidden_spread = spread(post, hidden, blocks_of(hidden_all), core, across_x, across_y)
    advance(hidden_spread)

    def hop(i):
        at = (dp + 5 - i) % 4
        first = i == 1
        return [
            post.send(query if first else query_all.at[at], query_all.at[at], following),
            post.send(
                compress.at[mine] if first else compress_all.at[at, mine],
                compress_all.at[at, mine],
                following,
            ),
            post.send(expand if first else expand_all.at[at], expand_all.at[at], following),
            post.send(gains if first else gains_all.at[at], gains_all.at[at], following),
            post.send(named if first else named_all.at[0, i - 1], named_all.at[0, i], following),
            post.send(
                output.at[own_strip] if first else output_all.at[at, own_strip],
                output_all.at[at, own_strip],
                following,
            ),
        ]

    def strip_spread(at):
        def place(index, part=None):
            if part is None:
                where = pl.ds(pl.multiple_of(index * strip, strip), strip)
            else:
                half = strip // 2
                where = pl.ds(pl.multiple_of(index * strip + part * half, half), half)
            return output_all.at[at, where]

        return spread(post, place(seq), place, core, across_x, across_y)

    ring = hop(1)
    locals_ = [
        pltpu.make_async_copy(source, target, local_sems.at[n])
        for n, (source, target) in enumerate(
            (
                (hidden, hidden_all.at[seq]),
                (named, named_all.at[0, 0]),
                (gains, gains_all.at[dp]),
                (query, query_all.at[dp]),
                (expand, expand_all.at[dp]),
                (compress, compress_all.at[dp]),
                (output, output_all.at[dp]),
            )
        )
    ]
    for copy in locals_:
        copy.start()
    spreads = []
    for i in (2, 3, 4):
        for copy in ring:
            post.take(copy)
        at = (dp + 5 - i) % 4
        if i < 4:
            ring = hop(i)
        post.send(compress_all.at[at, mine], compress_all.at[at, mine], core)
        advance(*spreads)
        if i < 4:
            advance(hidden_spread)
        spreads.append(strip_spread(at))
        advance(spreads[-1])
    locals_[1].wait()
    names_x = post.send(named_all.at[0], named_all.at[1], across_x)
    advance(*spreads)
    post.take(names_x)
    names_y = post.send(named_all.at[pl.ds(0, 2)], named_all.at[pl.ds(2, 2)], across_y)
    advance(*spreads)
    post.take(names_y)
    post.send(named_all.at[pl.ds(0, 4)], named_all.at[pl.ds(4, 4)], core)
    for n, copy in enumerate(locals_):
        if n != 1:
            copy.wait()
    post.finish()


def gather_start(hidden, named, gains, query, expand, compress, output, collective_id):
    anywhere = pl.BlockSpec(memory_space=pl.ANY)
    total = 8 + 6 * 3 + 3 + 3 + 8 * 3
    return pl.pallas_call(
        gather_start_kernel,
        out_shape=[
            jax.ShapeDtypeStruct((8, *hidden.shape), hidden.dtype),
            jax.ShapeDtypeStruct((8, 4, *named.shape), named.dtype),
        ]
        + [jax.ShapeDtypeStruct((4, *x.shape), x.dtype) for x in (gains, query, expand, compress, output)],
        in_specs=[anywhere] * 7,
        out_specs=[anywhere] * 7,
        scratch_shapes=[
            pltpu.SemaphoreType.DMA((total,)),
            pltpu.SemaphoreType.DMA((total,)),
            pltpu.SemaphoreType.DMA((7,)),
        ],
        compiler_params=pltpu.CompilerParams(
            collective_id=collective_id, has_side_effects=True, vmem_limit_bytes=16 * 2**20
        ),
        cost_estimate=pl.CostEstimate(flops=0, bytes_accessed=2**26, transcendentals=0),
    )(hidden, named, gains, query, expand, compress, output)


PADDED_HALF = 768
TILE = 256


def flip(value, change):
    return value + change - 2 * value * change


def pair_of(step, remote):
    if not remote:
        return step
    first = 1 - (step + 15) // 16
    last = (step + 3) // 16
    turn_of, place = (step + 3) // 4 - 1, (step + 3) % 4
    ahead = 1 - (place + 3) // 4
    return (1 - first) * (1 - last) * (4 * turn_of + place + 4 * ahead) + last * step


def experts_kernel(
    remote, capacity, rows_in, place_ref, gate_ref, weight_in_ref, weight_out_ref, shared_in,
    shared_out, rows_all, in_grad_ref, out_grad_ref, hidden_out, units_ref, part_ref,
    shared_in_grad, shared_out_grad, rows_buffer, cot_buffer, weight_in, weight_up, weight_out,
    slot_rows_pair, slot_up_pair, hidden_pair, back_pair, in_grad, out_grad, rows_out, load_sems,
    weight_sems, *sems
):
    step = pl.program_id(0)
    steps = pl.num_programs(0)
    rows = place_ref.shape[2]
    features = weight_in.shape[0]
    pair = pair_of(step, remote)
    slot = step % 2
    half_slots = 2 * capacity
    now = pl.ds(pl.multiple_of(slot * half_slots, half_slots), half_slots)
    slot_rows, slot_up = slot_rows_pair.at[now], slot_up_pair.at[now]
    hidden_ref, back_ref = hidden_pair.at[now], back_pair.at[now]
    gathered = rows_all if remote else rows_in

    def loads(at, into):
        found = []
        for b in range(2):
            block = 2 * pair_of(at, remote) + b
            part = pl.ds(b * rows, rows)
            for kind, buffer in enumerate((rows_buffer, cot_buffer)):
                found.append(
                    pltpu.make_async_copy(
                        gathered.at[block, kind],
                        buffer.at[into, part],
                        load_sems.at[into, 2 * b + kind],
                    )
                )
        return found

    if remote:
        send_sems, recv_sems, own_sem = sems
        core, across_x, across_y, following, previous = neighbours()
        half = rows // 2
        top, bottom = pl.ds(0, half), pl.ds(half, half)

        def copy(index, source, target, device):
            return pltpu.make_async_remote_copy(
                src_ref=source,
                dst_ref=target,
                send_sem=send_sems.at[index],
                recv_sem=recv_sems.at[index],
                device_id=device,
                device_id_type=MESH_ID,
            )

        def block_of(i):
            return rows_in if i == 0 else rows_all.at[8 * i]

        def along(i):
            return copy(9 * i, block_of(i), rows_all.at[8 * i + 8], following)

        def by_x(i):
            return copy(9 * i + 1, block_of(i), rows_all.at[8 * i + 2], across_x)

        def by_y(i):
            return copy(9 * i + 2, block_of(i), rows_all.at[8 * i + 3], across_y)

        def far(i, which):
            if which == 0:
                return copy(
                    9 * i + 3, rows_all.at[8 * i + 2, :, top], rows_all.at[8 * i + 6, :, top], across_y
                )
            return copy(
                9 * i + 4, rows_all.at[8 * i + 3, :, bottom], rows_all.at[8 * i + 6, :, bottom], across_x
            )

        def to_core(i, k):
            source = block_of(i) if k == 0 else rows_all.at[8 * i + OWN_SLOTS[k]]
            return copy(9 * i + 5 + k, source, rows_all.at[8 * i + CORE_SLOTS[k]], core)

        def begin_plane(i):
            by_x(i).start()
            by_y(i).start()

        def plane_arrived(i):
            by_x(i).wait_recv()
            far(i, 0).start()
            to_core(i, 1).start()
            by_y(i).wait_recv()
            far(i, 1).start()
            to_core(i, 2).start()

        def far_arrived(i):
            far(i, 0).wait_recv()
            far(i, 1).wait_recv()
            to_core(i, 3).start()

        def along_arrived(i):
            along(i).wait_recv()
            if i < 2:
                along(i + 1).start()
            to_core(i + 1, 0).start()

        def core_arrived(i, *which):
            for k in which:
                to_core(i, k).wait_recv()

        ready = {
            0: [(core_arrived, 0, 0)],
            1: [(along_arrived, 0), (plane_arrived, 0), (core_arrived, 1, 0)],
            2: [(begin_plane, 1)],
            3: [(core_arrived, 0, 1, 2), (far_arrived, 0)],
            4: [(core_arrived, 0, 3), (along_arrived, 1)],
            5: [(core_arrived, 2, 0), (plane_arrived, 1)],
            6: [(begin_plane, 2)],
            7: [(core_arrived, 1, 1, 2), (far_arrived, 1), (along_arrived, 2)],
            8: [(core_arrived, 1, 3)],
            9: [(core_arrived, 3, 0), (plane_arrived, 2)],
            10: [(begin_plane, 3)],
            11: [(core_arrived, 2, 1, 2), (far_arrived, 2)],
            12: [(core_arrived, 2, 3)],
            13: [(plane_arrived, 3)],
            14: [(core_arrived, 3, 1, 2)],
            15: [(far_arrived, 3), (core_arrived, 3, 3)],
        }

        def prepare(at):
            for event, *given in ready[at]:
                event(*given)

        @pl.when(step == 0)
        def _():
            greet((core, across_x, across_y, following, previous))
            own = pltpu.make_async_copy(rows_in, rows_all.at[0], own_sem)
            own.start()
            along(0).start()
            begin_plane(0)
            to_core(0, 0).start()
            own.wait()

    @pl.when(step == 0)
    def _():
        weights = (
            pltpu.make_async_copy(weight_in_ref, weight_in, weight_sems.at[0]),
            pltpu.make_async_copy(weight_out_ref, weight_out.at[pl.ds(0, HALF)], weight_sems.at[1]),
        )
        for copy_in in weights:
            copy_in.start()
        in_grad[...] = jnp.zeros_like(in_grad)
        out_grad[...] = jnp.zeros_like(out_grad)
        shared_in_grad[...] = jnp.zeros_like(shared_in_grad)
        shared_out_grad[...] = jnp.zeros_like(shared_out_grad)
        weight_out[pl.ds(HALF, PADDED_HALF - HALF)] = jnp.zeros(
            (PADDED_HALF - HALF, features), BF
        )
        for copy_in in weights:
            copy_in.wait()

        def split(k, carry):
            part = pl.ds(pl.multiple_of(k * 128, 128), 128)
            up = weight_in[part, HALF:].astype(F32)
            up = jnp.concatenate([up, jnp.zeros((128, PADDED_HALF - HALF), F32)], axis=1)
            weight_up[part] = up.astype(BF)
            return carry

        lax.fori_loop(0, features // 128, split, 0)
        if remote:
            prepare(0)
        for load in loads(0, 0):
            load.start()

    for load in loads(step, slot):
        load.wait()

    picks = []
    for b in range(2):
        chosen = one_hot(place_ref, 2 * pair + b, capacity)
        pick = chosen.astype(F32)
        picks.append(pick.T.astype(BF))
        pick = pick.astype(BF)
        gates = jnp.sum(jnp.where(chosen, gate_ref[2 * pair + b], 0.0), axis=1, keepdims=True)
        part = pl.ds(b * rows, rows)
        slots = pl.ds(b * capacity, capacity)
        slot_rows[slots] = dot(pick, rows_buffer[slot, part]).astype(BF)
        slot_up[slots] = (dot(pick, cot_buffer[slot, part]) * gates).astype(BF)

    def gated(gate, up, hidden_back):
        sigmoid = 1.0 / (1.0 + jnp.exp(-gate))
        active = gate * sigmoid
        gate_back = hidden_back * up * sigmoid * (1.0 + gate * (1.0 - sigmoid))
        return (active * up).astype(BF), gate_back.astype(BF), (hidden_back * active).astype(BF)

    def hidden_tile(t, carry):
        part = pl.ds(pl.multiple_of(t * TILE, TILE), TILE)
        second = pl.ds(pl.multiple_of(PADDED_HALF + t * TILE, TILE), TILE)
        gate = dot(slot_rows[...], weight_in[:, part])
        up = dot(slot_rows[...], weight_up[:, part])
        hidden_back = dot_nt(slot_up[...], weight_out[part])
        hidden_ref[:, part], back_ref[:, part], back_ref[:, second] = gated(gate, up, hidden_back)
        return carry

    lax.fori_loop(0, PADDED_HALF // TILE, hidden_tile, 0)
    hidden_out[...] = hidden_ref[...]

    width = shared_out.shape[0]
    rows_pair, cot_pair = rows_buffer[slot], cot_buffer[slot]
    gate_up = dot(rows_pair, shared_in[...])
    hidden_back = dot_nt(cot_pair, shared_out[...])
    units, gate_back, up_back = gated(gate_up[:, :width], gate_up[:, width:], hidden_back)
    units_ref[...] = units
    shared_back = jnp.concatenate([gate_back, up_back], axis=1)
    shared_in_grad[...] += dot_tn(shared_back, rows_pair)
    shared_out_grad[...] += dot_tn(units, cot_pair)

    if remote:
        for at in range(1, 16):

            @pl.when(step + 1 == at)
            def _():
                prepare(at)

    @pl.when(step + 1 < steps)
    def _():
        for load in loads(step + 1, 1 - slot):
            load.start()

    def back_tile(t, carry):
        part = pl.ds(pl.multiple_of(t * 2 * TILE, 2 * TILE), 2 * TILE)
        slot_back = dot_nt(back_ref[:, :PADDED_HALF], weight_in[part, :PADDED_HALF])
        slot_back = (slot_back + dot_nt(back_ref[:, PADDED_HALF:], weight_up[part])).astype(BF)
        shared_part = dot_nt(shared_back, shared_in[part])
        for b in range(2):
            tokens = slice(b * rows, (b + 1) * rows)
            total = dot(picks[b], slot_back[b * capacity : (b + 1) * capacity])
            part_ref[b, :, part] = (total + shared_part[tokens]).astype(BF)
        return carry

    lax.fori_loop(0, features // (2 * TILE), back_tile, 0)

    @pl.when(slot == 1)
    def _():
        def in_tile(t, carry):
            part = pl.ds(pl.multiple_of(t * TILE, TILE), TILE)
            in_grad[part] += dot_tn(slot_rows_pair[:, part], back_pair[...])
            return carry

        lax.fori_loop(0, features // TILE, in_tile, 0)

        def out_tile(t, carry):
            part = pl.ds(pl.multiple_of(t * TILE, TILE), TILE)
            out_grad[part] += dot_tn(hidden_pair[:, part], slot_up_pair[...])
            return carry

        lax.fori_loop(0, PADDED_HALF // TILE, out_tile, 0)

    @pl.when(step + 1 == steps)
    def _():
        whole_out = pltpu.make_async_copy(
            out_grad.at[pl.ds(0, HALF)], out_grad_ref, weight_sems.at[0]
        )
        whole_out.start()
        height = rows_out.shape[1]

        def out_copy(k):
            part = pl.ds(pl.multiple_of(k * height, height), height)
            return pltpu.make_async_copy(
                rows_out.at[k % 2], in_grad_ref.at[part], load_sems.at[k % 2, 0]
            )

        def write(k, carry):
            @pl.when(k >= 2)
            def _():
                out_copy(k - 2).wait()

            part = pl.ds(pl.multiple_of(k * height, height), height)
            rows_out[k % 2] = jnp.concatenate(
                [in_grad[part, :HALF], in_grad[part, PADDED_HALF : PADDED_HALF + HALF]], axis=1
            )
            out_copy(k).start()
            return carry

        count = features // height
        lax.fori_loop(0, count, write, 0)
        out_copy(count - 2).wait()
        out_copy(count - 1).wait()
        whole_out.wait()

    if remote:

        @pl.when(step + 1 == steps)
        def _():
            for i in range(4):
                if i < 3:
                    along(i).wait_send()
                by_x(i).wait_send()
                by_y(i).wait_send()
                far(i, 0).wait_send()
                far(i, 1).wait_send()
                for k in range(4):
                    to_core(i, k).wait_send()


def one_hot(place_ref, block, capacity):
    place = place_ref[block]
    rows = place.shape[1]
    return lax.broadcasted_iota(jnp.int32, (capacity, rows), 0) == place


def experts(
    remote, capacity, rows_in, places, gates, weight_in, weight_out, shared_in, shared_out
):
    blocks, _, rows = places.shape
    features = weight_in.shape[0]
    width = shared_out.shape[0]
    steps = blocks // 2

    def whole(array):
        return pl.BlockSpec(
            array.shape, lambda j: (0,) * array.ndim, pipeline_mode=pl.Buffered(1)
        )

    def tiled(height, columns):
        return pl.BlockSpec((height, columns), lambda j: (pair_of(j, remote), 0))

    anywhere = pl.BlockSpec(memory_space=pl.ANY)
    slots = 2 * capacity
    scratch = [
        pltpu.VMEM((2, 2 * rows, features), BF),
        pltpu.VMEM((2, 2 * rows, features), BF),
        pltpu.VMEM(weight_in.shape, BF),
        pltpu.VMEM((features, PADDED_HALF), BF),
        pltpu.VMEM((PADDED_HALF, features), BF),
        pltpu.VMEM((2 * slots, features), BF),
        pltpu.VMEM((2 * slots, features), BF),
        pltpu.VMEM((2 * slots, PADDED_HALF), BF),
        pltpu.VMEM((2 * slots, 2 * PADDED_HALF), BF),
        pltpu.VMEM((features, 2 * PADDED_HALF), F32),
        pltpu.VMEM((PADDED_HALF, features), F32),
        pltpu.VMEM((2, 64, 2 * HALF), F32),
        pltpu.SemaphoreType.DMA((2, 4)),
        pltpu.SemaphoreType.DMA((2,)),
    ]
    if remote:
        scratch += [
            pltpu.SemaphoreType.DMA((36,)),
            pltpu.SemaphoreType.DMA((36,)),
            pltpu.SemaphoreType.DMA,
        ]
    found = pl.pallas_call(
        functools.partial(experts_kernel, remote, capacity),
        grid=(steps,),
        in_specs=[anywhere, whole(places), whole(gates), anywhere, anywhere]
        + [whole(x) for x in (shared_in, shared_out)],
        out_specs=[
            anywhere,
            anywhere,
            anywhere,
            tiled(slots, PADDED_HALF),
            tiled(2 * rows, width),
            pl.BlockSpec((2, rows, features), lambda j: (pair_of(j, remote), 0, 0)),
            pl.BlockSpec(
                (2 * width, features), lambda j: (0, 0), pipeline_mode=pl.Buffered(1)
            ),
            pl.BlockSpec((width, features), lambda j: (0, 0), pipeline_mode=pl.Buffered(1)),
        ],
        out_shape=[
            jax.ShapeDtypeStruct((blocks if remote else 1, 2, rows, features), BF),
            jax.ShapeDtypeStruct(weight_in.shape, F32),
            jax.ShapeDtypeStruct(weight_out.shape, F32),
            jax.ShapeDtypeStruct((steps * slots, PADDED_HALF), BF),
            jax.ShapeDtypeStruct((blocks * rows, width), BF),
            jax.ShapeDtypeStruct((blocks, rows, features), BF),
            jax.ShapeDtypeStruct((2 * width, features), F32),
            jax.ShapeDtypeStruct((width, features), F32),
        ],
        scratch_shapes=scratch,
        compiler_params=pltpu.CompilerParams(
            vmem_limit_bytes=63 * 2**20,
            dimension_semantics=("arbitrary",),
            **({"collective_id": 3, "has_side_effects": True} if remote else {}),
        ),
        cost_estimate=pl.CostEstimate(
            flops=steps * slots * features * 2 * 3 * 2 * PADDED_HALF,
            bytes_accessed=blocks * features * 8 * rows,
            transcendentals=0,
        ),
    )(rows_in, places, gates, weight_in, weight_out, shared_in, shared_out)
    return found


def plane_scatter_kernel(
    in_ref, out_ref, held, far, near, stage, send_sems, recv_sems, local_sems
):
    core, across_x, across_y, _, _ = neighbours()
    greet((core, across_x, across_y))
    seq = lax.axis_index("seq")
    rows = out_ref.shape[0]
    top, bottom = pl.ds(0, rows // 2), pl.ds(rows // 2, rows // 2)
    post = Courier(send_sems, recv_sems)
    x_seq = seq + 2 - 4 * ((seq // 2) % 2)
    y_seq = seq + 4 - 8 * (seq // 4)
    xy_seq = x_seq + 4 - 8 * (seq // 4)
    core_step = 1 - 2 * (seq % 2)
    loads, arriving = {}, {}
    for k, place in ((3, xy_seq), (1, x_seq), (2, y_seq), (0, seq)):
        arriving[k] = post.send(in_ref.at[place + core_step], held.at[k], core)
        loads[k] = pltpu.make_async_copy(in_ref.at[place], stage.at[k], local_sems.at[k])
        loads[k].start()

    def join(k):
        loads[k].wait()
        post.take(arriving[k])
        accumulate(held.at[k], stage.at[k])

    join(3)
    far_top = post.send(held.at[3, top], far.at[0], across_y)
    far_bottom = post.send(held.at[3, bottom], far.at[1], across_x)
    join(1)
    x_bottom = post.send(held.at[1, bottom], near.at[0, bottom], across_x)
    join(2)
    y_top = post.send(held.at[2, top], near.at[1, top], across_y)
    join(0)
    post.take(far_top)
    accumulate(held.at[1, top], far.at[0])
    x_top = post.send(held.at[1, top], near.at[0, top], across_x)
    post.take(far_bottom)
    accumulate(held.at[2, bottom], far.at[1])
    y_bottom = post.send(held.at[2, bottom], near.at[1, bottom], across_y)
    for copy in (x_bottom, y_top, x_top, y_bottom):
        post.take(copy)
    accumulate(held.at[0], near.at[0], near.at[1])
    out_ref[...] = held[0]
    post.finish()


def plane_scatter(parts, collective_id):
    _, rows, columns = parts.shape
    return pl.pallas_call(
        plane_scatter_kernel,
        out_shape=jax.ShapeDtypeStruct((rows, columns), parts.dtype),
        in_specs=[pl.BlockSpec(memory_space=pl.ANY)],
        out_specs=pl.BlockSpec(memory_space=pltpu.VMEM),
        scratch_shapes=[
            pltpu.VMEM((4, rows, columns), parts.dtype),
            pltpu.VMEM((2, rows // 2, columns), parts.dtype),
            pltpu.VMEM((2, rows, columns), parts.dtype),
            pltpu.VMEM((4, rows, columns), parts.dtype),
            pltpu.SemaphoreType.DMA((10,)),
            pltpu.SemaphoreType.DMA((10,)),
            pltpu.SemaphoreType.DMA((4,)),
        ],
        compiler_params=pltpu.CompilerParams(
            collective_id=collective_id, has_side_effects=True, vmem_limit_bytes=32 * 2**20
        ),
        cost_estimate=pl.CostEstimate(
            flops=8 * rows * columns, bytes_accessed=16 * rows * columns, transcendentals=0
        ),
    )(parts)


def plane_gather_kernel(in_ref, out_ref, send_sems, recv_sems, local_sem):
    core, across_x, across_y, _, _ = neighbours()
    greet((core, across_x, across_y))
    own = pltpu.make_async_copy(in_ref, out_ref.at[lax.axis_index("seq")], local_sem)
    own.start()
    post = Courier(send_sems, recv_sems)
    for _ in spread(post, in_ref, blocks_of(out_ref), core, across_x, across_y):
        pass
    own.wait()
    post.finish()


def plane_gather(block, collective_id):
    anywhere = pl.BlockSpec(memory_space=pl.ANY)
    return pl.pallas_call(
        plane_gather_kernel,
        out_shape=jax.ShapeDtypeStruct((8, *block.shape), block.dtype),
        in_specs=[anywhere],
        out_specs=anywhere,
        scratch_shapes=[
            pltpu.SemaphoreType.DMA((8,)),
            pltpu.SemaphoreType.DMA((8,)),
            pltpu.SemaphoreType.DMA,
        ],
        compiler_params=pltpu.CompilerParams(
            collective_id=collective_id, has_side_effects=True, vmem_limit_bytes=16 * 2**20
        ),
        cost_estimate=pl.CostEstimate(
            flops=0, bytes_accessed=32 * block.size, transcendentals=0
        ),
    )(block)


def grads_kernel(in_ref, out_ref, total, ring, send_sems, recv_sems, local_sems):
    dp = lax.axis_index("dp")
    core, across_x, across_y, following, previous = neighbours()
    greet((core, across_x, across_y, following, previous))
    post = Courier(send_sems, recv_sems)
    loads = []
    for n, i in enumerate((1, 2, 3, 0)):
        load = pltpu.make_async_copy(in_ref.at[(dp + 4 - i) % 4], total.at[n], local_sems.at[n])
        load.start()
        loads.append(load)
    loads[0].wait()
    before = post.send(total.at[0], ring.at[0], following)
    for n in (1, 2, 3):
        loads[n].wait()
        post.take(before)
        accumulate(total.at[n], ring.at[n - 1])
        if n < 3:
            before = post.send(total.at[n], ring.at[n], following)
    own = pltpu.make_async_copy(total.at[3], out_ref.at[lax.axis_index("seq")], local_sems.at[0])
    own.start()
    for _ in spread(post, total.at[3], blocks_of(out_ref), core, across_x, across_y):
        pass
    own.wait()
    post.finish()


def sum_grads(parts, collective_id):
    _, rows, columns = parts.shape
    anywhere = pl.BlockSpec(memory_space=pl.ANY)
    return pl.pallas_call(
        grads_kernel,
        out_shape=jax.ShapeDtypeStruct((8, rows, columns), parts.dtype),
        in_specs=[anywhere],
        out_specs=anywhere,
        scratch_shapes=[
            pltpu.VMEM((4, rows, columns), parts.dtype),
            pltpu.VMEM((3, rows, columns), parts.dtype),
            pltpu.SemaphoreType.DMA((11,)),
            pltpu.SemaphoreType.DMA((11,)),
            pltpu.SemaphoreType.DMA((4,)),
        ],
        compiler_params=pltpu.CompilerParams(
            collective_id=collective_id, has_side_effects=True, vmem_limit_bytes=32 * 2**20
        ),
        cost_estimate=pl.CostEstimate(
            flops=0, bytes_accessed=32 * rows * columns, transcendentals=0
        ),
    )(parts)


OUT_EVENTS = (3, 5, 7, 9, 13, 17, 18, 23, 27, 30, 31, 31)


def out_terms(capacity, place_ref, gate_ref, hidden_ref, cot_ref, units_ref, weight_ref, shared_ref,
              gate_grad_ref, part_ref):
    features = part_ref.shape[2]
    chosen = one_hot(place_ref, 0, capacity)
    pick = chosen.astype(F32)
    pick, spread_pick = pick.astype(BF), pick.T.astype(BF)
    gates = jnp.sum(jnp.where(chosen, gate_ref[0], 0.0), axis=1, keepdims=True)

    def tile(t, slot_grad):
        part = pl.ds(pl.multiple_of(t * 2 * TILE, 2 * TILE), 2 * TILE)
        result = dot(hidden_ref[:, :HALF], weight_ref[:, part]).astype(BF).astype(F32)
        slot_grad += jnp.sum(result * dot(pick, cot_ref[0, 0, :, part]), axis=1, keepdims=True)
        total = dot(spread_pick, (result * gates).astype(BF)) + dot(units_ref[...], shared_ref[:, part])
        part_ref[0, :, part] = total.astype(BF)
        return slot_grad

    slot_grad = lax.fori_loop(0, features // (2 * TILE), tile, jnp.zeros((capacity, 1), F32))
    gate_grad_ref[0] = jnp.sum(jnp.where(chosen, slot_grad, 0.0), axis=0, keepdims=True)


def out_kernel(remote, capacity, back_ref, shared_ref, *refs):
    step = pl.program_id(0)
    terms, sum_ref, dealt_ref, scratch = refs[:9], refs[9], refs[10], refs[11:]
    if remote:
        *scratch, send_sems, recv_sems, own_sem = scratch
        scatter = ScatterAll(back_ref, *scratch)
        dp = lax.axis_index("dp")
        seq = lax.axis_index("seq")
        own = pltpu.make_async_copy(shared_ref.at[dp], dealt_ref.at[dp], own_sem)

        def deal(r):
            at = (dp + r) % 4
            return pltpu.make_async_remote_copy(
                src_ref=shared_ref.at[at],
                dst_ref=dealt_ref.at[dp],
                send_sem=send_sems.at[r - 1],
                recv_sem=recv_sems.at[r - 1],
                device_id={"dp": at, "seq": seq},
                device_id_type=MESH_ID,
            )

        @pl.when(step == 0)
        def _():
            scatter.begin({"dp": (dp + 2) % 4, "seq": seq})
            own.start()
            for r in range(1, 4):
                deal(r).start()

    out_terms(capacity, *terms)
    if remote:
        events = scatter.events()
        for at in sorted(set(OUT_EVENTS)):

            @pl.when(step == at)
            def _():
                for event, when in zip(events, OUT_EVENTS):
                    if when == at:
                        event()
                if at == OUT_EVENTS[-1]:
                    scatter.finish(sum_ref)
                    own.wait()
                    for r in range(1, 4):
                        deal(r).wait()


def out_side(remote, capacity, back_parts, shared_grad, places, gates, hidden, sent, units, weight_out, shared_out):
    blocks, _, rows = places.shape
    features = sent.shape[-1]
    one = pl.BlockSpec((1, 1, rows), lambda j: (j, 0, 0))

    def tiled(height, columns):
        return pl.BlockSpec((height, columns), lambda j: (j, 0))

    def whole(array):
        return pl.BlockSpec(array.shape, lambda j: (0, 0), pipeline_mode=pl.Buffered(1))

    return pl.pallas_call(
        functools.partial(out_kernel, remote, capacity),
        grid=(blocks,),
        in_specs=[
            pl.BlockSpec(memory_space=pl.ANY),
            pl.BlockSpec(memory_space=pl.ANY),
            one,
            one,
            tiled(capacity, PADDED_HALF),
            pl.BlockSpec((1, 1, rows, features), lambda j: (j, 1, 0, 0)),
            tiled(rows, units.shape[1]),
            whole(weight_out),
            whole(shared_out),
        ],
        out_specs=[
            one,
            pl.BlockSpec((1, rows, features), lambda j: (j, 0, 0)),
            pl.BlockSpec((rows, features), lambda j: (0, 0)),
            pl.BlockSpec(memory_space=pl.ANY),
        ],
        out_shape=[
            jax.ShapeDtypeStruct((blocks, 1, rows), F32),
            jax.ShapeDtypeStruct((blocks, rows, features), BF),
            jax.ShapeDtypeStruct((rows, features), BF),
            jax.ShapeDtypeStruct(shared_grad.shape, BF),
        ],
        scratch_shapes=ScatterAll.scratch(rows, features, BF)
        + [
            pltpu.SemaphoreType.DMA((3,)),
            pltpu.SemaphoreType.DMA((3,)),
            pltpu.SemaphoreType.DMA,
        ]
        if remote
        else [],
        compiler_params=pltpu.CompilerParams(
            vmem_limit_bytes=60 * 2**20,
            dimension_semantics=("arbitrary",),
            **({"collective_id": 4, "has_side_effects": True} if remote else {}),
        ),
        cost_estimate=pl.CostEstimate(
            flops=blocks * 2 * features * (capacity * PADDED_HALF + rows * 2 * capacity),
            bytes_accessed=blocks * features * 2 * (rows + capacity),
            transcendentals=0,
        ),
    )(back_parts, shared_grad, places, gates, hidden, sent, units, weight_out, shared_out)


def swap_halves(values):
    column = lax.broadcasted_iota(jnp.int32, values.shape, 1)
    return jnp.where(column % 64 < 32, pltpu.roll(values, 96, 1), pltpu.roll(values, 32, 1))


def turn(values, cosine, sine, sign):
    column = lax.broadcasted_iota(jnp.int32, values.shape, 1)
    signed = jnp.where(column % 64 < 32, -sign * sine, sign * sine)
    return values * cosine + swap_halves(values) * signed


def project_kernel(
    hidden_ref, gain_ref, query_ref, compress_ref, latent_gain_ref, expand_ref, cosine_ref, sine_ref,
    normed_out, query_out, key_out, value_out, latent_out, latent_normed_out
):
    entries = hidden_ref[...].astype(F32)
    normed = (entries * rms_scale(entries) * gain_ref[...]).astype(BF)
    normed_out[...] = normed
    cosine, sine = cosine_ref[...], sine_ref[...]
    query = dot(normed, query_ref[...])
    nope = query.shape[1] - 128
    query_out[:, :nope] = query[:, :nope].astype(BF)
    query_out[:, nope:] = turn(query[:, nope:], cosine, sine, 1.0).astype(BF)
    compressed = dot(normed, compress_ref[...])
    latent = compressed[:, :LATENT]
    latent_out[...] = latent
    latent_normed = (latent * rms_scale(latent) * latent_gain_ref[...]).astype(BF)
    latent_normed_out[...] = latent_normed
    rotary = compressed[:, LATENT:]
    rotary = jnp.concatenate([rotary, rotary], axis=1)
    expanded = dot(latent_normed, expand_ref[...]).astype(BF)
    key_out[:, :nope] = expanded[:, :nope]
    key_out[:, nope:] = turn(rotary, cosine, sine, 1.0).astype(BF)
    value_out[...] = expanded[:, nope:]


def project(hidden_all, first_gain, query_weight, compress_weight, latent_gain, expand_weight, cosine, sine):
    length, features = hidden_all.shape
    block = 256
    query_width = query_weight.shape[1]
    values = query_width - 128

    def tiled(columns):
        return pl.BlockSpec((block, columns), lambda j: (j, 0))

    def whole(array):
        return pl.BlockSpec(array.shape, lambda j: (0, 0), pipeline_mode=pl.Buffered(1))

    return pl.pallas_call(
        project_kernel,
        grid=(length // block,),
        in_specs=[
            tiled(features),
            whole(first_gain),
            whole(query_weight),
            whole(compress_weight),
            whole(latent_gain),
            whole(expand_weight),
            tiled(128),
            tiled(128),
        ],
        out_specs=[
            tiled(features), tiled(query_width), tiled(query_width), tiled(values), tiled(LATENT),
            tiled(LATENT),
        ],
        out_shape=[
            jax.ShapeDtypeStruct((length, features), BF),
            jax.ShapeDtypeStruct((length, query_width), BF),
            jax.ShapeDtypeStruct((length, query_width), BF),
            jax.ShapeDtypeStruct((length, values), BF),
            jax.ShapeDtypeStruct((length, LATENT), F32),
            jax.ShapeDtypeStruct((length, LATENT), BF),
        ],
        compiler_params=params(48),
        cost_estimate=pl.CostEstimate(
            flops=2 * length * features * (query_width + 640), bytes_accessed=2**25, transcendentals=0
        ),
    )(hidden_all, first_gain, query_weight, compress_weight, latent_gain, expand_weight, cosine, sine)


BLOCK = 512
SCALE = 1.0 / math.sqrt(QK)


def head_keys(key_ref, rotary_ref, part, head):
    rotary = rotary_ref[part]
    column = lax.broadcasted_iota(jnp.int32, rotary.shape, 1)
    rotary = jnp.where(column // 64 == head, rotary.astype(F32), 0.0).astype(BF)
    return jnp.concatenate([key_ref[part], rotary], axis=1)


def masked_scores(query, keys, block, j):
    scores = dot_nt(query, keys) * SCALE
    row = block * BLOCK + lax.broadcasted_iota(jnp.int32, scores.shape, 0)
    column = j * BLOCK + lax.broadcasted_iota(jnp.int32, scores.shape, 1)
    return jnp.where(column <= row, scores, -1e30)


def tile_of(j):
    return pl.ds(pl.multiple_of(j * BLOCK, BLOCK), BLOCK)


def attend_kernel(query_ref, turned_ref, key_ref, rotary_ref, value_ref, out_ref, log_ref, scores_ref):
    head, block = pl.program_id(0), pl.program_id(1)
    query = jnp.concatenate([query_ref[...], turned_ref[...]], axis=1)

    def score(j, largest):
        scores = masked_scores(query, head_keys(key_ref, rotary_ref, tile_of(j), head), block, j)
        scores_ref[j] = scores
        return jnp.maximum(largest, jnp.max(scores, axis=1, keepdims=True))

    largest = lax.fori_loop(0, block + 1, score, jnp.full((BLOCK, 1), -1e30, F32))

    def weigh(j, carry):
        total, found = carry
        weights = jnp.exp(scores_ref[j] - largest)
        total += jnp.sum(weights, axis=1, keepdims=True)
        return total, found + dot(weights.astype(BF), value_ref[tile_of(j)])

    total, found = lax.fori_loop(
        0, block + 1, weigh, (jnp.zeros((BLOCK, 1), F32), jnp.zeros((BLOCK, VDIM), F32))
    )
    out_ref[...] = (found / total).astype(BF)
    log_ref[0] = jnp.broadcast_to(largest + jnp.log(total), (BLOCK, 128))


def attention_specs(length, heads):
    return [
        pl.BlockSpec((BLOCK, 128), lambda h, b: (b, h)),
        pl.BlockSpec((BLOCK, 128), lambda h, b: (b, heads)),
        pl.BlockSpec((length, 128), lambda h, b: (0, h)),
        pl.BlockSpec((length, 128), lambda h, b: (0, heads)),
        pl.BlockSpec((length, VDIM), lambda h, b: (0, h)),
    ]


def attend(queries, keys, values):
    length = queries.shape[0]
    heads = values.shape[1] // VDIM
    blocks = length // BLOCK
    return pl.pallas_call(
        attend_kernel,
        grid=(heads, blocks),
        in_specs=attention_specs(length, heads),
        out_specs=[
            pl.BlockSpec((BLOCK, VDIM), lambda h, b: (b, h)),
            pl.BlockSpec((1, BLOCK, 128), lambda h, b: (h, b, 0)),
        ],
        out_shape=[
            jax.ShapeDtypeStruct((length, heads * VDIM), BF),
            jax.ShapeDtypeStruct((heads, length, 128), F32),
        ],
        scratch_shapes=[pltpu.VMEM((blocks, BLOCK, BLOCK), F32)],
        compiler_params=pltpu.CompilerParams(
            vmem_limit_bytes=40 * 2**20, dimension_semantics=("arbitrary", "arbitrary")
        ),
        cost_estimate=pl.CostEstimate(
            flops=heads * length * length * 384, bytes_accessed=2**23, transcendentals=0
        ),
    )(queries, queries, keys, keys, values)


BACK_EVENTS = (0, 1, 1, 2, 3, 4, 4, 5, 6, 6, 7, 7)


def attend_back_kernel(
    remote, query_ref, turned_ref, key_ref, rotary_ref, value_ref, upstream_ref, log_ref, cosine_ref,
    sine_ref, parts_ref, query_back, turned_back, key_back, rotary_back, value_back, sum_ref,
    shares_ref, slopes_ref, key_sum, value_sum, *scratch
):
    head, block = pl.program_id(0), pl.program_id(1)
    heads, blocks = pl.num_programs(0), pl.num_programs(1)
    step = head * blocks + block
    if remote:
        scatter = ScatterAll(parts_ref, *scratch)
        pl.when(step == 0)(scatter.begin)
    query = jnp.concatenate([query_ref[...], turned_ref[...]], axis=1)
    upstream = upstream_ref[...]
    log_row = log_ref[0][:, :1]

    @pl.when(block == 0)
    def _():
        key_sum[...] = jnp.zeros_like(key_sum)
        value_sum[...] = jnp.zeros_like(value_sum)

    def score(j, centre):
        scores = masked_scores(query, head_keys(key_ref, rotary_ref, tile_of(j), head), block, j)
        shares = jnp.exp(scores - log_row)
        slopes = dot_nt(upstream, value_ref[tile_of(j)])
        shares_ref[j] = shares
        slopes_ref[j] = slopes
        return centre + jnp.sum(shares * slopes, axis=1, keepdims=True)

    centre = lax.fori_loop(0, block + 1, score, jnp.zeros((BLOCK, 1), F32))

    def back(j, found):
        part = tile_of(j)
        shares = shares_ref[j]
        score_back = (shares * (slopes_ref[j] - centre)).astype(BF)
        value_sum[part] += dot_tn(shares.astype(BF), upstream)
        key_sum[part] += dot_tn(score_back, query)
        return found + dot(score_back, head_keys(key_ref, rotary_ref, part, head))

    found = lax.fori_loop(0, block + 1, back, jnp.zeros((BLOCK, 256), F32)) * SCALE
    query_back[...] = found[:, :128].astype(BF)
    turned = found[:, 128:].astype(BF).astype(F32)
    turned_back[...] = turn(turned, cosine_ref[...], sine_ref[...], -1.0).astype(BF)

    @pl.when(block == blocks - 1)
    def _():
        key_back[...] = (key_sum[:, :128] * SCALE).astype(BF)
        value_back[...] = value_sum[...].astype(BF)
        column = lax.broadcasted_iota(jnp.int32, rotary_back.shape, 1)
        rotary = jnp.where(column // 64 == head, key_sum[:, 128:] * SCALE, 0.0).astype(BF)
        rotary_back[...] = jnp.where(head == 0, rotary.astype(F32), rotary_back[...] + rotary.astype(F32))

    if remote:
        events = scatter.events()
        for at in sorted(set(BACK_EVENTS)):

            @pl.when(step == at)
            def _():
                for event, when in zip(events, BACK_EVENTS):
                    if when == at:
                        event()
                if at == BACK_EVENTS[-1]:
                    scatter.finish(sum_ref)


def attend_back(remote, queries, keys, values, upstream, logs, cosine, sine, parts):
    length = queries.shape[0]
    heads = values.shape[1] // VDIM
    blocks = length // BLOCK
    _, rows, features = parts.shape
    row = pl.BlockSpec((BLOCK, 128), lambda h, b: (b, 0))
    return pl.pallas_call(
        functools.partial(attend_back_kernel, remote),
        grid=(heads, blocks),
        in_specs=attention_specs(length, heads)
        + [
            pl.BlockSpec((BLOCK, VDIM), lambda h, b: (b, h)),
            pl.BlockSpec((1, BLOCK, 128), lambda h, b: (h, b, 0)),
            row,
            row,
            pl.BlockSpec(memory_space=pl.ANY),
        ],
        out_specs=[
            pl.BlockSpec((BLOCK, 128), lambda h, b: (b, h)),
            pl.BlockSpec((BLOCK, 128), lambda h, b: (b, h)),
            pl.BlockSpec((length, 128), lambda h, b: (0, h)),
            pl.BlockSpec((length, 128), lambda h, b: (0, 0)),
            pl.BlockSpec((length, VDIM), lambda h, b: (0, h)),
            pl.BlockSpec((rows, features), lambda h, b: (0, 0)),
        ],
        out_shape=[
            jax.ShapeDtypeStruct((length, heads * 128), BF),
            jax.ShapeDtypeStruct((length, heads * 128), BF),
            jax.ShapeDtypeStruct((length, heads * 128), BF),
            jax.ShapeDtypeStruct((length, 128), F32),
            jax.ShapeDtypeStruct((length, heads * VDIM), BF),
            jax.ShapeDtypeStruct((rows, features), BF),
        ],
        scratch_shapes=[
            pltpu.VMEM((blocks, BLOCK, BLOCK), F32),
            pltpu.VMEM((blocks, BLOCK, BLOCK), F32),
            pltpu.VMEM((length, 256), F32),
            pltpu.VMEM((length, VDIM), F32),
        ]
        + (ScatterAll.scratch(rows, features, BF) if remote else []),
        compiler_params=pltpu.CompilerParams(
            vmem_limit_bytes=62 * 2**20,
            dimension_semantics=("arbitrary", "arbitrary"),
            **({"collective_id": 8, "has_side_effects": True} if remote else {}),
        ),
        cost_estimate=pl.CostEstimate(
            flops=heads * length * length * 1024, bytes_accessed=2**26, transcendentals=0
        ),
    )(queries, queries, keys, keys, values, upstream, logs, cosine, sine, parts)


def partial_kernel(
    query_ref, turned_ref, key_ref, value_ref, rotary_ref, query_weight, expand_weight, out_ref
):
    nope = query_ref.shape[1]
    features = query_weight.shape[0]
    out_ref[:, :features] = (
        dot_nt(query_ref[...], query_weight[:, :nope])
        + dot_nt(turned_ref[...], query_weight[:, nope:])
    ).astype(BF)
    out_ref[:, features : features + LATENT] = (
        dot_nt(key_ref[...], expand_weight[:, :nope])
        + dot_nt(value_ref[...], expand_weight[:, nope:])
    ).astype(BF)
    rotary = rotary_ref[...]
    out_ref[:, features + LATENT :] = (rotary + pltpu.roll(rotary, ROPE, 1)).astype(BF)


def partial_terms(rows, query_back, turned_back, key_back, value_back, rotary_sum, query_weight, expand_weight):
    length = query_back.shape[0]
    columns = query_weight.shape[0] + LATENT + 128

    def tiled(array):
        return pl.BlockSpec((rows, array.shape[1]), lambda j: (j, 0))

    def whole(array):
        return pl.BlockSpec(array.shape, lambda j: (0, 0))

    given = (query_back, turned_back, key_back, value_back, rotary_sum)
    return pl.pallas_call(
        partial_kernel,
        grid=(length // rows,),
        in_specs=[tiled(x) for x in given] + [whole(query_weight), whole(expand_weight)],
        out_specs=pl.BlockSpec((rows, columns), lambda j: (j, 0)),
        out_shape=jax.ShapeDtypeStruct((length, columns), BF),
        compiler_params=params(40),
        cost_estimate=pl.CostEstimate(
            flops=2 * length * columns * 384, bytes_accessed=2**24, transcendentals=0
        ),
    )(*given, query_weight, expand_weight)


def tie_kernel(in_ref, _, out_ref):
    out_ref[...] = in_ref[...]


def tie(array, other):
    return pl.pallas_call(
        tie_kernel,
        in_specs=[pl.BlockSpec(memory_space=pltpu.VMEM), pl.BlockSpec(memory_space=pl.ANY)],
        out_specs=pl.BlockSpec(memory_space=pltpu.VMEM),
        out_shape=jax.ShapeDtypeStruct(array.shape, array.dtype),
        compiler_params=pltpu.CompilerParams(vmem_limit_bytes=16 * 2**20),
        cost_estimate=pl.CostEstimate(flops=0, bytes_accessed=4 * array.size, transcendentals=0),
    )(array, other)


def tail_scatter_kernel(
    in_ref, columns_ref, latents_ref, out_ref, columns_out, latents_out, held, far, near, stage,
    columns_total, columns_ring, latents_total, latents_ring, send_sems, recv_sems, local_sems
):
    core, across_x, across_y, following, previous = neighbours()
    greet((core, across_x, across_y, following, previous))
    dp = lax.axis_index("dp")
    seq = lax.axis_index("seq")
    rows = out_ref.shape[0]
    top, bottom = pl.ds(0, rows // 2), pl.ds(rows // 2, rows // 2)
    post = Courier(send_sems, recv_sems)
    x_seq = seq + 2 - 4 * ((seq // 2) % 2)
    y_seq = seq + 4 - 8 * (seq // 4)
    xy_seq = x_seq + 4 - 8 * (seq // 4)
    core_step = 1 - 2 * (seq % 2)
    sums = (
        (columns_ref, columns_total, columns_ring, columns_out),
        (latents_ref, latents_total, latents_ring, latents_out),
    )
    ring_loads = {}
    for n, i in enumerate(SCATTER_ORDER):
        for m, (source, total, _, _) in enumerate(sums):
            load = pltpu.make_async_copy(
                source.at[(dp + 4 - i) % 4], total.at[n], local_sems.at[4 + 2 * n + m]
            )
            load.start()
            ring_loads[n, m] = load
    loads, arriving, hops = {}, {}, {}
    for k, place in ((3, xy_seq), (1, x_seq), (2, y_seq), (0, seq)):
        arriving[k] = post.send(in_ref.at[place + core_step], held.at[k], core)
        loads[k] = pltpu.make_async_copy(in_ref.at[place], stage.at[k], local_sems.at[k])
        loads[k].start()

    def ring_step(n):
        for m, (_, total, ring, out) in enumerate(sums):
            ring_loads[n, m].wait()
            if n > 0:
                post.take(hops[n - 1, m])
                accumulate(total.at[n], ring.at[n - 1])
            if n < 3:
                hops[n, m] = post.send(total.at[n], ring.at[n], following)
            else:
                out[...] = total[3]

    def join(k):
        loads[k].wait()
        post.take(arriving[k])
        accumulate(held.at[k], stage.at[k])

    ring_step(0)
    join(3)
    far_top = post.send(held.at[3, top], far.at[0], across_y)
    far_bottom = post.send(held.at[3, bottom], far.at[1], across_x)
    join(1)
    x_bottom = post.send(held.at[1, bottom], near.at[0, bottom], across_x)
    join(2)
    y_top = post.send(held.at[2, top], near.at[1, top], across_y)
    join(0)
    post.take(far_top)
    accumulate(held.at[1, top], far.at[0])
    x_top = post.send(held.at[1, top], near.at[0, top], across_x)
    post.take(far_bottom)
    accumulate(held.at[2, bottom], far.at[1])
    y_bottom = post.send(held.at[2, bottom], near.at[1, bottom], across_y)
    ring_step(1)
    ring_step(2)
    for copy in (x_bottom, y_top, x_top, y_bottom):
        post.take(copy)
    accumulate(held.at[0], near.at[0], near.at[1])
    out_ref[...] = held[0]
    ring_step(3)
    post.finish()


def tail_scatter(parts, columns, latents, collective_id):
    _, rows, width = parts.shape
    anywhere = pl.BlockSpec(memory_space=pl.ANY)
    here = pl.BlockSpec(memory_space=pltpu.VMEM)
    return pl.pallas_call(
        tail_scatter_kernel,
        out_shape=[
            jax.ShapeDtypeStruct((rows, width), BF),
            jax.ShapeDtypeStruct(columns.shape[1:], BF),
            jax.ShapeDtypeStruct(latents.shape[1:], BF),
        ],
        in_specs=[anywhere] * 3,
        out_specs=[here] * 3,
        scratch_shapes=[
            pltpu.VMEM((4, rows, width), BF),
            pltpu.VMEM((2, rows // 2, width), BF),
            pltpu.VMEM((2, rows, width), BF),
            pltpu.VMEM((4, rows, width), BF),
            pltpu.VMEM(columns.shape, BF),
            pltpu.VMEM((3, *columns.shape[1:]), BF),
            pltpu.VMEM(latents.shape, BF),
            pltpu.VMEM((3, *latents.shape[1:]), BF),
            pltpu.SemaphoreType.DMA((16,)),
            pltpu.SemaphoreType.DMA((16,)),
            pltpu.SemaphoreType.DMA((12,)),
        ],
        compiler_params=pltpu.CompilerParams(
            collective_id=collective_id, has_side_effects=True, vmem_limit_bytes=48 * 2**20
        ),
        cost_estimate=pl.CostEstimate(flops=0, bytes_accessed=2**25, transcendentals=0),
    )(parts, columns, latents)


def tail_gather_kernel(*refs):
    sources, found = refs[:3], refs[3:6]
    send_sems, recv_sems, local_sems = refs[6:]
    core, across_x, across_y, _, _ = neighbours()
    greet((core, across_x, across_y))
    seq = lax.axis_index("seq")
    post = Courier(send_sems, recv_sems)
    owns = []
    for n in range(3):
        own = pltpu.make_async_copy(sources[n], found[n].at[seq], local_sems.at[n])
        own.start()
        owns.append(own)
    spreads = [
        spread(post, sources[n], blocks_of(found[n]), core, across_x, across_y) for n in range(3)
    ]
    for _ in range(3):
        advance(*spreads)
    for own in owns:
        own.wait()
    post.finish()


def tail_gather(blocks, collective_id):
    anywhere = pl.BlockSpec(memory_space=pl.ANY)
    return pl.pallas_call(
        tail_gather_kernel,
        out_shape=[jax.ShapeDtypeStruct((8, *b.shape), b.dtype) for b in blocks],
        in_specs=[anywhere] * 3,
        out_specs=[anywhere] * 3,
        scratch_shapes=[
            pltpu.SemaphoreType.DMA((24,)),
            pltpu.SemaphoreType.DMA((24,)),
            pltpu.SemaphoreType.DMA((3,)),
        ],
        compiler_params=pltpu.CompilerParams(
            collective_id=collective_id, has_side_effects=True, vmem_limit_bytes=16 * 2**20
        ),
        cost_estimate=pl.CostEstimate(flops=0, bytes_accessed=2**24, transcendentals=0),
    )(*blocks)


def chosen_columns(source, target):
    return jnp.where(source == target, 1.0, 0.0).astype(BF)


def layout_kernel(width, columns_ref, latents_ref, small_ref, query_out, expand_out, output_out, small_out):
    step = pl.program_id(0)
    query = columns_ref[0, :, : 3 * 128]
    row = lax.broadcasted_iota(jnp.int32, (3 * 128, 3 * 128), 0)
    column = lax.broadcasted_iota(jnp.int32, (3 * 128, 3 * 128), 1)
    head = jnp.where(column < QK, 0, 1)
    entry = column - QK * head
    source = jnp.where(entry < NOPE, NOPE * head + entry, 2 * NOPE + ROPE * head + entry - NOPE)
    query_out[...] = dot(query, chosen_columns(row, source))
    for part, place in enumerate((0, 2, 1, 3)):
        expand_out[:, 128 * place : 128 * place + 128] = latents_ref[
            0, :, 128 * part : 128 * part + 128
        ].astype(F32)
    output_out[...] = columns_ref[0, :, 3 * 128 :].astype(F32)
    row = lax.broadcasted_iota(jnp.int32, (128, small_out.shape[1]), 0)
    column = lax.broadcasted_iota(jnp.int32, (128, small_out.shape[1]), 1)
    place = jnp.where(row < width, row + width * step, -1)
    small = dot(small_ref[0], chosen_columns(place, column))

    @pl.when(step == 0)
    def _():
        small_out[...] = small

    @pl.when(step > 0)
    def _():
        small_out[...] += small


def layout_grads(columns, latents, small, width):
    count, shard, _ = columns.shape
    latent_shard = latents.shape[1]

    def given(array):
        return pl.BlockSpec((1, *array.shape[1:]), lambda j: (j, 0, 0))

    def made(rows, size):
        return pl.BlockSpec((rows, size), lambda j: (0, j))

    return pl.pallas_call(
        functools.partial(layout_kernel, width),
        grid=(count,),
        in_specs=[given(columns), given(latents), given(small)],
        out_specs=[
            made(shard, 384), made(latent_shard, 512), made(shard, 256),
            pl.BlockSpec((shard, count * width), lambda j: (0, 0)),
        ],
        out_shape=[
            jax.ShapeDtypeStruct((shard, count * 384), F32),
            jax.ShapeDtypeStruct((latent_shard, count * 512), F32),
            jax.ShapeDtypeStruct((shard, count * 256), F32),
            jax.ShapeDtypeStruct((shard, count * width), F32),
        ],
        compiler_params=params(32),
        cost_estimate=pl.CostEstimate(
            flops=2 * count * shard * 384 * 384, bytes_accessed=2**25, transcendentals=0
        ),
    )(columns, latents, small)


def shared_layout_kernel(units, in_ref, out_ref):
    n_seq, n_dp, both, _ = in_ref.shape
    row = lax.broadcasted_iota(jnp.int32, (both, 128), 0) - units * pl.program_id(1)
    column = lax.broadcasted_iota(jnp.int32, (both, 128), 1)
    inside = (row >= 0) & (row < units)
    for t in range(out_ref.shape[1] // 128):
        start = 128 * t
        total = None
        for device in range(start // units, min((start + 127) // units, n_seq * n_dp - 1) + 1):
            place = jnp.where(inside, row + (device * units - start), -1)
            piece = dot_tn(in_ref[device % n_seq, device // n_seq], chosen_columns(place, column))
            total = piece if total is None else total + piece
        out_ref[:, start : start + 128] = total


def shared_layout(found, units):
    n_seq, n_dp, both, shard = found.shape
    rows = min(256, shard)
    return pl.pallas_call(
        functools.partial(shared_layout_kernel, units),
        grid=(shard // rows, 2),
        in_specs=[pl.BlockSpec((n_seq, n_dp, both, rows), lambda r, g: (0, 0, 0, r))],
        out_specs=pl.BlockSpec((rows, SH_FF), lambda r, g: (r, g)),
        out_shape=jax.ShapeDtypeStruct((shard, 2 * SH_FF), F32),
        compiler_params=pltpu.CompilerParams(
            vmem_limit_bytes=60 * 2**20, dimension_semantics=("arbitrary", "arbitrary")
        ),
        cost_estimate=pl.CostEstimate(
            flops=2**32, bytes_accessed=2 * found.size + 8 * shard * SH_FF, transcendentals=0
        ),
    )(found)


def outer_kernel(left_ref, right_ref, out_ref):
    out_ref[...] = dot_tn(left_ref[0], right_ref[...]).astype(BF)


def outer(left, right, size):
    parts, tokens, columns = left.shape
    features = parts * columns
    last = right.shape[1] // size - 1
    return pl.pallas_call(
        outer_kernel,
        grid=(parts,),
        in_specs=[
            pl.BlockSpec((1, tokens, columns), lambda j: (j, 0, 0)),
            pl.BlockSpec((tokens, size), lambda j: (0, last)),
        ],
        out_specs=pl.BlockSpec((columns, size), lambda j: (j, 0)),
        out_shape=jax.ShapeDtypeStruct((features, size), BF),
        compiler_params=params(32),
        cost_estimate=pl.CostEstimate(
            flops=2 * tokens * features * size, bytes_accessed=2 * tokens * features, transcendentals=0
        ),
    )(left, right)


def exchange_kernel(in_ref, out_ref, send_sems, recv_sems, local_sem):
    dp = lax.axis_index("dp")
    seq = lax.axis_index("seq")
    width = in_ref.shape[1] // 8

    def columns(j):
        return in_ref.at[:, pl.ds(pl.multiple_of(j * width, width), width)]

    others = [(seq + r) % 8 for r in range(1, 8)]
    greet([{"dp": dp, "seq": other} for other in others])
    own = pltpu.make_async_copy(columns(seq), out_ref.at[seq], local_sem)
    own.start()
    post = Courier(send_sems, recv_sems)
    for other in others:
        post.send(columns(other), out_ref.at[seq], {"dp": dp, "seq": other})
    own.wait()
    post.finish()


def exchange(array, collective_id):
    rows, columns = array.shape
    anywhere = pl.BlockSpec(memory_space=pl.ANY)
    return pl.pallas_call(
        exchange_kernel,
        out_shape=jax.ShapeDtypeStruct((8, rows, columns // 8), array.dtype),
        in_specs=[anywhere],
        out_specs=anywhere,
        scratch_shapes=[
            pltpu.SemaphoreType.DMA((7,)),
            pltpu.SemaphoreType.DMA((7,)),
            pltpu.SemaphoreType.DMA,
        ],
        compiler_params=pltpu.CompilerParams(
            collective_id=collective_id, has_side_effects=True, vmem_limit_bytes=16 * 2**20
        ),
        cost_estimate=pl.CostEstimate(flops=0, bytes_accessed=4 * array.size, transcendentals=0),
    )(array).reshape(8 * rows, columns // 8)


def on_device(
    hidden_in,
    positions,
    expert_ids,
    gate_weights,
    attention_gain,
    w_query,
    w_compress,
    latent_gain,
    w_expand,
    w_output,
    feedforward_gain,
    w_shared_in,
    w_shared_out,
    w_expert_in,
    w_expert_out,
    cotangent,
):
    n_dp = lax.axis_size("dp")
    n_seq = lax.axis_size("seq")
    n_all = n_dp * n_seq
    fast = (n_dp, n_seq) == (4, 8)
    both = ("dp", "seq")
    dp_index = lax.axis_index("dp")
    seq_index = lax.axis_index("seq")
    sequence_count, rows, features = hidden_in.shape
    rows = sequence_count * rows
    length = rows * n_seq
    heads = HEADS // n_seq
    shard = features // n_dp
    expert_count = n_all // 2
    capacity = max(2, rows * TOP * 5 // (expert_count * 3))
    capacity = (capacity + 15) // 16 * 16
    units = SH_FF // n_all
    padded_units = (units + 127) // 128 * 128
    expand_width = heads * (NOPE + VDIM)

    hidden = hidden_in.reshape(rows, features)
    upstream_rows = cotangent.reshape(rows, features)
    upstream_float = upstream_rows.astype(F32)
    id_rows = expert_ids.reshape(rows, TOP)
    gate_table = gate_weights.reshape(rows, TOP)

    gains_own = jnp.concatenate([attention_gain, feedforward_gain, latent_gain])
    named_own = jnp.concatenate(
        [id_rows.T.astype(F32), gate_table.T, positions.reshape(1, rows).astype(F32)]
    )
    query_width = heads * NOPE + 128
    query_part = lax.dynamic_slice_in_dim(w_query, seq_index * heads * QK, heads * QK, 1)
    query_part = query_part.reshape(shard, heads, QK)
    query_part = jnp.concatenate(
        [
            query_part[..., :NOPE].reshape(shard, -1),
            query_part[..., NOPE:].reshape(shard, -1),
            jnp.zeros((shard, 128 - heads * ROPE), BF),
        ],
        axis=1,
    )
    expand_part = lax.dynamic_slice_in_dim(w_expand, seq_index * expand_width, expand_width, 1)
    expand_part = expand_part.reshape(-1, heads, NOPE + VDIM)
    expand_part = jnp.concatenate(
        [part.reshape(-1, heads * NOPE) for part in jnp.split(expand_part, 2, axis=-1)], axis=1
    )
    if fast:
        named_own = jnp.pad(named_own, ((0, 16 - named_own.shape[0]), (0, 0)))
        gains_size = gains_own.shape[0]
        gains_own = jnp.pad(gains_own, (0, 2048 - gains_size)).reshape(16, 128)
        (
            hidden_all, named_all, gains, query_weight, expand_weight, compress_weight,
            output_weight,
        ) = gather_start(
            hidden, named_own, gains_own, query_part, expand_part, w_compress, w_output, 1
        )
        gains = gains.reshape(n_dp, 2048)[:, :gains_size]
        dp_places = (dp_index - jnp.arange(n_dp)) % n_dp
        slot_of_seq = small_take([0, 1, 2, 4, 3, 5, 6, 7], seq_index ^ jnp.arange(n_seq))
        named_all = jnp.stack([named_all[k] for k in (0, 4, 1, 2, 5, 6, 3, 7)])
        positions_all = reorder(named_all[:, 0, 2 * TOP], slot_of_seq)
        named_all = named_all.swapaxes(0, 1).reshape(n_all, 16, rows)
    else:
        hidden_all = lax.all_gather(hidden, "seq", axis=0)
        named_all = lax.all_gather(named_own, both, axis=0)
        positions_all = lax.dynamic_slice_in_dim(named_all, dp_index * n_seq, n_seq, 0)[:, 2 * TOP]
        gains = lax.all_gather(gains_own, "dp", axis=0)
        query_weight = lax.all_gather(query_part, "dp", axis=0)
        expand_weight = lax.all_gather(expand_part, "dp", axis=0)
        compress_weight = lax.all_gather(w_compress, "dp", axis=0)
        output_weight = lax.all_gather(w_output, "dp", axis=0)
    hidden_all = hidden_all.reshape(length, features)
    query_weight = query_weight.reshape(features, query_width)
    expand_weight = expand_weight.reshape(LATENT, expand_width)
    compress_weight = compress_weight.reshape(features, LATENT + ROPE)
    gains = gains.astype(F32)
    first_gain = gains[:, :shard].reshape(features)
    second_gain = gains[:, shard : 2 * shard].reshape(features)
    latent_gain_row = gains[:, 2 * shard :].reshape(LATENT)
    output_weight = output_weight.reshape(HEADS * VDIM, features)
    shared_part = jnp.stack(
        [
            jnp.stack(
                [
                    lax.dynamic_slice_in_dim(
                        w_shared_in, half * SH_FF + (z * n_seq + seq_index) * units, units, 1
                    )
                    for half in range(2)
                ],
                axis=1,
            )
            for z in range(n_dp)
        ]
    )
    shared_in = lax.all_to_all(
        shared_part, "dp", split_axis=0, concat_axis=0, tiled=True
    ).reshape(features, 2, units)
    pad = padded_units - units
    shared_in = jnp.pad(shared_in, ((0, 0), (0, 0), (0, pad))).reshape(features, 2 * padded_units)
    shared_out = lax.dynamic_slice_in_dim(w_shared_out, seq_index * units, units, 0)
    shared_out = jnp.pad(shared_out, ((0, pad), (0, 0)))
    weight_in, weight_out = w_expert_in[0], w_expert_out[0]
    expert = (dp_index * n_seq + seq_index) // 2
    named = named_all[:, :TOP] == expert.astype(F32)
    chosen = jnp.any(named, axis=1)
    gate_rows = jnp.sum(jnp.where(named, named_all[:, TOP : 2 * TOP], 0.0), axis=1)[:, None]
    before = (jnp.arange(rows)[:, None] < jnp.arange(rows)[None, :]).astype(BF)
    place = dot(chosen.astype(BF), before).astype(jnp.int32)
    place = jnp.where(chosen, place, -1)[:, None]

    angles = rotary_angles(positions_all.reshape(length))
    angles = jnp.concatenate([angles] * 4, axis=1)
    cosine_all, sine_all = jnp.cos(angles), jnp.sin(angles)
    normed_all, queries, keys_all, values_all, latent, latent_normed = project(
        hidden_all, first_gain[None], query_weight, compress_weight, latent_gain_row[None],
        expand_weight, cosine_all, sine_all,
    )
    attended_heads, logs = attend(queries, keys_all, values_all)
    if fast:
        attended_all = plane_gather(attended_heads, 9)
        attended = lax.dynamic_slice_in_dim(attended_all, seq_index * rows, rows, 1)
        attended = attended.swapaxes(0, 1).reshape(rows, HEADS * VDIM)
    else:
        attended_all = lax.all_gather(attended_heads, "seq", axis=0)
        attended = lax.all_to_all(
            attended_heads, "seq", split_axis=0, concat_axis=1, tiled=True
        )
    hidden_float = hidden.astype(F32)
    middle = hidden_float + dot(attended, output_weight)
    second_scale = rms_scale(middle)
    moe_rows = (middle * second_scale * second_gain).astype(BF)

    sent = jnp.stack([moe_rows, upstream_rows])
    if not fast:
        sent = lax.all_gather(sent, both, axis=0)
    (
        sent_all, expert_in_grad, expert_out_grad, hidden_units, shared_units, back_parts,
        shared_in_grad, shared_out_grad,
    ) = experts(
        fast, capacity, sent, place, gate_rows, weight_in, weight_out, shared_in, shared_out
    )
    shared_in_grad = shared_in_grad.reshape(2, padded_units, n_dp, shard)[:, :units].astype(BF)
    shared_in_grad = shared_in_grad.reshape(2 * units, n_dp, shard).swapaxes(0, 1)
    gate_grads, out_parts, moe_back, shared_dealt = out_side(
        fast, capacity, back_parts, shared_in_grad, place, gate_rows, hidden_units, sent_all if fast else sent, shared_units,
        weight_out, shared_out,
    )
    if fast:
        gate_grads = reorder(gate_grads.reshape(n_dp, n_seq, rows), dp_places)
        gate_grads = reorder(gate_grads.swapaxes(0, 1), slot_of_seq).swapaxes(0, 1)
        gate_grads = gate_grads.reshape(n_all, 1, rows)
    else:
        moe_back = lax.psum_scatter(
            back_parts.reshape(n_all * rows, features), both, scatter_dimension=0, tiled=True
        )
    moe_back = moe_back.astype(F32)
    gate_grads = lax.all_to_all(gate_grads, both, split_axis=0, concat_axis=0, tiled=True)
    gate_grads = jnp.sum(gate_grads.reshape(expert_count, 2, rows), axis=1)
    gate_gradient = jnp.sum(
        jnp.where(
            id_rows[:, :, None] == jnp.arange(expert_count, dtype=jnp.int32),
            gate_grads.T[:, None, :],
            0.0,
        ),
        axis=-1,
    )
    second_gain_grad = jnp.sum(moe_back * middle * second_scale, axis=0)
    middle_back = upstream_float + norm_backward(moe_back, middle, second_scale, second_gain)
    middle_low = middle_back.astype(BF)
    attended_back = dot_nt(middle_low, output_weight).astype(BF)
    part = features // n_seq
    packed = jnp.concatenate(
        [attended_back.reshape(rows, n_seq, -1), middle_low.reshape(rows, n_seq, part)], axis=2
    ).reshape(rows, -1)
    if fast:
        packed = exchange(packed, 10)
    else:
        packed = lax.all_to_all(packed, "seq", split_axis=1, concat_axis=0, tiled=True)
    output_grad = outer(attended_all, packed, part)

    query_back, turned_back, key_back, rotary_sum, value_back, out_sum = attend_back(
        fast, queries, keys_all, values_all, packed, logs, cosine_all, sine_all, out_parts
    )
    if not fast:
        out_sum = lax.psum_scatter(
            out_parts.reshape(n_all * rows, features), both, scatter_dimension=0, tiled=True
        )
    block_out = (middle + out_sum.astype(F32)).astype(BF)
    turned_back = sum(turned_back[:, 128 * h : 128 * h + 128] for h in range(heads))
    query_raw_back = jnp.concatenate([query_back, turned_back], axis=1)
    expanded_back = jnp.concatenate([key_back, value_back], axis=1)
    partial_back = partial_terms(
        rows, query_back, turned_back, key_back, value_back, rotary_sum, query_weight, expand_weight
    )
    query_grad = dot_tn(normed_all, query_raw_back).astype(BF)
    expand_grad = dot_tn(latent_normed, expanded_back).astype(BF)
    if fast:
        column_grads = jnp.concatenate([query_grad, output_grad], axis=1)
        summed_back, column_grads, latent_grads = tail_scatter(
            partial_back.reshape(n_seq, rows, -1),
            column_grads.reshape(n_dp, shard, -1),
            expand_grad.reshape(n_dp, LATENT // n_dp, -1),
            5,
        )
    else:
        summed_back = lax.psum_scatter(partial_back, "seq", scatter_dimension=0, tiled=True)
    summed_back = summed_back[:, : features + LATENT + ROPE].astype(F32)
    latent_normed_back = summed_back[:, features : features + LATENT]
    own = seq_index * rows

    def mine(array):
        return lax.dynamic_slice_in_dim(array, own, rows, 0)

    latent_own = mine(latent)
    latent_scale_own = rms_scale(latent_own)
    latent_gain_grad = jnp.sum(latent_normed_back * latent_own * latent_scale_own, axis=0)
    latent_back = norm_backward(latent_normed_back, latent_own, latent_scale_own, latent_gain_row)
    half_turn = ROPE // 2
    rotary_back = rotate(
        summed_back[:, features + LATENT :],
        mine(cosine_all)[:, :half_turn],
        -mine(sine_all)[:, :half_turn],
    )
    compressed_back = jnp.concatenate([latent_back, rotary_back], axis=-1).astype(BF)
    width = (LATENT + ROPE) // n_seq
    if fast:
        compressed_back_all, column_grads, latent_grads = tail_gather(
            (jnp.pad(compressed_back, ((0, 0), (0, 64))), column_grads, latent_grads), 6
        )
        compressed_back_all = compressed_back_all[:, :, : LATENT + ROPE]
    else:
        compressed_back_all = lax.all_gather(compressed_back, "seq", axis=0)
    compressed_back_all = compressed_back_all.reshape(length, LATENT + ROPE)
    compress_grad = dot_tn(
        normed_all, lax.dynamic_slice_in_dim(compressed_back_all, seq_index * width, width, 1)
    )
    normed_back = summed_back[:, :features] + dot_nt(compressed_back, compress_weight)
    first_scale = rms_scale(hidden_float)
    first_gain_grad = jnp.sum(normed_back * hidden_float * first_scale, axis=0)
    hidden_gradient = (
        middle_back + norm_backward(normed_back, hidden_float, first_scale, first_gain)
    ).astype(BF)

    gain_grads = jnp.concatenate([first_gain_grad, second_gain_grad, latent_gain_grad])
    bit = 1
    while bit < n_seq:
        gain_grads = gain_grads + lax.ppermute(
            gain_grads, "seq", [(i, i ^ bit) for i in range(n_seq)]
        )
        bit *= 2
    bit = 1
    while bit < n_dp:
        gain_grads = gain_grads + lax.ppermute(
            gain_grads, "dp", [(i, i ^ bit) for i in range(n_dp)]
        )
        bit *= 2
    latent_shard = LATENT // n_dp

    def gain_part(start, size):
        return lax.dynamic_slice_in_dim(gain_grads, start + dp_index * size, size, 0)

    def over_dp(grad):
        total = lax.psum_scatter(grad, "dp", scatter_dimension=0, tiled=True)
        return lax.all_gather(total.astype(BF), "seq", axis=0)

    def in_heads(found, first, second):
        height, cut = found.shape[1], heads * first
        found = jnp.concatenate(
            [
                found[:, :, :cut].reshape(n_seq, height, heads, first),
                found[:, :, cut : cut + heads * second].reshape(n_seq, height, heads, second),
            ],
            axis=-1,
        )
        return found.transpose(1, 0, 2, 3).reshape(height, -1).astype(F32)

    def columns(found):
        return found.transpose(1, 0, 2).reshape(found.shape[1], -1).astype(F32)

    if fast:
        compress_grad = jnp.pad(compress_grad.astype(BF), ((0, 0), (0, 128 - width)))
        small_grads = sum_grads(compress_grad.reshape(n_dp, shard, 128), 7)
        query_out, expand_out, output_out, compress_out = layout_grads(
            column_grads, latent_grads, small_grads, width
        )
    else:
        query_out = in_heads(over_dp(query_grad), NOPE, ROPE)
        expand_out = in_heads(over_dp(expand_grad), NOPE, VDIM)
        output_out = columns(over_dp(output_grad))
        compress_out = columns(over_dp(compress_grad))
    if not fast:
        shared_dealt = lax.all_to_all(
            shared_in_grad, "dp", split_axis=0, concat_axis=0, tiled=True
        )
    shared_in_out = lax.all_gather(tie(shared_dealt, query_back), "seq", axis=0)
    shared_in_out = shared_layout(shared_in_out, units)
    shared_out_out = lax.all_gather(
        shared_out_grad[:units].astype(BF), "seq", axis=0, tiled=True
    ).astype(F32)
    return (
        block_out.reshape(hidden_in.shape),
        hidden_gradient.reshape(hidden_in.shape),
        gate_gradient.reshape(gate_weights.shape),
        gain_part(0, shard),
        query_out,
        compress_out,
        gain_part(2 * features, latent_shard),
        expand_out,
        output_out,
        gain_part(features, shard),
        shared_in_out,
        shared_out_out,
        expert_in_grad[None],
        expert_out_grad[None],
    )


def solution(mesh):
    token = P("dp", "seq", None)
    row = P("dp", None)
    half = P(("dp", "seq"), None, None)
    return jax.shard_map(
        on_device,
        mesh=mesh,
        in_specs=(
            token, P("dp", "seq"), token, token, P("dp"), row, row, P("dp"), row, row,
            P("dp"), row, row, half, half, token,
        ),
        out_specs=(
            token, token, token, P("dp"), row, row, P("dp"), row, row, P("dp"), row, row,
            half, half,
        ),
        check_vma=False,
    )
```

```python
import functools
import math

import jax
import jax.numpy as jnp
from jax import lax
from jax.experimental import pallas as pl
from jax.experimental.pallas import tpu as pltpu
from jax.sharding import PartitionSpec as P

HEADS = 16
NOPE = 128
ROPE = 64
VDIM = 128
LATENT = 512
TOP = 6
QK = 192
SH_FF = 2816
HALF = 704
EPSILON = 1e-06
BF = jnp.bfloat16
F32 = jnp.float32


def rms_scale(entries):
    return lax.rsqrt(jnp.mean(entries * entries, axis=-1, keepdims=True) + EPSILON)


def rotary_angles(position_rows):
    steps_index = jnp.arange(ROPE // 2, dtype=F32)
    frequency = 10000.0 ** (-2.0 * steps_index / ROPE)
    return position_rows.astype(F32)[..., None] * frequency


def rotate(values, cosine_values, sine_values):
    half_width = values.shape[-1] // 2
    front_half = values[..., :half_width]
    back_half = values[..., half_width:]
    return jnp.concatenate(
        [
            front_half * cosine_values - back_half * sine_values,
            front_half * sine_values + back_half * cosine_values,
        ],
        axis=-1,
    )


def norm_backward(upstream, entries, inverse_scale, gain_row):
    scaled = upstream * gain_row
    return inverse_scale * scaled - entries * inverse_scale**3 * jnp.mean(
        scaled * entries, axis=-1, keepdims=True
    )


def dot(a, b):
    return jnp.dot(a, b, preferred_element_type=F32)


def dot_nt(a, b):
    return jnp.einsum("ik,jk->ij", a, b, preferred_element_type=F32)


def dot_tn(a, b):
    return jnp.einsum("ki,kj->ij", a, b, preferred_element_type=F32)


def copy_kernel(places_ref, in_ref, out_ref):
    out_ref[...] = in_ref[...]


def reorder(stack, places):
    count = stack.shape[0]
    if stack.size * stack.dtype.itemsize < 2**20 or stack.ndim != 3:
        return jnp.stack(
            [lax.dynamic_index_in_dim(stack, places[j], 0, keepdims=False) for j in range(count)]
        )
    block = (1, *stack.shape[1:])
    return pl.pallas_call(
        copy_kernel,
        grid_spec=pltpu.PrefetchScalarGridSpec(
            num_scalar_prefetch=1,
            grid=(count,),
            in_specs=[pl.BlockSpec(block, lambda j, order: (order[j], 0, 0))],
            out_specs=pl.BlockSpec(block, lambda j, order: (j, 0, 0)),
        ),
        out_shape=jax.ShapeDtypeStruct(stack.shape, stack.dtype),
        compiler_params=params(40),
        cost_estimate=pl.CostEstimate(
            flops=0, bytes_accessed=2 * stack.size * stack.dtype.itemsize, transcendentals=0
        ),
    )(places.astype(jnp.int32), stack)


def small_take(table, index):
    table = jnp.array(table, jnp.int32)
    hit = index[:, None] == jnp.arange(table.shape[0])[None, :]
    return jnp.sum(jnp.where(hit, table[None, :], 0), axis=1)


def params(limit=60):
    return pltpu.CompilerParams(
        vmem_limit_bytes=limit * 2**20, dimension_semantics=("arbitrary",)
    )


MESH_ID = pl.DeviceIdType.MESH
OWN_SLOTS = (0, 2, 3, 6)
CORE_SLOTS = (1, 4, 5, 7)


def neighbours():
    dp = lax.axis_index("dp")
    seq = lax.axis_index("seq")
    core = {"dp": dp, "seq": seq + 1 - 2 * (seq % 2)}
    across_x = {"dp": dp, "seq": seq + 2 - 4 * ((seq // 2) % 2)}
    across_y = {"dp": dp, "seq": seq + 4 - 8 * (seq // 4)}
    following = {"dp": (dp + 1) % 4, "seq": seq}
    previous = {"dp": (dp + 3) % 4, "seq": seq}
    return core, across_x, across_y, following, previous


def greet(devices):
    barrier = pltpu.get_barrier_semaphore()
    for device in devices:
        pl.semaphore_signal(barrier, inc=1, device_id=device, device_id_type=MESH_ID)
    pl.semaphore_wait(barrier, len(devices))


class Courier:
    def __init__(self, send_sems, recv_sems):
        self.send_sems, self.recv_sems = send_sems, recv_sems
        self.sent, self.open = [], []

    def send(self, source, target, device):
        index = len(self.sent)
        copy = pltpu.make_async_remote_copy(
            src_ref=source,
            dst_ref=target,
            send_sem=self.send_sems.at[index],
            recv_sem=self.recv_sems.at[index],
            device_id=device,
            device_id_type=MESH_ID,
        )
        copy.start()
        self.sent.append(copy)
        self.open.append(copy)
        return copy

    def take(self, copy):
        copy.wait_recv()
        self.open = [other for other in self.open if other is not copy]

    def finish(self):
        for copy in list(self.open):
            self.take(copy)
        for copy in self.sent:
            copy.wait_send()


def accumulate(target, *sources):
    rows = target.shape[0]
    step = 16

    def body(k, carry):
        part = pl.ds(pl.multiple_of(k * step, step), step)
        total = target[part].astype(F32)
        for source in sources:
            total = total + source[part].astype(F32)
        target[part] = total.astype(target.dtype)
        return carry

    lax.fori_loop(0, rows // step, body, 0)


SCATTER_ORDER = (1, 2, 3, 0)


class ScatterAll:
    @staticmethod
    def scratch(rows, columns, dtype):
        return [
            pltpu.VMEM((4, 4, rows, columns), dtype),
            pltpu.VMEM((4, 2, rows // 2, columns), dtype),
            pltpu.VMEM((4, 2, rows, columns), dtype),
            pltpu.VMEM((3, rows, columns), dtype),
            pltpu.VMEM((4, rows, columns), dtype),
            pltpu.SemaphoreType.DMA((35,)),
            pltpu.SemaphoreType.DMA((35,)),
            pltpu.SemaphoreType.DMA((4,)),
        ]

    def __init__(self, in_ref, held, far, near, ring, stage, send_sems, recv_sems, local_sems):
        self.in_ref, self.held, self.far, self.near = in_ref, held, far, near
        self.ring, self.stage = ring, stage
        self.send_sems, self.recv_sems, self.local_sems = send_sems, recv_sems, local_sems
        self.core, self.across_x, self.across_y, self.following, self.previous = neighbours()
        rows = held.shape[2]
        self.top, self.bottom = pl.ds(0, rows // 2), pl.ds(rows // 2, rows // 2)

    def copy(self, index, source, target, device):
        return pltpu.make_async_remote_copy(
            src_ref=source,
            dst_ref=target,
            send_sem=self.send_sems.at[index],
            recv_sem=self.recv_sems.at[index],
            device_id=device,
            device_id_type=MESH_ID,
        )

    def to_core(self, i, k):
        source = self.in_ref.at[8 * i + CORE_SLOTS[k]]
        return self.copy(19 + 4 * i + k, source, self.held.at[i, k], self.core)

    def far_copy(self, i, which):
        part = self.bottom if which else self.top
        device = self.across_x if which else self.across_y
        return self.copy(2 * i + which, self.held.at[i, 3, part], self.far.at[i, which], device)

    def near_copy(self, i, which):
        device = self.across_y if which else self.across_x
        return self.copy(8 + 2 * i + which, self.held.at[i, 1 + which], self.near.at[i, which], device)

    def ring_copy(self, n):
        return self.copy(
            16 + n, self.held.at[SCATTER_ORDER[n], 0], self.ring.at[n], self.following
        )

    def loads(self, n):
        i = SCATTER_ORDER[n]
        return [
            pltpu.make_async_copy(
                self.in_ref.at[8 * i + OWN_SLOTS[k]], self.stage.at[k], self.local_sems.at[k]
            )
            for k in range(4)
        ]

    def begin(self, *others):
        greet((self.core, self.across_x, self.across_y, self.following, self.previous, *others))
        for i in SCATTER_ORDER:
            for k in (3, 1, 2, 0):
                self.to_core(i, k).start()
        for load in self.loads(0):
            load.start()

    def first(self, n):
        i = SCATTER_ORDER[n]
        loads = self.loads(n)
        later = self.loads(n + 1) if n < 3 else None
        for k in (3, 1, 2, 0):
            loads[k].wait()
            self.to_core(i, k).wait_recv()
            accumulate(self.held.at[i, k], self.stage.at[k])
            if later:
                later[k].start()
            if k == 3:
                self.far_copy(i, 0).start()
                self.far_copy(i, 1).start()

    def second(self, n):
        i = SCATTER_ORDER[n]
        self.far_copy(i, 0).wait_recv()
        accumulate(self.held.at[i, 1, self.top], self.far.at[i, 0])
        self.near_copy(i, 0).start()
        self.far_copy(i, 1).wait_recv()
        accumulate(self.held.at[i, 2, self.bottom], self.far.at[i, 1])
        self.near_copy(i, 1).start()

    def third(self, n):
        i = SCATTER_ORDER[n]
        self.near_copy(i, 0).wait_recv()
        self.near_copy(i, 1).wait_recv()
        sources = [self.near.at[i, 0], self.near.at[i, 1]]
        if n > 0:
            self.ring_copy(n - 1).wait_recv()
            sources.append(self.ring.at[n - 1])
        accumulate(self.held.at[i, 0], *sources)
        if n < 3:
            self.ring_copy(n).start()

    def events(self):
        first, second, third = self.first, self.second, self.third
        plan = [
            (first, 0), (first, 1), (second, 0), (first, 2), (second, 1), (third, 0), (first, 3),
            (second, 2), (third, 1), (second, 3), (third, 2), (third, 3),
        ]
        return [functools.partial(f, n) for f, n in plan]

    def finish(self, out_ref):
        out_ref[...] = self.held[0, 0]
        for i in range(4):
            for k in range(4):
                self.to_core(i, k).wait_send()
            for which in range(2):
                self.far_copy(i, which).wait_send()
                self.near_copy(i, which).wait_send()
        for n in range(3):
            self.ring_copy(n).wait_send()


def scatter_all_kernel(in_ref, out_ref, *scratch):
    scatter = ScatterAll(in_ref, *scratch)
    scatter.begin()
    for event in scatter.events():
        event()
    scatter.finish(out_ref)


def scatter_all(parts, collective_id):
    _, rows, columns = parts.shape
    return pl.pallas_call(
        scatter_all_kernel,
        out_shape=jax.ShapeDtypeStruct((rows, columns), parts.dtype),
        in_specs=[pl.BlockSpec(memory_space=pl.ANY)],
        out_specs=pl.BlockSpec(memory_space=pltpu.VMEM),
        scratch_shapes=ScatterAll.scratch(rows, columns, parts.dtype),
        compiler_params=pltpu.CompilerParams(
            collective_id=collective_id, has_side_effects=True, vmem_limit_bytes=56 * 2**20
        ),
        cost_estimate=pl.CostEstimate(
            flops=32 * rows * columns, bytes_accessed=64 * rows * columns * 2, transcendentals=0
        ),
    )(parts)


def spread(post, source, place, core, across_x, across_y):
    seq = lax.axis_index("seq")
    x_seq = seq + 2 - 4 * ((seq // 2) % 2)
    y_seq = seq + 4 - 8 * (seq // 4)
    xy_seq = x_seq + 4 - 8 * (seq // 4)
    x_copy = post.send(source, place(seq), across_x)
    y_copy = post.send(source, place(seq), across_y)
    post.send(source, place(seq), core)
    yield
    post.take(x_copy)
    far_top = post.send(place(x_seq, 0), place(x_seq, 0), across_y)
    post.send(place(x_seq), place(x_seq), core)
    post.take(y_copy)
    far_bottom = post.send(place(y_seq, 1), place(y_seq, 1), across_x)
    post.send(place(y_seq), place(y_seq), core)
    yield
    post.take(far_top)
    post.take(far_bottom)
    post.send(place(xy_seq), place(xy_seq), core)


def blocks_of(found):
    half = found.shape[1] // 2

    def place(index, part=None):
        if part is None:
            return found.at[index]
        return found.at[index, pl.ds(part * half, half)]

    return place


def advance(*spreads):
    for one in spreads:
        for _ in one:
            break


def gather_start_kernel(
    hidden, named, gains, query, expand, compress, output, hidden_all, named_all, gains_all,
    query_all, expand_all, compress_all, output_all, send_sems, recv_sems, local_sems
):
    dp = lax.axis_index("dp")
    seq = lax.axis_index("seq")
    core, across_x, across_y, following, previous = neighbours()
    greet((core, across_x, across_y, following, previous))
    post = Courier(send_sems, recv_sems)
    strip = output.shape[0] // 8
    own_strip = pl.ds(pl.multiple_of(seq * strip, strip), strip)
    hidden_spread = spread(post, hidden, blocks_of(hidden_all), core, across_x, across_y)
    advance(hidden_spread)

    def hop(i):
        at = (dp + 5 - i) % 4
        first = i == 1
        return [
            post.send(query if first else query_all.at[at], query_all.at[at], following),
            post.send(
                compress.at[own_strip] if first else compress_all.at[at, own_strip],
                compress_all.at[at, own_strip],
                following,
            ),
            post.send(expand if first else expand_all.at[at], expand_all.at[at], following),
            post.send(gains if first else gains_all.at[at], gains_all.at[at], following),
            post.send(named if first else named_all.at[0, i - 1], named_all.at[0, i], following),
            post.send(
                output.at[own_strip] if first else output_all.at[at, own_strip],
                output_all.at[at, own_strip],
                following,
            ),
        ]

    def strip_spread(whole, at):
        def place(index, part=None):
            if part is None:
                where = pl.ds(pl.multiple_of(index * strip, strip), strip)
            else:
                half = strip // 2
                where = pl.ds(pl.multiple_of(index * strip + part * half, half), half)
            return whole.at[at, where]

        return spread(post, place(seq), place, core, across_x, across_y)

    ring = hop(1)
    locals_ = [
        pltpu.make_async_copy(source, target, local_sems.at[n])
        for n, (source, target) in enumerate(
            (
                (hidden, hidden_all.at[seq]),
                (named, named_all.at[0, 0]),
                (gains, gains_all.at[dp]),
                (query, query_all.at[dp]),
                (expand, expand_all.at[dp]),
                (compress, compress_all.at[dp]),
                (output, output_all.at[dp]),
            )
        )
    ]
    for copy in locals_:
        copy.start()
    spreads = []
    for i in (2, 3, 4):
        for copy in ring:
            post.take(copy)
        at = (dp + 5 - i) % 4
        if i < 4:
            ring = hop(i)
        advance(*spreads)
        if i < 4:
            advance(hidden_spread)
        spreads += [strip_spread(compress_all, at), strip_spread(output_all, at)]
        advance(*spreads[-2:])
    locals_[1].wait()
    names_x = post.send(named_all.at[0], named_all.at[1], across_x)
    advance(*spreads)
    post.take(names_x)
    names_y = post.send(named_all.at[pl.ds(0, 2)], named_all.at[pl.ds(2, 2)], across_y)
    advance(*spreads)
    post.take(names_y)
    post.send(named_all.at[pl.ds(0, 4)], named_all.at[pl.ds(4, 4)], core)
    for n, copy in enumerate(locals_):
        if n != 1:
            copy.wait()
    post.finish()


def gather_start(hidden, named, gains, query, expand, compress, output, collective_id):
    anywhere = pl.BlockSpec(memory_space=pl.ANY)
    total = 8 + 6 * 3 + 3 + 2 * 3 * 8
    return pl.pallas_call(
        gather_start_kernel,
        out_shape=[
            jax.ShapeDtypeStruct((8, *hidden.shape), hidden.dtype),
            jax.ShapeDtypeStruct((8, 4, *named.shape), named.dtype),
        ]
        + [jax.ShapeDtypeStruct((4, *x.shape), x.dtype) for x in (gains, query, expand, compress, output)],
        in_specs=[anywhere] * 7,
        out_specs=[anywhere] * 7,
        scratch_shapes=[
            pltpu.SemaphoreType.DMA((total,)),
            pltpu.SemaphoreType.DMA((total,)),
            pltpu.SemaphoreType.DMA((7,)),
        ],
        compiler_params=pltpu.CompilerParams(
            collective_id=collective_id, has_side_effects=True, vmem_limit_bytes=16 * 2**20
        ),
        cost_estimate=pl.CostEstimate(flops=0, bytes_accessed=2**26, transcendentals=0),
    )(hidden, named, gains, query, expand, compress, output)


PADDED_HALF = 768
TILE = 256


def flip(value, change):
    return value + change - 2 * value * change


def pair_of(step, remote):
    if not remote:
        return step
    first = 1 - (step + 15) // 16
    last = (step + 3) // 16
    turn_of, place = (step + 3) // 4 - 1, (step + 3) % 4
    ahead = 1 - (place + 3) // 4
    return (1 - first) * (1 - last) * (4 * turn_of + place + 4 * ahead) + last * step


def experts_kernel(
    remote, capacity, rows_in, place_ref, gate_ref, weight_in_ref, weight_out_ref, shared_in,
    shared_out, rows_all, in_grad_ref, out_grad_ref, hidden_out, units_ref, part_ref,
    shared_in_grad, shared_out_grad, rows_buffer, cot_buffer, weight_in, weight_up, weight_out,
    slot_rows_pair, slot_up_pair, hidden_pair, back_pair, in_grad, out_grad, rows_out, load_sems,
    weight_sems, *sems
):
    step = pl.program_id(0)
    steps = pl.num_programs(0)
    rows = place_ref.shape[2]
    features = weight_in.shape[0]
    pair = pair_of(step, remote)
    slot = step % 2
    half_slots = 2 * capacity
    now = pl.ds(pl.multiple_of(slot * half_slots, half_slots), half_slots)
    slot_rows, slot_up = slot_rows_pair.at[now], slot_up_pair.at[now]
    hidden_ref, back_ref = hidden_pair.at[now], back_pair.at[now]
    gathered = rows_all if remote else rows_in

    def loads(at, into):
        found = []
        for b in range(2):
            block = 2 * pair_of(at, remote) + b
            part = pl.ds(b * rows, rows)
            for kind, buffer in enumerate((rows_buffer, cot_buffer)):
                found.append(
                    pltpu.make_async_copy(
                        gathered.at[block, kind],
                        buffer.at[into, part],
                        load_sems.at[into, 2 * b + kind],
                    )
                )
        return found

    if remote:
        send_sems, recv_sems, own_sem = sems
        core, across_x, across_y, following, previous = neighbours()
        half = rows // 2
        top, bottom = pl.ds(0, half), pl.ds(half, half)

        def copy(index, source, target, device):
            return pltpu.make_async_remote_copy(
                src_ref=source,
                dst_ref=target,
                send_sem=send_sems.at[index],
                recv_sem=recv_sems.at[index],
                device_id=device,
                device_id_type=MESH_ID,
            )

        def block_of(i):
            return rows_in if i == 0 else rows_all.at[8 * i]

        def along(i):
            return copy(9 * i, block_of(i), rows_all.at[8 * i + 8], following)

        def by_x(i):
            return copy(9 * i + 1, block_of(i), rows_all.at[8 * i + 2], across_x)

        def by_y(i):
            return copy(9 * i + 2, block_of(i), rows_all.at[8 * i + 3], across_y)

        def far(i, which):
            if which == 0:
                return copy(
                    9 * i + 3, rows_all.at[8 * i + 2, :, top], rows_all.at[8 * i + 6, :, top], across_y
                )
            return copy(
                9 * i + 4, rows_all.at[8 * i + 3, :, bottom], rows_all.at[8 * i + 6, :, bottom], across_x
            )

        def to_core(i, k):
            source = block_of(i) if k == 0 else rows_all.at[8 * i + OWN_SLOTS[k]]
            return copy(9 * i + 5 + k, source, rows_all.at[8 * i + CORE_SLOTS[k]], core)

        def begin_plane(i):
            by_x(i).start()
            by_y(i).start()

        def plane_arrived(i):
            by_x(i).wait_recv()
            far(i, 0).start()
            to_core(i, 1).start()
            by_y(i).wait_recv()
            far(i, 1).start()
            to_core(i, 2).start()

        def far_arrived(i):
            far(i, 0).wait_recv()
            far(i, 1).wait_recv()
            to_core(i, 3).start()

        def along_arrived(i):
            along(i).wait_recv()
            if i < 2:
                along(i + 1).start()
            to_core(i + 1, 0).start()

        def core_arrived(i, *which):
            for k in which:
                to_core(i, k).wait_recv()

        ready = {
            0: [(core_arrived, 0, 0)],
            1: [(along_arrived, 0), (plane_arrived, 0), (core_arrived, 1, 0)],
            2: [(begin_plane, 1)],
            3: [(core_arrived, 0, 1, 2), (far_arrived, 0)],
            4: [(core_arrived, 0, 3), (along_arrived, 1)],
            5: [(core_arrived, 2, 0), (plane_arrived, 1)],
            6: [(begin_plane, 2)],
            7: [(core_arrived, 1, 1, 2), (far_arrived, 1), (along_arrived, 2)],
            8: [(core_arrived, 1, 3)],
            9: [(core_arrived, 3, 0), (plane_arrived, 2)],
            10: [(begin_plane, 3)],
            11: [(core_arrived, 2, 1, 2), (far_arrived, 2)],
            12: [(core_arrived, 2, 3)],
            13: [(plane_arrived, 3)],
            14: [(core_arrived, 3, 1, 2)],
            15: [(far_arrived, 3), (core_arrived, 3, 3)],
        }

        def prepare(at):
            for event, *given in ready[at]:
                event(*given)

        @pl.when(step == 0)
        def _():
            greet((core, across_x, across_y, following, previous))
            own = pltpu.make_async_copy(rows_in, rows_all.at[0], own_sem)
            own.start()
            along(0).start()
            begin_plane(0)
            to_core(0, 0).start()
            own.wait()

    @pl.when(step == 0)
    def _():
        weights = (
            pltpu.make_async_copy(weight_in_ref, weight_in, weight_sems.at[0]),
            pltpu.make_async_copy(weight_out_ref, weight_out.at[pl.ds(0, HALF)], weight_sems.at[1]),
        )
        for copy_in in weights:
            copy_in.start()
        in_grad[...] = jnp.zeros_like(in_grad)
        out_grad[...] = jnp.zeros_like(out_grad)
        shared_in_grad[...] = jnp.zeros_like(shared_in_grad)
        shared_out_grad[...] = jnp.zeros_like(shared_out_grad)
        weight_out[pl.ds(HALF, PADDED_HALF - HALF)] = jnp.zeros(
            (PADDED_HALF - HALF, features), BF
        )
        for copy_in in weights:
            copy_in.wait()

        def split(k, carry):
            part = pl.ds(pl.multiple_of(k * 128, 128), 128)
            up = weight_in[part, HALF:].astype(F32)
            up = jnp.concatenate([up, jnp.zeros((128, PADDED_HALF - HALF), F32)], axis=1)
            weight_up[part] = up.astype(BF)
            return carry

        lax.fori_loop(0, features // 128, split, 0)
        if remote:
            prepare(0)
        for load in loads(0, 0):
            load.start()

    for load in loads(step, slot):
        load.wait()

    picks = []
    for b in range(2):
        chosen = one_hot(place_ref, 2 * pair + b, capacity)
        pick = chosen.astype(F32)
        picks.append(pick.T.astype(BF))
        pick = pick.astype(BF)
        gates = jnp.sum(jnp.where(chosen, gate_ref[2 * pair + b], 0.0), axis=1, keepdims=True)
        part = pl.ds(b * rows, rows)
        slots = pl.ds(b * capacity, capacity)
        slot_rows[slots] = dot(pick, rows_buffer[slot, part]).astype(BF)
        slot_up[slots] = (dot(pick, cot_buffer[slot, part]) * gates).astype(BF)

    def gated(gate, up, hidden_back):
        sigmoid = 1.0 / (1.0 + jnp.exp(-gate))
        active = gate * sigmoid
        gate_back = hidden_back * up * sigmoid * (1.0 + gate * (1.0 - sigmoid))
        return (active * up).astype(BF), gate_back.astype(BF), (hidden_back * active).astype(BF)

    def hidden_tile(t, carry):
        part = pl.ds(pl.multiple_of(t * TILE, TILE), TILE)
        second = pl.ds(pl.multiple_of(PADDED_HALF + t * TILE, TILE), TILE)
        gate = dot(slot_rows[...], weight_in[:, part])
        up = dot(slot_rows[...], weight_up[:, part])
        hidden_back = dot_nt(slot_up[...], weight_out[part])
        hidden_ref[:, part], back_ref[:, part], back_ref[:, second] = gated(gate, up, hidden_back)
        return carry

    lax.fori_loop(0, PADDED_HALF // TILE, hidden_tile, 0)
    hidden_out[...] = hidden_ref[...]

    width = shared_out.shape[0]
    rows_pair, cot_pair = rows_buffer[slot], cot_buffer[slot]
    gate_up = dot(rows_pair, shared_in[...])
    hidden_back = dot_nt(cot_pair, shared_out[...])
    units, gate_back, up_back = gated(gate_up[:, :width], gate_up[:, width:], hidden_back)
    units_ref[...] = units
    shared_back = jnp.concatenate([gate_back, up_back], axis=1)
    shared_in_grad[...] += dot_tn(shared_back, rows_pair)
    shared_out_grad[...] += dot_tn(units, cot_pair)

    if remote:
        for at in range(1, 16):

            @pl.when(step + 1 == at)
            def _():
                prepare(at)

    @pl.when(step + 1 < steps)
    def _():
        for load in loads(step + 1, 1 - slot):
            load.start()

    def back_tile(t, carry):
        part = pl.ds(pl.multiple_of(t * 2 * TILE, 2 * TILE), 2 * TILE)
        slot_back = dot_nt(back_ref[:, :PADDED_HALF], weight_in[part, :PADDED_HALF])
        slot_back = (slot_back + dot_nt(back_ref[:, PADDED_HALF:], weight_up[part])).astype(BF)
        shared_part = dot_nt(shared_back, shared_in[part])
        for b in range(2):
            tokens = slice(b * rows, (b + 1) * rows)
            total = dot(picks[b], slot_back[b * capacity : (b + 1) * capacity])
            part_ref[b, :, part] = (total + shared_part[tokens]).astype(BF)
        return carry

    lax.fori_loop(0, features // (2 * TILE), back_tile, 0)

    @pl.when(slot == 1)
    def _():
        def in_tile(t, carry):
            part = pl.ds(pl.multiple_of(t * TILE, TILE), TILE)
            in_grad[part] += dot_tn(slot_rows_pair[:, part], back_pair[...])
            return carry

        lax.fori_loop(0, features // TILE, in_tile, 0)

        def out_tile(t, carry):
            part = pl.ds(pl.multiple_of(t * TILE, TILE), TILE)
            out_grad[part] += dot_tn(hidden_pair[:, part], slot_up_pair[...])
            return carry

        lax.fori_loop(0, PADDED_HALF // TILE, out_tile, 0)

    @pl.when(step + 1 == steps)
    def _():
        whole_out = pltpu.make_async_copy(
            out_grad.at[pl.ds(0, HALF)], out_grad_ref, weight_sems.at[0]
        )
        whole_out.start()
        height = rows_out.shape[1]

        def out_copy(k):
            part = pl.ds(pl.multiple_of(k * height, height), height)
            return pltpu.make_async_copy(
                rows_out.at[k % 2], in_grad_ref.at[part], load_sems.at[k % 2, 0]
            )

        def write(k, carry):
            @pl.when(k >= 2)
            def _():
                out_copy(k - 2).wait()

            part = pl.ds(pl.multiple_of(k * height, height), height)
            rows_out[k % 2] = jnp.concatenate(
                [in_grad[part, :HALF], in_grad[part, PADDED_HALF : PADDED_HALF + HALF]], axis=1
            )
            out_copy(k).start()
            return carry

        count = features // height
        lax.fori_loop(0, count, write, 0)
        out_copy(count - 2).wait()
        out_copy(count - 1).wait()
        whole_out.wait()

    if remote:

        @pl.when(step + 1 == steps)
        def _():
            for i in range(4):
                if i < 3:
                    along(i).wait_send()
                by_x(i).wait_send()
                by_y(i).wait_send()
                far(i, 0).wait_send()
                far(i, 1).wait_send()
                for k in range(4):
                    to_core(i, k).wait_send()


def one_hot(place_ref, block, capacity):
    place = place_ref[block]
    rows = place.shape[1]
    return lax.broadcasted_iota(jnp.int32, (capacity, rows), 0) == place


def experts(
    remote, capacity, rows_in, places, gates, weight_in, weight_out, shared_in, shared_out
):
    blocks, _, rows = places.shape
    features = weight_in.shape[0]
    width = shared_out.shape[0]
    steps = blocks // 2

    def whole(array):
        return pl.BlockSpec(
            array.shape, lambda j: (0,) * array.ndim, pipeline_mode=pl.Buffered(1)
        )

    def tiled(height, columns):
        return pl.BlockSpec((height, columns), lambda j: (pair_of(j, remote), 0))

    anywhere = pl.BlockSpec(memory_space=pl.ANY)
    slots = 2 * capacity
    scratch = [
        pltpu.VMEM((2, 2 * rows, features), BF),
        pltpu.VMEM((2, 2 * rows, features), BF),
        pltpu.VMEM(weight_in.shape, BF),
        pltpu.VMEM((features, PADDED_HALF), BF),
        pltpu.VMEM((PADDED_HALF, features), BF),
        pltpu.VMEM((2 * slots, features), BF),
        pltpu.VMEM((2 * slots, features), BF),
        pltpu.VMEM((2 * slots, PADDED_HALF), BF),
        pltpu.VMEM((2 * slots, 2 * PADDED_HALF), BF),
        pltpu.VMEM((features, 2 * PADDED_HALF), F32),
        pltpu.VMEM((PADDED_HALF, features), F32),
        pltpu.VMEM((2, 64, 2 * HALF), F32),
        pltpu.SemaphoreType.DMA((2, 4)),
        pltpu.SemaphoreType.DMA((2,)),
    ]
    if remote:
        scratch += [
            pltpu.SemaphoreType.DMA((36,)),
            pltpu.SemaphoreType.DMA((36,)),
            pltpu.SemaphoreType.DMA,
        ]
    found = pl.pallas_call(
        functools.partial(experts_kernel, remote, capacity),
        grid=(steps,),
        in_specs=[anywhere, whole(places), whole(gates), anywhere, anywhere]
        + [whole(x) for x in (shared_in, shared_out)],
        out_specs=[
            anywhere,
            anywhere,
            anywhere,
            tiled(slots, PADDED_HALF),
            tiled(2 * rows, width),
            pl.BlockSpec((2, rows, features), lambda j: (pair_of(j, remote), 0, 0)),
            pl.BlockSpec(
                (2 * width, features), lambda j: (0, 0), pipeline_mode=pl.Buffered(1)
            ),
            pl.BlockSpec((width, features), lambda j: (0, 0), pipeline_mode=pl.Buffered(1)),
        ],
        out_shape=[
            jax.ShapeDtypeStruct((blocks if remote else 1, 2, rows, features), BF),
            jax.ShapeDtypeStruct(weight_in.shape, F32),
            jax.ShapeDtypeStruct(weight_out.shape, F32),
            jax.ShapeDtypeStruct((steps * slots, PADDED_HALF), BF),
            jax.ShapeDtypeStruct((blocks * rows, width), BF),
            jax.ShapeDtypeStruct((blocks, rows, features), BF),
            jax.ShapeDtypeStruct((2 * width, features), F32),
            jax.ShapeDtypeStruct((width, features), F32),
        ],
        scratch_shapes=scratch,
        compiler_params=pltpu.CompilerParams(
            vmem_limit_bytes=63 * 2**20,
            dimension_semantics=("arbitrary",),
            **({"collective_id": 3, "has_side_effects": True} if remote else {}),
        ),
        cost_estimate=pl.CostEstimate(
            flops=steps * slots * features * 2 * 3 * 2 * PADDED_HALF,
            bytes_accessed=blocks * features * 8 * rows,
            transcendentals=0,
        ),
    )(rows_in, places, gates, weight_in, weight_out, shared_in, shared_out)
    return found


def plane_gather_kernel(in_ref, out_ref, send_sems, recv_sems, local_sem):
    core, across_x, across_y, _, _ = neighbours()
    greet((core, across_x, across_y))
    own = pltpu.make_async_copy(in_ref, out_ref.at[lax.axis_index("seq")], local_sem)
    own.start()
    post = Courier(send_sems, recv_sems)
    for _ in spread(post, in_ref, blocks_of(out_ref), core, across_x, across_y):
        pass
    own.wait()
    post.finish()


def plane_gather(block, collective_id):
    anywhere = pl.BlockSpec(memory_space=pl.ANY)
    return pl.pallas_call(
        plane_gather_kernel,
        out_shape=jax.ShapeDtypeStruct((8, *block.shape), block.dtype),
        in_specs=[anywhere],
        out_specs=anywhere,
        scratch_shapes=[
            pltpu.SemaphoreType.DMA((8,)),
            pltpu.SemaphoreType.DMA((8,)),
            pltpu.SemaphoreType.DMA,
        ],
        compiler_params=pltpu.CompilerParams(
            collective_id=collective_id, has_side_effects=True, vmem_limit_bytes=16 * 2**20
        ),
        cost_estimate=pl.CostEstimate(
            flops=0, bytes_accessed=32 * block.size, transcendentals=0
        ),
    )(block)


def grads_kernel(
    in_ref, columns_ref, latents_ref, out_ref, columns_out, latents_out, total, ring, send_sems,
    recv_sems, local_sems
):
    dp = lax.axis_index("dp")
    seq = lax.axis_index("seq")
    core, across_x, across_y, following, previous = neighbours()
    greet((core, across_x, across_y, following, previous))
    post = Courier(send_sems, recv_sems)
    loads = []
    for n, i in enumerate((1, 2, 3, 0)):
        load = pltpu.make_async_copy(in_ref.at[(dp + 4 - i) % 4], total.at[n], local_sems.at[n])
        load.start()
        loads.append(load)
    loads[0].wait()
    before = post.send(total.at[0], ring.at[0], following)
    spreads = [
        spread(post, source, blocks_of(found), core, across_x, across_y)
        for source, found in ((columns_ref, columns_out), (latents_ref, latents_out))
    ]
    advance(*spreads)
    owns = [
        pltpu.make_async_copy(columns_ref, columns_out.at[seq], local_sems.at[4]),
        pltpu.make_async_copy(latents_ref, latents_out.at[seq], local_sems.at[5]),
    ]
    for own in owns:
        own.start()
    for n in (1, 2, 3):
        loads[n].wait()
        post.take(before)
        accumulate(total.at[n], ring.at[n - 1])
        if n < 3:
            before = post.send(total.at[n], ring.at[n], following)
    owns.append(pltpu.make_async_copy(total.at[3], out_ref.at[seq], local_sems.at[0]))
    owns[2].start()
    spreads.append(spread(post, total.at[3], blocks_of(out_ref), core, across_x, across_y))
    advance(spreads[2])
    advance(*spreads)
    advance(*spreads)
    for own in owns:
        own.wait()
    post.finish()


def sum_grads(parts, columns, latents, collective_id):
    _, rows, width = parts.shape
    anywhere = pl.BlockSpec(memory_space=pl.ANY)
    return pl.pallas_call(
        grads_kernel,
        out_shape=[
            jax.ShapeDtypeStruct((8, rows, width), parts.dtype),
            jax.ShapeDtypeStruct((8, *columns.shape), columns.dtype),
            jax.ShapeDtypeStruct((8, *latents.shape), latents.dtype),
        ],
        in_specs=[anywhere] * 3,
        out_specs=[anywhere] * 3,
        scratch_shapes=[
            pltpu.VMEM((4, rows, width), parts.dtype),
            pltpu.VMEM((3, rows, width), parts.dtype),
            pltpu.SemaphoreType.DMA((27,)),
            pltpu.SemaphoreType.DMA((27,)),
            pltpu.SemaphoreType.DMA((6,)),
        ],
        compiler_params=pltpu.CompilerParams(
            collective_id=collective_id, has_side_effects=True, vmem_limit_bytes=32 * 2**20
        ),
        cost_estimate=pl.CostEstimate(
            flops=0, bytes_accessed=32 * rows * width, transcendentals=0
        ),
    )(parts, columns, latents)


OUT_EVENTS = (3, 5, 7, 9, 13, 17, 18, 23, 27, 30, 31, 31)


def out_terms(capacity, place_ref, gate_ref, hidden_ref, cot_ref, units_ref, weight_ref, shared_ref,
              gate_grad_ref, part_ref):
    features = part_ref.shape[2]
    chosen = one_hot(place_ref, 0, capacity)
    pick = chosen.astype(F32)
    pick, spread_pick = pick.astype(BF), pick.T.astype(BF)
    gates = jnp.sum(jnp.where(chosen, gate_ref[0], 0.0), axis=1, keepdims=True)

    def tile(t, slot_grad):
        part = pl.ds(pl.multiple_of(t * 2 * TILE, 2 * TILE), 2 * TILE)
        result = dot(hidden_ref[:, :HALF], weight_ref[:, part]).astype(BF).astype(F32)
        slot_grad += jnp.sum(result * dot(pick, cot_ref[0, 0, :, part]), axis=1, keepdims=True)
        total = dot(spread_pick, (result * gates).astype(BF)) + dot(units_ref[...], shared_ref[:, part])
        part_ref[0, :, part] = total.astype(BF)
        return slot_grad

    slot_grad = lax.fori_loop(0, features // (2 * TILE), tile, jnp.zeros((capacity, 1), F32))
    gate_grad_ref[0] = jnp.sum(jnp.where(chosen, slot_grad, 0.0), axis=0, keepdims=True)


def out_kernel(remote, capacity, back_ref, shared_ref, *refs):
    step = pl.program_id(0)
    terms, sum_ref, dealt_ref, scratch = refs[:9], refs[9], refs[10], refs[11:]
    if remote:
        *scratch, send_sems, recv_sems, own_sem = scratch
        scatter = ScatterAll(back_ref, *scratch)
        dp = lax.axis_index("dp")
        seq = lax.axis_index("seq")
        own = pltpu.make_async_copy(shared_ref.at[dp], dealt_ref.at[dp], own_sem)

        def deal(r):
            at = (dp + r) % 4
            return pltpu.make_async_remote_copy(
                src_ref=shared_ref.at[at],
                dst_ref=dealt_ref.at[dp],
                send_sem=send_sems.at[r - 1],
                recv_sem=recv_sems.at[r - 1],
                device_id={"dp": at, "seq": seq},
                device_id_type=MESH_ID,
            )

        @pl.when(step == 0)
        def _():
            scatter.begin({"dp": (dp + 2) % 4, "seq": seq})
            own.start()
            for r in range(1, 4):
                deal(r).start()

    out_terms(capacity, *terms)
    if remote:
        events = scatter.events()
        for at in sorted(set(OUT_EVENTS)):

            @pl.when(step == at)
            def _():
                for event, when in zip(events, OUT_EVENTS):
                    if when == at:
                        event()
                if at == OUT_EVENTS[-1]:
                    scatter.finish(sum_ref)
                    own.wait()
                    for r in range(1, 4):
                        deal(r).wait()


def out_side(remote, capacity, back_parts, shared_grad, places, gates, hidden, sent, units, weight_out, shared_out):
    blocks, _, rows = places.shape
    features = sent.shape[-1]
    one = pl.BlockSpec((1, 1, rows), lambda j: (j, 0, 0))

    def tiled(height, columns):
        return pl.BlockSpec((height, columns), lambda j: (j, 0))

    def whole(array):
        return pl.BlockSpec(array.shape, lambda j: (0, 0), pipeline_mode=pl.Buffered(1))

    return pl.pallas_call(
        functools.partial(out_kernel, remote, capacity),
        grid=(blocks,),
        in_specs=[
            pl.BlockSpec(memory_space=pl.ANY),
            pl.BlockSpec(memory_space=pl.ANY),
            one,
            one,
            tiled(capacity, PADDED_HALF),
            pl.BlockSpec((1, 1, rows, features), lambda j: (j, 1, 0, 0)),
            tiled(rows, units.shape[1]),
            whole(weight_out),
            whole(shared_out),
        ],
        out_specs=[
            one,
            pl.BlockSpec((1, rows, features), lambda j: (j, 0, 0)),
            pl.BlockSpec((rows, features), lambda j: (0, 0)),
            pl.BlockSpec(memory_space=pl.ANY),
        ],
        out_shape=[
            jax.ShapeDtypeStruct((blocks, 1, rows), F32),
            jax.ShapeDtypeStruct((blocks, rows, features), BF),
            jax.ShapeDtypeStruct((rows, features), BF),
            jax.ShapeDtypeStruct(shared_grad.shape, BF),
        ],
        scratch_shapes=ScatterAll.scratch(rows, features, BF)
        + [
            pltpu.SemaphoreType.DMA((3,)),
            pltpu.SemaphoreType.DMA((3,)),
            pltpu.SemaphoreType.DMA,
        ]
        if remote
        else [],
        compiler_params=pltpu.CompilerParams(
            vmem_limit_bytes=60 * 2**20,
            dimension_semantics=("arbitrary",),
            **({"collective_id": 4, "has_side_effects": True} if remote else {}),
        ),
        cost_estimate=pl.CostEstimate(
            flops=blocks * 2 * features * (capacity * PADDED_HALF + rows * 2 * capacity),
            bytes_accessed=blocks * features * 2 * (rows + capacity),
            transcendentals=0,
        ),
    )(back_parts, shared_grad, places, gates, hidden, sent, units, weight_out, shared_out)


def swap_halves(values):
    column = lax.broadcasted_iota(jnp.int32, values.shape, 1)
    return jnp.where(column % 64 < 32, pltpu.roll(values, 96, 1), pltpu.roll(values, 32, 1))


def turn(values, cosine, sine, sign):
    column = lax.broadcasted_iota(jnp.int32, values.shape, 1)
    signed = jnp.where(column % 64 < 32, -sign * sine, sign * sine)
    return values * cosine + swap_halves(values) * signed


def project_kernel(
    hidden_ref, gain_ref, query_ref, compress_ref, latent_gain_ref, expand_ref, cosine_ref, sine_ref,
    normed_out, query_out, key_out, value_out, latent_out, latent_normed_out
):
    entries = hidden_ref[...].astype(F32)
    normed = (entries * rms_scale(entries) * gain_ref[...]).astype(BF)
    normed_out[...] = normed
    cosine, sine = cosine_ref[...], sine_ref[...]
    query = dot(normed, query_ref[...])
    nope = query.shape[1] - 128
    query_out[:, :nope] = query[:, :nope].astype(BF)
    query_out[:, nope:] = turn(query[:, nope:], cosine, sine, 1.0).astype(BF)
    compressed = dot(normed, compress_ref[...])
    latent = compressed[:, :LATENT]
    latent_out[...] = latent
    latent_normed = (latent * rms_scale(latent) * latent_gain_ref[...]).astype(BF)
    latent_normed_out[...] = latent_normed
    rotary = compressed[:, LATENT:]
    rotary = jnp.concatenate([rotary, rotary], axis=1)
    expanded = dot(latent_normed, expand_ref[...]).astype(BF)
    key_out[:, :nope] = expanded[:, :nope]
    key_out[:, nope:] = turn(rotary, cosine, sine, 1.0).astype(BF)
    value_out[...] = expanded[:, nope:]


def project(hidden_all, first_gain, query_weight, compress_weight, latent_gain, expand_weight, cosine, sine):
    length, features = hidden_all.shape
    block = 256
    query_width = query_weight.shape[1]
    values = query_width - 128

    def tiled(columns):
        return pl.BlockSpec((block, columns), lambda j: (j, 0))

    def whole(array):
        return pl.BlockSpec(array.shape, lambda j: (0, 0), pipeline_mode=pl.Buffered(1))

    return pl.pallas_call(
        project_kernel,
        grid=(length // block,),
        in_specs=[
            tiled(features),
            whole(first_gain),
            whole(query_weight),
            whole(compress_weight),
            whole(latent_gain),
            whole(expand_weight),
            tiled(128),
            tiled(128),
        ],
        out_specs=[
            tiled(features), tiled(query_width), tiled(query_width), tiled(values), tiled(LATENT),
            tiled(LATENT),
        ],
        out_shape=[
            jax.ShapeDtypeStruct((length, features), BF),
            jax.ShapeDtypeStruct((length, query_width), BF),
            jax.ShapeDtypeStruct((length, query_width), BF),
            jax.ShapeDtypeStruct((length, values), BF),
            jax.ShapeDtypeStruct((length, LATENT), F32),
            jax.ShapeDtypeStruct((length, LATENT), BF),
        ],
        compiler_params=params(48),
        cost_estimate=pl.CostEstimate(
            flops=2 * length * features * (query_width + 640), bytes_accessed=2**25, transcendentals=0
        ),
    )(hidden_all, first_gain, query_weight, compress_weight, latent_gain, expand_weight, cosine, sine)


BLOCK = 512
SCALE = 1.0 / math.sqrt(QK)


def head_keys(key_ref, rotary_ref, part, head):
    rotary = rotary_ref[part]
    column = lax.broadcasted_iota(jnp.int32, rotary.shape, 1)
    rotary = jnp.where(column // 64 == head, rotary.astype(F32), 0.0).astype(BF)
    return jnp.concatenate([key_ref[part], rotary], axis=1)


def masked_scores(query, keys, block, j):
    scores = dot_nt(query, keys) * SCALE
    row = block * BLOCK + lax.broadcasted_iota(jnp.int32, scores.shape, 0)
    column = j * BLOCK + lax.broadcasted_iota(jnp.int32, scores.shape, 1)
    return jnp.where(column <= row, scores, -1e30)


def tile_of(j):
    return pl.ds(pl.multiple_of(j * BLOCK, BLOCK), BLOCK)


def attend_kernel(query_ref, turned_ref, key_ref, rotary_ref, value_ref, out_ref, log_ref, scores_ref):
    head, block = pl.program_id(0), pl.program_id(1)
    query = jnp.concatenate([query_ref[...], turned_ref[...]], axis=1)

    def score(j, largest):
        scores = masked_scores(query, head_keys(key_ref, rotary_ref, tile_of(j), head), block, j)
        scores_ref[j] = scores
        return jnp.maximum(largest, jnp.max(scores, axis=1, keepdims=True))

    largest = lax.fori_loop(0, block + 1, score, jnp.full((BLOCK, 1), -1e30, F32))

    def weigh(j, carry):
        total, found = carry
        weights = jnp.exp(scores_ref[j] - largest)
        total += jnp.sum(weights, axis=1, keepdims=True)
        return total, found + dot(weights.astype(BF), value_ref[tile_of(j)])

    total, found = lax.fori_loop(
        0, block + 1, weigh, (jnp.zeros((BLOCK, 1), F32), jnp.zeros((BLOCK, VDIM), F32))
    )
    out_ref[...] = (found / total).astype(BF)
    log_ref[0] = jnp.broadcast_to(largest + jnp.log(total), (BLOCK, 128))


def attention_specs(length, heads):
    return [
        pl.BlockSpec((BLOCK, 128), lambda h, b: (b, h)),
        pl.BlockSpec((BLOCK, 128), lambda h, b: (b, heads)),
        pl.BlockSpec((length, 128), lambda h, b: (0, h)),
        pl.BlockSpec((length, 128), lambda h, b: (0, heads)),
        pl.BlockSpec((length, VDIM), lambda h, b: (0, h)),
    ]


def attend(queries, keys, values):
    length = queries.shape[0]
    heads = values.shape[1] // VDIM
    blocks = length // BLOCK
    return pl.pallas_call(
        attend_kernel,
        grid=(heads, blocks),
        in_specs=attention_specs(length, heads),
        out_specs=[
            pl.BlockSpec((BLOCK, VDIM), lambda h, b: (b, h)),
            pl.BlockSpec((1, BLOCK, 128), lambda h, b: (h, b, 0)),
        ],
        out_shape=[
            jax.ShapeDtypeStruct((length, heads * VDIM), BF),
            jax.ShapeDtypeStruct((heads, length, 128), F32),
        ],
        scratch_shapes=[pltpu.VMEM((blocks, BLOCK, BLOCK), F32)],
        compiler_params=pltpu.CompilerParams(
            vmem_limit_bytes=40 * 2**20, dimension_semantics=("arbitrary", "arbitrary")
        ),
        cost_estimate=pl.CostEstimate(
            flops=heads * length * length * 384, bytes_accessed=2**23, transcendentals=0
        ),
    )(queries, queries, keys, keys, values)


BACK_EVENTS = (0, 1, 1, 2, 3, 4, 4, 5, 6, 6, 7, 7)


def attend_back_kernel(
    remote, query_ref, turned_ref, key_ref, rotary_ref, value_ref, upstream_ref, log_ref, cosine_ref,
    sine_ref, parts_ref, query_back, turned_back, key_back, rotary_back, value_back, sum_ref,
    shares_ref, slopes_ref, key_sum, value_sum, *scratch
):
    head, block = pl.program_id(0), pl.program_id(1)
    heads, blocks = pl.num_programs(0), pl.num_programs(1)
    step = head * blocks + block
    if remote:
        scatter = ScatterAll(parts_ref, *scratch)
        pl.when(step == 0)(scatter.begin)
    query = jnp.concatenate([query_ref[...], turned_ref[...]], axis=1)
    upstream = upstream_ref[...]
    log_row = log_ref[0][:, :1]

    @pl.when(block == 0)
    def _():
        key_sum[...] = jnp.zeros_like(key_sum)
        value_sum[...] = jnp.zeros_like(value_sum)

    def score(j, centre):
        scores = masked_scores(query, head_keys(key_ref, rotary_ref, tile_of(j), head), block, j)
        shares = jnp.exp(scores - log_row)
        slopes = dot_nt(upstream, value_ref[tile_of(j)])
        shares_ref[j] = shares
        slopes_ref[j] = slopes
        return centre + jnp.sum(shares * slopes, axis=1, keepdims=True)

    centre = lax.fori_loop(0, block + 1, score, jnp.zeros((BLOCK, 1), F32))

    def back(j, found):
        part = tile_of(j)
        shares = shares_ref[j]
        score_back = (shares * (slopes_ref[j] - centre)).astype(BF)
        value_sum[part] += dot_tn(shares.astype(BF), upstream)
        key_sum[part] += dot_tn(score_back, query)
        return found + dot(score_back, head_keys(key_ref, rotary_ref, part, head))

    found = lax.fori_loop(0, block + 1, back, jnp.zeros((BLOCK, 256), F32)) * SCALE
    query_back[...] = found[:, :128].astype(BF)
    turned = found[:, 128:].astype(BF).astype(F32)
    turned_back[...] = turn(turned, cosine_ref[...], sine_ref[...], -1.0).astype(BF)

    @pl.when(block == blocks - 1)
    def _():
        key_back[...] = (key_sum[:, :128] * SCALE).astype(BF)
        value_back[...] = value_sum[...].astype(BF)
        column = lax.broadcasted_iota(jnp.int32, rotary_back.shape, 1)
        rotary = jnp.where(column // 64 == head, key_sum[:, 128:] * SCALE, 0.0).astype(BF)
        rotary_back[...] = jnp.where(head == 0, rotary.astype(F32), rotary_back[...] + rotary.astype(F32))

    if remote:
        events = scatter.events()
        for at in sorted(set(BACK_EVENTS)):

            @pl.when(step == at)
            def _():
                for event, when in zip(events, BACK_EVENTS):
                    if when == at:
                        event()
                if at == BACK_EVENTS[-1]:
                    scatter.finish(sum_ref)


def attend_back(remote, queries, keys, values, upstream, logs, cosine, sine, parts):
    length = queries.shape[0]
    heads = values.shape[1] // VDIM
    blocks = length // BLOCK
    _, rows, features = parts.shape
    row = pl.BlockSpec((BLOCK, 128), lambda h, b: (b, 0))
    return pl.pallas_call(
        functools.partial(attend_back_kernel, remote),
        grid=(heads, blocks),
        in_specs=attention_specs(length, heads)
        + [
            pl.BlockSpec((BLOCK, VDIM), lambda h, b: (b, h)),
            pl.BlockSpec((1, BLOCK, 128), lambda h, b: (h, b, 0)),
            row,
            row,
            pl.BlockSpec(memory_space=pl.ANY),
        ],
        out_specs=[
            pl.BlockSpec((BLOCK, 128), lambda h, b: (b, h)),
            pl.BlockSpec((BLOCK, 128), lambda h, b: (b, h)),
            pl.BlockSpec((length, 128), lambda h, b: (0, h)),
            pl.BlockSpec((length, 128), lambda h, b: (0, 0)),
            pl.BlockSpec((length, VDIM), lambda h, b: (0, h)),
            pl.BlockSpec((rows, features), lambda h, b: (0, 0)),
        ],
        out_shape=[
            jax.ShapeDtypeStruct((length, heads * 128), BF),
            jax.ShapeDtypeStruct((length, heads * 128), BF),
            jax.ShapeDtypeStruct((length, heads * 128), BF),
            jax.ShapeDtypeStruct((length, 128), F32),
            jax.ShapeDtypeStruct((length, heads * VDIM), BF),
            jax.ShapeDtypeStruct((rows, features), BF),
        ],
        scratch_shapes=[
            pltpu.VMEM((blocks, BLOCK, BLOCK), F32),
            pltpu.VMEM((blocks, BLOCK, BLOCK), F32),
            pltpu.VMEM((length, 256), F32),
            pltpu.VMEM((length, VDIM), F32),
        ]
        + (ScatterAll.scratch(rows, features, BF) if remote else []),
        compiler_params=pltpu.CompilerParams(
            vmem_limit_bytes=62 * 2**20,
            dimension_semantics=("arbitrary", "arbitrary"),
            **({"collective_id": 8, "has_side_effects": True} if remote else {}),
        ),
        cost_estimate=pl.CostEstimate(
            flops=heads * length * length * 1024, bytes_accessed=2**26, transcendentals=0
        ),
    )(queries, queries, keys, keys, values, upstream, logs, cosine, sine, parts)


def partial_kernel(
    query_ref, turned_ref, key_ref, value_ref, rotary_ref, query_weight, expand_weight, out_ref
):
    nope = query_ref.shape[1]
    features = query_weight.shape[0]
    out_ref[:, :features] = (
        dot_nt(query_ref[...], query_weight[:, :nope])
        + dot_nt(turned_ref[...], query_weight[:, nope:])
    ).astype(BF)
    out_ref[:, features : features + LATENT] = (
        dot_nt(key_ref[...], expand_weight[:, :nope])
        + dot_nt(value_ref[...], expand_weight[:, nope:])
    ).astype(BF)
    rotary = rotary_ref[...]
    out_ref[:, features + LATENT :] = (rotary + pltpu.roll(rotary, ROPE, 1)).astype(BF)


def partial_terms(rows, query_back, turned_back, key_back, value_back, rotary_sum, query_weight, expand_weight):
    length = query_back.shape[0]
    columns = query_weight.shape[0] + LATENT + 128

    def tiled(array):
        return pl.BlockSpec((rows, array.shape[1]), lambda j: (j, 0))

    def whole(array):
        return pl.BlockSpec(array.shape, lambda j: (0, 0))

    given = (query_back, turned_back, key_back, value_back, rotary_sum)
    return pl.pallas_call(
        partial_kernel,
        grid=(length // rows,),
        in_specs=[tiled(x) for x in given] + [whole(query_weight), whole(expand_weight)],
        out_specs=pl.BlockSpec((rows, columns), lambda j: (j, 0)),
        out_shape=jax.ShapeDtypeStruct((length, columns), BF),
        compiler_params=params(40),
        cost_estimate=pl.CostEstimate(
            flops=2 * length * columns * 384, bytes_accessed=2**24, transcendentals=0
        ),
    )(*given, query_weight, expand_weight)


def tie_kernel(in_ref, _, out_ref):
    out_ref[...] = in_ref[...]


def tie(array, other):
    return pl.pallas_call(
        tie_kernel,
        in_specs=[pl.BlockSpec(memory_space=pltpu.VMEM), pl.BlockSpec(memory_space=pl.ANY)],
        out_specs=pl.BlockSpec(memory_space=pltpu.VMEM),
        out_shape=jax.ShapeDtypeStruct(array.shape, array.dtype),
        compiler_params=pltpu.CompilerParams(vmem_limit_bytes=16 * 2**20),
        cost_estimate=pl.CostEstimate(flops=0, bytes_accessed=4 * array.size, transcendentals=0),
    )(array, other)


def tail_scatter_kernel(
    in_ref, columns_ref, latents_ref, out_ref, columns_out, latents_out, held, far, near, stage,
    columns_total, columns_ring, latents_total, latents_ring, send_sems, recv_sems, local_sems
):
    core, across_x, across_y, following, previous = neighbours()
    greet((core, across_x, across_y, following, previous))
    dp = lax.axis_index("dp")
    seq = lax.axis_index("seq")
    rows = out_ref.shape[0]
    top, bottom = pl.ds(0, rows // 2), pl.ds(rows // 2, rows // 2)
    post = Courier(send_sems, recv_sems)
    x_seq = seq + 2 - 4 * ((seq // 2) % 2)
    y_seq = seq + 4 - 8 * (seq // 4)
    xy_seq = x_seq + 4 - 8 * (seq // 4)
    core_step = 1 - 2 * (seq % 2)
    sums = (
        (columns_ref, columns_total, columns_ring, columns_out),
        (latents_ref, latents_total, latents_ring, latents_out),
    )
    ring_loads = {}
    for n, i in enumerate(SCATTER_ORDER):
        for m, (source, total, _, _) in enumerate(sums):
            load = pltpu.make_async_copy(
                source.at[(dp + 4 - i) % 4], total.at[n], local_sems.at[4 + 2 * n + m]
            )
            load.start()
            ring_loads[n, m] = load
    loads, arriving, hops = {}, {}, {}
    for k, place in ((3, xy_seq), (1, x_seq), (2, y_seq), (0, seq)):
        arriving[k] = post.send(in_ref.at[place + core_step], held.at[k], core)
        loads[k] = pltpu.make_async_copy(in_ref.at[place], stage.at[k], local_sems.at[k])
        loads[k].start()

    def ring_step(n):
        for m, (_, total, ring, out) in enumerate(sums):
            ring_loads[n, m].wait()
            if n > 0:
                post.take(hops[n - 1, m])
                accumulate(total.at[n], ring.at[n - 1])
            if n < 3:
                hops[n, m] = post.send(total.at[n], ring.at[n], following)
            else:
                out[...] = total[3]

    def join(k):
        loads[k].wait()
        post.take(arriving[k])
        accumulate(held.at[k], stage.at[k])

    ring_step(0)
    join(3)
    far_top = post.send(held.at[3, top], far.at[0], across_y)
    far_bottom = post.send(held.at[3, bottom], far.at[1], across_x)
    join(1)
    x_bottom = post.send(held.at[1, bottom], near.at[0, bottom], across_x)
    join(2)
    y_top = post.send(held.at[2, top], near.at[1, top], across_y)
    join(0)
    post.take(far_top)
    accumulate(held.at[1, top], far.at[0])
    x_top = post.send(held.at[1, top], near.at[0, top], across_x)
    post.take(far_bottom)
    accumulate(held.at[2, bottom], far.at[1])
    y_bottom = post.send(held.at[2, bottom], near.at[1, bottom], across_y)
    ring_step(1)
    ring_step(2)
    for copy in (x_bottom, y_top, x_top, y_bottom):
        post.take(copy)
    accumulate(held.at[0], near.at[0], near.at[1])
    out_ref[...] = held[0]
    ring_step(3)
    post.finish()


def tail_scatter(parts, columns, latents, collective_id):
    _, rows, width = parts.shape
    anywhere = pl.BlockSpec(memory_space=pl.ANY)
    here = pl.BlockSpec(memory_space=pltpu.VMEM)
    return pl.pallas_call(
        tail_scatter_kernel,
        out_shape=[
            jax.ShapeDtypeStruct((rows, width), BF),
            jax.ShapeDtypeStruct(columns.shape[1:], BF),
            jax.ShapeDtypeStruct(latents.shape[1:], BF),
        ],
        in_specs=[anywhere] * 3,
        out_specs=[here] * 3,
        scratch_shapes=[
            pltpu.VMEM((4, rows, width), BF),
            pltpu.VMEM((2, rows // 2, width), BF),
            pltpu.VMEM((2, rows, width), BF),
            pltpu.VMEM((4, rows, width), BF),
            pltpu.VMEM(columns.shape, BF),
            pltpu.VMEM((3, *columns.shape[1:]), BF),
            pltpu.VMEM(latents.shape, BF),
            pltpu.VMEM((3, *latents.shape[1:]), BF),
            pltpu.SemaphoreType.DMA((16,)),
            pltpu.SemaphoreType.DMA((16,)),
            pltpu.SemaphoreType.DMA((12,)),
        ],
        compiler_params=pltpu.CompilerParams(
            collective_id=collective_id, has_side_effects=True, vmem_limit_bytes=48 * 2**20
        ),
        cost_estimate=pl.CostEstimate(flops=0, bytes_accessed=2**25, transcendentals=0),
    )(parts, columns, latents)


def chosen_columns(source, target):
    return jnp.where(source == target, 1.0, 0.0).astype(BF)


def layout_kernel(width, columns_ref, latents_ref, small_ref, query_out, expand_out, output_out, small_out):
    step = pl.program_id(0)
    query = columns_ref[0, :, : 3 * 128]
    row = lax.broadcasted_iota(jnp.int32, (3 * 128, 3 * 128), 0)
    column = lax.broadcasted_iota(jnp.int32, (3 * 128, 3 * 128), 1)
    head = jnp.where(column < QK, 0, 1)
    entry = column - QK * head
    source = jnp.where(entry < NOPE, NOPE * head + entry, 2 * NOPE + ROPE * head + entry - NOPE)
    query_out[...] = dot(query, chosen_columns(row, source))
    for part, place in enumerate((0, 2, 1, 3)):
        expand_out[:, 128 * place : 128 * place + 128] = latents_ref[
            0, :, 128 * part : 128 * part + 128
        ].astype(F32)
    output_out[...] = columns_ref[0, :, 3 * 128 :].astype(F32)
    row = lax.broadcasted_iota(jnp.int32, (128, small_out.shape[1]), 0)
    column = lax.broadcasted_iota(jnp.int32, (128, small_out.shape[1]), 1)
    place = jnp.where(row < width, row + width * step, -1)
    small = dot(small_ref[0], chosen_columns(place, column))

    @pl.when(step == 0)
    def _():
        small_out[...] = small

    @pl.when(step > 0)
    def _():
        small_out[...] += small


def layout_grads(columns, latents, small, width):
    count, shard, _ = columns.shape
    latent_shard = latents.shape[1]

    def given(array):
        return pl.BlockSpec((1, *array.shape[1:]), lambda j: (j, 0, 0))

    def made(rows, size):
        return pl.BlockSpec((rows, size), lambda j: (0, j))

    return pl.pallas_call(
        functools.partial(layout_kernel, width),
        grid=(count,),
        in_specs=[given(columns), given(latents), given(small)],
        out_specs=[
            made(shard, 384), made(latent_shard, 512), made(shard, 256),
            pl.BlockSpec((shard, count * width), lambda j: (0, 0)),
        ],
        out_shape=[
            jax.ShapeDtypeStruct((shard, count * 384), F32),
            jax.ShapeDtypeStruct((latent_shard, count * 512), F32),
            jax.ShapeDtypeStruct((shard, count * 256), F32),
            jax.ShapeDtypeStruct((shard, count * width), F32),
        ],
        compiler_params=params(32),
        cost_estimate=pl.CostEstimate(
            flops=2 * count * shard * 384 * 384, bytes_accessed=2**25, transcendentals=0
        ),
    )(columns, latents, small)


def shared_layout_kernel(units, in_ref, out_ref):
    n_seq, n_dp, both, _ = in_ref.shape
    row = lax.broadcasted_iota(jnp.int32, (both, 128), 0) - units * pl.program_id(1)
    column = lax.broadcasted_iota(jnp.int32, (both, 128), 1)
    inside = (row >= 0) & (row < units)
    for t in range(out_ref.shape[1] // 128):
        start = 128 * t
        total = None
        for device in range(start // units, min((start + 127) // units, n_seq * n_dp - 1) + 1):
            place = jnp.where(inside, row + (device * units - start), -1)
            piece = dot_tn(in_ref[device % n_seq, device // n_seq], chosen_columns(place, column))
            total = piece if total is None else total + piece
        out_ref[:, start : start + 128] = total


def shared_layout(found, units):
    n_seq, n_dp, both, shard = found.shape
    rows = min(256, shard)
    return pl.pallas_call(
        functools.partial(shared_layout_kernel, units),
        grid=(shard // rows, 2),
        in_specs=[pl.BlockSpec((n_seq, n_dp, both, rows), lambda r, g: (0, 0, 0, r))],
        out_specs=pl.BlockSpec((rows, SH_FF), lambda r, g: (r, g)),
        out_shape=jax.ShapeDtypeStruct((shard, 2 * SH_FF), F32),
        compiler_params=pltpu.CompilerParams(
            vmem_limit_bytes=60 * 2**20, dimension_semantics=("arbitrary", "arbitrary")
        ),
        cost_estimate=pl.CostEstimate(
            flops=2**32, bytes_accessed=2 * found.size + 8 * shard * SH_FF, transcendentals=0
        ),
    )(found)


def outer_kernel(left_ref, right_ref, out_ref):
    out_ref[...] = dot_tn(left_ref[0], right_ref[...]).astype(BF)


def outer(left, right, size):
    parts, tokens, columns = left.shape
    features = parts * columns
    last = right.shape[1] // size - 1
    return pl.pallas_call(
        outer_kernel,
        grid=(parts,),
        in_specs=[
            pl.BlockSpec((1, tokens, columns), lambda j: (j, 0, 0)),
            pl.BlockSpec((tokens, size), lambda j: (0, last)),
        ],
        out_specs=pl.BlockSpec((columns, size), lambda j: (j, 0)),
        out_shape=jax.ShapeDtypeStruct((features, size), BF),
        compiler_params=params(32),
        cost_estimate=pl.CostEstimate(
            flops=2 * tokens * features * size, bytes_accessed=2 * tokens * features, transcendentals=0
        ),
    )(left, right)


def exchange_kernel(in_ref, out_ref, send_sems, recv_sems, local_sem):
    dp = lax.axis_index("dp")
    seq = lax.axis_index("seq")
    width = in_ref.shape[1] // 8

    def columns(j):
        return in_ref.at[:, pl.ds(pl.multiple_of(j * width, width), width)]

    others = [(seq + r) % 8 for r in range(1, 8)]
    greet([{"dp": dp, "seq": other} for other in others])
    own = pltpu.make_async_copy(columns(seq), out_ref.at[seq], local_sem)
    own.start()
    post = Courier(send_sems, recv_sems)
    for other in others:
        post.send(columns(other), out_ref.at[seq], {"dp": dp, "seq": other})
    own.wait()
    post.finish()


def exchange(array, collective_id):
    rows, columns = array.shape
    anywhere = pl.BlockSpec(memory_space=pl.ANY)
    return pl.pallas_call(
        exchange_kernel,
        out_shape=jax.ShapeDtypeStruct((8, rows, columns // 8), array.dtype),
        in_specs=[anywhere],
        out_specs=anywhere,
        scratch_shapes=[
            pltpu.SemaphoreType.DMA((7,)),
            pltpu.SemaphoreType.DMA((7,)),
            pltpu.SemaphoreType.DMA,
        ],
        compiler_params=pltpu.CompilerParams(
            collective_id=collective_id, has_side_effects=True, vmem_limit_bytes=16 * 2**20
        ),
        cost_estimate=pl.CostEstimate(flops=0, bytes_accessed=4 * array.size, transcendentals=0),
    )(array).reshape(8 * rows, columns // 8)


def on_device(
    hidden_in,
    positions,
    expert_ids,
    gate_weights,
    attention_gain,
    w_query,
    w_compress,
    latent_gain,
    w_expand,
    w_output,
    feedforward_gain,
    w_shared_in,
    w_shared_out,
    w_expert_in,
    w_expert_out,
    cotangent,
):
    n_dp = lax.axis_size("dp")
    n_seq = lax.axis_size("seq")
    n_all = n_dp * n_seq
    fast = (n_dp, n_seq) == (4, 8)
    both = ("dp", "seq")
    dp_index = lax.axis_index("dp")
    seq_index = lax.axis_index("seq")
    sequence_count, rows, features = hidden_in.shape
    rows = sequence_count * rows
    length = rows * n_seq
    heads = HEADS // n_seq
    shard = features // n_dp
    expert_count = n_all // 2
    capacity = max(2, rows * TOP * 5 // (expert_count * 3))
    capacity = (capacity + 15) // 16 * 16
    units = SH_FF // n_all
    padded_units = (units + 127) // 128 * 128
    expand_width = heads * (NOPE + VDIM)

    hidden = hidden_in.reshape(rows, features)
    upstream_rows = cotangent.reshape(rows, features)
    upstream_float = upstream_rows.astype(F32)
    id_rows = expert_ids.reshape(rows, TOP)
    gate_table = gate_weights.reshape(rows, TOP)

    gains_own = jnp.concatenate([attention_gain, feedforward_gain, latent_gain])
    named_own = jnp.concatenate(
        [id_rows.T.astype(F32), gate_table.T, positions.reshape(1, rows).astype(F32)]
    )
    query_width = heads * NOPE + 128
    query_part = lax.dynamic_slice_in_dim(w_query, seq_index * heads * QK, heads * QK, 1)
    query_part = query_part.reshape(shard, heads, QK)
    query_part = jnp.concatenate(
        [
            query_part[..., :NOPE].reshape(shard, -1),
            query_part[..., NOPE:].reshape(shard, -1),
            jnp.zeros((shard, 128 - heads * ROPE), BF),
        ],
        axis=1,
    )
    expand_part = lax.dynamic_slice_in_dim(w_expand, seq_index * expand_width, expand_width, 1)
    expand_part = expand_part.reshape(-1, heads, NOPE + VDIM)
    expand_part = jnp.concatenate(
        [part.reshape(-1, heads * NOPE) for part in jnp.split(expand_part, 2, axis=-1)], axis=1
    )
    if fast:
        named_own = jnp.pad(named_own, ((0, 16 - named_own.shape[0]), (0, 0)))
        gains_size = gains_own.shape[0]
        gains_own = jnp.pad(gains_own, (0, 2048 - gains_size)).reshape(16, 128)
        (
            hidden_all, named_all, gains, query_weight, expand_weight, compress_weight,
            output_weight,
        ) = gather_start(
            hidden, named_own, gains_own, query_part, expand_part, w_compress, w_output, 1
        )
        gains = gains.reshape(n_dp, 2048)[:, :gains_size]
        dp_places = (dp_index - jnp.arange(n_dp)) % n_dp
        slot_of_seq = small_take([0, 1, 2, 4, 3, 5, 6, 7], seq_index ^ jnp.arange(n_seq))
        named_all = jnp.stack([named_all[k] for k in (0, 4, 1, 2, 5, 6, 3, 7)])
        positions_all = reorder(named_all[:, 0, 2 * TOP], slot_of_seq)
        named_all = named_all.swapaxes(0, 1).reshape(n_all, 16, rows)
    else:
        hidden_all = lax.all_gather(hidden, "seq", axis=0)
        named_all = lax.all_gather(named_own, both, axis=0)
        positions_all = lax.dynamic_slice_in_dim(named_all, dp_index * n_seq, n_seq, 0)[:, 2 * TOP]
        gains = lax.all_gather(gains_own, "dp", axis=0)
        query_weight = lax.all_gather(query_part, "dp", axis=0)
        expand_weight = lax.all_gather(expand_part, "dp", axis=0)
        compress_weight = lax.all_gather(w_compress, "dp", axis=0)
        output_weight = lax.all_gather(w_output, "dp", axis=0)
    hidden_all = hidden_all.reshape(length, features)
    query_weight = query_weight.reshape(features, query_width)
    expand_weight = expand_weight.reshape(LATENT, expand_width)
    compress_weight = compress_weight.reshape(features, LATENT + ROPE)
    gains = gains.astype(F32)
    first_gain = gains[:, :shard].reshape(features)
    second_gain = gains[:, shard : 2 * shard].reshape(features)
    latent_gain_row = gains[:, 2 * shard :].reshape(LATENT)
    output_weight = output_weight.reshape(HEADS * VDIM, features)
    shared_part = jnp.stack(
        [
            jnp.stack(
                [
                    lax.dynamic_slice_in_dim(
                        w_shared_in, half * SH_FF + (z * n_seq + seq_index) * units, units, 1
                    )
                    for half in range(2)
                ],
                axis=1,
            )
            for z in range(n_dp)
        ]
    )
    shared_in = lax.all_to_all(
        shared_part, "dp", split_axis=0, concat_axis=0, tiled=True
    ).reshape(features, 2, units)
    pad = padded_units - units
    shared_in = jnp.pad(shared_in, ((0, 0), (0, 0), (0, pad))).reshape(features, 2 * padded_units)
    shared_out = lax.dynamic_slice_in_dim(w_shared_out, seq_index * units, units, 0)
    shared_out = jnp.pad(shared_out, ((0, pad), (0, 0)))
    weight_in, weight_out = w_expert_in[0], w_expert_out[0]
    expert = (dp_index * n_seq + seq_index) // 2
    named = named_all[:, :TOP] == expert.astype(F32)
    chosen = jnp.any(named, axis=1)
    gate_rows = jnp.sum(jnp.where(named, named_all[:, TOP : 2 * TOP], 0.0), axis=1)[:, None]
    before = (jnp.arange(rows)[:, None] < jnp.arange(rows)[None, :]).astype(BF)
    place = dot(chosen.astype(BF), before).astype(jnp.int32)
    place = jnp.where(chosen, place, -1)[:, None]

    angles = rotary_angles(positions_all.reshape(length))
    angles = jnp.concatenate([angles] * 4, axis=1)
    cosine_all, sine_all = jnp.cos(angles), jnp.sin(angles)
    normed_all, queries, keys_all, values_all, latent, latent_normed = project(
        hidden_all, first_gain[None], query_weight, compress_weight, latent_gain_row[None],
        expand_weight, cosine_all, sine_all,
    )
    attended_heads, logs = attend(queries, keys_all, values_all)
    if fast:
        attended_all = plane_gather(attended_heads, 9)
        attended = lax.dynamic_slice_in_dim(attended_all, seq_index * rows, rows, 1)
        attended = attended.swapaxes(0, 1).reshape(rows, HEADS * VDIM)
    else:
        attended_all = lax.all_gather(attended_heads, "seq", axis=0)
        attended = lax.all_to_all(
            attended_heads, "seq", split_axis=0, concat_axis=1, tiled=True
        )
    hidden_float = hidden.astype(F32)
    middle = hidden_float + dot(attended, output_weight)
    second_scale = rms_scale(middle)
    moe_rows = (middle * second_scale * second_gain).astype(BF)

    sent = jnp.stack([moe_rows, upstream_rows])
    if not fast:
        sent = lax.all_gather(sent, both, axis=0)
    (
        sent_all, expert_in_grad, expert_out_grad, hidden_units, shared_units, back_parts,
        shared_in_grad, shared_out_grad,
    ) = experts(
        fast, capacity, sent, place, gate_rows, weight_in, weight_out, shared_in, shared_out
    )
    shared_in_grad = shared_in_grad.reshape(2, padded_units, n_dp, shard)[:, :units].astype(BF)
    shared_in_grad = shared_in_grad.reshape(2 * units, n_dp, shard).swapaxes(0, 1)
    gate_grads, out_parts, moe_back, shared_dealt = out_side(
        fast, capacity, back_parts, shared_in_grad, place, gate_rows, hidden_units, sent_all if fast else sent, shared_units,
        weight_out, shared_out,
    )
    if fast:
        gate_grads = reorder(gate_grads.reshape(n_dp, n_seq, rows), dp_places)
        gate_grads = reorder(gate_grads.swapaxes(0, 1), slot_of_seq).swapaxes(0, 1)
        gate_grads = gate_grads.reshape(n_all, 1, rows)
    else:
        moe_back = lax.psum_scatter(
            back_parts.reshape(n_all * rows, features), both, scatter_dimension=0, tiled=True
        )
    moe_back = moe_back.astype(F32)
    gate_grads = lax.all_to_all(gate_grads, both, split_axis=0, concat_axis=0, tiled=True)
    gate_grads = jnp.sum(gate_grads.reshape(expert_count, 2, rows), axis=1)
    gate_gradient = jnp.sum(
        jnp.where(
            id_rows[:, :, None] == jnp.arange(expert_count, dtype=jnp.int32),
            gate_grads.T[:, None, :],
            0.0,
        ),
        axis=-1,
    )
    second_gain_grad = jnp.sum(moe_back * middle * second_scale, axis=0)
    middle_back = upstream_float + norm_backward(moe_back, middle, second_scale, second_gain)
    middle_low = middle_back.astype(BF)
    attended_back = dot_nt(middle_low, output_weight).astype(BF)
    part = features // n_seq
    packed = jnp.concatenate(
        [attended_back.reshape(rows, n_seq, -1), middle_low.reshape(rows, n_seq, part)], axis=2
    ).reshape(rows, -1)
    if fast:
        packed = exchange(packed, 10)
    else:
        packed = lax.all_to_all(packed, "seq", split_axis=1, concat_axis=0, tiled=True)
    output_grad = outer(attended_all, packed, part)

    query_back, turned_back, key_back, rotary_sum, value_back, out_sum = attend_back(
        fast, queries, keys_all, values_all, packed, logs, cosine_all, sine_all, out_parts
    )
    if not fast:
        out_sum = lax.psum_scatter(
            out_parts.reshape(n_all * rows, features), both, scatter_dimension=0, tiled=True
        )
    block_out = (middle + out_sum.astype(F32)).astype(BF)
    turned_back = sum(turned_back[:, 128 * h : 128 * h + 128] for h in range(heads))
    query_raw_back = jnp.concatenate([query_back, turned_back], axis=1)
    expanded_back = jnp.concatenate([key_back, value_back], axis=1)
    partial_back = partial_terms(
        rows, query_back, turned_back, key_back, value_back, rotary_sum, query_weight, expand_weight
    )
    query_grad = dot_tn(normed_all, query_raw_back).astype(BF)
    expand_grad = dot_tn(latent_normed, expanded_back).astype(BF)
    if fast:
        column_grads = jnp.concatenate([query_grad, output_grad], axis=1)
        summed_back, column_grads, latent_grads = tail_scatter(
            partial_back.reshape(n_seq, rows, -1),
            column_grads.reshape(n_dp, shard, -1),
            expand_grad.reshape(n_dp, LATENT // n_dp, -1),
            5,
        )
    else:
        summed_back = lax.psum_scatter(partial_back, "seq", scatter_dimension=0, tiled=True)
    summed_back = summed_back[:, : features + LATENT + ROPE].astype(F32)
    latent_normed_back = summed_back[:, features : features + LATENT]
    own = seq_index * rows

    def mine(array):
        return lax.dynamic_slice_in_dim(array, own, rows, 0)

    latent_own = mine(latent)
    latent_scale_own = rms_scale(latent_own)
    latent_gain_grad = jnp.sum(latent_normed_back * latent_own * latent_scale_own, axis=0)
    latent_back = norm_backward(latent_normed_back, latent_own, latent_scale_own, latent_gain_row)
    half_turn = ROPE // 2
    rotary_back = rotate(
        summed_back[:, features + LATENT :],
        mine(cosine_all)[:, :half_turn],
        -mine(sine_all)[:, :half_turn],
    )
    compressed_back = jnp.concatenate([latent_back, rotary_back], axis=-1).astype(BF)
    width = (LATENT + ROPE) // n_seq
    if fast:
        compressed_back_all = plane_gather(jnp.pad(compressed_back, ((0, 0), (0, 64))), 6)
        compressed_back_all = compressed_back_all[:, :, : LATENT + ROPE]
    else:
        compressed_back_all = lax.all_gather(compressed_back, "seq", axis=0)
    compressed_back_all = compressed_back_all.reshape(length, LATENT + ROPE)
    compress_grad = dot_tn(
        normed_all, lax.dynamic_slice_in_dim(compressed_back_all, seq_index * width, width, 1)
    )
    normed_back = summed_back[:, :features] + dot_nt(compressed_back, compress_weight)
    first_scale = rms_scale(hidden_float)
    first_gain_grad = jnp.sum(normed_back * hidden_float * first_scale, axis=0)
    hidden_gradient = (
        middle_back + norm_backward(normed_back, hidden_float, first_scale, first_gain)
    ).astype(BF)

    gain_grads = jnp.concatenate([first_gain_grad, second_gain_grad, latent_gain_grad])
    bit = 1
    while bit < n_seq:
        gain_grads = gain_grads + lax.ppermute(
            gain_grads, "seq", [(i, i ^ bit) for i in range(n_seq)]
        )
        bit *= 2
    bit = 1
    while bit < n_dp:
        gain_grads = gain_grads + lax.ppermute(
            gain_grads, "dp", [(i, i ^ bit) for i in range(n_dp)]
        )
        bit *= 2
    latent_shard = LATENT // n_dp

    def gain_part(start, size):
        return lax.dynamic_slice_in_dim(gain_grads, start + dp_index * size, size, 0)

    def over_dp(grad):
        total = lax.psum_scatter(grad, "dp", scatter_dimension=0, tiled=True)
        return lax.all_gather(total.astype(BF), "seq", axis=0)

    def in_heads(found, first, second):
        height, cut = found.shape[1], heads * first
        found = jnp.concatenate(
            [
                found[:, :, :cut].reshape(n_seq, height, heads, first),
                found[:, :, cut : cut + heads * second].reshape(n_seq, height, heads, second),
            ],
            axis=-1,
        )
        return found.transpose(1, 0, 2, 3).reshape(height, -1).astype(F32)

    def columns(found):
        return found.transpose(1, 0, 2).reshape(found.shape[1], -1).astype(F32)

    if fast:
        compress_grad = jnp.pad(compress_grad.astype(BF), ((0, 0), (0, 128 - width)))
        small_grads, column_grads, latent_grads = sum_grads(
            compress_grad.reshape(n_dp, shard, 128), column_grads, latent_grads, 7
        )
        query_out, expand_out, output_out, compress_out = layout_grads(
            column_grads, latent_grads, small_grads, width
        )
    else:
        query_out = in_heads(over_dp(query_grad), NOPE, ROPE)
        expand_out = in_heads(over_dp(expand_grad), NOPE, VDIM)
        output_out = columns(over_dp(output_grad))
        compress_out = columns(over_dp(compress_grad))
    if not fast:
        shared_dealt = lax.all_to_all(
            shared_in_grad, "dp", split_axis=0, concat_axis=0, tiled=True
        )
    shared_in_out = lax.all_gather(tie(shared_dealt, query_back), "seq", axis=0)
    shared_in_out = shared_layout(shared_in_out, units)
    shared_out_out = lax.all_gather(
        shared_out_grad[:units].astype(BF), "seq", axis=0, tiled=True
    ).astype(F32)
    return (
        block_out.reshape(hidden_in.shape),
        hidden_gradient.reshape(hidden_in.shape),
        gate_gradient.reshape(gate_weights.shape),
        gain_part(0, shard),
        query_out,
        compress_out,
        gain_part(2 * features, latent_shard),
        expand_out,
        output_out,
        gain_part(features, shard),
        shared_in_out,
        shared_out_out,
        expert_in_grad[None],
        expert_out_grad[None],
    )


def solution(mesh):
    token = P("dp", "seq", None)
    row = P("dp", None)
    half = P(("dp", "seq"), None, None)
    return jax.shard_map(
        on_device,
        mesh=mesh,
        in_specs=(
            token, P("dp", "seq"), token, token, P("dp"), row, row, P("dp"), row, row,
            P("dp"), row, row, half, half, token,
        ),
        out_specs=(
            token, token, token, P("dp"), row, row, P("dp"), row, row, P("dp"), row, row,
            half, half,
        ),
        check_vma=False,
    )
```

```python
import functools
import math

import jax
import jax.numpy as jnp
from jax import lax
from jax.experimental import pallas as pl
from jax.experimental.pallas import tpu as pltpu
from jax.sharding import PartitionSpec as P

HEADS = 16
NOPE = 128
ROPE = 64
VDIM = 128
LATENT = 512
TOP = 6
QK = 192
SH_FF = 2816
HALF = 704
EPSILON = 1e-06
BF = jnp.bfloat16
F32 = jnp.float32


def rms_scale(entries):
    return lax.rsqrt(jnp.mean(entries * entries, axis=-1, keepdims=True) + EPSILON)


def rotary_angles(position_rows):
    steps_index = jnp.arange(ROPE // 2, dtype=F32)
    frequency = 10000.0 ** (-2.0 * steps_index / ROPE)
    return position_rows.astype(F32)[..., None] * frequency


def rotate(values, cosine_values, sine_values):
    half_width = values.shape[-1] // 2
    front_half = values[..., :half_width]
    back_half = values[..., half_width:]
    return jnp.concatenate(
        [
            front_half * cosine_values - back_half * sine_values,
            front_half * sine_values + back_half * cosine_values,
        ],
        axis=-1,
    )


def norm_backward(upstream, entries, inverse_scale, gain_row):
    scaled = upstream * gain_row
    return inverse_scale * scaled - entries * inverse_scale**3 * jnp.mean(
        scaled * entries, axis=-1, keepdims=True
    )


def dot(a, b):
    return jnp.dot(a, b, preferred_element_type=F32)


def dot_nt(a, b):
    return jnp.einsum("ik,jk->ij", a, b, preferred_element_type=F32)


def dot_tn(a, b):
    return jnp.einsum("ki,kj->ij", a, b, preferred_element_type=F32)


def copy_kernel(places_ref, in_ref, out_ref):
    out_ref[...] = in_ref[...]


def reorder(stack, places):
    count = stack.shape[0]
    if stack.size * stack.dtype.itemsize < 2**20 or stack.ndim != 3:
        return jnp.stack(
            [lax.dynamic_index_in_dim(stack, places[j], 0, keepdims=False) for j in range(count)]
        )
    block = (1, *stack.shape[1:])
    return pl.pallas_call(
        copy_kernel,
        grid_spec=pltpu.PrefetchScalarGridSpec(
            num_scalar_prefetch=1,
            grid=(count,),
            in_specs=[pl.BlockSpec(block, lambda j, order: (order[j], 0, 0))],
            out_specs=pl.BlockSpec(block, lambda j, order: (j, 0, 0)),
        ),
        out_shape=jax.ShapeDtypeStruct(stack.shape, stack.dtype),
        compiler_params=params(40),
        cost_estimate=pl.CostEstimate(
            flops=0, bytes_accessed=2 * stack.size * stack.dtype.itemsize, transcendentals=0
        ),
    )(places.astype(jnp.int32), stack)


def small_take(table, index):
    table = jnp.array(table, jnp.int32)
    hit = index[:, None] == jnp.arange(table.shape[0])[None, :]
    return jnp.sum(jnp.where(hit, table[None, :], 0), axis=1)


def params(limit=60):
    return pltpu.CompilerParams(
        vmem_limit_bytes=limit * 2**20, dimension_semantics=("arbitrary",)
    )


MESH_ID = pl.DeviceIdType.MESH
OWN_SLOTS = (0, 2, 3, 6)
CORE_SLOTS = (1, 4, 5, 7)


def neighbours():
    dp = lax.axis_index("dp")
    seq = lax.axis_index("seq")
    core = {"dp": dp, "seq": seq + 1 - 2 * (seq % 2)}
    across_x = {"dp": dp, "seq": seq + 2 - 4 * ((seq // 2) % 2)}
    across_y = {"dp": dp, "seq": seq + 4 - 8 * (seq // 4)}
    following = {"dp": (dp + 1) % 4, "seq": seq}
    previous = {"dp": (dp + 3) % 4, "seq": seq}
    return core, across_x, across_y, following, previous


def greet(devices):
    barrier = pltpu.get_barrier_semaphore()
    for device in devices:
        pl.semaphore_signal(barrier, inc=1, device_id=device, device_id_type=MESH_ID)
    pl.semaphore_wait(barrier, len(devices))


class Courier:
    def __init__(self, send_sems, recv_sems):
        self.send_sems, self.recv_sems = send_sems, recv_sems
        self.sent, self.open = [], []

    def send(self, source, target, device):
        index = len(self.sent)
        copy = pltpu.make_async_remote_copy(
            src_ref=source,
            dst_ref=target,
            send_sem=self.send_sems.at[index],
            recv_sem=self.recv_sems.at[index],
            device_id=device,
            device_id_type=MESH_ID,
        )
        copy.start()
        self.sent.append(copy)
        self.open.append(copy)
        return copy

    def take(self, copy):
        copy.wait_recv()
        self.open = [other for other in self.open if other is not copy]

    def finish(self):
        for copy in list(self.open):
            self.take(copy)
        for copy in self.sent:
            copy.wait_send()


def accumulate(target, *sources):
    rows = target.shape[0]
    step = 16

    def body(k, carry):
        part = pl.ds(pl.multiple_of(k * step, step), step)
        total = target[part].astype(F32)
        for source in sources:
            total = total + source[part].astype(F32)
        target[part] = total.astype(target.dtype)
        return carry

    lax.fori_loop(0, rows // step, body, 0)


SCATTER_ORDER = (1, 2, 3, 0)


class ScatterAll:
    @staticmethod
    def scratch(rows, columns, dtype):
        return [
            pltpu.VMEM((4, 4, rows, columns), dtype),
            pltpu.VMEM((4, 2, rows // 2, columns), dtype),
            pltpu.VMEM((4, 2, rows, columns), dtype),
            pltpu.VMEM((3, rows, columns), dtype),
            pltpu.VMEM((4, rows, columns), dtype),
            pltpu.SemaphoreType.DMA((35,)),
            pltpu.SemaphoreType.DMA((35,)),
            pltpu.SemaphoreType.DMA((4,)),
        ]

    def __init__(self, in_ref, held, far, near, ring, stage, send_sems, recv_sems, local_sems):
        self.in_ref, self.held, self.far, self.near = in_ref, held, far, near
        self.ring, self.stage = ring, stage
        self.send_sems, self.recv_sems, self.local_sems = send_sems, recv_sems, local_sems
        self.core, self.across_x, self.across_y, self.following, self.previous = neighbours()
        rows = held.shape[2]
        self.top, self.bottom = pl.ds(0, rows // 2), pl.ds(rows // 2, rows // 2)

    def copy(self, index, source, target, device):
        return pltpu.make_async_remote_copy(
            src_ref=source,
            dst_ref=target,
            send_sem=self.send_sems.at[index],
            recv_sem=self.recv_sems.at[index],
            device_id=device,
            device_id_type=MESH_ID,
        )

    def to_core(self, i, k):
        source = self.in_ref.at[8 * i + CORE_SLOTS[k]]
        return self.copy(19 + 4 * i + k, source, self.held.at[i, k], self.core)

    def far_copy(self, i, which):
        part = self.bottom if which else self.top
        device = self.across_x if which else self.across_y
        return self.copy(2 * i + which, self.held.at[i, 3, part], self.far.at[i, which], device)

    def near_copy(self, i, which):
        device = self.across_y if which else self.across_x
        return self.copy(8 + 2 * i + which, self.held.at[i, 1 + which], self.near.at[i, which], device)

    def ring_copy(self, n):
        return self.copy(
            16 + n, self.held.at[SCATTER_ORDER[n], 0], self.ring.at[n], self.following
        )

    def loads(self, n):
        i = SCATTER_ORDER[n]
        return [
            pltpu.make_async_copy(
                self.in_ref.at[8 * i + OWN_SLOTS[k]], self.stage.at[k], self.local_sems.at[k]
            )
            for k in range(4)
        ]

    def begin(self, *others):
        greet((self.core, self.across_x, self.across_y, self.following, self.previous, *others))
        for i in SCATTER_ORDER:
            for k in (3, 1, 2, 0):
                self.to_core(i, k).start()
        for load in self.loads(0):
            load.start()

    def first(self, n):
        i = SCATTER_ORDER[n]
        loads = self.loads(n)
        later = self.loads(n + 1) if n < 3 else None
        for k in (3, 1, 2, 0):
            loads[k].wait()
            self.to_core(i, k).wait_recv()
            accumulate(self.held.at[i, k], self.stage.at[k])
            if later:
                later[k].start()
            if k == 3:
                self.far_copy(i, 0).start()
                self.far_copy(i, 1).start()

    def second(self, n):
        i = SCATTER_ORDER[n]
        self.far_copy(i, 0).wait_recv()
        accumulate(self.held.at[i, 1, self.top], self.far.at[i, 0])
        self.near_copy(i, 0).start()
        self.far_copy(i, 1).wait_recv()
        accumulate(self.held.at[i, 2, self.bottom], self.far.at[i, 1])
        self.near_copy(i, 1).start()

    def third(self, n):
        i = SCATTER_ORDER[n]
        self.near_copy(i, 0).wait_recv()
        self.near_copy(i, 1).wait_recv()
        sources = [self.near.at[i, 0], self.near.at[i, 1]]
        if n > 0:
            self.ring_copy(n - 1).wait_recv()
            sources.append(self.ring.at[n - 1])
        accumulate(self.held.at[i, 0], *sources)
        if n < 3:
            self.ring_copy(n).start()

    def events(self):
        first, second, third = self.first, self.second, self.third
        plan = [
            (first, 0), (first, 1), (second, 0), (first, 2), (second, 1), (third, 0), (first, 3),
            (second, 2), (third, 1), (second, 3), (third, 2), (third, 3),
        ]
        return [functools.partial(f, n) for f, n in plan]

    def finish(self, out_ref):
        out_ref[...] = self.held[0, 0]
        for i in range(4):
            for k in range(4):
                self.to_core(i, k).wait_send()
            for which in range(2):
                self.far_copy(i, which).wait_send()
                self.near_copy(i, which).wait_send()
        for n in range(3):
            self.ring_copy(n).wait_send()


def scatter_all_kernel(in_ref, out_ref, *scratch):
    scatter = ScatterAll(in_ref, *scratch)
    scatter.begin()
    for event in scatter.events():
        event()
    scatter.finish(out_ref)


def scatter_all(parts, collective_id):
    _, rows, columns = parts.shape
    return pl.pallas_call(
        scatter_all_kernel,
        out_shape=jax.ShapeDtypeStruct((rows, columns), parts.dtype),
        in_specs=[pl.BlockSpec(memory_space=pl.ANY)],
        out_specs=pl.BlockSpec(memory_space=pltpu.VMEM),
        scratch_shapes=ScatterAll.scratch(rows, columns, parts.dtype),
        compiler_params=pltpu.CompilerParams(
            collective_id=collective_id, has_side_effects=True, vmem_limit_bytes=56 * 2**20
        ),
        cost_estimate=pl.CostEstimate(
            flops=32 * rows * columns, bytes_accessed=64 * rows * columns * 2, transcendentals=0
        ),
    )(parts)


def spread(post, source, place, core, across_x, across_y):
    seq = lax.axis_index("seq")
    x_seq = seq + 2 - 4 * ((seq // 2) % 2)
    y_seq = seq + 4 - 8 * (seq // 4)
    xy_seq = x_seq + 4 - 8 * (seq // 4)
    x_copy = post.send(source, place(seq), across_x)
    y_copy = post.send(source, place(seq), across_y)
    post.send(source, place(seq), core)
    yield
    post.take(x_copy)
    far_top = post.send(place(x_seq, 0), place(x_seq, 0), across_y)
    post.send(place(x_seq), place(x_seq), core)
    post.take(y_copy)
    far_bottom = post.send(place(y_seq, 1), place(y_seq, 1), across_x)
    post.send(place(y_seq), place(y_seq), core)
    yield
    post.take(far_top)
    post.take(far_bottom)
    post.send(place(xy_seq), place(xy_seq), core)


def blocks_of(found):
    half = found.shape[1] // 2

    def place(index, part=None):
        if part is None:
            return found.at[index]
        return found.at[index, pl.ds(part * half, half)]

    return place


def advance(*spreads):
    for one in spreads:
        for _ in one:
            break


def gather_start_kernel(
    hidden, named, gains, query, expand, compress, output, hidden_all, named_all, gains_all,
    query_all, expand_all, compress_all, output_all, send_sems, recv_sems, local_sems
):
    dp = lax.axis_index("dp")
    seq = lax.axis_index("seq")
    core, across_x, across_y, following, previous = neighbours()
    greet((core, across_x, across_y, following, previous))
    post = Courier(send_sems, recv_sems)
    strip = output.shape[0] // 8
    own_strip = pl.ds(pl.multiple_of(seq * strip, strip), strip)
    hidden_spread = spread(post, hidden, blocks_of(hidden_all), core, across_x, across_y)
    advance(hidden_spread)

    def hop(i):
        at = (dp + 5 - i) % 4
        first = i == 1
        return [
            post.send(query if first else query_all.at[at], query_all.at[at], following),
            post.send(
                compress.at[own_strip] if first else compress_all.at[at, own_strip],
                compress_all.at[at, own_strip],
                following,
            ),
            post.send(expand if first else expand_all.at[at], expand_all.at[at], following),
            post.send(gains if first else gains_all.at[at], gains_all.at[at], following),
            post.send(named if first else named_all.at[0, i - 1], named_all.at[0, i], following),
            post.send(
                output.at[own_strip] if first else output_all.at[at, own_strip],
                output_all.at[at, own_strip],
                following,
            ),
        ]

    def strip_spread(whole, at):
        def place(index, part=None):
            if part is None:
                where = pl.ds(pl.multiple_of(index * strip, strip), strip)
            else:
                half = strip // 2
                where = pl.ds(pl.multiple_of(index * strip + part * half, half), half)
            return whole.at[at, where]

        return spread(post, place(seq), place, core, across_x, across_y)

    ring = hop(1)
    locals_ = [
        pltpu.make_async_copy(source, target, local_sems.at[n])
        for n, (source, target) in enumerate(
            (
                (hidden, hidden_all.at[seq]),
                (named, named_all.at[0, 0]),
                (gains, gains_all.at[dp]),
                (query, query_all.at[dp]),
                (expand, expand_all.at[dp]),
                (compress, compress_all.at[dp]),
                (output, output_all.at[dp]),
            )
        )
    ]
    for copy in locals_:
        copy.start()
    spreads = []
    for i in (2, 3, 4):
        for copy in ring:
            post.take(copy)
        at = (dp + 5 - i) % 4
        if i < 4:
            ring = hop(i)
        advance(*spreads)
        if i < 4:
            advance(hidden_spread)
        spreads += [strip_spread(compress_all, at), strip_spread(output_all, at)]
        advance(*spreads[-2:])
    locals_[1].wait()
    names_x = post.send(named_all.at[0], named_all.at[1], across_x)
    advance(*spreads)
    post.take(names_x)
    names_y = post.send(named_all.at[pl.ds(0, 2)], named_all.at[pl.ds(2, 2)], across_y)
    advance(*spreads)
    post.take(names_y)
    post.send(named_all.at[pl.ds(0, 4)], named_all.at[pl.ds(4, 4)], core)
    for n, copy in enumerate(locals_):
        if n != 1:
            copy.wait()
    post.finish()


def gather_start(hidden, named, gains, query, expand, compress, output, collective_id):
    anywhere = pl.BlockSpec(memory_space=pl.ANY)
    total = 8 + 6 * 3 + 3 + 2 * 3 * 8
    return pl.pallas_call(
        gather_start_kernel,
        out_shape=[
            jax.ShapeDtypeStruct((8, *hidden.shape), hidden.dtype),
            jax.ShapeDtypeStruct((8, 4, *named.shape), named.dtype),
        ]
        + [jax.ShapeDtypeStruct((4, *x.shape), x.dtype) for x in (gains, query, expand, compress, output)],
        in_specs=[anywhere] * 7,
        out_specs=[anywhere] * 7,
        scratch_shapes=[
            pltpu.SemaphoreType.DMA((total,)),
            pltpu.SemaphoreType.DMA((total,)),
            pltpu.SemaphoreType.DMA((7,)),
        ],
        compiler_params=pltpu.CompilerParams(
            collective_id=collective_id, has_side_effects=True, vmem_limit_bytes=16 * 2**20
        ),
        cost_estimate=pl.CostEstimate(flops=0, bytes_accessed=2**26, transcendentals=0),
    )(hidden, named, gains, query, expand, compress, output)


PADDED_HALF = 768
TILE = 256


def flip(value, change):
    return value + change - 2 * value * change


def pair_of(step, remote):
    if not remote:
        return step
    first = 1 - (step + 15) // 16
    last = (step + 3) // 16
    turn_of, place = (step + 3) // 4 - 1, (step + 3) % 4
    ahead = 1 - (place + 3) // 4
    return (1 - first) * (1 - last) * (4 * turn_of + place + 4 * ahead) + last * step


def experts_kernel(
    remote, capacity, rows_in, place_ref, gate_ref, weight_in_ref, weight_out_ref, shared_in,
    shared_out, rows_all, in_grad_ref, out_grad_ref, hidden_out, units_ref, part_ref,
    shared_in_grad, shared_out_grad, rows_buffer, cot_buffer, weight_in, weight_up, weight_out,
    slot_rows_pair, slot_up_pair, hidden_pair, back_pair, in_grad, out_grad, rows_out, load_sems,
    weight_sems, *sems
):
    step = pl.program_id(0)
    steps = pl.num_programs(0)
    rows = place_ref.shape[2]
    features = weight_in.shape[0]
    pair = pair_of(step, remote)
    slot = step % 2
    half_slots = 2 * capacity
    now = pl.ds(pl.multiple_of(slot * half_slots, half_slots), half_slots)
    slot_rows, slot_up = slot_rows_pair.at[now], slot_up_pair.at[now]
    hidden_ref, back_ref = hidden_pair.at[now], back_pair.at[now]
    gathered = rows_all if remote else rows_in

    def loads(at, into):
        found = []
        for b in range(2):
            block = 2 * pair_of(at, remote) + b
            part = pl.ds(b * rows, rows)
            for kind, buffer in enumerate((rows_buffer, cot_buffer)):
                found.append(
                    pltpu.make_async_copy(
                        gathered.at[block, kind],
                        buffer.at[into, part],
                        load_sems.at[into, 2 * b + kind],
                    )
                )
        return found

    if remote:
        send_sems, recv_sems, own_sem = sems
        core, across_x, across_y, following, previous = neighbours()
        half = rows // 2
        top, bottom = pl.ds(0, half), pl.ds(half, half)

        def copy(index, source, target, device):
            return pltpu.make_async_remote_copy(
                src_ref=source,
                dst_ref=target,
                send_sem=send_sems.at[index],
                recv_sem=recv_sems.at[index],
                device_id=device,
                device_id_type=MESH_ID,
            )

        def block_of(i):
            return rows_in if i == 0 else rows_all.at[8 * i]

        def along(i):
            return copy(9 * i, block_of(i), rows_all.at[8 * i + 8], following)

        def by_x(i):
            return copy(9 * i + 1, block_of(i), rows_all.at[8 * i + 2], across_x)

        def by_y(i):
            return copy(9 * i + 2, block_of(i), rows_all.at[8 * i + 3], across_y)

        def far(i, which):
            if which == 0:
                return copy(
                    9 * i + 3, rows_all.at[8 * i + 2, :, top], rows_all.at[8 * i + 6, :, top], across_y
                )
            return copy(
                9 * i + 4, rows_all.at[8 * i + 3, :, bottom], rows_all.at[8 * i + 6, :, bottom], across_x
            )

        def to_core(i, k):
            source = block_of(i) if k == 0 else rows_all.at[8 * i + OWN_SLOTS[k]]
            return copy(9 * i + 5 + k, source, rows_all.at[8 * i + CORE_SLOTS[k]], core)

        def begin_plane(i):
            by_x(i).start()
            by_y(i).start()

        def plane_arrived(i):
            by_x(i).wait_recv()
            far(i, 0).start()
            to_core(i, 1).start()
            by_y(i).wait_recv()
            far(i, 1).start()
            to_core(i, 2).start()

        def far_arrived(i):
            far(i, 0).wait_recv()
            far(i, 1).wait_recv()
            to_core(i, 3).start()

        def along_arrived(i):
            along(i).wait_recv()
            if i < 2:
                along(i + 1).start()
            to_core(i + 1, 0).start()

        def core_arrived(i, *which):
            for k in which:
                to_core(i, k).wait_recv()

        ready = {
            0: [(core_arrived, 0, 0)],
            1: [(along_arrived, 0), (plane_arrived, 0), (core_arrived, 1, 0)],
            2: [(begin_plane, 1)],
            3: [(core_arrived, 0, 1, 2), (far_arrived, 0)],
            4: [(core_arrived, 0, 3), (along_arrived, 1)],
            5: [(core_arrived, 2, 0), (plane_arrived, 1)],
            6: [(begin_plane, 2)],
            7: [(core_arrived, 1, 1, 2), (far_arrived, 1), (along_arrived, 2)],
            8: [(core_arrived, 1, 3)],
            9: [(core_arrived, 3, 0), (plane_arrived, 2)],
            10: [(begin_plane, 3)],
            11: [(core_arrived, 2, 1, 2), (far_arrived, 2)],
            12: [(core_arrived, 2, 3)],
            13: [(plane_arrived, 3)],
            14: [(core_arrived, 3, 1, 2)],
            15: [(far_arrived, 3), (core_arrived, 3, 3)],
        }

        def prepare(at):
            for event, *given in ready[at]:
                event(*given)

        @pl.when(step == 0)
        def _():
            greet((core, across_x, across_y, following, previous))
            own = pltpu.make_async_copy(rows_in, rows_all.at[0], own_sem)
            own.start()
            along(0).start()
            begin_plane(0)
            to_core(0, 0).start()
            own.wait()

    @pl.when(step == 0)
    def _():
        weights = (
            pltpu.make_async_copy(weight_in_ref, weight_in, weight_sems.at[0]),
            pltpu.make_async_copy(weight_out_ref, weight_out.at[pl.ds(0, HALF)], weight_sems.at[1]),
        )
        for copy_in in weights:
            copy_in.start()
        in_grad[...] = jnp.zeros_like(in_grad)
        out_grad[...] = jnp.zeros_like(out_grad)
        shared_in_grad[...] = jnp.zeros_like(shared_in_grad)
        shared_out_grad[...] = jnp.zeros_like(shared_out_grad)
        weight_out[pl.ds(HALF, PADDED_HALF - HALF)] = jnp.zeros(
            (PADDED_HALF - HALF, features), BF
        )
        for copy_in in weights:
            copy_in.wait()

        def split(k, carry):
            part = pl.ds(pl.multiple_of(k * 128, 128), 128)
            up = weight_in[part, HALF:].astype(F32)
            up = jnp.concatenate([up, jnp.zeros((128, PADDED_HALF - HALF), F32)], axis=1)
            weight_up[part] = up.astype(BF)
            return carry

        lax.fori_loop(0, features // 128, split, 0)
        if remote:
            prepare(0)
        for load in loads(0, 0):
            load.start()

    for load in loads(step, slot):
        load.wait()

    picks = []
    for b in range(2):
        chosen = one_hot(place_ref, 2 * pair + b, capacity)
        pick = chosen.astype(F32)
        picks.append(pick.T.astype(BF))
        pick = pick.astype(BF)
        gates = jnp.sum(jnp.where(chosen, gate_ref[2 * pair + b], 0.0), axis=1, keepdims=True)
        part = pl.ds(b * rows, rows)
        slots = pl.ds(b * capacity, capacity)
        slot_rows[slots] = dot(pick, rows_buffer[slot, part]).astype(BF)
        slot_up[slots] = (dot(pick, cot_buffer[slot, part]) * gates).astype(BF)

    def gated(gate, up, hidden_back):
        sigmoid = 1.0 / (1.0 + jnp.exp(-gate))
        active = gate * sigmoid
        gate_back = hidden_back * up * sigmoid * (1.0 + gate * (1.0 - sigmoid))
        return (active * up).astype(BF), gate_back.astype(BF), (hidden_back * active).astype(BF)

    def hidden_tile(t, carry):
        part = pl.ds(pl.multiple_of(t * TILE, TILE), TILE)
        second = pl.ds(pl.multiple_of(PADDED_HALF + t * TILE, TILE), TILE)
        gate = dot(slot_rows[...], weight_in[:, part])
        up = dot(slot_rows[...], weight_up[:, part])
        hidden_back = dot_nt(slot_up[...], weight_out[part])
        hidden_ref[:, part], back_ref[:, part], back_ref[:, second] = gated(gate, up, hidden_back)
        return carry

    lax.fori_loop(0, PADDED_HALF // TILE, hidden_tile, 0)
    hidden_out[...] = hidden_ref[...]

    width = shared_out.shape[0]
    rows_pair, cot_pair = rows_buffer[slot], cot_buffer[slot]
    gate_up = dot(rows_pair, shared_in[...])
    hidden_back = dot_nt(cot_pair, shared_out[...])
    units, gate_back, up_back = gated(gate_up[:, :width], gate_up[:, width:], hidden_back)
    units_ref[...] = units
    shared_back = jnp.concatenate([gate_back, up_back], axis=1)
    shared_in_grad[...] += dot_tn(shared_back, rows_pair)
    shared_out_grad[...] += dot_tn(units, cot_pair)

    if remote:
        for at in range(1, 16):

            @pl.when(step + 1 == at)
            def _():
                prepare(at)

    @pl.when(step + 1 < steps)
    def _():
        for load in loads(step + 1, 1 - slot):
            load.start()

    def back_tile(t, carry):
        part = pl.ds(pl.multiple_of(t * 2 * TILE, 2 * TILE), 2 * TILE)
        slot_back = dot_nt(back_ref[:, :PADDED_HALF], weight_in[part, :PADDED_HALF])
        slot_back = (slot_back + dot_nt(back_ref[:, PADDED_HALF:], weight_up[part])).astype(BF)
        shared_part = dot_nt(shared_back, shared_in[part])
        for b in range(2):
            tokens = slice(b * rows, (b + 1) * rows)
            total = dot(picks[b], slot_back[b * capacity : (b + 1) * capacity])
            part_ref[b, :, part] = (total + shared_part[tokens]).astype(BF)
        return carry

    lax.fori_loop(0, features // (2 * TILE), back_tile, 0)

    @pl.when(slot == 1)
    def _():
        def in_tile(t, carry):
            part = pl.ds(pl.multiple_of(t * TILE, TILE), TILE)
            in_grad[part] += dot_tn(slot_rows_pair[:, part], back_pair[...])
            return carry

        lax.fori_loop(0, features // TILE, in_tile, 0)

        def out_tile(t, carry):
            part = pl.ds(pl.multiple_of(t * TILE, TILE), TILE)
            out_grad[part] += dot_tn(hidden_pair[:, part], slot_up_pair[...])
            return carry

        lax.fori_loop(0, PADDED_HALF // TILE, out_tile, 0)

    @pl.when(step + 1 == steps)
    def _():
        whole_out = pltpu.make_async_copy(
            out_grad.at[pl.ds(0, HALF)], out_grad_ref, weight_sems.at[0]
        )
        whole_out.start()
        height = rows_out.shape[1]

        def out_copy(k):
            part = pl.ds(pl.multiple_of(k * height, height), height)
            return pltpu.make_async_copy(
                rows_out.at[k % 2], in_grad_ref.at[part], load_sems.at[k % 2, 0]
            )

        def write(k, carry):
            @pl.when(k >= 2)
            def _():
                out_copy(k - 2).wait()

            part = pl.ds(pl.multiple_of(k * height, height), height)
            rows_out[k % 2] = jnp.concatenate(
                [in_grad[part, :HALF], in_grad[part, PADDED_HALF : PADDED_HALF + HALF]], axis=1
            )
            out_copy(k).start()
            return carry

        count = features // height
        lax.fori_loop(0, count, write, 0)
        out_copy(count - 2).wait()
        out_copy(count - 1).wait()
        whole_out.wait()

    if remote:

        @pl.when(step + 1 == steps)
        def _():
            for i in range(4):
                if i < 3:
                    along(i).wait_send()
                by_x(i).wait_send()
                by_y(i).wait_send()
                far(i, 0).wait_send()
                far(i, 1).wait_send()
                for k in range(4):
                    to_core(i, k).wait_send()


def one_hot(place_ref, block, capacity):
    place = place_ref[block]
    rows = place.shape[1]
    return lax.broadcasted_iota(jnp.int32, (capacity, rows), 0) == place


def experts(
    remote, capacity, rows_in, places, gates, weight_in, weight_out, shared_in, shared_out
):
    blocks, _, rows = places.shape
    features = weight_in.shape[0]
    width = shared_out.shape[0]
    steps = blocks // 2

    def whole(array):
        return pl.BlockSpec(
            array.shape, lambda j: (0,) * array.ndim, pipeline_mode=pl.Buffered(1)
        )

    def tiled(height, columns):
        return pl.BlockSpec((height, columns), lambda j: (pair_of(j, remote), 0))

    anywhere = pl.BlockSpec(memory_space=pl.ANY)
    slots = 2 * capacity
    scratch = [
        pltpu.VMEM((2, 2 * rows, features), BF),
        pltpu.VMEM((2, 2 * rows, features), BF),
        pltpu.VMEM(weight_in.shape, BF),
        pltpu.VMEM((features, PADDED_HALF), BF),
        pltpu.VMEM((PADDED_HALF, features), BF),
        pltpu.VMEM((2 * slots, features), BF),
        pltpu.VMEM((2 * slots, features), BF),
        pltpu.VMEM((2 * slots, PADDED_HALF), BF),
        pltpu.VMEM((2 * slots, 2 * PADDED_HALF), BF),
        pltpu.VMEM((features, 2 * PADDED_HALF), F32),
        pltpu.VMEM((PADDED_HALF, features), F32),
        pltpu.VMEM((2, 64, 2 * HALF), F32),
        pltpu.SemaphoreType.DMA((2, 4)),
        pltpu.SemaphoreType.DMA((2,)),
    ]
    if remote:
        scratch += [
            pltpu.SemaphoreType.DMA((36,)),
            pltpu.SemaphoreType.DMA((36,)),
            pltpu.SemaphoreType.DMA,
        ]
    found = pl.pallas_call(
        functools.partial(experts_kernel, remote, capacity),
        grid=(steps,),
        in_specs=[anywhere, whole(places), whole(gates), anywhere, anywhere]
        + [whole(x) for x in (shared_in, shared_out)],
        out_specs=[
            anywhere,
            anywhere,
            anywhere,
            tiled(slots, PADDED_HALF),
            tiled(2 * rows, width),
            pl.BlockSpec((2, rows, features), lambda j: (pair_of(j, remote), 0, 0)),
            pl.BlockSpec(
                (2 * width, features), lambda j: (0, 0), pipeline_mode=pl.Buffered(1)
            ),
            pl.BlockSpec((width, features), lambda j: (0, 0), pipeline_mode=pl.Buffered(1)),
        ],
        out_shape=[
            jax.ShapeDtypeStruct((blocks if remote else 1, 2, rows, features), BF),
            jax.ShapeDtypeStruct(weight_in.shape, F32),
            jax.ShapeDtypeStruct(weight_out.shape, F32),
            jax.ShapeDtypeStruct((steps * slots, PADDED_HALF), BF),
            jax.ShapeDtypeStruct((blocks * rows, width), BF),
            jax.ShapeDtypeStruct((blocks, rows, features), BF),
            jax.ShapeDtypeStruct((2 * width, features), F32),
            jax.ShapeDtypeStruct((width, features), F32),
        ],
        scratch_shapes=scratch,
        compiler_params=pltpu.CompilerParams(
            vmem_limit_bytes=63 * 2**20,
            dimension_semantics=("arbitrary",),
            **({"collective_id": 3, "has_side_effects": True} if remote else {}),
        ),
        cost_estimate=pl.CostEstimate(
            flops=steps * slots * features * 2 * 3 * 2 * PADDED_HALF,
            bytes_accessed=blocks * features * 8 * rows,
            transcendentals=0,
        ),
    )(rows_in, places, gates, weight_in, weight_out, shared_in, shared_out)
    return found


def plane_gather_kernel(in_ref, out_ref, send_sems, recv_sems, local_sem):
    core, across_x, across_y, _, _ = neighbours()
    greet((core, across_x, across_y))
    own = pltpu.make_async_copy(in_ref, out_ref.at[lax.axis_index("seq")], local_sem)
    own.start()
    post = Courier(send_sems, recv_sems)
    for _ in spread(post, in_ref, blocks_of(out_ref), core, across_x, across_y):
        pass
    own.wait()
    post.finish()


def plane_gather(block, collective_id):
    anywhere = pl.BlockSpec(memory_space=pl.ANY)
    return pl.pallas_call(
        plane_gather_kernel,
        out_shape=jax.ShapeDtypeStruct((8, *block.shape), block.dtype),
        in_specs=[anywhere],
        out_specs=anywhere,
        scratch_shapes=[
            pltpu.SemaphoreType.DMA((8,)),
            pltpu.SemaphoreType.DMA((8,)),
            pltpu.SemaphoreType.DMA,
        ],
        compiler_params=pltpu.CompilerParams(
            collective_id=collective_id, has_side_effects=True, vmem_limit_bytes=16 * 2**20
        ),
        cost_estimate=pl.CostEstimate(
            flops=0, bytes_accessed=32 * block.size, transcendentals=0
        ),
    )(block)


def grads_kernel(
    in_ref, columns_ref, latents_ref, out_ref, columns_out, latents_out, total, ring, send_sems,
    recv_sems, local_sems
):
    dp = lax.axis_index("dp")
    seq = lax.axis_index("seq")
    core, across_x, across_y, following, previous = neighbours()
    greet((core, across_x, across_y, following, previous))
    post = Courier(send_sems, recv_sems)
    loads = []
    for n, i in enumerate((1, 2, 3, 0)):
        load = pltpu.make_async_copy(in_ref.at[(dp + 4 - i) % 4], total.at[n], local_sems.at[n])
        load.start()
        loads.append(load)
    loads[0].wait()
    before = post.send(total.at[0], ring.at[0], following)
    spreads = [
        spread(post, source, blocks_of(found), core, across_x, across_y)
        for source, found in ((columns_ref, columns_out), (latents_ref, latents_out))
    ]
    advance(*spreads)
    owns = [
        pltpu.make_async_copy(columns_ref, columns_out.at[seq], local_sems.at[4]),
        pltpu.make_async_copy(latents_ref, latents_out.at[seq], local_sems.at[5]),
    ]
    for own in owns:
        own.start()
    for n in (1, 2, 3):
        loads[n].wait()
        post.take(before)
        accumulate(total.at[n], ring.at[n - 1])
        if n < 3:
            before = post.send(total.at[n], ring.at[n], following)
    owns.append(pltpu.make_async_copy(total.at[3], out_ref.at[seq], local_sems.at[0]))
    owns[2].start()
    spreads.append(spread(post, total.at[3], blocks_of(out_ref), core, across_x, across_y))
    advance(spreads[2])
    advance(*spreads)
    advance(*spreads)
    for own in owns:
        own.wait()
    post.finish()


def sum_grads(parts, columns, latents, collective_id):
    _, rows, width = parts.shape
    anywhere = pl.BlockSpec(memory_space=pl.ANY)
    return pl.pallas_call(
        grads_kernel,
        out_shape=[
            jax.ShapeDtypeStruct((8, rows, width), parts.dtype),
            jax.ShapeDtypeStruct((8, *columns.shape), columns.dtype),
            jax.ShapeDtypeStruct((8, *latents.shape), latents.dtype),
        ],
        in_specs=[anywhere] * 3,
        out_specs=[anywhere] * 3,
        scratch_shapes=[
            pltpu.VMEM((4, rows, width), parts.dtype),
            pltpu.VMEM((3, rows, width), parts.dtype),
            pltpu.SemaphoreType.DMA((27,)),
            pltpu.SemaphoreType.DMA((27,)),
            pltpu.SemaphoreType.DMA((6,)),
        ],
        compiler_params=pltpu.CompilerParams(
            collective_id=collective_id, has_side_effects=True, vmem_limit_bytes=32 * 2**20
        ),
        cost_estimate=pl.CostEstimate(
            flops=0, bytes_accessed=32 * rows * width, transcendentals=0
        ),
    )(parts, columns, latents)


OUT_EVENTS = (3, 5, 7, 9, 13, 17, 18, 23, 27, 30, 31, 31)


def out_terms(capacity, place_ref, gate_ref, hidden_ref, cot_ref, units_ref, weight_ref, shared_ref,
              gate_grad_ref, part_ref):
    features = part_ref.shape[2]
    chosen = one_hot(place_ref, 0, capacity)
    pick = chosen.astype(F32)
    pick, spread_pick = pick.astype(BF), pick.T.astype(BF)
    gates = jnp.sum(jnp.where(chosen, gate_ref[0], 0.0), axis=1, keepdims=True)

    def tile(t, slot_grad):
        part = pl.ds(pl.multiple_of(t * 2 * TILE, 2 * TILE), 2 * TILE)
        result = dot(hidden_ref[:, :HALF], weight_ref[:, part]).astype(BF).astype(F32)
        slot_grad += jnp.sum(result * dot(pick, cot_ref[0, 0, :, part]), axis=1, keepdims=True)
        total = dot(spread_pick, (result * gates).astype(BF)) + dot(units_ref[...], shared_ref[:, part])
        part_ref[0, :, part] = total.astype(BF)
        return slot_grad

    slot_grad = lax.fori_loop(0, features // (2 * TILE), tile, jnp.zeros((capacity, 1), F32))
    gate_grad_ref[0] = jnp.sum(jnp.where(chosen, slot_grad, 0.0), axis=0, keepdims=True)


def out_kernel(remote, capacity, back_ref, shared_ref, *refs):
    step = pl.program_id(0)
    terms, sum_ref, dealt_ref, scratch = refs[:9], refs[9], refs[10], refs[11:]
    if remote:
        *scratch, send_sems, recv_sems, own_sem = scratch
        scatter = ScatterAll(back_ref, *scratch)
        dp = lax.axis_index("dp")
        seq = lax.axis_index("seq")
        own = pltpu.make_async_copy(shared_ref.at[dp], dealt_ref.at[dp], own_sem)

        def deal(r):
            at = (dp + r) % 4
            return pltpu.make_async_remote_copy(
                src_ref=shared_ref.at[at],
                dst_ref=dealt_ref.at[dp],
                send_sem=send_sems.at[r - 1],
                recv_sem=recv_sems.at[r - 1],
                device_id={"dp": at, "seq": seq},
                device_id_type=MESH_ID,
            )

        @pl.when(step == 0)
        def _():
            scatter.begin({"dp": (dp + 2) % 4, "seq": seq})
            own.start()
            for r in range(1, 4):
                deal(r).start()

    out_terms(capacity, *terms)
    if remote:
        events = scatter.events()
        for at in sorted(set(OUT_EVENTS)):

            @pl.when(step == at)
            def _():
                for event, when in zip(events, OUT_EVENTS):
                    if when == at:
                        event()
                if at == OUT_EVENTS[-1]:
                    scatter.finish(sum_ref)
                    own.wait()
                    for r in range(1, 4):
                        deal(r).wait()


def out_side(remote, capacity, back_parts, shared_grad, places, gates, hidden, sent, units, weight_out, shared_out):
    blocks, _, rows = places.shape
    features = sent.shape[-1]
    one = pl.BlockSpec((1, 1, rows), lambda j: (j, 0, 0))

    def tiled(height, columns):
        return pl.BlockSpec((height, columns), lambda j: (j, 0))

    def whole(array):
        return pl.BlockSpec(array.shape, lambda j: (0, 0), pipeline_mode=pl.Buffered(1))

    return pl.pallas_call(
        functools.partial(out_kernel, remote, capacity),
        grid=(blocks,),
        in_specs=[
            pl.BlockSpec(memory_space=pl.ANY),
            pl.BlockSpec(memory_space=pl.ANY),
            one,
            one,
            tiled(capacity, PADDED_HALF),
            pl.BlockSpec((1, 1, rows, features), lambda j: (j, 1, 0, 0)),
            tiled(rows, units.shape[1]),
            whole(weight_out),
            whole(shared_out),
        ],
        out_specs=[
            one,
            pl.BlockSpec((1, rows, features), lambda j: (j, 0, 0)),
            pl.BlockSpec((rows, features), lambda j: (0, 0)),
            pl.BlockSpec(memory_space=pl.ANY),
        ],
        out_shape=[
            jax.ShapeDtypeStruct((blocks, 1, rows), F32),
            jax.ShapeDtypeStruct((blocks, rows, features), BF),
            jax.ShapeDtypeStruct((rows, features), BF),
            jax.ShapeDtypeStruct(shared_grad.shape, BF),
        ],
        scratch_shapes=ScatterAll.scratch(rows, features, BF)
        + [
            pltpu.SemaphoreType.DMA((3,)),
            pltpu.SemaphoreType.DMA((3,)),
            pltpu.SemaphoreType.DMA,
        ]
        if remote
        else [],
        compiler_params=pltpu.CompilerParams(
            vmem_limit_bytes=60 * 2**20,
            dimension_semantics=("arbitrary",),
            **({"collective_id": 4, "has_side_effects": True} if remote else {}),
        ),
        cost_estimate=pl.CostEstimate(
            flops=blocks * 2 * features * (capacity * PADDED_HALF + rows * 2 * capacity),
            bytes_accessed=blocks * features * 2 * (rows + capacity),
            transcendentals=0,
        ),
    )(back_parts, shared_grad, places, gates, hidden, sent, units, weight_out, shared_out)


def swap_halves(values):
    column = lax.broadcasted_iota(jnp.int32, values.shape, 1)
    return jnp.where(column % 64 < 32, pltpu.roll(values, 96, 1), pltpu.roll(values, 32, 1))


def turn(values, cosine, sine, sign):
    column = lax.broadcasted_iota(jnp.int32, values.shape, 1)
    signed = jnp.where(column % 64 < 32, -sign * sine, sign * sine)
    return values * cosine + swap_halves(values) * signed


def project_kernel(
    hidden_ref, gain_ref, query_ref, compress_ref, latent_gain_ref, expand_ref, cosine_ref, sine_ref,
    normed_out, query_out, key_out, value_out, latent_out, latent_normed_out
):
    entries = hidden_ref[...].astype(F32)
    normed = (entries * rms_scale(entries) * gain_ref[...]).astype(BF)
    normed_out[...] = normed
    cosine, sine = cosine_ref[...], sine_ref[...]
    query = dot(normed, query_ref[...])
    nope = query.shape[1] - 128
    query_out[:, :nope] = query[:, :nope].astype(BF)
    query_out[:, nope:] = turn(query[:, nope:], cosine, sine, 1.0).astype(BF)
    compressed = dot(normed, compress_ref[...])
    latent = compressed[:, :LATENT]
    latent_out[...] = latent
    latent_normed = (latent * rms_scale(latent) * latent_gain_ref[...]).astype(BF)
    latent_normed_out[...] = latent_normed
    rotary = compressed[:, LATENT:]
    rotary = jnp.concatenate([rotary, rotary], axis=1)
    expanded = dot(latent_normed, expand_ref[...]).astype(BF)
    key_out[:, :nope] = expanded[:, :nope]
    key_out[:, nope:] = turn(rotary, cosine, sine, 1.0).astype(BF)
    value_out[...] = expanded[:, nope:]


def project(hidden_all, first_gain, query_weight, compress_weight, latent_gain, expand_weight, cosine, sine):
    length, features = hidden_all.shape
    block = 256
    query_width = query_weight.shape[1]
    values = query_width - 128

    def tiled(columns):
        return pl.BlockSpec((block, columns), lambda j: (j, 0))

    def whole(array):
        return pl.BlockSpec(array.shape, lambda j: (0, 0), pipeline_mode=pl.Buffered(1))

    return pl.pallas_call(
        project_kernel,
        grid=(length // block,),
        in_specs=[
            tiled(features),
            whole(first_gain),
            whole(query_weight),
            whole(compress_weight),
            whole(latent_gain),
            whole(expand_weight),
            tiled(128),
            tiled(128),
        ],
        out_specs=[
            tiled(features), tiled(query_width), tiled(query_width), tiled(values), tiled(LATENT),
            tiled(LATENT),
        ],
        out_shape=[
            jax.ShapeDtypeStruct((length, features), BF),
            jax.ShapeDtypeStruct((length, query_width), BF),
            jax.ShapeDtypeStruct((length, query_width), BF),
            jax.ShapeDtypeStruct((length, values), BF),
            jax.ShapeDtypeStruct((length, LATENT), F32),
            jax.ShapeDtypeStruct((length, LATENT), BF),
        ],
        compiler_params=params(48),
        cost_estimate=pl.CostEstimate(
            flops=2 * length * features * (query_width + 640), bytes_accessed=2**25, transcendentals=0
        ),
    )(hidden_all, first_gain, query_weight, compress_weight, latent_gain, expand_weight, cosine, sine)


BLOCK = 512
SCALE = 1.0 / math.sqrt(QK)


def head_keys(key_ref, rotary_ref, part, head):
    rotary = rotary_ref[part]
    column = lax.broadcasted_iota(jnp.int32, rotary.shape, 1)
    rotary = jnp.where(column // 64 == head, rotary.astype(F32), 0.0).astype(BF)
    return jnp.concatenate([key_ref[part], rotary], axis=1)


def masked_scores(query, keys, block, j):
    scores = dot_nt(query, keys) * SCALE
    row = block * BLOCK + lax.broadcasted_iota(jnp.int32, scores.shape, 0)
    column = j * BLOCK + lax.broadcasted_iota(jnp.int32, scores.shape, 1)
    return jnp.where(column <= row, scores, -1e30)


def tile_of(j):
    return pl.ds(pl.multiple_of(j * BLOCK, BLOCK), BLOCK)


def attend_kernel(query_ref, turned_ref, key_ref, rotary_ref, value_ref, out_ref, log_ref, scores_ref):
    head, block = pl.program_id(0), pl.program_id(1)
    query = jnp.concatenate([query_ref[...], turned_ref[...]], axis=1)

    def score(j, largest):
        scores = masked_scores(query, head_keys(key_ref, rotary_ref, tile_of(j), head), block, j)
        scores_ref[j] = scores
        return jnp.maximum(largest, jnp.max(scores, axis=1, keepdims=True))

    largest = lax.fori_loop(0, block + 1, score, jnp.full((BLOCK, 1), -1e30, F32))

    def weigh(j, carry):
        total, found = carry
        weights = jnp.exp(scores_ref[j] - largest)
        total += jnp.sum(weights, axis=1, keepdims=True)
        return total, found + dot(weights.astype(BF), value_ref[tile_of(j)])

    total, found = lax.fori_loop(
        0, block + 1, weigh, (jnp.zeros((BLOCK, 1), F32), jnp.zeros((BLOCK, VDIM), F32))
    )
    out_ref[...] = (found / total).astype(BF)
    log_ref[0] = jnp.broadcast_to(largest + jnp.log(total), (BLOCK, 128))


def attention_specs(length, heads):
    return [
        pl.BlockSpec((BLOCK, 128), lambda h, b: (b, h)),
        pl.BlockSpec((BLOCK, 128), lambda h, b: (b, heads)),
        pl.BlockSpec((length, 128), lambda h, b: (0, h)),
        pl.BlockSpec((length, 128), lambda h, b: (0, heads)),
        pl.BlockSpec((length, VDIM), lambda h, b: (0, h)),
    ]


def attend(queries, keys, values):
    length = queries.shape[0]
    heads = values.shape[1] // VDIM
    blocks = length // BLOCK
    return pl.pallas_call(
        attend_kernel,
        grid=(heads, blocks),
        in_specs=attention_specs(length, heads),
        out_specs=[
            pl.BlockSpec((BLOCK, VDIM), lambda h, b: (b, h)),
            pl.BlockSpec((1, BLOCK, 128), lambda h, b: (h, b, 0)),
        ],
        out_shape=[
            jax.ShapeDtypeStruct((length, heads * VDIM), BF),
            jax.ShapeDtypeStruct((heads, length, 128), F32),
        ],
        scratch_shapes=[pltpu.VMEM((blocks, BLOCK, BLOCK), F32)],
        compiler_params=pltpu.CompilerParams(
            vmem_limit_bytes=40 * 2**20, dimension_semantics=("arbitrary", "arbitrary")
        ),
        cost_estimate=pl.CostEstimate(
            flops=heads * length * length * 384, bytes_accessed=2**23, transcendentals=0
        ),
    )(queries, queries, keys, keys, values)


BACK_EVENTS = (0, 1, 1, 2, 3, 4, 4, 5, 6, 6, 7, 7)


def attend_back_kernel(
    remote, query_ref, turned_ref, key_ref, rotary_ref, value_ref, upstream_ref, log_ref, cosine_ref,
    sine_ref, parts_ref, query_back, turned_back, key_back, rotary_back, value_back, sum_ref,
    shares_ref, slopes_ref, key_sum, value_sum, *scratch
):
    head, block = pl.program_id(0), pl.program_id(1)
    heads, blocks = pl.num_programs(0), pl.num_programs(1)
    step = head * blocks + block
    if remote:
        scatter = ScatterAll(parts_ref, *scratch)
        pl.when(step == 0)(scatter.begin)
    query = jnp.concatenate([query_ref[...], turned_ref[...]], axis=1)
    upstream = upstream_ref[...]
    log_row = log_ref[0][:, :1]

    @pl.when(block == 0)
    def _():
        key_sum[...] = jnp.zeros_like(key_sum)
        value_sum[...] = jnp.zeros_like(value_sum)

    def score(j, centre):
        scores = masked_scores(query, head_keys(key_ref, rotary_ref, tile_of(j), head), block, j)
        shares = jnp.exp(scores - log_row)
        slopes = dot_nt(upstream, value_ref[tile_of(j)])
        shares_ref[j] = shares
        slopes_ref[j] = slopes
        return centre + jnp.sum(shares * slopes, axis=1, keepdims=True)

    centre = lax.fori_loop(0, block + 1, score, jnp.zeros((BLOCK, 1), F32))

    def back(j, found):
        part = tile_of(j)
        shares = shares_ref[j]
        score_back = (shares * (slopes_ref[j] - centre)).astype(BF)
        value_sum[part] += dot_tn(shares.astype(BF), upstream)
        key_sum[part] += dot_tn(score_back, query)
        return found + dot(score_back, head_keys(key_ref, rotary_ref, part, head))

    found = lax.fori_loop(0, block + 1, back, jnp.zeros((BLOCK, 256), F32)) * SCALE
    query_back[...] = found[:, :128].astype(BF)
    turned = found[:, 128:].astype(BF).astype(F32)
    turned_back[...] = turn(turned, cosine_ref[...], sine_ref[...], -1.0).astype(BF)

    @pl.when(block == blocks - 1)
    def _():
        key_back[...] = (key_sum[:, :128] * SCALE).astype(BF)
        value_back[...] = value_sum[...].astype(BF)
        column = lax.broadcasted_iota(jnp.int32, rotary_back.shape, 1)
        rotary = jnp.where(column // 64 == head, key_sum[:, 128:] * SCALE, 0.0).astype(BF)
        rotary_back[...] = jnp.where(head == 0, rotary.astype(F32), rotary_back[...] + rotary.astype(F32))

    if remote:
        events = scatter.events()
        for at in sorted(set(BACK_EVENTS)):

            @pl.when(step == at)
            def _():
                for event, when in zip(events, BACK_EVENTS):
                    if when == at:
                        event()
                if at == BACK_EVENTS[-1]:
                    scatter.finish(sum_ref)


def attend_back(remote, queries, keys, values, upstream, logs, cosine, sine, parts):
    length = queries.shape[0]
    heads = values.shape[1] // VDIM
    blocks = length // BLOCK
    _, rows, features = parts.shape
    row = pl.BlockSpec((BLOCK, 128), lambda h, b: (b, 0))
    return pl.pallas_call(
        functools.partial(attend_back_kernel, remote),
        grid=(heads, blocks),
        in_specs=attention_specs(length, heads)
        + [
            pl.BlockSpec((BLOCK, VDIM), lambda h, b: (b, h)),
            pl.BlockSpec((1, BLOCK, 128), lambda h, b: (h, b, 0)),
            row,
            row,
            pl.BlockSpec(memory_space=pl.ANY),
        ],
        out_specs=[
            pl.BlockSpec((BLOCK, 128), lambda h, b: (b, h)),
            pl.BlockSpec((BLOCK, 128), lambda h, b: (b, h)),
            pl.BlockSpec((length, 128), lambda h, b: (0, h)),
            pl.BlockSpec((length, 128), lambda h, b: (0, 0)),
            pl.BlockSpec((length, VDIM), lambda h, b: (0, h)),
            pl.BlockSpec((rows, features), lambda h, b: (0, 0)),
        ],
        out_shape=[
            jax.ShapeDtypeStruct((length, heads * 128), BF),
            jax.ShapeDtypeStruct((length, heads * 128), BF),
            jax.ShapeDtypeStruct((length, heads * 128), BF),
            jax.ShapeDtypeStruct((length, 128), F32),
            jax.ShapeDtypeStruct((length, heads * VDIM), BF),
            jax.ShapeDtypeStruct((rows, features), BF),
        ],
        scratch_shapes=[
            pltpu.VMEM((blocks, BLOCK, BLOCK), F32),
            pltpu.VMEM((blocks, BLOCK, BLOCK), F32),
            pltpu.VMEM((length, 256), F32),
            pltpu.VMEM((length, VDIM), F32),
        ]
        + (ScatterAll.scratch(rows, features, BF) if remote else []),
        compiler_params=pltpu.CompilerParams(
            vmem_limit_bytes=62 * 2**20,
            dimension_semantics=("arbitrary", "arbitrary"),
            **({"collective_id": 8, "has_side_effects": True} if remote else {}),
        ),
        cost_estimate=pl.CostEstimate(
            flops=heads * length * length * 1024, bytes_accessed=2**26, transcendentals=0
        ),
    )(queries, queries, keys, keys, values, upstream, logs, cosine, sine, parts)


def partial_kernel(
    query_ref, turned_ref, key_ref, value_ref, rotary_ref, query_weight, expand_weight, out_ref
):
    nope = query_ref.shape[1]
    features = query_weight.shape[0]
    out_ref[:, :features] = (
        dot_nt(query_ref[...], query_weight[:, :nope])
        + dot_nt(turned_ref[...], query_weight[:, nope:])
    ).astype(BF)
    out_ref[:, features : features + LATENT] = (
        dot_nt(key_ref[...], expand_weight[:, :nope])
        + dot_nt(value_ref[...], expand_weight[:, nope:])
    ).astype(BF)
    rotary = rotary_ref[...]
    out_ref[:, features + LATENT :] = (rotary + pltpu.roll(rotary, ROPE, 1)).astype(BF)


def partial_terms(rows, query_back, turned_back, key_back, value_back, rotary_sum, query_weight, expand_weight):
    length = query_back.shape[0]
    columns = query_weight.shape[0] + LATENT + 128

    def tiled(array):
        return pl.BlockSpec((rows, array.shape[1]), lambda j: (j, 0))

    def whole(array):
        return pl.BlockSpec(array.shape, lambda j: (0, 0))

    given = (query_back, turned_back, key_back, value_back, rotary_sum)
    return pl.pallas_call(
        partial_kernel,
        grid=(length // rows,),
        in_specs=[tiled(x) for x in given] + [whole(query_weight), whole(expand_weight)],
        out_specs=pl.BlockSpec((rows, columns), lambda j: (j, 0)),
        out_shape=jax.ShapeDtypeStruct((length, columns), BF),
        compiler_params=params(40),
        cost_estimate=pl.CostEstimate(
            flops=2 * length * columns * 384, bytes_accessed=2**24, transcendentals=0
        ),
    )(*given, query_weight, expand_weight)


def tie_kernel(in_ref, _, out_ref):
    out_ref[...] = in_ref[...]


def tie(array, other):
    return pl.pallas_call(
        tie_kernel,
        in_specs=[pl.BlockSpec(memory_space=pltpu.VMEM), pl.BlockSpec(memory_space=pl.ANY)],
        out_specs=pl.BlockSpec(memory_space=pltpu.VMEM),
        out_shape=jax.ShapeDtypeStruct(array.shape, array.dtype),
        compiler_params=pltpu.CompilerParams(vmem_limit_bytes=16 * 2**20),
        cost_estimate=pl.CostEstimate(flops=0, bytes_accessed=4 * array.size, transcendentals=0),
    )(array, other)


def tail_scatter_kernel(
    in_ref, columns_ref, latents_ref, out_ref, columns_out, latents_out, held, far, near, stage,
    columns_total, columns_ring, latents_total, latents_ring, send_sems, recv_sems, local_sems
):
    core, across_x, across_y, following, previous = neighbours()
    greet((core, across_x, across_y, following, previous))
    dp = lax.axis_index("dp")
    seq = lax.axis_index("seq")
    rows = out_ref.shape[0]
    top, bottom = pl.ds(0, rows // 2), pl.ds(rows // 2, rows // 2)
    post = Courier(send_sems, recv_sems)
    x_seq = seq + 2 - 4 * ((seq // 2) % 2)
    y_seq = seq + 4 - 8 * (seq // 4)
    xy_seq = x_seq + 4 - 8 * (seq // 4)
    core_step = 1 - 2 * (seq % 2)
    sums = (
        (columns_ref, columns_total, columns_ring, columns_out),
        (latents_ref, latents_total, latents_ring, latents_out),
    )
    ring_loads = {}
    for n, i in enumerate(SCATTER_ORDER):
        for m, (source, total, _, _) in enumerate(sums):
            load = pltpu.make_async_copy(
                source.at[(dp + 4 - i) % 4], total.at[n], local_sems.at[4 + 2 * n + m]
            )
            load.start()
            ring_loads[n, m] = load
    loads, arriving, hops = {}, {}, {}
    for k, place in ((3, xy_seq), (1, x_seq), (2, y_seq), (0, seq)):
        arriving[k] = post.send(in_ref.at[place + core_step], held.at[k], core)
        loads[k] = pltpu.make_async_copy(in_ref.at[place], stage.at[k], local_sems.at[k])
        loads[k].start()

    def ring_step(n):
        for m, (_, total, ring, out) in enumerate(sums):
            ring_loads[n, m].wait()
            if n > 0:
                post.take(hops[n - 1, m])
                accumulate(total.at[n], ring.at[n - 1])
            if n < 3:
                hops[n, m] = post.send(total.at[n], ring.at[n], following)
            else:
                out[...] = total[3]

    def join(k):
        loads[k].wait()
        post.take(arriving[k])
        accumulate(held.at[k], stage.at[k])

    ring_step(0)
    join(3)
    far_top = post.send(held.at[3, top], far.at[0], across_y)
    far_bottom = post.send(held.at[3, bottom], far.at[1], across_x)
    join(1)
    x_bottom = post.send(held.at[1, bottom], near.at[0, bottom], across_x)
    join(2)
    y_top = post.send(held.at[2, top], near.at[1, top], across_y)
    join(0)
    post.take(far_top)
    accumulate(held.at[1, top], far.at[0])
    x_top = post.send(held.at[1, top], near.at[0, top], across_x)
    post.take(far_bottom)
    accumulate(held.at[2, bottom], far.at[1])
    y_bottom = post.send(held.at[2, bottom], near.at[1, bottom], across_y)
    ring_step(1)
    ring_step(2)
    for copy in (x_bottom, y_top, x_top, y_bottom):
        post.take(copy)
    accumulate(held.at[0], near.at[0], near.at[1])
    out_ref[...] = held[0]
    ring_step(3)
    post.finish()


def tail_scatter(parts, columns, latents, collective_id):
    _, rows, width = parts.shape
    anywhere = pl.BlockSpec(memory_space=pl.ANY)
    here = pl.BlockSpec(memory_space=pltpu.VMEM)
    return pl.pallas_call(
        tail_scatter_kernel,
        out_shape=[
            jax.ShapeDtypeStruct((rows, width), BF),
            jax.ShapeDtypeStruct(columns.shape[1:], BF),
            jax.ShapeDtypeStruct(latents.shape[1:], BF),
        ],
        in_specs=[anywhere] * 3,
        out_specs=[here] * 3,
        scratch_shapes=[
            pltpu.VMEM((4, rows, width), BF),
            pltpu.VMEM((2, rows // 2, width), BF),
            pltpu.VMEM((2, rows, width), BF),
            pltpu.VMEM((4, rows, width), BF),
            pltpu.VMEM(columns.shape, BF),
            pltpu.VMEM((3, *columns.shape[1:]), BF),
            pltpu.VMEM(latents.shape, BF),
            pltpu.VMEM((3, *latents.shape[1:]), BF),
            pltpu.SemaphoreType.DMA((16,)),
            pltpu.SemaphoreType.DMA((16,)),
            pltpu.SemaphoreType.DMA((12,)),
        ],
        compiler_params=pltpu.CompilerParams(
            collective_id=collective_id, has_side_effects=True, vmem_limit_bytes=48 * 2**20
        ),
        cost_estimate=pl.CostEstimate(flops=0, bytes_accessed=2**25, transcendentals=0),
    )(parts, columns, latents)


def chosen_columns(source, target):
    return jnp.where(source == target, 1.0, 0.0).astype(BF)


def layout_kernel(width, columns_ref, latents_ref, small_ref, query_out, expand_out, output_out, small_out):
    step = pl.program_id(0)
    query = columns_ref[0, :, : 3 * 128]
    row = lax.broadcasted_iota(jnp.int32, (3 * 128, 3 * 128), 0)
    column = lax.broadcasted_iota(jnp.int32, (3 * 128, 3 * 128), 1)
    head = jnp.where(column < QK, 0, 1)
    entry = column - QK * head
    source = jnp.where(entry < NOPE, NOPE * head + entry, 2 * NOPE + ROPE * head + entry - NOPE)
    query_out[...] = dot(query, chosen_columns(row, source))
    for part, place in enumerate((0, 2, 1, 3)):
        expand_out[:, 128 * place : 128 * place + 128] = latents_ref[
            0, :, 128 * part : 128 * part + 128
        ].astype(F32)
    output_out[...] = columns_ref[0, :, 3 * 128 :].astype(F32)
    row = lax.broadcasted_iota(jnp.int32, (128, small_out.shape[1]), 0)
    column = lax.broadcasted_iota(jnp.int32, (128, small_out.shape[1]), 1)
    place = jnp.where(row < width, row + width * step, -1)
    small = dot(small_ref[0], chosen_columns(place, column))

    @pl.when(step == 0)
    def _():
        small_out[...] = small

    @pl.when(step > 0)
    def _():
        small_out[...] += small


def layout_grads(columns, latents, small, width):
    count, shard, _ = columns.shape
    latent_shard = latents.shape[1]

    def given(array):
        return pl.BlockSpec((1, *array.shape[1:]), lambda j: (j, 0, 0))

    def made(rows, size):
        return pl.BlockSpec((rows, size), lambda j: (0, j))

    return pl.pallas_call(
        functools.partial(layout_kernel, width),
        grid=(count,),
        in_specs=[given(columns), given(latents), given(small)],
        out_specs=[
            made(shard, 384), made(latent_shard, 512), made(shard, 256),
            pl.BlockSpec((shard, count * width), lambda j: (0, 0)),
        ],
        out_shape=[
            jax.ShapeDtypeStruct((shard, count * 384), F32),
            jax.ShapeDtypeStruct((latent_shard, count * 512), F32),
            jax.ShapeDtypeStruct((shard, count * 256), F32),
            jax.ShapeDtypeStruct((shard, count * width), F32),
        ],
        compiler_params=params(32),
        cost_estimate=pl.CostEstimate(
            flops=2 * count * shard * 384 * 384, bytes_accessed=2**25, transcendentals=0
        ),
    )(columns, latents, small)


def shared_layout_kernel(units, in_ref, out_ref):
    n_seq, n_dp, both, _ = in_ref.shape
    row = lax.broadcasted_iota(jnp.int32, (both, 128), 0) - units * pl.program_id(1)
    column = lax.broadcasted_iota(jnp.int32, (both, 128), 1)
    inside = (row >= 0) & (row < units)
    for t in range(out_ref.shape[1] // 128):
        start = 128 * t
        total = None
        for device in range(start // units, min((start + 127) // units, n_seq * n_dp - 1) + 1):
            place = jnp.where(inside, row + (device * units - start), -1)
            piece = dot_tn(in_ref[device % n_seq, device // n_seq], chosen_columns(place, column))
            total = piece if total is None else total + piece
        out_ref[:, start : start + 128] = total


def shared_layout(found, units):
    n_seq, n_dp, both, shard = found.shape
    rows = min(256, shard)
    return pl.pallas_call(
        functools.partial(shared_layout_kernel, units),
        grid=(shard // rows, 2),
        in_specs=[pl.BlockSpec((n_seq, n_dp, both, rows), lambda r, g: (0, 0, 0, r))],
        out_specs=pl.BlockSpec((rows, SH_FF), lambda r, g: (r, g)),
        out_shape=jax.ShapeDtypeStruct((shard, 2 * SH_FF), F32),
        compiler_params=pltpu.CompilerParams(
            vmem_limit_bytes=60 * 2**20, dimension_semantics=("arbitrary", "arbitrary")
        ),
        cost_estimate=pl.CostEstimate(
            flops=2**32, bytes_accessed=2 * found.size + 8 * shard * SH_FF, transcendentals=0
        ),
    )(found)


def outer_kernel(left_ref, right_ref, out_ref):
    out_ref[...] = dot_tn(left_ref[0], right_ref[...]).astype(BF)


def outer(left, right, size):
    parts, tokens, columns = left.shape
    features = parts * columns
    last = right.shape[1] // size - 1
    return pl.pallas_call(
        outer_kernel,
        grid=(parts,),
        in_specs=[
            pl.BlockSpec((1, tokens, columns), lambda j: (j, 0, 0)),
            pl.BlockSpec((tokens, size), lambda j: (0, last)),
        ],
        out_specs=pl.BlockSpec((columns, size), lambda j: (j, 0)),
        out_shape=jax.ShapeDtypeStruct((features, size), BF),
        compiler_params=params(32),
        cost_estimate=pl.CostEstimate(
            flops=2 * tokens * features * size, bytes_accessed=2 * tokens * features, transcendentals=0
        ),
    )(left, right)


def column_kernel(normed_ref, query_ref, left_ref, right_ref, out_ref):
    size = query_ref.shape[1]
    out_ref[:, :size] = dot_tn(normed_ref[...], query_ref[...]).astype(BF)
    out_ref[:, size:] = dot_tn(left_ref[0], right_ref[...]).astype(BF)


def column_terms(normed, query_back, left, right, size):
    parts, tokens, columns = left.shape
    last = right.shape[1] // size - 1
    width = query_back.shape[1] + size
    return pl.pallas_call(
        column_kernel,
        grid=(parts,),
        in_specs=[
            pl.BlockSpec((tokens, columns), lambda j: (0, j)),
            pl.BlockSpec(query_back.shape, lambda j: (0, 0)),
            pl.BlockSpec((1, tokens, columns), lambda j: (j, 0, 0)),
            pl.BlockSpec((tokens, size), lambda j: (0, last)),
        ],
        out_specs=pl.BlockSpec((columns, width), lambda j: (j, 0)),
        out_shape=jax.ShapeDtypeStruct((parts * columns, width), BF),
        compiler_params=params(48),
        cost_estimate=pl.CostEstimate(
            flops=2 * tokens * parts * columns * width, bytes_accessed=2**24, transcendentals=0
        ),
    )(normed, query_back, left, right)


def exchange_kernel(in_ref, out_ref, send_sems, recv_sems, local_sem):
    dp = lax.axis_index("dp")
    seq = lax.axis_index("seq")
    width = in_ref.shape[1] // 8

    def columns(j):
        return in_ref.at[:, pl.ds(pl.multiple_of(j * width, width), width)]

    others = [(seq + r) % 8 for r in range(1, 8)]
    greet([{"dp": dp, "seq": other} for other in others])
    own = pltpu.make_async_copy(columns(seq), out_ref.at[seq], local_sem)
    own.start()
    post = Courier(send_sems, recv_sems)
    for other in others:
        post.send(columns(other), out_ref.at[seq], {"dp": dp, "seq": other})
    own.wait()
    post.finish()


def exchange(array, collective_id):
    rows, columns = array.shape
    anywhere = pl.BlockSpec(memory_space=pl.ANY)
    return pl.pallas_call(
        exchange_kernel,
        out_shape=jax.ShapeDtypeStruct((8, rows, columns // 8), array.dtype),
        in_specs=[anywhere],
        out_specs=anywhere,
        scratch_shapes=[
            pltpu.SemaphoreType.DMA((7,)),
            pltpu.SemaphoreType.DMA((7,)),
            pltpu.SemaphoreType.DMA,
        ],
        compiler_params=pltpu.CompilerParams(
            collective_id=collective_id, has_side_effects=True, vmem_limit_bytes=16 * 2**20
        ),
        cost_estimate=pl.CostEstimate(flops=0, bytes_accessed=4 * array.size, transcendentals=0),
    )(array).reshape(8 * rows, columns // 8)


def on_device(
    hidden_in,
    positions,
    expert_ids,
    gate_weights,
    attention_gain,
    w_query,
    w_compress,
    latent_gain,
    w_expand,
    w_output,
    feedforward_gain,
    w_shared_in,
    w_shared_out,
    w_expert_in,
    w_expert_out,
    cotangent,
):
    n_dp = lax.axis_size("dp")
    n_seq = lax.axis_size("seq")
    n_all = n_dp * n_seq
    fast = (n_dp, n_seq) == (4, 8)
    both = ("dp", "seq")
    dp_index = lax.axis_index("dp")
    seq_index = lax.axis_index("seq")
    sequence_count, rows, features = hidden_in.shape
    rows = sequence_count * rows
    length = rows * n_seq
    heads = HEADS // n_seq
    shard = features // n_dp
    expert_count = n_all // 2
    capacity = max(2, rows * TOP * 5 // (expert_count * 3))
    capacity = (capacity + 15) // 16 * 16
    units = SH_FF // n_all
    padded_units = (units + 127) // 128 * 128
    expand_width = heads * (NOPE + VDIM)

    hidden = hidden_in.reshape(rows, features)
    upstream_rows = cotangent.reshape(rows, features)
    upstream_float = upstream_rows.astype(F32)
    id_rows = expert_ids.reshape(rows, TOP)
    gate_table = gate_weights.reshape(rows, TOP)

    gains_own = jnp.concatenate([attention_gain, feedforward_gain, latent_gain])
    named_own = jnp.concatenate(
        [id_rows.T.astype(F32), gate_table.T, positions.reshape(1, rows).astype(F32)]
    )
    query_width = heads * NOPE + 128
    query_part = lax.dynamic_slice_in_dim(w_query, seq_index * heads * QK, heads * QK, 1)
    query_part = query_part.reshape(shard, heads, QK)
    query_part = jnp.concatenate(
        [
            query_part[..., :NOPE].reshape(shard, -1),
            query_part[..., NOPE:].reshape(shard, -1),
            jnp.zeros((shard, 128 - heads * ROPE), BF),
        ],
        axis=1,
    )
    expand_part = lax.dynamic_slice_in_dim(w_expand, seq_index * expand_width, expand_width, 1)
    expand_part = expand_part.reshape(-1, heads, NOPE + VDIM)
    expand_part = jnp.concatenate(
        [part.reshape(-1, heads * NOPE) for part in jnp.split(expand_part, 2, axis=-1)], axis=1
    )
    if fast:
        named_own = jnp.pad(named_own, ((0, 16 - named_own.shape[0]), (0, 0)))
        gains_size = gains_own.shape[0]
        gains_own = jnp.pad(gains_own, (0, 2048 - gains_size)).reshape(16, 128)
        (
            hidden_all, named_all, gains, query_weight, expand_weight, compress_weight,
            output_weight,
        ) = gather_start(
            hidden, named_own, gains_own, query_part, expand_part, w_compress, w_output, 1
        )
        gains = gains.reshape(n_dp, 2048)[:, :gains_size]
        dp_places = (dp_index - jnp.arange(n_dp)) % n_dp
        slot_of_seq = small_take([0, 1, 2, 4, 3, 5, 6, 7], seq_index ^ jnp.arange(n_seq))
        named_all = jnp.stack([named_all[k] for k in (0, 4, 1, 2, 5, 6, 3, 7)])
        positions_all = reorder(named_all[:, 0, 2 * TOP], slot_of_seq)
        named_all = named_all.swapaxes(0, 1).reshape(n_all, 16, rows)
    else:
        hidden_all = lax.all_gather(hidden, "seq", axis=0)
        named_all = lax.all_gather(named_own, both, axis=0)
        positions_all = lax.dynamic_slice_in_dim(named_all, dp_index * n_seq, n_seq, 0)[:, 2 * TOP]
        gains = lax.all_gather(gains_own, "dp", axis=0)
        query_weight = lax.all_gather(query_part, "dp", axis=0)
        expand_weight = lax.all_gather(expand_part, "dp", axis=0)
        compress_weight = lax.all_gather(w_compress, "dp", axis=0)
        output_weight = lax.all_gather(w_output, "dp", axis=0)
    hidden_all = hidden_all.reshape(length, features)
    query_weight = query_weight.reshape(features, query_width)
    expand_weight = expand_weight.reshape(LATENT, expand_width)
    compress_weight = compress_weight.reshape(features, LATENT + ROPE)
    gains = gains.astype(F32)
    first_gain = gains[:, :shard].reshape(features)
    second_gain = gains[:, shard : 2 * shard].reshape(features)
    latent_gain_row = gains[:, 2 * shard :].reshape(LATENT)
    output_weight = output_weight.reshape(HEADS * VDIM, features)
    shared_part = jnp.stack(
        [
            jnp.stack(
                [
                    lax.dynamic_slice_in_dim(
                        w_shared_in, half * SH_FF + (z * n_seq + seq_index) * units, units, 1
                    )
                    for half in range(2)
                ],
                axis=1,
            )
            for z in range(n_dp)
        ]
    )
    shared_in = lax.all_to_all(
        shared_part, "dp", split_axis=0, concat_axis=0, tiled=True
    ).reshape(features, 2, units)
    pad = padded_units - units
    shared_in = jnp.pad(shared_in, ((0, 0), (0, 0), (0, pad))).reshape(features, 2 * padded_units)
    shared_out = lax.dynamic_slice_in_dim(w_shared_out, seq_index * units, units, 0)
    shared_out = jnp.pad(shared_out, ((0, pad), (0, 0)))
    weight_in, weight_out = w_expert_in[0], w_expert_out[0]
    expert = (dp_index * n_seq + seq_index) // 2
    named = named_all[:, :TOP] == expert.astype(F32)
    chosen = jnp.any(named, axis=1)
    gate_rows = jnp.sum(jnp.where(named, named_all[:, TOP : 2 * TOP], 0.0), axis=1)[:, None]
    before = (jnp.arange(rows)[:, None] < jnp.arange(rows)[None, :]).astype(BF)
    place = dot(chosen.astype(BF), before).astype(jnp.int32)
    place = jnp.where(chosen, place, -1)[:, None]

    angles = rotary_angles(positions_all.reshape(length))
    angles = jnp.concatenate([angles] * 4, axis=1)
    cosine_all, sine_all = jnp.cos(angles), jnp.sin(angles)
    normed_all, queries, keys_all, values_all, latent, latent_normed = project(
        hidden_all, first_gain[None], query_weight, compress_weight, latent_gain_row[None],
        expand_weight, cosine_all, sine_all,
    )
    attended_heads, logs = attend(queries, keys_all, values_all)
    if fast:
        attended_all = plane_gather(attended_heads, 9)
        attended = lax.dynamic_slice_in_dim(attended_all, seq_index * rows, rows, 1)
        attended = attended.swapaxes(0, 1).reshape(rows, HEADS * VDIM)
    else:
        attended_all = lax.all_gather(attended_heads, "seq", axis=0)
        attended = lax.all_to_all(
            attended_heads, "seq", split_axis=0, concat_axis=1, tiled=True
        )
    hidden_float = hidden.astype(F32)
    middle = hidden_float + dot(attended, output_weight)
    second_scale = rms_scale(middle)
    moe_rows = (middle * second_scale * second_gain).astype(BF)

    sent = jnp.stack([moe_rows, upstream_rows])
    if not fast:
        sent = lax.all_gather(sent, both, axis=0)
    (
        sent_all, expert_in_grad, expert_out_grad, hidden_units, shared_units, back_parts,
        shared_in_grad, shared_out_grad,
    ) = experts(
        fast, capacity, sent, place, gate_rows, weight_in, weight_out, shared_in, shared_out
    )
    shared_in_grad = shared_in_grad.reshape(2, padded_units, n_dp, shard)[:, :units].astype(BF)
    shared_in_grad = shared_in_grad.reshape(2 * units, n_dp, shard).swapaxes(0, 1)
    gate_grads, out_parts, moe_back, shared_dealt = out_side(
        fast, capacity, back_parts, shared_in_grad, place, gate_rows, hidden_units, sent_all if fast else sent, shared_units,
        weight_out, shared_out,
    )
    if fast:
        gate_grads = reorder(gate_grads.reshape(n_dp, n_seq, rows), dp_places)
        gate_grads = reorder(gate_grads.swapaxes(0, 1), slot_of_seq).swapaxes(0, 1)
        gate_grads = gate_grads.reshape(n_all, 1, rows)
    else:
        moe_back = lax.psum_scatter(
            back_parts.reshape(n_all * rows, features), both, scatter_dimension=0, tiled=True
        )
    moe_back = moe_back.astype(F32)
    gate_grads = lax.all_to_all(gate_grads, both, split_axis=0, concat_axis=0, tiled=True)
    gate_grads = jnp.sum(gate_grads.reshape(expert_count, 2, rows), axis=1)
    gate_gradient = jnp.sum(
        jnp.where(
            id_rows[:, :, None] == jnp.arange(expert_count, dtype=jnp.int32),
            gate_grads.T[:, None, :],
            0.0,
        ),
        axis=-1,
    )
    second_gain_grad = jnp.sum(moe_back * middle * second_scale, axis=0)
    middle_back = upstream_float + norm_backward(moe_back, middle, second_scale, second_gain)
    middle_low = middle_back.astype(BF)
    attended_back = dot_nt(middle_low, output_weight).astype(BF)
    part = features // n_seq
    packed = jnp.concatenate(
        [attended_back.reshape(rows, n_seq, -1), middle_low.reshape(rows, n_seq, part)], axis=2
    ).reshape(rows, -1)
    if fast:
        packed = exchange(packed, 10)
    else:
        packed = lax.all_to_all(packed, "seq", split_axis=1, concat_axis=0, tiled=True)

    query_back, turned_back, key_back, rotary_sum, value_back, out_sum = attend_back(
        fast, queries, keys_all, values_all, packed, logs, cosine_all, sine_all, out_parts
    )
    if not fast:
        out_sum = lax.psum_scatter(
            out_parts.reshape(n_all * rows, features), both, scatter_dimension=0, tiled=True
        )
    block_out = (middle + out_sum.astype(F32)).astype(BF)
    turned_back = sum(turned_back[:, 128 * h : 128 * h + 128] for h in range(heads))
    query_raw_back = jnp.concatenate([query_back, turned_back], axis=1)
    expanded_back = jnp.concatenate([key_back, value_back], axis=1)
    partial_back = partial_terms(
        rows, query_back, turned_back, key_back, value_back, rotary_sum, query_weight, expand_weight
    )
    expand_grad = dot_tn(latent_normed, expanded_back).astype(BF)
    if fast:
        column_grads = column_terms(normed_all, query_raw_back, attended_all, packed, part)
        summed_back, column_grads, latent_grads = tail_scatter(
            partial_back.reshape(n_seq, rows, -1),
            column_grads.reshape(n_dp, shard, -1),
            expand_grad.reshape(n_dp, LATENT // n_dp, -1),
            5,
        )
    else:
        query_grad = dot_tn(normed_all, query_raw_back).astype(BF)
        output_grad = outer(attended_all, packed, part)
        summed_back = lax.psum_scatter(partial_back, "seq", scatter_dimension=0, tiled=True)
    summed_back = summed_back[:, : features + LATENT + ROPE].astype(F32)
    latent_normed_back = summed_back[:, features : features + LATENT]
    own = seq_index * rows

    def mine(array):
        return lax.dynamic_slice_in_dim(array, own, rows, 0)

    latent_own = mine(latent)
    latent_scale_own = rms_scale(latent_own)
    latent_gain_grad = jnp.sum(latent_normed_back * latent_own * latent_scale_own, axis=0)
    latent_back = norm_backward(latent_normed_back, latent_own, latent_scale_own, latent_gain_row)
    half_turn = ROPE // 2
    rotary_back = rotate(
        summed_back[:, features + LATENT :],
        mine(cosine_all)[:, :half_turn],
        -mine(sine_all)[:, :half_turn],
    )
    compressed_back = jnp.concatenate([latent_back, rotary_back], axis=-1).astype(BF)
    width = (LATENT + ROPE) // n_seq
    if fast:
        compressed_back_all = plane_gather(jnp.pad(compressed_back, ((0, 0), (0, 64))), 6)
        compressed_back_all = compressed_back_all[:, :, : LATENT + ROPE]
    else:
        compressed_back_all = lax.all_gather(compressed_back, "seq", axis=0)
    compressed_back_all = compressed_back_all.reshape(length, LATENT + ROPE)
    compress_grad = dot_tn(
        normed_all, lax.dynamic_slice_in_dim(compressed_back_all, seq_index * width, width, 1)
    )
    normed_back = summed_back[:, :features] + dot_nt(compressed_back, compress_weight)
    first_scale = rms_scale(hidden_float)
    first_gain_grad = jnp.sum(normed_back * hidden_float * first_scale, axis=0)
    hidden_gradient = (
        middle_back + norm_backward(normed_back, hidden_float, first_scale, first_gain)
    ).astype(BF)

    gain_grads = jnp.concatenate([first_gain_grad, second_gain_grad, latent_gain_grad])
    bit = 1
    while bit < n_seq:
        gain_grads = gain_grads + lax.ppermute(
            gain_grads, "seq", [(i, i ^ bit) for i in range(n_seq)]
        )
        bit *= 2
    bit = 1
    while bit < n_dp:
        gain_grads = gain_grads + lax.ppermute(
            gain_grads, "dp", [(i, i ^ bit) for i in range(n_dp)]
        )
        bit *= 2
    latent_shard = LATENT // n_dp

    def gain_part(start, size):
        return lax.dynamic_slice_in_dim(gain_grads, start + dp_index * size, size, 0)

    def over_dp(grad):
        total = lax.psum_scatter(grad, "dp", scatter_dimension=0, tiled=True)
        return lax.all_gather(total.astype(BF), "seq", axis=0)

    def in_heads(found, first, second):
        height, cut = found.shape[1], heads * first
        found = jnp.concatenate(
            [
                found[:, :, :cut].reshape(n_seq, height, heads, first),
                found[:, :, cut : cut + heads * second].reshape(n_seq, height, heads, second),
            ],
            axis=-1,
        )
        return found.transpose(1, 0, 2, 3).reshape(height, -1).astype(F32)

    def columns(found):
        return found.transpose(1, 0, 2).reshape(found.shape[1], -1).astype(F32)

    if fast:
        compress_grad = jnp.pad(compress_grad.astype(BF), ((0, 0), (0, 128 - width)))
        small_grads, column_grads, latent_grads = sum_grads(
            compress_grad.reshape(n_dp, shard, 128), column_grads, latent_grads, 7
        )
        query_out, expand_out, output_out, compress_out = layout_grads(
            column_grads, latent_grads, small_grads, width
        )
    else:
        query_out = in_heads(over_dp(query_grad), NOPE, ROPE)
        expand_out = in_heads(over_dp(expand_grad), NOPE, VDIM)
        output_out = columns(over_dp(output_grad))
        compress_out = columns(over_dp(compress_grad))
    if not fast:
        shared_dealt = lax.all_to_all(
            shared_in_grad, "dp", split_axis=0, concat_axis=0, tiled=True
        )
    shared_in_out = lax.all_gather(tie(shared_dealt, query_back), "seq", axis=0)
    shared_in_out = shared_layout(shared_in_out, units)
    shared_out_out = lax.all_gather(
        shared_out_grad[:units].astype(BF), "seq", axis=0, tiled=True
    ).astype(F32)
    return (
        block_out.reshape(hidden_in.shape),
        hidden_gradient.reshape(hidden_in.shape),
        gate_gradient.reshape(gate_weights.shape),
        gain_part(0, shard),
        query_out,
        compress_out,
        gain_part(2 * features, latent_shard),
        expand_out,
        output_out,
        gain_part(features, shard),
        shared_in_out,
        shared_out_out,
        expert_in_grad[None],
        expert_out_grad[None],
    )


def solution(mesh):
    token = P("dp", "seq", None)
    row = P("dp", None)
    half = P(("dp", "seq"), None, None)
    return jax.shard_map(
        on_device,
        mesh=mesh,
        in_specs=(
            token, P("dp", "seq"), token, token, P("dp"), row, row, P("dp"), row, row,
            P("dp"), row, row, half, half, token,
        ),
        out_specs=(
            token, token, token, P("dp"), row, row, P("dp"), row, row, P("dp"), row, row,
            half, half,
        ),
        check_vma=False,
    )
```
